32 devices in a mesh: batch: 16 (over z, y, x), tm: 2 (over core).
Axes of the slice: x: 2, y: 2, z: 4, core: 2. Of those that a mesh axis runs over, the one named last changes fastest.
Arguments:
- tokens: bfloat16 [16, 2048, 384], P('batch', 'tm'), may hold values from -6 to 6
- cotangent: bfloat16 [16, 2048, 384], P('batch', 'tm'), may hold values from -6 to 6
- sample_ids: int32 [16, 2048], P('batch'), may hold values from 0 to 3, as said below
- pad_flags: int32 [16, 2048], P('batch'), may hold values from 0 to 1, as said below
- offsets: int32 [16, 2048], P('batch'), may hold values from 0 to 63
- w_qkv: float32 [384, 1152], P('batch'), may hold values from -0.3125 to 0.3125
- w_out: float32 [384, 384], P('batch'), may hold values from -1.25 to 1.25
- w_gate_up: float32 [384, 2048], P('batch'), may hold values from -0.3125 to 0.3125
- w_down: float32 [1024, 384], P('batch'), may hold values from -0.1875 to 0.1875
- gains: float32 [2, 384], P(None, 'batch'), may hold values from 0.25 to 2.6, as said below
- m_qkv: float32 [384, 1152], P('batch'), may hold values from -0.0048828125 to 0.0048828125
- m_out: float32 [384, 384], P('batch'), may hold values from -0.0048828125 to 0.0048828125
- m_gate_up: float32 [384, 2048], P('batch'), may hold values from -0.0048828125 to 0.0048828125
- m_down: float32 [1024, 384], P('batch'), may hold values from -0.0048828125 to 0.0048828125
- m_gains: float32 [2, 384], P(None, 'batch'), may hold values from -0.01953125 to 0.01953125
- v_qkv: float32 [384, 1152], P('batch'), may hold values from 5.648952e-07 to 2.2595807e-06
- v_out: float32 [384, 384], P('batch'), may hold values from 5.648952e-07 to 2.2595807e-06
- v_gate_up: float32 [384, 2048], P('batch'), may hold values from 5.648952e-07 to 2.2595807e-06
- v_down: float32 [1024, 384], P('batch'), may hold values from 5.648952e-07 to 2.2595807e-06
- v_gains: float32 [2, 384], P(None, 'batch'), may hold values from 9.038323e-06 to 3.615329e-05
Outputs:
- result: bfloat16 [16, 2048, 384], P('batch', 'tm')
- grad_tokens: bfloat16 [16, 2048, 384], P('batch', 'tm')
- grad_norm: float32 [], replicated
- new_m_qkv: float32 [384, 1152], P('batch')
- new_m_out: float32 [384, 384], P('batch')
- new_m_gate_up: float32 [384, 2048], P('batch')
- new_m_down: float32 [1024, 384], P('batch')
- new_m_gains: float32 [2, 384], P(None, 'batch')
- new_v_qkv: float32 [384, 1152], P('batch')
- new_v_out: float32 [384, 384], P('batch')
- new_v_gate_up: float32 [384, 2048], P('batch')
- new_v_down: float32 [1024, 384], P('batch')
- new_v_gains: float32 [2, 384], P(None, 'batch')
- new_w_qkv: float32 [384, 1152], P('batch')
- new_w_out: float32 [384, 384], P('batch')
- new_w_gate_up: float32 [384, 2048], P('batch')
- new_w_down: float32 [1024, 384], P('batch')
- new_gains: float32 [2, 384], P(None, 'batch')
- copy_qkv: bfloat16 [384, 1152], P('batch')
- copy_out: bfloat16 [384, 384], P('batch')
- copy_gate_up: bfloat16 [384, 2048], P('batch')
- copy_down: bfloat16 [1024, 384], P('batch')
- copy_gains: bfloat16 [2, 384], P(None, 'batch')
The draws below stay inside these ranges and needn't reach their ends.
Inputs may be any that keep to these rules, and one draw needn't show every extreme that they name: `sample_ids`: along each row the numbers never fall and start at 0; the series numbered 1 covers at least positions 512 to 1535. `pad_flags`: each row ends in 1 to 256 padded slots, and no other slot is padded. Positive gains.
All inputs are finite; a program needn't handle non-finite values.
Results may differ from the reference program's by a relative error of at most 0.013.
The reference program's roundings to bfloat16 on the way count: a program that leaves them out, or rounds other values in their place, can miss the bound.
Values may be sent and summed in bfloat16 or wider, within the bound.
No kernel may reach another device: no remote copies, remote signals or barrier semaphores. Data moves between devices by JAX's collectives and lax.ppermute only.
A program may use at most 320 MiB of HBM per device.

```python
import math
from functools import partial
import jax
import jax.numpy as jnp
from jax import lax

D = 384
FF = 1024
HEADS = 6
HD = 64
SEQ = 2048
STEP = 3
ROWS = 16
NPARAM = 1770240


def draw_sample_ids(key, part):
    key = jax.random.fold_in(key, 11)
    first_key, second_key, third_key = jax.random.split(key, 3)
    cut_one = jax.random.randint(first_key, (ROWS, 1), SEQ // 8, SEQ // 4)
    cut_two = jax.random.randint(second_key, (ROWS, 1), 3 * SEQ // 4, 7 * SEQ // 8)
    cut_three = jax.random.randint(third_key, (ROWS, 1), 7 * SEQ // 8, SEQ)
    places = jnp.arange(SEQ, dtype=jnp.int32)[None, :]
    return (places >= cut_one).astype(jnp.int32) + (places >= cut_two).astype(jnp.int32) + (places >= cut_three).astype(jnp.int32)


def draw_pad_flags(key, part):
    key = jax.random.fold_in(key, 23)
    counts = jax.random.randint(key, (ROWS, 1), 1, SEQ // 8 + 1)
    places = jnp.arange(SEQ, dtype=jnp.int32)[None, :]
    return (places >= SEQ - counts).astype(jnp.int32)


def draw_gains(key, part):
    key = jax.random.fold_in(key, 37)
    ramp = jnp.arange(D, dtype=jnp.float32)[None, :] / (D - 1)
    noise = jax.random.uniform(key, (2, D), jnp.float32, 0.8, 1.2)
    return 0.6 * jnp.exp(ramp * math.log(3.0)) * noise


def set_ends(result, stream_key, least, high):
    dims = result.shape
    place = [jax.random.randint(jax.random.fold_in(stream_key, axis), (), 0, dims[axis]) for axis in range(len(dims))]
    result = result.at[tuple(place)].set(least)
    longest = dims.index(max(dims))
    place[longest] = (place[longest] + 1) % dims[longest]
    return result.at[tuple(place)].set(high)


def levels(own_key, dims, cuts, smallest, top_value):
    loudness, own = 1.0, jax.random.fold_in(own_key, 6)
    for position, blocks in cuts:
        draws = jnp.exp(jax.random.uniform(jax.random.fold_in(own, position), (blocks,), jnp.float32, smallest / len(cuts), top_value / len(cuts)))
        loudness = loudness * jnp.repeat(draws, dims[position] // blocks).reshape([-1 if axis == position else 1 for axis in range(len(dims))])
    return loudness


def normal_values(key, extent, scale, most, pieces=(), kind=jnp.bfloat16):
    gain = levels(key, extent, pieces, -0.22, 0.18) if pieces else 1.0
    result = jax.random.normal(key, extent, jnp.float32) * scale * gain
    return jnp.minimum(jnp.maximum(result, -most), most).astype(kind)


def setup_inputs(seed: int = 0) -> dict:
    key_of = jax.random.split(jax.random.key(seed), 21)
    return {
        "tokens": normal_values(key_of[0], (ROWS, SEQ, D), 1.0, 6.0, ((0, 16), (1, 2))),
        "cotangent": normal_values(key_of[1], (ROWS, SEQ, D), 1.0, 6.0, ((0, 16), (1, 2))),
        "sample_ids": draw_sample_ids(jax.random.fold_in(key_of[20], 71), 0),
        "pad_flags": draw_pad_flags(jax.random.fold_in(key_of[20], 71), 0),
        "offsets": set_ends(jax.random.randint(key_of[4], (ROWS, SEQ), 0, 64), jax.random.fold_in(key_of[4], 1), 0, 63).astype(jnp.int32),
        "w_qkv": normal_values(key_of[5], (D, 3 * D), D ** -0.5, 0.3125, ((0, 16),), jnp.float32),
        "w_out": normal_values(key_of[6], (D, D), (D // 16) ** -0.5, 1.25, ((0, 16),), jnp.float32),
        "w_gate_up": normal_values(key_of[7], (D, 2 * FF), D ** -0.5, 0.3125, ((0, 16),), jnp.float32),
        "w_down": normal_values(key_of[8], (FF, D), FF ** -0.5, 0.1875, ((0, 16),), jnp.float32),
        "gains": draw_gains(jax.random.fold_in(key_of[20], 71), 0),
        "m_qkv": normal_values(key_of[10], (D, 3 * D), (NPARAM ** -0.5), 0.0048828125, ((0, 16),), jnp.float32),
        "m_out": normal_values(key_of[11], (D, D), (NPARAM ** -0.5), 0.0048828125, ((0, 16),), jnp.float32),
        "m_gate_up": normal_values(key_of[12], (D, 2 * FF), (NPARAM ** -0.5), 0.0048828125, ((0, 16),), jnp.float32),
        "m_down": normal_values(key_of[13], (FF, D), (NPARAM ** -0.5), 0.0048828125, ((0, 16),), jnp.float32),
        "m_gains": normal_values(key_of[14], (2, D), (4 * NPARAM ** -0.5), 0.01953125, ((1, 16),), jnp.float32),
        "v_qkv": jnp.clip(jnp.exp(math.log(2.2595806967729004e-06) - 1.3862944 * jax.random.uniform(key_of[15], (D, 3 * D), jnp.float32) ** levels(key_of[15], (D, 3 * D), ((0, 16),), -0.2, 0.2)), 5.648951741932251e-07, 2.2595806967729004e-06),
        "v_out": jnp.clip(jnp.exp(math.log(2.2595806967729004e-06) - 1.3862944 * jax.random.uniform(key_of[16], (D, D), jnp.float32) ** levels(key_of[16], (D, D), ((0, 16),), -0.2, 0.2)), 5.648951741932251e-07, 2.2595806967729004e-06),
        "v_gate_up": jnp.clip(jnp.exp(math.log(2.2595806967729004e-06) - 1.3862944 * jax.random.uniform(key_of[17], (D, 2 * FF), jnp.float32) ** levels(key_of[17], (D, 2 * FF), ((0, 16),), -0.2, 0.2)), 5.648951741932251e-07, 2.2595806967729004e-06),
        "v_down": jnp.clip(jnp.exp(math.log(2.2595806967729004e-06) - 1.3862944 * jax.random.uniform(key_of[18], (FF, D), jnp.float32) ** levels(key_of[18], (FF, D), ((0, 16),), -0.2, 0.2)), 5.648951741932251e-07, 2.2595806967729004e-06),
        "v_gains": jnp.clip(jnp.exp(math.log(3.6153291148366407e-05) - 1.3862944 * jax.random.uniform(key_of[19], (2, D), jnp.float32) ** levels(key_of[19], (2, D), ((1, 16),), -0.2, 0.2)), 9.038322787091602e-06, 3.6153291148366407e-05),
    }


@jax.custom_vjp
def low(v):
    return lax.optimization_barrier(v.astype(jnp.bfloat16)).astype(jnp.float32)

@jax.custom_vjp
def low_back(v):
    return v

def low_keep(v):
    return (low(v), None)

def low_pass(kept, grad):
    return (grad,)

def back_keep(v):
    return (v, None)

def back_low(kept, grad):
    return (low(grad),)
low.defvjp(low_keep, low_pass)
low_back.defvjp(back_keep, back_low)
norm_eps = 1e-06
beta_one = 0.5
beta_two = 0.5
adam_eps = 1e-08
decay_rate = 0.1
clip_limit = 1.0
masked_score = -1e+30
highest = lax.Precision.HIGHEST

def rms_scale(values):
    return lax.rsqrt(lax.optimization_barrier(jnp.mean(values * values, axis=-1, keepdims=True)) + norm_eps)

def rotary_tables(positions):
    frequency = jnp.exp(jnp.arange(HD // 2, dtype=jnp.float32) * (-2.0 * math.log(10000.0) / HD))
    angles = positions.astype(jnp.float32)[..., None] * frequency
    return (jnp.cos(angles)[:, :, None, :], jnp.sin(angles)[:, :, None, :])

def rotary(field, cosine, sine):
    half_size = field.shape[-1] // 2
    first_half = field[..., :half_size]
    second_half = field[..., half_size:]
    return jnp.concatenate([first_half * cosine - second_half * sine, second_half * cosine + first_half * sine], axis=-1)

def group_layer(weights, batch_in):
    attn_in, attn_out, ffn_in, ffn_out, gain_pair = weights
    inputs, group_ids, group_pads, group_offsets = batch_in
    rows_here = inputs.shape[0]
    normed = low(inputs * rms_scale(inputs) * gain_pair[0])
    projected = low_back(jnp.einsum('rtd,de->rte', normed, attn_in, precision=highest))
    positions = jnp.arange(SEQ, dtype=jnp.int32)[None, :] + group_offsets
    cosine, sine = rotary_tables(positions)
    split_heads = projected.reshape(rows_here, SEQ, 3, HEADS, HD)
    queries = low(rotary(split_heads[:, :, 0], cosine, sine))
    keys_all = low(rotary(split_heads[:, :, 1], cosine, sine))
    values_all = low(split_heads[:, :, 2])
    scores = low_back(jnp.einsum('rqhd,rkhd->rhqk', queries, keys_all, precision=highest) * HD ** (-0.5))
    allowed = (group_ids[:, :, None] == group_ids[:, None, :]) & (group_pads[:, :, None] == group_pads[:, None, :])
    scores = jnp.where(allowed[:, None], scores, masked_score)
    attend = low(jax.nn.softmax(scores, axis=-1))
    mixed = low(low_back(jnp.einsum('rhqk,rkhd->rqhd', attend, values_all, precision=highest)))
    mixed = mixed.reshape(rows_here, SEQ, D)
    branch = low_back(jnp.einsum('rtd,de->rte', mixed, attn_out, precision=highest))
    middle = inputs + branch
    normed_two = low(middle * rms_scale(middle) * gain_pair[1])
    gate_up = low_back(jnp.einsum('rtd,de->rte', normed_two, ffn_in, precision=highest))
    hidden_act = low(jax.nn.silu(gate_up[..., :FF]) * gate_up[..., FF:])
    ffn_result = low_back(jnp.einsum('rtf,fd->rtd', hidden_act, ffn_out, precision=highest))
    keep = (1 - group_pads).astype(inputs.dtype)[..., None]
    return keep * (middle + ffn_result)

def grouped(array):
    return array.reshape((ROWS // 4, 4) + array.shape[1:])

def forward(inputs, attn_in, attn_out, ffn_in, ffn_out, gain_pair, sample_ids, pad_flags, offsets):
    weights = (low(attn_in), low(attn_out), low(ffn_in), low(ffn_out), low(gain_pair))
    stepper = jax.checkpoint(partial(group_layer, weights))
    outcome = lax.map(stepper, (grouped(inputs), grouped(sample_ids), grouped(pad_flags), grouped(offsets)))
    return outcome.reshape(inputs.shape)

def adam_update(master, grad, first, second, rate, decay):
    first_new = beta_one * first + (1.0 - beta_one) * grad
    second_new = beta_two * second + (1.0 - beta_two) * grad * grad
    direction = first_new / (1.0 - beta_one ** STEP) / (jnp.sqrt(second_new / (1.0 - beta_two ** STEP)) + adam_eps)
    return (first_new, second_new, master - rate * (direction + decay * master))

def square_total(arrays):
    total = jnp.sum(arrays[0] * arrays[0])
    for item in arrays[1:]:
        total = total + jnp.sum(item * item)
    return total

def reference(tokens, cotangent, sample_ids, pad_flags, offsets, w_qkv, w_out, w_gate_up, w_down, gains, m_qkv, m_out, m_gate_up, m_down, m_gains, v_qkv, v_out, v_gate_up, v_down, v_gains):

    def layer_fn(inputs, attn_in, attn_out, ffn_in, ffn_out, gain_pair):
        return forward(inputs, attn_in, attn_out, ffn_in, ffn_out, gain_pair, sample_ids, pad_flags, offsets)
    outcome, pullback = jax.vjp(layer_fn, tokens.astype(jnp.float32), w_qkv, w_out, w_gate_up, w_down, gains)
    grads = pullback(cotangent.astype(jnp.float32))
    weight_grads = grads[1:]
    grad_norm = jnp.sqrt(square_total(weight_grads))
    factor = clip_limit / jnp.maximum(grad_norm, clip_limit)
    masters = (w_qkv, w_out, w_gate_up, w_down, gains)
    firsts = (m_qkv, m_out, m_gate_up, m_down, m_gains)
    seconds = (v_qkv, v_out, v_gate_up, v_down, v_gains)
    rates = (D ** (-0.5), 4.0 * D ** (-0.5), D ** (-0.5), FF ** (-0.5), 0.5)
    decays = (decay_rate, decay_rate, decay_rate, decay_rate, 0.0)
    new_first = []
    new_second = []
    new_master = []
    for index in range(5):
        first_new, second_new, master_new = adam_update(masters[index], factor * weight_grads[index], firsts[index], seconds[index], rates[index], decays[index])
        new_first.append(first_new)
        new_second.append(second_new)
        new_master.append(master_new)
    copies = [item.astype(jnp.bfloat16) for item in new_master]
    return (outcome.astype(jnp.bfloat16), grads[0].astype(jnp.bfloat16), grad_norm, new_first[0], new_first[1], new_first[2], new_first[3], new_first[4], new_second[0], new_second[1], new_second[2], new_second[3], new_second[4], new_master[0], new_master[1], new_master[2], new_master[3], new_master[4], copies[0], copies[1], copies[2], copies[3], copies[4])
```

```python
import math
from functools import partial

import jax
import jax.numpy as jnp
from jax import lax
from jax.sharding import PartitionSpec as P

D = 384
FF = 1024
HEADS = 6
HD = 64
STEP = 3


norm_eps = 1e-06
beta_one = 0.5
beta_two = 0.5
adam_eps = 1e-08
decay_rate = 0.1
clip_limit = 1.0
masked_score = -1e30


def rms_scale(values):
    return lax.rsqrt(jnp.mean(values * values, axis=-1, keepdims=True) + norm_eps)


def norm_back(grad_normed, values, scale):
    return scale * grad_normed - values * scale * scale * scale * jnp.mean(
        grad_normed * values, axis=-1, keepdims=True
    )


def rotary_tables(positions):
    frequency = jnp.exp(jnp.arange(HD // 2, dtype=jnp.float32) * (-2.0 * math.log(10000.0) / HD))
    angles = positions.astype(jnp.float32)[..., None] * frequency
    return (jnp.cos(angles)[:, :, None, :], jnp.sin(angles)[:, :, None, :])


def rotary(field, cosine, sine, direction):
    half_size = field.shape[-1] // 2
    first_half = field[..., :half_size]
    second_half = field[..., half_size:]
    return jnp.concatenate(
        [
            first_half * cosine - direction * second_half * sine,
            second_half * cosine + direction * first_half * sine,
        ],
        axis=-1,
    )


def adam_update(master, grad, first, second, rate, decay):
    first_new = beta_one * first + (1.0 - beta_one) * grad
    second_new = beta_two * second + (1.0 - beta_two) * grad * grad
    direction = (
        first_new
        / (1.0 - beta_one**STEP)
        / (jnp.sqrt(second_new / (1.0 - beta_two**STEP)) + adam_eps)
    )
    return (first_new, second_new, master - rate * (direction + decay * master))


def square_total(arrays):
    total = jnp.sum(arrays[0] * arrays[0])
    for item in arrays[1:]:
        total = total + jnp.sum(item * item)
    return total


def bit_groups(count):
    groups = []
    low, bits = 0, count.bit_length() - 1
    while low < bits:
        width = min(2, bits - low)
        groups.append((low, width))
        low += width
    return groups


def permute_batch(value, flip, count):
    return lax.ppermute(value, "batch", [(i, i ^ flip) for i in range(count)])


def swap_tm(value):
    return lax.ppermute(value, "tm", [(0, 1), (1, 0)])


def gather_batch(chunk, owner, count):
    held = chunk[None]
    for low, width in reversed(bit_groups(count)):
        pieces = [held] + [permute_batch(held, k << low, count) for k in range(1, 1 << width)]
        for bit in range(width):
            flag = ((owner >> (low + bit)) & 1) == 1
            pieces = [
                jnp.where(flag, pieces[p ^ (1 << bit)], pieces[p]) for p in range(1 << width)
            ]
        held = jnp.stack(pieces, axis=1).reshape((-1,) + chunk.shape)
    return held


def scatter_sum(parts, owner, count):
    held = parts
    rest = parts.shape[1:]
    for low, width in bit_groups(count):
        fan = 1 << width
        view = held.reshape((-1, fan) + rest)
        mine = (owner >> low) & (fan - 1)
        total = lax.dynamic_index_in_dim(view, mine, 1, keepdims=False).astype(jnp.float32)
        got = []
        for k in range(1, fan):
            piece = lax.dynamic_index_in_dim(view, mine ^ k, 1, keepdims=False)
            got.append(permute_batch(piece.astype(jnp.bfloat16), k << low, count))
        for item in got:
            total = total + item.astype(jnp.float32)
        held = total
    return held.reshape(rest)


def sum_all(value, count):
    value = value + swap_tm(value)
    for low, width in bit_groups(count):
        pieces = [value] + [permute_batch(value, k << low, count) for k in range(1, 1 << width)]
        while len(pieces) > 1:
            pieces = [pieces[i] + pieces[i + 1] for i in range(0, len(pieces), 2)]
        value = pieces[0]
    return value


def slabs(matrix):
    rows, columns = matrix.shape
    return matrix.reshape(rows, columns // 128, 128).transpose(1, 0, 2)


def unslab(stack):
    count, rows, _ = stack.shape
    return stack.transpose(1, 0, 2).reshape(rows, count * 128)


def pad_rows(array, rows):
    return jnp.pad(array, ((0, rows - array.shape[0]), (0, 0)))


def per_device(
    count,
    tokens,
    cotangent,
    sample_ids,
    pad_flags,
    offsets,
    w_qkv,
    w_out,
    w_gate_up,
    w_down,
    gains,
    m_qkv,
    m_out,
    m_gate_up,
    m_down,
    m_gains,
    v_qkv,
    v_out,
    v_gate_up,
    v_down,
    v_gains,
):
    bf16 = jnp.bfloat16
    f32 = jnp.float32
    owner = lax.axis_index("batch")
    core = lax.axis_index("tm")
    shard = w_qkv.shape[0]
    shard_down = w_down.shape[0]
    low_qkv, low_out, low_gate_up, low_down = (
        slabs(w_qkv.astype(bf16)),
        slabs(w_out.astype(bf16)),
        slabs(w_gate_up.astype(bf16)),
        slabs(w_down.astype(bf16)),
    )
    low_gains = jnp.pad(gains.astype(bf16).reshape(1, -1), ((0, 0), (0, 128 - 2 * shard)))
    first_rows = -(-(5 * shard + 1) // 16) * 16
    first_slabs = jnp.concatenate([low_qkv, low_out[:1]], axis=0).reshape(2, 5 * shard, 128)
    first_send = jnp.where(core == 0, first_slabs[0], first_slabs[1])
    first_send = pad_rows(jnp.concatenate([first_send, low_gains], axis=0), first_rows)
    second_slabs = jnp.concatenate([low_out[1:], low_gate_up], axis=0).reshape(2, 9 * shard, 128)
    half_down = shard_down // 2
    down_halves = low_down.reshape(3, 2, half_down, 128).transpose(1, 0, 2, 3).reshape(2, 3 * half_down, 128)
    second_send = jnp.where(
        core == 0,
        jnp.concatenate([second_slabs[0], down_halves[0]], axis=0),
        jnp.concatenate([second_slabs[1], down_halves[1]], axis=0),
    )
    second_rows = -(-second_send.shape[0] // 16) * 16
    second_send = pad_rows(second_send, second_rows)

    def whole(send):
        mine = gather_batch(send, owner, count)
        other = swap_tm(mine)
        return jnp.where(core == 0, mine, other), jnp.where(core == 0, other, mine)

    first_low, first_high = whole(first_send)
    second_low, second_high = whole(second_send)

    def take(source, start, number, rows):
        return (
            source[:, start : start + number * rows]
            .reshape(count, number, rows, 128)
            .transpose(1, 0, 2, 3)
            .reshape(number, count * rows, 128)
        )

    first_all = jnp.concatenate(
        [take(first_low, 0, 5, shard), take(first_high, 0, 5, shard)], axis=0
    )
    second_all = jnp.concatenate(
        [take(second_low, 0, 9, shard), take(second_high, 0, 9, shard)], axis=0
    )
    attn_in = unslab(first_all[:9])
    attn_out = unslab(jnp.concatenate([first_all[9:], second_all[:2]], axis=0))
    ffn_in = unslab(second_all[2:])
    down_at = 9 * shard
    down_parts = [
        item[:, down_at : down_at + 3 * half_down].reshape(count, 3, half_down, 128)
        for item in (second_low, second_high)
    ]
    ffn_out = jnp.stack(down_parts, axis=1).transpose(0, 1, 3, 2, 4).reshape(count * shard_down, D)
    gain_pair = (
        first_low[:, 5 * shard, : 2 * shard].reshape(count, 2, shard).transpose(1, 0, 2).reshape(2, D)
    )
    gain_one = gain_pair[0].astype(f32)
    gain_two = gain_pair[1].astype(f32)
    rows_dev, local_len, width = tokens.shape
    seq_len = sample_ids.shape[1]
    start = lax.axis_index("tm") * local_len
    local_ids = lax.dynamic_slice_in_dim(sample_ids, start, local_len, 1)
    local_pads = lax.dynamic_slice_in_dim(pad_flags, start, local_len, 1)
    local_offsets = lax.dynamic_slice_in_dim(offsets, start, local_len, 1)
    positions = start + jnp.arange(local_len, dtype=jnp.int32)[None, :] + local_offsets
    cosine, sine = rotary_tables(positions)
    score_scale = HD ** (-0.5)
    allowed = (
        (local_ids[:, :, None] == sample_ids[:, None, :])
        & (local_pads[:, :, None] == pad_flags[:, None, :])
    )[:, None]
    inputs = tokens.astype(f32)
    scale_one = rms_scale(inputs)
    normed = (inputs * scale_one * gain_one).astype(bf16)
    projected = jnp.einsum("rtd,de->rte", normed, attn_in, preferred_element_type=f32)
    split_heads = projected.reshape(rows_dev, local_len, 3, HEADS, HD)
    queries = rotary(split_heads[:, :, 0], cosine, sine, 1.0).astype(bf16)
    keys_here = (
        rotary(split_heads[:, :, 1], cosine, sine, 1.0).astype(bf16).reshape(rows_dev, local_len, D)
    )
    values_here = split_heads[:, :, 2].astype(bf16).reshape(rows_dev, local_len, D)
    both_here = jnp.stack([keys_here, values_here])
    both_there = swap_tm(both_here)
    keys_flat, values_flat = jnp.where(
        core == 0,
        jnp.concatenate([both_here, both_there], axis=2),
        jnp.concatenate([both_there, both_here], axis=2),
    )
    keys_all = keys_flat.reshape(rows_dev, seq_len, HEADS, HD)
    values_all = values_flat.reshape(rows_dev, seq_len, HEADS, HD)

    def scores_of():
        raw_scores = (
            jnp.einsum("rqhd,rkhd->rhqk", queries, keys_all, preferred_element_type=f32)
            * score_scale
        )
        return jnp.where(allowed, raw_scores, masked_score)

    scores = scores_of()
    top_score = jnp.max(scores, axis=-1, keepdims=True)
    exp_scores = jnp.exp(scores - top_score)
    exp_total = jnp.sum(exp_scores, axis=-1, keepdims=True)
    log_total = top_score + jnp.log(exp_total)
    attend_low = (exp_scores / exp_total).astype(bf16)
    mixed = jnp.einsum("rhqk,rkhd->rqhd", attend_low, values_all, preferred_element_type=f32)
    mixed = mixed.astype(bf16).reshape(rows_dev, local_len, D)
    branch = jnp.einsum("rtd,de->rte", mixed, attn_out, preferred_element_type=f32)
    middle = inputs + branch
    scale_two = rms_scale(middle)
    normed_two = (middle * scale_two * gain_two).astype(bf16)
    gate_up = jnp.einsum("rtd,de->rte", normed_two, ffn_in, preferred_element_type=f32)
    gate_part = gate_up[..., :FF]
    up_part = gate_up[..., FF:]
    sigmoid_gate = jax.nn.sigmoid(gate_part)
    hidden_act = (gate_part * sigmoid_gate * up_part).astype(bf16)
    ffn_result = jnp.einsum("rtf,fd->rtd", hidden_act, ffn_out, preferred_element_type=f32)
    keep = (1 - local_pads).astype(f32)[..., None]
    result = (keep * (middle + ffn_result)).astype(bf16)
    upstream = cotangent.astype(f32) * keep
    upstream_low = upstream.astype(bf16)
    grad_ffn_out = jnp.einsum("rtf,rtd->fd", hidden_act, upstream_low, preferred_element_type=f32)
    grad_hidden = jnp.einsum("rtd,fd->rtf", upstream_low, ffn_out, preferred_element_type=f32)
    grad_up = grad_hidden * gate_part * sigmoid_gate
    grad_gate = grad_hidden * up_part * sigmoid_gate * (1.0 + gate_part * (1.0 - sigmoid_gate))
    gate_up_low = jnp.concatenate([grad_gate, grad_up], axis=-1).astype(bf16)
    grad_ffn_in = jnp.einsum("rtd,rte->de", normed_two, gate_up_low, preferred_element_type=f32)
    grad_normed_two = jnp.einsum("rte,de->rtd", gate_up_low, ffn_in, preferred_element_type=f32)
    grad_gain_two = jnp.sum(grad_normed_two * middle * scale_two, axis=(0, 1))
    grad_middle = upstream + norm_back(grad_normed_two * gain_two, middle, scale_two)
    middle_low = grad_middle.astype(bf16)
    grad_attn_out = jnp.einsum("rtd,rte->de", mixed, middle_low, preferred_element_type=f32)
    grad_mixed = jnp.einsum("rte,de->rtd", middle_low, attn_out, preferred_element_type=f32)
    grad_mixed = grad_mixed.astype(bf16).reshape(rows_dev, local_len, HEADS, HD)
    attend = jnp.exp(scores_of() - log_total)
    grad_attend = jnp.einsum("rqhd,rkhd->rhqk", grad_mixed, values_all, preferred_element_type=f32)
    grad_scores = (
        attend * (grad_attend - jnp.sum(attend * grad_attend, axis=-1, keepdims=True))
    ).astype(bf16)
    grad_queries = (
        jnp.einsum("rhqk,rkhd->rqhd", grad_scores, keys_all, preferred_element_type=f32)
        * score_scale
    )
    keys_part = (
        jnp.einsum("rhqk,rqhd->rkhd", grad_scores, queries, preferred_element_type=f32)
        * score_scale
    )
    values_part = jnp.einsum(
        "rhqk,rqhd->rkhd", attend.astype(bf16), grad_mixed, preferred_element_type=f32
    )
    parts = jnp.stack([keys_part.reshape(rows_dev, seq_len, D), values_part.reshape(rows_dev, seq_len, D)])
    there = lax.dynamic_slice_in_dim(parts, (1 - core) * local_len, local_len, 2).astype(bf16)
    here = lax.dynamic_slice_in_dim(parts, start, local_len, 2)
    grad_keys, grad_values = here + swap_tm(there).astype(f32)
    grad_query_pre = rotary(grad_queries, cosine, sine, -1.0)
    grad_key_pre = rotary(grad_keys.reshape(rows_dev, local_len, HEADS, HD), cosine, sine, -1.0)
    qkv_low = jnp.concatenate(
        [
            grad_query_pre.reshape(rows_dev, local_len, D),
            grad_key_pre.reshape(rows_dev, local_len, D),
            grad_values,
        ],
        axis=-1,
    ).astype(bf16)
    grad_attn_in = jnp.einsum("rtd,rte->de", normed, qkv_low, preferred_element_type=f32)
    grad_normed = jnp.einsum("rte,de->rtd", qkv_low, attn_in, preferred_element_type=f32)
    grad_gain_one = jnp.sum(grad_normed * inputs * scale_one, axis=(0, 1))
    grad_tokens = (grad_middle + norm_back(grad_normed * gain_one, inputs, scale_one)).astype(bf16)
    grad_gains = jnp.stack([grad_gain_one, grad_gain_two], axis=0)
    column_one, column_two = [
        jnp.pad(item[:, None], ((0, 0), (0, 127)))[None] for item in (grad_gain_one, grad_gain_two)
    ]

    def reduce(halves):
        keep = jnp.where(core == 0, halves[0], halves[1])
        give = jnp.where(core == 0, halves[1], halves[0]).astype(bf16)
        return scatter_sum(keep + swap_tm(give).astype(f32), owner, count)

    def by_device(stack, rows):
        number = stack.shape[0]
        return (
            stack.reshape(number, count, rows, 128)
            .transpose(1, 0, 2, 3)
            .reshape(count, number * rows, 128)
        )

    second_grads = jnp.concatenate(
        [slabs(grad_attn_out), slabs(grad_ffn_in), column_two], axis=0
    )
    down_grads = (
        slabs(grad_ffn_out)
        .reshape(3, count, 2, half_down, 128)
        .transpose(2, 1, 0, 3, 4)
        .reshape(2, count, 3 * half_down, 128)
    )
    second_sum = reduce(
        [
            jnp.concatenate([by_device(second_grads[:10], shard), down_grads[0]], axis=1),
            jnp.concatenate([by_device(second_grads[10:], shard), down_grads[1]], axis=1),
        ]
    )
    first_grads = jnp.concatenate([slabs(grad_attn_in), column_one], axis=0)
    first_sum = reduce([by_device(first_grads[:5], shard), by_device(first_grads[5:], shard)])
    squares = jnp.sum(first_sum * first_sum) + jnp.sum(second_sum * second_sum)
    grad_norm = jnp.sqrt(sum_all(squares.reshape(1, 1), count)[0, 0])
    sums = jnp.concatenate([first_sum, second_sum], axis=0)
    sums_there = swap_tm(sums)
    sums_low = jnp.where(core == 0, sums, sums_there)
    sums_high = jnp.where(core == 0, sums_there, sums)
    five, fifteen = 5 * shard, 15 * shard
    first_shard = jnp.concatenate([sums_low[:five], sums_high[:five]]).reshape(10, shard, 128)
    second_shard = jnp.concatenate([sums_low[five:fifteen], sums_high[five:fifteen]]).reshape(20, shard, 128)
    down_shard = jnp.stack(
        [item[fifteen:].reshape(3, half_down, 128) for item in (sums_low, sums_high)], axis=1
    ).reshape(3, shard_down, 128)
    shard_grads = (
        unslab(first_shard[:9]),
        unslab(second_shard[:3]),
        unslab(second_shard[3:19]),
        unslab(down_shard),
        jnp.stack([first_shard[9, :, 0], second_shard[19, :, 0]]),
    )
    factor = clip_limit / jnp.maximum(grad_norm, clip_limit)
    masters = (w_qkv, w_out, w_gate_up, w_down, gains)
    firsts = (m_qkv, m_out, m_gate_up, m_down, m_gains)
    seconds = (v_qkv, v_out, v_gate_up, v_down, v_gains)
    rates = (D ** (-0.5), 4.0 * D ** (-0.5), D ** (-0.5), FF ** (-0.5), 0.5)
    decays = (decay_rate, decay_rate, decay_rate, decay_rate, 0.0)
    new_first = []
    new_second = []
    new_master = []
    for index in range(5):
        first_new, second_new, master_new = adam_update(
            masters[index],
            factor * shard_grads[index],
            firsts[index],
            seconds[index],
            rates[index],
            decays[index],
        )
        new_first.append(first_new)
        new_second.append(second_new)
        new_master.append(master_new)
    copies = [item.astype(bf16) for item in new_master]
    return (
        result,
        grad_tokens,
        grad_norm,
        new_first[0],
        new_first[1],
        new_first[2],
        new_first[3],
        new_first[4],
        new_second[0],
        new_second[1],
        new_second[2],
        new_second[3],
        new_second[4],
        new_master[0],
        new_master[1],
        new_master[2],
        new_master[3],
        new_master[4],
        copies[0],
        copies[1],
        copies[2],
        copies[3],
        copies[4],
    )


def solution(mesh):
    in_specs = (
        P("batch", "tm", None),
        P("batch", "tm", None),
        P("batch", None),
        P("batch", None),
        P("batch", None),
        P("batch", None),
        P("batch", None),
        P("batch", None),
        P("batch", None),
        P(None, "batch"),
        P("batch", None),
        P("batch", None),
        P("batch", None),
        P("batch", None),
        P(None, "batch"),
        P("batch", None),
        P("batch", None),
        P("batch", None),
        P("batch", None),
        P(None, "batch"),
    )
    out_specs = (
        P("batch", "tm", None),
        P("batch", "tm", None),
        P(),
        P("batch", None),
        P("batch", None),
        P("batch", None),
        P("batch", None),
        P(None, "batch"),
        P("batch", None),
        P("batch", None),
        P("batch", None),
        P("batch", None),
        P(None, "batch"),
        P("batch", None),
        P("batch", None),
        P("batch", None),
        P("batch", None),
        P(None, "batch"),
        P("batch", None),
        P("batch", None),
        P("batch", None),
        P("batch", None),
        P(None, "batch"),
    )
    return jax.shard_map(
        partial(per_device, mesh.shape["batch"]), mesh=mesh, in_specs=in_specs, out_specs=out_specs, check_vma=False
    )
```

```python
import math
from functools import partial

import jax
import jax.numpy as jnp
from jax import lax
from jax.experimental import pallas as pl
from jax.experimental.pallas import tpu as pltpu
from jax.sharding import PartitionSpec as P

D = 384
FF = 1024
HEADS = 6
HD = 64
STEP = 3


norm_eps = 1e-06
beta_one = 0.5
beta_two = 0.5
adam_eps = 1e-08
decay_rate = 0.1
clip_limit = 1.0
masked_score = -1e30


def adam_update(master, grad, first, second, rate, decay):
    first_new = beta_one * first + (1.0 - beta_one) * grad
    second_new = beta_two * second + (1.0 - beta_two) * grad * grad
    direction = (
        first_new
        / (1.0 - beta_one**STEP)
        / (jnp.sqrt(second_new / (1.0 - beta_two**STEP)) + adam_eps)
    )
    return (first_new, second_new, master - rate * (direction + decay * master))


def bit_groups(count):
    groups = []
    low, bits = 0, count.bit_length() - 1
    while low < bits:
        width = min(2, bits - low)
        groups.append((low, width))
        low += width
    return groups


def permute_batch(value, flip, count):
    return lax.ppermute(value, "batch", [(i, i ^ flip) for i in range(count)])


def swap_tm(value):
    return lax.ppermute(value, "tm", [(0, 1), (1, 0)])


def scatter_sum(parts, owner, count):
    held = parts
    rest = parts.shape[1:]
    for low, width in bit_groups(count):
        fan = 1 << width
        view = held.reshape((-1, fan) + rest)
        mine = (owner >> low) & (fan - 1)
        total = lax.dynamic_index_in_dim(view, mine, 1, keepdims=False).astype(jnp.float32)
        got = []
        for k in range(1, fan):
            piece = lax.dynamic_index_in_dim(view, mine ^ k, 1, keepdims=False)
            got.append(permute_batch(piece.astype(jnp.bfloat16), k << low, count))
        for item in got:
            total = total + item.astype(jnp.float32)
        held = total
    return held.reshape(rest)


def sum_all(value, count):
    value = value + swap_tm(value)
    for low, width in bit_groups(count):
        pieces = [value] + [permute_batch(value, k << low, count) for k in range(1, 1 << width)]
        while len(pieces) > 1:
            pieces = [pieces[i] + pieces[i + 1] for i in range(0, len(pieces), 2)]
        value = pieces[0]
    return value


def slabs(matrix):
    rows, columns = matrix.shape
    return matrix.reshape(rows, columns // 128, 128).transpose(1, 0, 2)


def unslab(stack):
    count, rows, _ = stack.shape
    return stack.transpose(1, 0, 2).reshape(rows, count * 128)


bf16 = jnp.bfloat16
f32 = jnp.float32
BLOCK = 256
LANES = 128
VMEM_LIMIT = 56 * 2**20
NN = (((1,), (0,)), ((), ()))
NT = (((1,), (1,)), ((), ()))
TN = (((0,), (0,)), ((), ()))


def dot(left, right, dims):
    return lax.dot_general(left, right, dims, preferred_element_type=f32)


def cost(flops, moved):
    return pl.CostEstimate(flops=flops, bytes_accessed=moved, transcendentals=0)


def block(start, size=BLOCK):
    return pl.ds(pl.multiple_of(start * size, size), size)


def row_scale(values):
    return lax.rsqrt(jnp.mean(values * values, axis=-1, keepdims=True) + norm_eps)


def norm_back(grad_normed, values, scale):
    return scale * grad_normed - values * scale * scale * scale * jnp.mean(
        grad_normed * values, axis=-1, keepdims=True
    )


def split_three(values):
    high = values.astype(bf16)
    rest = values - high.astype(f32)
    middle = rest.astype(bf16)
    return high, middle, (rest - middle.astype(f32)).astype(bf16)


def swap_halves(pair):
    lane = lax.broadcasted_iota(jnp.int32, pair.shape, 1)
    return jnp.where(lane % HD < HD // 2, pltpu.roll(pair, 96, 1), pltpu.roll(pair, 32, 1))


def gather_relative(chunk, count):
    held = chunk[None]
    for low, width in reversed(bit_groups(count)):
        pieces = [held] + [permute_batch(held, k << low, count) for k in range(1, 1 << width)]
        held = jnp.concatenate(pieces, axis=0)
    return held


def relative_places(owner, count):
    flips = jnp.arange(count, dtype=jnp.int32) ^ owner
    place = jnp.zeros((count,), jnp.int32)
    scale = 1
    for low, width in reversed(bit_groups(count)):
        place = place + ((flips >> low) & ((1 << width) - 1)) * scale
        scale <<= width
    return place


def assemble_kernel(count, number, shard, down, scalars, mine, other, *refs):
    outs, stage = refs[:-1], refs[-1]
    core = scalars[0]
    for source, half in ((mine, core), (other, 1 - core)):

        def one(device, carry, source=source, half=half):
            chunk = source[scalars[1 + device]].astype(f32)
            for i in range(number):
                stage[half * number + i, pl.ds(pl.multiple_of(device * shard, 8), shard), :] = chunk[
                    i * shard : (i + 1) * shard
                ]
            if down:
                at = number * shard
                for i in range(3):
                    outs[2][
                        pl.ds(pl.multiple_of(device * 2 * down + half * down, 16), down),
                        i * LANES : (i + 1) * LANES,
                    ] = chunk[at + i * down : at + (i + 1) * down].astype(bf16)
            return carry

        lax.fori_loop(0, count, one, 0)
    if down:
        for i in range(3):
            outs[0][:, i * LANES : (i + 1) * LANES] = stage[i].astype(bf16)
        for i in range(16):
            outs[1][:, i * LANES : (i + 1) * LANES] = stage[3 + i].astype(bf16)
    else:
        for i in range(9):
            outs[0][:, i * LANES : (i + 1) * LANES] = stage[i].astype(bf16)
        outs[1][...] = stage[9].T[:8]


def assemble(count, core, places, mine, number, shard, down):
    other = swap_tm(mine)
    if down:
        shapes = [((D, D), bf16), ((D, 2 * FF), bf16), ((FF, D), bf16)]
    else:
        shapes = [((D, 3 * D), bf16), ((8, D), f32)]
    if shard % 8 == 0 and down % 16 == 0:
        spec = pl.BlockSpec(memory_space=pltpu.VMEM)
        return pl.pallas_call(
            partial(assemble_kernel, count, number, shard, down),
            out_shape=[jax.ShapeDtypeStruct(*item) for item in shapes],
            in_specs=[pl.BlockSpec(memory_space=pltpu.SMEM), spec, spec],
            out_specs=[spec] * len(shapes),
            scratch_shapes=[pltpu.VMEM((2 * number, D, LANES), f32)],
            compiler_params=pltpu.CompilerParams(vmem_limit_bytes=VMEM_LIMIT),
            name="assemble_ffn" if down else "assemble_qkv",
        )(jnp.concatenate([core[None], places]), mine, other)
    low = jnp.take(jnp.where(core == 0, mine, other), places, axis=0)
    high = jnp.take(jnp.where(core == 0, other, mine), places, axis=0)

    def part(source):
        return (
            source[:, : number * shard]
            .reshape(count, number, shard, LANES)
            .transpose(1, 0, 2, 3)
            .reshape(number, D, LANES)
        )

    stack = jnp.concatenate([part(low), part(high)], axis=0)
    if not down:
        return unslab(stack[:9]), stack[9].T[:8].astype(f32)
    downs = [
        item[:, number * shard : number * shard + 3 * down].reshape(count, 3, down, LANES)
        for item in (low, high)
    ]
    w_down = jnp.stack(downs, axis=1).transpose(0, 1, 3, 2, 4).reshape(FF, D)
    return unslab(stack[:3]), unslab(stack[3:19]), w_down


def pack_kernel(count, number, shard, down, scalars, *refs):
    if down:
        grads, (keep, give, give_stage, column) = refs[:4], refs[4:]
        slab_refs = [(grads[0], i) for i in range(3)] + [(grads[1], i) for i in range(16)]
        gain = grads[3]
    else:
        grads, (keep, give, give_stage, column) = refs[:2], refs[2:]
        slab_refs = [(grads[0], i) for i in range(9)]
        gain = grads[1]
    column[...] = jnp.concatenate([gain[...], jnp.zeros((LANES - 8, D), f32)], axis=0).T
    slab_refs.append((column, 0))
    core = scalars[0]

    def copy(low_to, high_to):
        def one(device, carry):
            rows = pl.ds(pl.multiple_of(device * shard, 8), shard)
            for half, target in ((0, low_to), (1, high_to)):
                for i in range(number):
                    source, at = slab_refs[half * number + i]
                    target[device, i * shard : (i + 1) * shard, :] = source[
                        rows, at * LANES : (at + 1) * LANES
                    ]
                if down:
                    rows_down = pl.ds(pl.multiple_of(device * 2 * down + half * down, 8), down)
                    for i in range(3):
                        start = number * shard + i * down
                        target[device, start : start + down, :] = grads[2][
                            rows_down, i * LANES : (i + 1) * LANES
                        ]
            return carry

        lax.fori_loop(0, count, one, 0)

    @pl.when(core == 0)
    def _():
        copy(keep, give_stage)

    @pl.when(core == 1)
    def _():
        copy(give_stage, keep)

    give[...] = give_stage[...].astype(bf16)


def pack(count, core, grads, number, shard, down):
    rows = number * shard + 3 * down
    if shard % 8 == 0 and down % 8 == 0:
        spec = pl.BlockSpec(memory_space=pltpu.VMEM)
        return pl.pallas_call(
            partial(pack_kernel, count, number, shard, down),
            out_shape=[
                jax.ShapeDtypeStruct((count, rows, LANES), f32),
                jax.ShapeDtypeStruct((count, rows, LANES), bf16),
            ],
            in_specs=[pl.BlockSpec(memory_space=pltpu.SMEM)] + [spec] * len(grads),
            out_specs=[spec] * 2,
            scratch_shapes=[
                pltpu.VMEM((count, rows, LANES), f32),
                pltpu.VMEM((D, LANES), f32),
            ],
            compiler_params=pltpu.CompilerParams(vmem_limit_bytes=VMEM_LIMIT),
            name="pack_ffn" if down else "pack_qkv",
        )(core[None], *grads)
    column = jnp.pad(grads[-1][:1].T, ((0, 0), (0, LANES - 1)))[None]
    stack = jnp.concatenate([slabs(item) for item in (grads[:2] if down else grads[:1])] + [column])

    def by_device(part):
        return (
            part.reshape(number, count, shard, LANES)
            .transpose(1, 0, 2, 3)
            .reshape(count, number * shard, LANES)
        )

    halves = [by_device(stack[:number]), by_device(stack[number:])]
    if down:
        downs = (
            slabs(grads[2])
            .reshape(3, count, 2, down, LANES)
            .transpose(2, 1, 0, 3, 4)
            .reshape(2, count, 3 * down, LANES)
        )
        halves = [jnp.concatenate([halves[i], downs[i]], axis=1) for i in range(2)]
    return (
        jnp.where(core == 0, halves[0], halves[1]),
        jnp.where(core == 0, halves[1], halves[0]).astype(bf16),
    )


def project_kernel(
    own, there, cosine, sine, key_aux, query_aux, w, gains, qa, ka, va, kt, vt
):
    step = pl.program_id(0)
    is_own = step < pl.num_programs(0) // 2
    x = jnp.where(is_own, own[...], there[...]).astype(f32)
    normed = (x * row_scale(x) * gains[0:1, :]).astype(bf16)
    cos, sin = cosine[...], sine[...]
    low = lax.broadcasted_iota(jnp.int32, (BLOCK, LANES), 1) < HD
    key_extra = key_aux[...].astype(f32)
    query_extra = query_aux[...].astype(f32)
    lane = lax.broadcasted_iota(jnp.int32, (BLOCK, LANES), 1)
    value_extra = jnp.where((lane >= HD) & (lane < HD + 3), 1.0, 0.0)
    ones = jnp.ones((8, BLOCK), bf16)

    @pl.when(is_own)
    def _():
        for pair in range(HEADS // 2):
            z = dot(normed, w[:, pair * LANES : (pair + 1) * LANES], NN)
            z = (z * cos + swap_halves(z) * sin).astype(bf16).astype(f32) * HD**-0.5
            qa[2 * pair] = jnp.where(low, z, query_extra).astype(bf16)
            qa[2 * pair + 1] = jnp.where(low, pltpu.roll(z, HD, 1), query_extra).astype(bf16)

    for pair in range(HEADS // 2):
        z = dot(normed, w[:, D + pair * LANES : D + (pair + 1) * LANES], NN)
        z = z * cos + swap_halves(z) * sin
        ka[2 * pair] = jnp.where(low, z, key_extra).astype(bf16)
        ka[2 * pair + 1] = jnp.where(low, pltpu.roll(z, HD, 1), key_extra).astype(bf16)
        turned = z.T.astype(bf16)
        kt[2 * pair] = turned[:HD]
        kt[2 * pair + 1] = turned[HD:]
    for pair in range(HEADS // 2):
        z = dot(normed, w[:, 2 * D + pair * LANES : 2 * D + (pair + 1) * LANES], NN)
        va[2 * pair] = jnp.where(low, z, value_extra).astype(bf16)
        va[2 * pair + 1] = jnp.where(low, pltpu.roll(z, HD, 1), value_extra).astype(bf16)
        turned = z.T.astype(bf16)
        vt[2 * pair, :HD] = turned[:HD]
        vt[2 * pair + 1, :HD] = turned[HD:]
        vt[2 * pair, HD:] = ones
        vt[2 * pair + 1, HD:] = ones


def project(own, there, cosine, sine, key_aux, query_aux, w, gains):
    length = own.shape[0]
    steps = length // BLOCK
    whole = 2 * length
    first = lambda i: (jnp.minimum(i, steps - 1), 0)
    last = lambda i: (jnp.maximum(i - steps, 0), 0)
    return pl.pallas_call(
        project_kernel,
        out_shape=[
            jax.ShapeDtypeStruct((HEADS, length, LANES), bf16),
            jax.ShapeDtypeStruct((HEADS, whole, LANES), bf16),
            jax.ShapeDtypeStruct((HEADS, whole, LANES), bf16),
            jax.ShapeDtypeStruct((HEADS, HD, whole), bf16),
            jax.ShapeDtypeStruct((HEADS, HD + 8, whole), bf16),
        ],
        grid=(2 * steps,),
        in_specs=[
            pl.BlockSpec((BLOCK, D), first),
            pl.BlockSpec((BLOCK, D), last),
            pl.BlockSpec((BLOCK, LANES), lambda i: (i, 0)),
            pl.BlockSpec((BLOCK, LANES), lambda i: (i, 0)),
            pl.BlockSpec((BLOCK, LANES), lambda i: (i, 0)),
            pl.BlockSpec((BLOCK, LANES), first),
            pl.BlockSpec((D, 3 * D), lambda i: (0, 0)),
            pl.BlockSpec((8, D), lambda i: (0, 0)),
        ],
        out_specs=[
            pl.BlockSpec((HEADS, BLOCK, LANES), lambda i: (0, jnp.minimum(i, steps - 1), 0)),
            pl.BlockSpec((HEADS, BLOCK, LANES), lambda i: (0, i, 0)),
            pl.BlockSpec((HEADS, BLOCK, LANES), lambda i: (0, i, 0)),
            pl.BlockSpec((HEADS, HD, BLOCK), lambda i: (0, 0, i)),
            pl.BlockSpec((HEADS, HD + 8, BLOCK), lambda i: (0, 0, i)),
        ],
        compiler_params=pltpu.CompilerParams(vmem_limit_bytes=VMEM_LIMIT),
        cost_estimate=cost(2 * whole * D * 3 * D, 16 * 2**20),
        name="project",
    )(own, there, cosine, sine, key_aux, query_aux, w, gains)


def key_block(ranges, step, n):
    return jnp.where(n < ranges[1, step], ranges[0, step] + n, ranges[2, step] + n)


def attend_kernel(ranges, qa, ka, vt, mixed, exact, qb, total, peak):
    step = pl.program_id(0)
    peak[...] = jnp.full((HEADS, 8, BLOCK), -3e38, f32)
    total[...] = jnp.zeros_like(total)

    def body(n, carry):
        rows = block(key_block(ranges, step, n))
        scores = [dot(ka[h, rows, :], qa[h], NT) for h in range(HEADS)]
        weights = []
        for h in range(HEADS):
            old = peak[h][:1]
            new = jnp.maximum(old, jnp.max(scores[h], axis=0, keepdims=True))
            weights.append((jnp.exp(scores[h] - new).astype(bf16), jnp.exp(old - new)))
            peak[h] = jnp.broadcast_to(new, (8, BLOCK))
        for h in range(HEADS):
            weight, shrink = weights[h]
            total[h] = total[h] * shrink + dot(vt[h, :, rows], weight, NN)
        return carry

    lax.fori_loop(0, ranges[3, step], body, 0)
    terms = []
    for h in range(HEADS):
        bottom = total[h][HD : HD + 1]
        terms.append(total[h][:HD] / bottom)
        logs = -(peak[h][:1] + jnp.log(bottom))
        for piece in split_three(logs):
            terms.append(piece.astype(f32))
    for pair in range(HEADS // 2):
        both = jnp.concatenate([terms[8 * pair], terms[8 * pair + 4]], axis=0).T
        mixed[:, pair * LANES : (pair + 1) * LANES] = both.astype(bf16)
        exact[:, pair * LANES : (pair + 1) * LANES] = both
    pieces = [terms[4 * h + 1 + i] for h in range(HEADS) for i in range(3)]
    table = jnp.concatenate(
        [jnp.zeros((HD + 8, BLOCK), f32)]
        + pieces
        + [jnp.zeros((LANES - HD - 8 - 3 * HEADS, BLOCK), f32)],
        axis=0,
    ).T
    lane = lax.broadcasted_iota(jnp.int32, (BLOCK, LANES), 1)
    for h in range(HEADS):
        start = HD + 8 + 3 * h
        qb[h] = jnp.where(
            (lane >= start) & (lane < start + 3), table, qa[h].astype(f32)
        ).astype(bf16)


def attend(ranges, qa, ka, vt):
    heads, length, _ = qa.shape
    whole = ka.shape[1]
    return pl.pallas_call(
        attend_kernel,
        out_shape=[
            jax.ShapeDtypeStruct((length, D), bf16),
            jax.ShapeDtypeStruct((length, D), f32),
            jax.ShapeDtypeStruct(qa.shape, bf16),
        ],
        grid_spec=pltpu.PrefetchScalarGridSpec(
            num_scalar_prefetch=1,
            grid=(length // BLOCK,),
            in_specs=[
                pl.BlockSpec((heads, BLOCK, LANES), lambda i, *_: (0, i, 0)),
                pl.BlockSpec((heads, whole, LANES), lambda i, *_: (0, 0, 0)),
                pl.BlockSpec((heads, HD + 8, whole), lambda i, *_: (0, 0, 0)),
            ],
            out_specs=[
                pl.BlockSpec((BLOCK, D), lambda i, *_: (i, 0)),
                pl.BlockSpec((BLOCK, D), lambda i, *_: (i, 0)),
                pl.BlockSpec((heads, BLOCK, LANES), lambda i, *_: (0, i, 0)),
            ],
            scratch_shapes=[
                pltpu.VMEM((heads, HD + 8, BLOCK), f32),
                pltpu.VMEM((heads, 8, BLOCK), f32),
            ],
        ),
        compiler_params=pltpu.CompilerParams(vmem_limit_bytes=VMEM_LIMIT),
        cost_estimate=cost(12 * 10**9, 12 * 2**20),
        name="attend",
    )(ranges, qa, ka, vt)


def attend_back_kernel(ranges, qb, ka, da, va, kt, dq, own, there, sums, acc):
    step = pl.program_id(0)
    heads = qb.shape[0]

    @pl.when(step == 0)
    def _():
        sums[...] = jnp.zeros_like(sums)

    acc[...] = jnp.zeros_like(acc)
    zero = jnp.zeros((BLOCK, HD), bf16)

    def body(n, carry):
        rows = block(key_block(ranges, step, n))
        first = [
            (dot(ka[h, rows, :], qb[h], NT), dot(va[h, rows, :], da[h], NT)) for h in range(heads)
        ]
        second = []
        for scores, grads in first:
            probs = jnp.exp(scores)
            second.append((probs.astype(bf16), (probs * grads).astype(bf16)))
        for h in range(heads):
            probs_low, grads_low = second[h]
            grad_side = jnp.concatenate([da[h][:, :HD], zero], axis=1)
            query_side = jnp.concatenate([zero, qb[h][:, :HD]], axis=1)
            sums[h, rows, :] += dot(probs_low, grad_side, NN) + dot(grads_low, query_side, NN)
            acc[h] += dot(kt[h, :, rows], grads_low, NN)
        return carry

    lax.fori_loop(0, ranges[3, step], body, 0)
    dq[...] = acc[...]

    @pl.when(step == pl.num_programs(0) - 1)
    def _():
        length = own.shape[1]
        own[...] = sums[:, :length, :]
        there[...] = sums[:, length:, :].astype(bf16)


def attend_back(group, heads, ranges, qb, ka, da, va, kt):
    length, whole = qb.shape[1], ka.shape[1]
    return pl.pallas_call(
        attend_back_kernel,
        out_shape=[
            jax.ShapeDtypeStruct((heads, HD, length), f32),
            jax.ShapeDtypeStruct((heads, length, LANES), f32),
            jax.ShapeDtypeStruct((heads, whole - length, LANES), bf16),
        ],
        grid_spec=pltpu.PrefetchScalarGridSpec(
            num_scalar_prefetch=1,
            grid=(length // BLOCK,),
            in_specs=[
                pl.BlockSpec((heads, BLOCK, LANES), lambda i, *_: (group, i, 0)),
                pl.BlockSpec((heads, whole, LANES), lambda i, *_: (group, 0, 0)),
                pl.BlockSpec((heads, BLOCK, LANES), lambda i, *_: (group, i, 0)),
                pl.BlockSpec((heads, whole, LANES), lambda i, *_: (group, 0, 0)),
                pl.BlockSpec((heads, HD, whole), lambda i, *_: (group, 0, 0)),
            ],
            out_specs=[
                pl.BlockSpec((heads, HD, BLOCK), lambda i, *_: (0, 0, i)),
                pl.BlockSpec((heads, length, LANES), lambda i, *_: (0, 0, 0)),
                pl.BlockSpec((heads, whole - length, LANES), lambda i, *_: (0, 0, 0)),
            ],
            scratch_shapes=[
                pltpu.VMEM((heads, whole, LANES), f32),
                pltpu.VMEM((heads, HD, BLOCK), f32),
            ],
        ),
        compiler_params=pltpu.CompilerParams(vmem_limit_bytes=VMEM_LIMIT),
        cost_estimate=cost(12 * 10**9, 8 * 2**20),
        name="attend_back",
    )(ranges, qb, ka, da, va, kt)


def feed_kernel(
    own, mixed, exact, cotangent, keep, wo, wgu, wd, gains,
    result, grad_middle, da, g_out, g_gate_up, g_down, g_gain,
    normed_all, low_all, hidden_all, up_all, middle_all,
):
    gain = gains[1:2, :]
    g_gain[...] = jnp.zeros_like(g_gain)
    chunks = FF // BLOCK
    lane = lax.broadcasted_iota(jnp.int32, (BLOCK, LANES), 1)

    def body(i, carry):
        rows = block(i)
        x = own[rows, :].astype(f32)
        middle = x + dot(mixed[rows, :], wo[...], NN)
        scale = row_scale(middle)
        normed = (middle * scale * gain).astype(bf16)
        normed_all[rows, :] = normed
        kept = keep[rows, :]
        upstream = cotangent[rows, :].astype(f32) * kept
        up_low = upstream.astype(bf16)
        up_all[rows, :] = up_low
        gates = [dot(normed, wgu[:, c * BLOCK : (c + 1) * BLOCK], NN) for c in range(chunks)]
        ups = [
            dot(normed, wgu[:, FF + c * BLOCK : FF + (c + 1) * BLOCK], NN) for c in range(chunks)
        ]
        hiddens = [dot(up_low, wd[c * BLOCK : (c + 1) * BLOCK, :], NT) for c in range(chunks)]
        for c in range(chunks):
            gate, up, grad_hidden = gates[c], ups[c], hiddens[c]
            sig = 1.0 / (1.0 + jnp.exp(-gate))
            silu = gate * sig
            hidden_all[rows, c * BLOCK : (c + 1) * BLOCK] = (silu * up).astype(bf16)
            low_all[rows, FF + c * BLOCK : FF + (c + 1) * BLOCK] = (grad_hidden * silu).astype(bf16)
            low_all[rows, c * BLOCK : (c + 1) * BLOCK] = (
                grad_hidden * up * (sig + silu * (1.0 - sig))
            ).astype(bf16)
        ffn = dot(hidden_all[rows, :], wd[...], NN)
        result[rows, :] = (kept * (middle + ffn)).astype(bf16)
        grad_normed = dot(low_all[rows, :], wgu[...], NT)
        g_gain[0:1, :] += jnp.sum(grad_normed * middle * scale, axis=0, keepdims=True)
        grad = upstream + norm_back(grad_normed * gain, middle, scale)
        grad_middle[rows, :] = grad
        low = grad.astype(bf16)
        middle_all[rows, :] = low
        grad_mixed = dot(low, wo[...], NT).astype(bf16).astype(f32)
        products = grad_mixed * exact[rows, :]
        for h in range(HEADS):
            pair = h // 2
            head = grad_mixed[:, pair * LANES : (pair + 1) * LANES]
            product = products[:, pair * LANES : (pair + 1) * LANES]
            mine = (lane < HD) if h % 2 == 0 else (lane >= HD)
            delta = -jnp.sum(jnp.where(mine, product, 0.0), axis=1, keepdims=True)
            if h % 2:
                head = pltpu.roll(head, HD, 1)
            high, mid, last = split_three(delta)
            extra = jnp.where(
                lane == HD,
                high.astype(f32),
                jnp.where(
                    lane == HD + 1,
                    mid.astype(f32),
                    jnp.where(lane == HD + 2, last.astype(f32), 0.0),
                ),
            )
            da[h, rows, :] = jnp.where(lane < HD, head, extra).astype(bf16)
        return carry

    lax.fori_loop(0, own.shape[0] // BLOCK, body, 0)
    g_out[...] = dot(mixed[...], middle_all[...], TN)
    for c in range(2 * FF // 512):
        g_gate_up[:, c * 512 : (c + 1) * 512] = dot(
            normed_all[...], low_all[:, c * 512 : (c + 1) * 512], TN
        )
    for c in range(chunks):
        g_down[c * BLOCK : (c + 1) * BLOCK, :] = dot(
            hidden_all[:, c * BLOCK : (c + 1) * BLOCK], up_all[...], TN
        )


def feed(own, mixed, exact, cotangent, keep, wo, wgu, wd, gains):
    length = own.shape[0]
    spec = pl.BlockSpec(memory_space=pltpu.VMEM)
    return pl.pallas_call(
        feed_kernel,
        out_shape=[
            jax.ShapeDtypeStruct((length, D), bf16),
            jax.ShapeDtypeStruct((length, D), f32),
            jax.ShapeDtypeStruct((HEADS, length, LANES), bf16),
            jax.ShapeDtypeStruct((D, D), f32),
            jax.ShapeDtypeStruct((D, 2 * FF), f32),
            jax.ShapeDtypeStruct((FF, D), f32),
            jax.ShapeDtypeStruct((8, D), f32),
        ],
        in_specs=[spec] * 9,
        out_specs=[spec] * 7,
        scratch_shapes=[
            pltpu.VMEM((length, D), bf16),
            pltpu.VMEM((length, 2 * FF), bf16),
            pltpu.VMEM((length, FF), bf16),
            pltpu.VMEM((length, D), bf16),
            pltpu.VMEM((length, D), bf16),
        ],
        compiler_params=pltpu.CompilerParams(vmem_limit_bytes=VMEM_LIMIT),
        cost_estimate=cost(10 * 10**9, 16 * 2**20),
        name="feed",
    )(own, mixed, exact, cotangent, keep, wo, wgu, wd, gains)


def project_back_kernel(
    own, grad_middle, cosine, sine, w, gains, *refs
):
    groups = (len(refs) - 5) // 3
    dqs, owns, recvs = refs[:groups], refs[groups : 2 * groups], refs[2 * groups : 3 * groups]
    grad_tokens, g_qkv, g_gain, normed_all, low_all = refs[3 * groups :]
    heads = HEADS // groups
    step = pl.program_id(0)
    rows = block(step)
    cos, sin = cosine[...], -sine[...]
    low = lax.broadcasted_iota(jnp.int32, (BLOCK, LANES), 1) < HD
    for pair in range(HEADS // 2):
        spots = [((2 * pair + i) // heads, (2 * pair + i) % heads) for i in range(2)]
        z = jnp.concatenate([dqs[g][h] for g, h in spots], axis=0).T * HD**-0.5
        low_all[rows, pair * LANES : (pair + 1) * LANES] = (
            z * cos + swap_halves(z) * sin
        ).astype(bf16)
        first, second = [owns[g][h] + recvs[g][h].astype(f32) for g, h in spots]
        z = jnp.where(low, pltpu.roll(first, HD, 1), second)
        low_all[rows, D + pair * LANES : D + (pair + 1) * LANES] = (
            z * cos + swap_halves(z) * sin
        ).astype(bf16)
        low_all[rows, 2 * D + pair * LANES : 2 * D + (pair + 1) * LANES] = jnp.where(
            low, first, pltpu.roll(second, HD, 1)
        ).astype(bf16)
    x = own[...].astype(f32)
    scale = row_scale(x)
    gain = gains[0:1, :]
    normed_all[rows, :] = (x * scale * gain).astype(bf16)
    grad_normed = dot(low_all[rows, :], w[...], NT)
    sums = jnp.sum(grad_normed * x * scale, axis=0, keepdims=True)

    @pl.when(step == 0)
    def _():
        g_gain[...] = jnp.zeros_like(g_gain)

    g_gain[0:1, :] += sums
    grad_tokens[...] = (grad_middle[...] + norm_back(grad_normed * gain, x, scale)).astype(bf16)

    @pl.when(step == pl.num_programs(0) - 1)
    def _():
        for c in range(3):
            g_qkv[:, c * D : (c + 1) * D] = dot(
                normed_all[...], low_all[:, c * D : (c + 1) * D], TN
            )


def project_back(own, grad_middle, cosine, sine, w, gains, dqs, owns, recvs):
    length = own.shape[0]
    heads = dqs[0].shape[0]
    groups = len(dqs)
    return pl.pallas_call(
        project_back_kernel,
        out_shape=[
            jax.ShapeDtypeStruct((length, D), bf16),
            jax.ShapeDtypeStruct((D, 3 * D), f32),
            jax.ShapeDtypeStruct((8, D), f32),
        ],
        grid=(length // BLOCK,),
        in_specs=[
            pl.BlockSpec((BLOCK, D), lambda i: (i, 0)),
            pl.BlockSpec((BLOCK, D), lambda i: (i, 0)),
            pl.BlockSpec((BLOCK, LANES), lambda i: (i, 0)),
            pl.BlockSpec((BLOCK, LANES), lambda i: (i, 0)),
            pl.BlockSpec((D, 3 * D), lambda i: (0, 0)),
            pl.BlockSpec((8, D), lambda i: (0, 0)),
        ]
        + [pl.BlockSpec((heads, HD, BLOCK), lambda i: (0, 0, i))] * groups
        + [pl.BlockSpec((heads, BLOCK, LANES), lambda i: (0, i, 0))] * (2 * groups),
        out_specs=[
            pl.BlockSpec((BLOCK, D), lambda i: (i, 0)),
            pl.BlockSpec((D, 3 * D), lambda i: (0, 0)),
            pl.BlockSpec((8, D), lambda i: (0, 0)),
        ],
        scratch_shapes=[pltpu.VMEM((length, D), bf16), pltpu.VMEM((length, 3 * D), bf16)],
        compiler_params=pltpu.CompilerParams(vmem_limit_bytes=VMEM_LIMIT),
        cost_estimate=cost(4 * 10**9, 10 * 2**20),
        name="project_back",
    )(own, grad_middle, cosine, sine, w, gains, *dqs, *owns, *recvs)


def per_device(
    count,
    tokens,
    cotangent,
    sample_ids,
    pad_flags,
    offsets,
    w_qkv,
    w_out,
    w_gate_up,
    w_down,
    gains,
    m_qkv,
    m_out,
    m_gate_up,
    m_down,
    m_gains,
    v_qkv,
    v_out,
    v_gate_up,
    v_down,
    v_gains,
):
    owner = lax.axis_index("batch")
    core = lax.axis_index("tm")
    shard = w_qkv.shape[0]
    down = w_down.shape[0] // 2
    own = tokens[0]
    length = own.shape[0]
    places = relative_places(owner, count)

    gain_slab = jnp.pad(gains.T, ((0, 0), (0, LANES - 2)))[None]
    first = jnp.concatenate([slabs(w_qkv), gain_slab]).reshape(2, 5 * shard, LANES)
    first = jnp.where(core == 0, first[0], first[1]).astype(bf16)
    first_rows = -(-first.shape[0] // 16) * 16
    first = jnp.pad(first, ((0, first_rows - first.shape[0]), (0, 0)))
    second = jnp.concatenate(
        [slabs(w_out), slabs(w_gate_up), jnp.zeros((1, shard, LANES), f32)]
    ).reshape(2, 10 * shard, LANES)
    downs = slabs(w_down).reshape(3, 2, down, LANES).transpose(1, 0, 2, 3)
    downs = downs.reshape(2, 3 * down, LANES)
    second = jnp.where(
        core == 0,
        jnp.concatenate([second[0], downs[0]]),
        jnp.concatenate([second[1], downs[1]]),
    ).astype(bf16)
    first_held = gather_relative(first, count)
    second_held = gather_relative(second, count)
    there = swap_tm(own)

    def rotate(row):
        both = row[0].reshape(2, length)
        return jnp.where(core == 0, both, both[::-1]).reshape(-1)

    starts = jnp.stack([core, 1 - core]) * length
    place = (starts[:, None] + jnp.arange(length, dtype=jnp.int32)).reshape(-1)
    positions = (place + rotate(offsets)).astype(f32)
    frequency = jnp.exp(
        jnp.arange(HD // 2, dtype=f32) * (-2.0 * math.log(10000.0) / HD)
    )
    angles = positions[:, None] * frequency
    cosine = jnp.tile(jnp.cos(angles), (1, 4))
    sine = jnp.sin(angles)
    sine = jnp.tile(jnp.concatenate([-sine, sine], axis=1), (1, 2))
    classes = 2 * sample_ids[0] + pad_flags[0]
    turned = 2 * rotate(sample_ids) + rotate(pad_flags)
    lane = jnp.arange(LANES, dtype=jnp.int32)[None, :]
    is_class = (lane >= HD) & (lane < HD + 8)
    same = turned[:, None] == lane - HD
    is_log = (lane >= HD + 8) & (lane < HD + 8 + 3 * HEADS)
    key_aux = jnp.where((is_class & same) | is_log, 1.0, 0.0).astype(bf16)
    query_aux = jnp.where(is_class & ~same[:length], masked_score, 0.0).astype(bf16)
    own_classes = turned[:length].reshape(-1, BLOCK)
    low_key = jnp.sum(classes[None, :] < own_classes[:, :1], axis=1)
    high_key = jnp.sum(classes[None, :] <= own_classes[:, -1:], axis=1)
    bounds = []
    for part in range(2):
        low_part = jnp.clip(low_key - starts[part], 0, length)
        high_part = jnp.clip(high_key - starts[part], 0, length)
        bounds.append((low_part // BLOCK, (high_part + BLOCK - 1) // BLOCK))
    near = jnp.maximum(bounds[0][1] - bounds[0][0], 0)
    far = jnp.maximum(bounds[1][1] - bounds[1][0], 0)
    ranges = jnp.stack(
        [bounds[0][0], near, bounds[1][0] + length // BLOCK - near, near + far]
    ).astype(jnp.int32)
    keep = (turned[:length, None] % 2 == 0).astype(f32)

    attn_in, gain_pair = assemble(count, core, places, first_held, 5, shard, 0)
    qa, ka, va, kt, vt = project(
        own, there, cosine, sine, key_aux, query_aux, attn_in, gain_pair
    )
    mixed, exact, qb = attend(ranges, qa, ka, vt)
    attn_out, ffn_in, ffn_out = assemble(count, core, places, second_held, 10, shard, down)
    result, grad_middle, da, g_out, g_gate_up, g_down, g_gain_two = feed(
        own, mixed, exact, cotangent[0], keep, attn_out, ffn_in, ffn_out, gain_pair
    )

    def reduce(kept, given):
        return scatter_sum(kept + swap_tm(given).astype(f32), owner, count)

    second_sum = reduce(
        *pack(count, core, (g_out, g_gate_up, g_down, g_gain_two), 10, shard, down)
    )
    dqs, owns, recvs = [], [], []
    for group in range(2):
        dq, kept, given = attend_back(group, HEADS // 2, ranges, qb, ka, da, va, kt)
        dqs.append(dq)
        owns.append(kept)
        recvs.append(swap_tm(given))
    grad_tokens, g_qkv, g_gain_one = project_back(
        own, grad_middle, cosine, sine, attn_in, gain_pair, dqs, owns, recvs
    )
    first_sum = reduce(*pack(count, core, (g_qkv, g_gain_one), 5, shard, 0))

    squares = jnp.sum(first_sum * first_sum) + jnp.sum(second_sum * second_sum)
    grad_norm = jnp.sqrt(sum_all(squares.reshape(1, 1), count)[0, 0])
    sums = jnp.concatenate([first_sum, second_sum], axis=0)
    sums_there = swap_tm(sums)
    sums_low = jnp.where(core == 0, sums, sums_there)
    sums_high = jnp.where(core == 0, sums_there, sums)
    five, fifteen = 5 * shard, 15 * shard
    first_shard = jnp.concatenate([sums_low[:five], sums_high[:five]]).reshape(10, shard, LANES)
    second_shard = jnp.concatenate([sums_low[five:fifteen], sums_high[five:fifteen]])
    second_shard = second_shard.reshape(20, shard, LANES)
    down_shard = jnp.stack(
        [item[fifteen:].reshape(3, down, LANES) for item in (sums_low, sums_high)], axis=1
    ).reshape(3, 2 * down, LANES)
    shard_grads = (
        unslab(first_shard[:9]),
        unslab(second_shard[:3]),
        unslab(second_shard[3:19]),
        unslab(down_shard),
        jnp.stack([first_shard[9, :, 0], second_shard[19, :, 0]]),
    )
    factor = clip_limit / jnp.maximum(grad_norm, clip_limit)
    masters = (w_qkv, w_out, w_gate_up, w_down, gains)
    firsts = (m_qkv, m_out, m_gate_up, m_down, m_gains)
    seconds = (v_qkv, v_out, v_gate_up, v_down, v_gains)
    rates = (D ** (-0.5), 4.0 * D ** (-0.5), D ** (-0.5), FF ** (-0.5), 0.5)
    decays = (decay_rate, decay_rate, decay_rate, decay_rate, 0.0)
    updates = [
        adam_update(
            masters[i], factor * shard_grads[i], firsts[i], seconds[i], rates[i], decays[i]
        )
        for i in range(5)
    ]
    new_first, new_second, new_master = zip(*updates)
    copies = [item.astype(bf16) for item in new_master]
    return (
        result[None],
        grad_tokens[None],
        grad_norm,
        *new_first,
        *new_second,
        *new_master,
        *copies,
    )


def solution(mesh):
    in_specs = (
        P("batch", "tm", None),
        P("batch", "tm", None),
        P("batch", None),
        P("batch", None),
        P("batch", None),
        P("batch", None),
        P("batch", None),
        P("batch", None),
        P("batch", None),
        P(None, "batch"),
        P("batch", None),
        P("batch", None),
        P("batch", None),
        P("batch", None),
        P(None, "batch"),
        P("batch", None),
        P("batch", None),
        P("batch", None),
        P("batch", None),
        P(None, "batch"),
    )
    out_specs = (
        P("batch", "tm", None),
        P("batch", "tm", None),
        P(),
        P("batch", None),
        P("batch", None),
        P("batch", None),
        P("batch", None),
        P(None, "batch"),
        P("batch", None),
        P("batch", None),
        P("batch", None),
        P("batch", None),
        P(None, "batch"),
        P("batch", None),
        P("batch", None),
        P("batch", None),
        P("batch", None),
        P(None, "batch"),
        P("batch", None),
        P("batch", None),
        P("batch", None),
        P("batch", None),
        P(None, "batch"),
    )
    return jax.shard_map(
        partial(per_device, mesh.shape["batch"]), mesh=mesh, in_specs=in_specs, out_specs=out_specs, check_vma=False
    )
```

```python
import math
from functools import partial

import jax
import jax.numpy as jnp
from jax import lax
from jax.experimental import pallas as pl
from jax.experimental.pallas import tpu as pltpu
from jax.sharding import PartitionSpec as P

D = 384
FF = 1024
HEADS = 6
HD = 64
STEP = 3


norm_eps = 1e-06
beta_one = 0.5
beta_two = 0.5
adam_eps = 1e-08
decay_rate = 0.1
clip_limit = 1.0
masked_score = -1e30


def adam_update(master, grad, first, second, rate, decay):
    first_new = beta_one * first + (1.0 - beta_one) * grad
    second_new = beta_two * second + (1.0 - beta_two) * grad * grad
    direction = (
        first_new
        / (1.0 - beta_one**STEP)
        / (jnp.sqrt(second_new / (1.0 - beta_two**STEP)) + adam_eps)
    )
    return (first_new, second_new, master - rate * (direction + decay * master))


def bit_groups(count):
    groups = []
    low, bits = 0, count.bit_length() - 1
    while low < bits:
        width = min(2, bits - low)
        groups.append((low, width))
        low += width
    return groups


def permute_batch(value, flip, count):
    return lax.ppermute(value, "batch", [(i, i ^ flip) for i in range(count)])


def swap_tm(value):
    return lax.ppermute(value, "tm", [(0, 1), (1, 0)])


def slabs(matrix):
    rows, columns = matrix.shape
    return matrix.reshape(rows, columns // 128, 128).transpose(1, 0, 2)


def unslab(stack):
    count, rows, _ = stack.shape
    return stack.transpose(1, 0, 2).reshape(rows, count * 128)


bf16 = jnp.bfloat16
f32 = jnp.float32
BLOCK = 256
LANES = 128
KEEP_LANE = 96
STORED = (2, 3, 4, 5, 0, 1)
SPOT = tuple(STORED.index(head) for head in range(HEADS))
GROUPS = ((2, 2), (4, 0))
VMEM_LIMIT = 58 * 2**20
NN = (((1,), (0,)), ((), ()))
NT = (((1,), (1,)), ((), ()))
TN = (((0,), (0,)), ((), ()))


def dot(left, right, dims):
    return lax.dot_general(left, right, dims, preferred_element_type=f32)


def cost(flops, moved):
    return pl.CostEstimate(flops=flops, bytes_accessed=moved, transcendentals=0)


def block(start, size=BLOCK):
    return pl.ds(pl.multiple_of(start * size, size), size)


def sum_batch(value, count):
    for low, width in bit_groups(count):
        pieces = [value] + [permute_batch(value, k << low, count) for k in range(1, 1 << width)]
        while len(pieces) > 1:
            pieces = [pieces[i] + pieces[i + 1] for i in range(0, len(pieces), 2)]
        value = pieces[0]
    return value


def row_scale(values):
    return lax.rsqrt(jnp.mean(values * values, axis=-1, keepdims=True) + norm_eps)


def norm_back(grad_normed, values, scale):
    return scale * grad_normed - values * scale * scale * scale * jnp.mean(
        grad_normed * values, axis=-1, keepdims=True
    )


def split_three(values):
    high = values.astype(bf16)
    rest = values - high.astype(f32)
    middle = rest.astype(bf16)
    return high, middle, (rest - middle.astype(f32)).astype(bf16)


def swap_halves(pair):
    lane = lax.broadcasted_iota(jnp.int32, pair.shape, 1)
    return jnp.where(lane % HD < HD // 2, pltpu.roll(pair, 96, 1), pltpu.roll(pair, 32, 1))


def relative_place(device, owner, count):
    flips = device ^ owner
    place, scale = 0, 1
    for low, width in reversed(bit_groups(count)):
        place = place + ((flips >> low) & ((1 << width) - 1)) * scale
        scale <<= width
    return place


def tie(value, other):
    if other is None:
        return value
    return value + other.reshape(-1)[0] * jnp.zeros((), value.dtype)


def gather_steps(chunk, count, after=None, first_after=None, last_after=None):
    held, steps = chunk[None], []
    for n, (low, width) in enumerate(reversed(bit_groups(count))):
        held = tie(held, after[n] if after else None)
        pieces = [held] + [permute_batch(held, k << low, count) for k in range(1, 1 << width)]
        held = jnp.concatenate(pieces, axis=0)
        if n == 0:
            held = tie(held, first_after)
        steps.append(held)
    return steps


def send_kernel(shard, down, where, w_qkv, w_out, w_gate_up, w_down, gains, first, second, a, b, c):
    core = where[0]
    a[...] = jnp.zeros_like(a)
    c[...] = jnp.zeros_like(c)
    c[0:2, 0:shard] = gains[...]
    column = c[...].T
    pieces = [(w_qkv, i) for i in range(9)] + [(None, 0)]
    more = [(w_out, i) for i in range(3)] + [(w_gate_up, i) for i in range(16)] + [(None, 1)]

    def fill(half):
        for target, items in ((a, pieces), (b, more)):
            number = len(items) // 2
            for i in range(number):
                source, at = items[half * number + i]
                rows = slice(i * shard, (i + 1) * shard)
                if source is not None:
                    target[rows, :] = source[:, at * LANES : (at + 1) * LANES]
                else:
                    target[rows, :] = column[:shard] if at == 0 else jnp.zeros((shard, LANES), f32)
        for i in range(3):
            start = 10 * shard + i * down
            b[start : start + down, :] = w_down[
                half * down : (half + 1) * down, i * LANES : (i + 1) * LANES
            ]

    @pl.when(core == 0)
    def _():
        fill(0)

    @pl.when(core == 1)
    def _():
        fill(1)

    first[...] = a[...].astype(bf16)
    second[...] = b[...].astype(bf16)


def send_chunks(where, w_qkv, w_out, w_gate_up, w_down, gains):
    shard, down = w_qkv.shape[0], w_down.shape[0] // 2
    core = where[0]
    first_rows = -(-5 * shard // 16) * 16
    second_rows = 10 * shard + 3 * down
    if shard % 8 == 0 and down % 8 == 0:
        spec = pl.BlockSpec(memory_space=pltpu.VMEM)
        return pl.pallas_call(
            partial(send_kernel, shard, down),
            out_shape=[
                jax.ShapeDtypeStruct((first_rows, LANES), bf16),
                jax.ShapeDtypeStruct((second_rows, LANES), bf16),
            ],
            in_specs=[pl.BlockSpec(memory_space=pltpu.SMEM)] + [spec] * 5,
            out_specs=[spec] * 2,
            scratch_shapes=[
                pltpu.VMEM((first_rows, LANES), f32),
                pltpu.VMEM((second_rows, LANES), f32),
                pltpu.VMEM((LANES, LANES), f32),
            ],
            compiler_params=pltpu.CompilerParams(vmem_limit_bytes=VMEM_LIMIT),
            name="send_chunks",
        )(where, w_qkv, w_out, w_gate_up, w_down, gains)
    gain_slab = jnp.pad(gains.T, ((0, 0), (0, LANES - 2)))[None]
    first = jnp.concatenate([slabs(w_qkv), gain_slab]).reshape(2, 5 * shard, LANES)
    first = jnp.where(core == 0, first[0], first[1]).astype(bf16)
    first = jnp.pad(first, ((0, first_rows - first.shape[0]), (0, 0)))
    second = jnp.concatenate(
        [slabs(w_out), slabs(w_gate_up), jnp.zeros((1, shard, LANES), f32)]
    ).reshape(2, 10 * shard, LANES)
    downs = slabs(w_down).reshape(3, 2, down, LANES).transpose(1, 0, 2, 3)
    downs = downs.reshape(2, 3 * down, LANES)
    second = jnp.where(
        core == 0,
        jnp.concatenate([second[0], downs[0]]),
        jnp.concatenate([second[1], downs[1]]),
    ).astype(bf16)
    return first, second


def unpack(count, number, shard, down, where, mine, other, stage, w_down):
    core, owner = where[0], where[1]
    for source, half in ((mine, core), (other, 1 - core)):

        def one(device, carry, source=source, half=half):
            chunk = source[relative_place(device, owner, count)].astype(f32)
            for i in range(number):
                rows = pl.ds(pl.multiple_of(device * shard, 8), shard)
                stage[half * number + i, rows, :] = chunk[i * shard : (i + 1) * shard]
            for i in range(3 if down else 0):
                start = number * shard + i * down
                rows = pl.ds(pl.multiple_of((device * 2 + half) * down, 16), down)
                w_down[rows, i * LANES : (i + 1) * LANES] = chunk[start : start + down].astype(bf16)
            return carry

        lax.fori_loop(0, count, one, 0)


def can_unpack(shard, down):
    return shard % 8 == 0 and down % 16 == 0


def unpack_plain(count, number, shard, down, where, mine, other):
    core, owner = where[0], where[1]
    places = relative_place(jnp.arange(count, dtype=jnp.int32), owner, count)
    low = jnp.take(jnp.where(core == 0, mine, other), places, axis=0)
    high = jnp.take(jnp.where(core == 0, other, mine), places, axis=0)

    def part(source):
        return (
            source[:, : number * shard]
            .reshape(count, number, shard, LANES)
            .transpose(1, 0, 2, 3)
            .reshape(number, D, LANES)
        )

    stack = jnp.concatenate([part(low), part(high)], axis=0)
    if number == 5:
        return unslab(stack[:9]), stack[9].T[:8].astype(f32)
    downs = [
        item[:, number * shard : number * shard + 3 * down].reshape(count, 3, down, LANES)
        for item in (low, high)
    ]
    w_down = jnp.stack(downs, axis=1).transpose(0, 1, 3, 2, 4).reshape(FF, D)
    return unslab(stack[:3]), unslab(stack[3:19]), w_down


def put_slab(stage, core, number, shard, at, slab):
    half, row = at // number, (at % number) * shard
    slot = core if half == 0 else 1 - core
    stage[slot, :, row : row + shard, :] = slab.reshape(-1, shard, LANES)


def put_down(stage, core, number, shard, down, column, slab, first):
    parts = slab.reshape(-1, 2, down, LANES)
    row = number * shard + column * down
    devices = slice(first, first + parts.shape[0])
    stage[core, devices, row : row + down, :] = parts[:, 0]
    stage[1 - core, devices, row : row + down, :] = parts[:, 1]


def gain_column(row):
    return jnp.concatenate([row, jnp.zeros((LANES - 8, D), f32)], axis=0).T


def pack_plain(count, core, grads, number, shard, down):
    column = jnp.pad(grads[-1][:1].T, ((0, 0), (0, LANES - 1)))[None]
    stack = jnp.concatenate([slabs(item) for item in (grads[:2] if down else grads[:1])] + [column])

    def by_device(part):
        return (
            part.reshape(number, count, shard, LANES)
            .transpose(1, 0, 2, 3)
            .reshape(count, number * shard, LANES)
        )

    halves = [by_device(stack[:number]), by_device(stack[number:])]
    if down:
        downs = (
            slabs(grads[2])
            .reshape(3, count, 2, down, LANES)
            .transpose(2, 1, 0, 3, 4)
            .reshape(2, count, 3 * down, LANES)
        )
        halves = [jnp.concatenate([halves[i], downs[i]], axis=1) for i in range(2)]
    return (
        jnp.where(core == 0, jnp.stack(halves), jnp.stack(halves[::-1])),
        jnp.where(core == 0, halves[1], halves[0]).astype(bf16),
    )


def scatter_steps(parts, count, owner):
    held, steps = parts, []
    rest = parts.shape[1:]
    for low, width in bit_groups(count):
        fan = 1 << width
        view = held.reshape((-1, fan) + rest)
        mine = (owner >> low) & (fan - 1)
        total = lax.dynamic_index_in_dim(view, mine, 1, keepdims=False).astype(f32)
        got = []
        for k in range(1, fan):
            piece = lax.dynamic_index_in_dim(view, mine ^ k, 1, keepdims=False)
            got.append(permute_batch(piece.astype(bf16), k << low, count))
        for item in got:
            total = total + item.astype(f32)
        held = total
        steps.append(held)
    return steps


def tables_kernel(length, where, ids, pads, offsets, cosine, sine, key_aux, query_aux, ranges):
    core = where[0]
    whole = 2 * length

    def turn(row):
        low, high = row[:, :length], row[:, length:]
        return jnp.concatenate(
            [jnp.where(core == 0, low, high), jnp.where(core == 0, high, low)], axis=1
        )

    classes = (2 * ids[...] + pads[...]).astype(f32)
    spot = lax.broadcasted_iota(jnp.int32, (1, whole), 1)
    position = (turn(spot) + turn(offsets[...])).astype(f32)
    turned = turn(classes)
    index = lax.broadcasted_iota(jnp.int32, (HD // 2, whole), 0).astype(f32)
    angle = position * jnp.exp(index * (-2.0 * math.log(10000.0) / HD))
    cos, sin = jnp.cos(angle), jnp.sin(angle)
    cosine[...] = jnp.concatenate([cos, cos, cos, cos], axis=0).T
    sine[...] = jnp.concatenate([-sin, sin, -sin, sin], axis=0).T
    at = lax.broadcasted_iota(jnp.int32, (LANES, whole), 0)
    is_class = (at >= HD) & (at < HD + 8)
    same = (at - HD).astype(f32) == turned
    is_log = (at >= HD + 8) & (at < HD + 8 + 3 * HEADS)
    key_aux[...] = jnp.where((is_class & same) | is_log, 1.0, 0.0).T.astype(bf16)
    own = turned[:, :length]
    kept = jnp.where(turn(pads[...])[:, :length] == 0, 1.0, 0.0)
    extra = jnp.where(is_class & ~same, masked_score, 0.0)[:, :length]
    query_aux[...] = jnp.where(at[:, :length] == KEEP_LANE, kept, extra).T.astype(bf16)
    starts = (core * length, (1 - core) * length)
    for n in range(length // BLOCK):
        mine = own[:, n * BLOCK : (n + 1) * BLOCK]
        first = jnp.min(mine)
        last = jnp.max(mine)
        low_key = jnp.sum(jnp.where(classes < first, 1.0, 0.0)).astype(jnp.int32)
        high_key = jnp.sum(jnp.where(classes <= last, 1.0, 0.0)).astype(jnp.int32)
        bounds = []
        for start in starts:
            low_part = jnp.clip(low_key - start, 0, length)
            high_part = jnp.clip(high_key - start, 0, length)
            low_block = low_part // BLOCK
            bounds.append((low_block, jnp.maximum((high_part + BLOCK - 1) // BLOCK - low_block, 0)))
        ranges[0, n] = bounds[0][0]
        ranges[1, n] = bounds[0][1]
        ranges[2, n] = bounds[1][0] + length // BLOCK - bounds[0][1]
        ranges[3, n] = bounds[0][1] + bounds[1][1]


def tables(where, ids, pads, offsets):
    whole = ids.shape[1]
    length = whole // 2
    spec = pl.BlockSpec(memory_space=pltpu.VMEM)
    smem = pl.BlockSpec(memory_space=pltpu.SMEM)
    return pl.pallas_call(
        partial(tables_kernel, length),
        out_shape=[
            jax.ShapeDtypeStruct((whole, LANES), f32),
            jax.ShapeDtypeStruct((whole, LANES), f32),
            jax.ShapeDtypeStruct((whole, LANES), bf16),
            jax.ShapeDtypeStruct((length, LANES), bf16),
            jax.ShapeDtypeStruct((4, length // BLOCK), jnp.int32),
        ],
        in_specs=[smem, spec, spec, spec],
        out_specs=[spec] * 4 + [smem],
        compiler_params=pltpu.CompilerParams(vmem_limit_bytes=VMEM_LIMIT),
        cost_estimate=cost(3 * 10**9, 4 * 2**20),
        name="tables",
    )(where, ids, pads, offsets)


def project_kernel(
    fused, own, there, cosine, sine, key_aux, query_aux, *refs
):
    if fused:
        where, mine, other, qa, ka, va, kt, vt, w, gains, stage = refs[:3] + refs[-8:]
    else:
        w_in, gains_in, qa, ka, va, kt, vt, w, gains = refs[:2] + refs[-7:]

    @pl.when(pl.program_id(0) == 0)
    def _():
        if fused:
            unpack(*fused, where, mine, other, stage, None)
            for i in range(9):
                w[:, i * LANES : (i + 1) * LANES] = stage[i].astype(bf16)
            gains[...] = stage[9].T[:8]
        else:
            w[...] = w_in[...]
            gains[...] = gains_in[...]

    step = pl.program_id(0)
    is_own = step < pl.num_programs(0) // 2
    x = jnp.where(is_own, own[...], there[...]).astype(f32)
    normed = (x * row_scale(x) * gains[0:1, :]).astype(bf16)
    cos, sin = cosine[...], sine[...]
    low = lax.broadcasted_iota(jnp.int32, (BLOCK, LANES), 1) < HD
    products = [dot(normed, w[:, i * LANES : (i + 1) * LANES], NN) for i in range(3, 9)]
    key_extra = key_aux[...].astype(f32)
    query_extra = query_aux[...].astype(f32)
    lane = lax.broadcasted_iota(jnp.int32, (BLOCK, LANES), 1)
    value_extra = jnp.where((lane >= HD) & (lane < HD + 3), 1.0, 0.0)
    ones = jnp.ones((8, BLOCK), bf16)

    @pl.when(is_own)
    def _():
        for pair in range(HEADS // 2):
            z = dot(normed, w[:, pair * LANES : (pair + 1) * LANES], NN)
            z = (z * cos + swap_halves(z) * sin).astype(bf16).astype(f32) * HD**-0.5
            qa[SPOT[2 * pair]] = jnp.where(low, z, query_extra).astype(bf16)
            qa[SPOT[2 * pair + 1]] = jnp.where(low, pltpu.roll(z, HD, 1), query_extra).astype(bf16)

    for pair in range(HEADS // 2):
        z = products[pair]
        z = z * cos + swap_halves(z) * sin
        ka[SPOT[2 * pair]] = jnp.where(low, z, key_extra).astype(bf16)
        ka[SPOT[2 * pair + 1]] = jnp.where(low, pltpu.roll(z, HD, 1), key_extra).astype(bf16)
        turned = z.T.astype(bf16)
        kt[SPOT[2 * pair]] = turned[:HD]
        kt[SPOT[2 * pair + 1]] = turned[HD:]
    for pair in range(HEADS // 2):
        z = products[3 + pair]
        va[SPOT[2 * pair]] = jnp.where(low, z, value_extra).astype(bf16)
        va[SPOT[2 * pair + 1]] = jnp.where(low, pltpu.roll(z, HD, 1), value_extra).astype(bf16)
        turned = z.T.astype(bf16)
        vt[SPOT[2 * pair], :HD] = turned[:HD]
        vt[SPOT[2 * pair + 1], :HD] = turned[HD:]
        vt[SPOT[2 * pair], HD:] = ones
        vt[SPOT[2 * pair + 1], HD:] = ones


def project(own, there, cosine, sine, key_aux, query_aux, weights, fused, waits):
    length = own.shape[0]
    steps = length // BLOCK
    whole = 2 * length
    first = lambda i: (jnp.minimum(i, steps - 1), 0)
    last = lambda i: (jnp.maximum(i - steps, 0), 0)
    spec = pl.BlockSpec(memory_space=pltpu.VMEM)
    if fused:
        weight_specs = [pl.BlockSpec(memory_space=pltpu.SMEM), spec, spec]
    else:
        weight_specs = [spec, spec]
    return pl.pallas_call(
        partial(project_kernel, fused),
        out_shape=[
            jax.ShapeDtypeStruct((HEADS, length, LANES), bf16),
            jax.ShapeDtypeStruct((HEADS, whole, LANES), bf16),
            jax.ShapeDtypeStruct((HEADS, whole, LANES), bf16),
            jax.ShapeDtypeStruct((HEADS, HD, whole), bf16),
            jax.ShapeDtypeStruct((HEADS, HD + 8, whole), bf16),
            jax.ShapeDtypeStruct((D, 3 * D), bf16),
            jax.ShapeDtypeStruct((8, D), f32),
        ],
        grid=(2 * steps,),
        in_specs=[
            pl.BlockSpec((BLOCK, D), first),
            pl.BlockSpec((BLOCK, D), last),
            pl.BlockSpec((BLOCK, LANES), lambda i: (i, 0)),
            pl.BlockSpec((BLOCK, LANES), lambda i: (i, 0)),
            pl.BlockSpec((BLOCK, LANES), lambda i: (i, 0)),
            pl.BlockSpec((BLOCK, LANES), first),
        ]
        + weight_specs
        + [pl.BlockSpec(memory_space=pl.ANY)] * len(waits),
        out_specs=[
            pl.BlockSpec((HEADS, BLOCK, LANES), lambda i: (0, jnp.minimum(i, steps - 1), 0)),
            pl.BlockSpec((HEADS, BLOCK, LANES), lambda i: (0, i, 0)),
            pl.BlockSpec((HEADS, BLOCK, LANES), lambda i: (0, i, 0)),
            pl.BlockSpec((HEADS, HD, BLOCK), lambda i: (0, 0, i)),
            pl.BlockSpec((HEADS, HD + 8, BLOCK), lambda i: (0, 0, i)),
            pl.BlockSpec((D, 3 * D), lambda i: (0, 0)),
            pl.BlockSpec((8, D), lambda i: (0, 0)),
        ],
        scratch_shapes=[pltpu.VMEM((10, D, LANES), f32)] if fused else [],
        compiler_params=pltpu.CompilerParams(vmem_limit_bytes=VMEM_LIMIT),
        cost_estimate=cost(9 * 10**9, 16 * 2**20),
        name="project",
    )(own, there, cosine, sine, key_aux, query_aux, *weights, *waits)


def key_block(ranges, step, n):
    return jnp.where(n < ranges[1, step], ranges[0, step] + n, ranges[2, step] + n)


def attend_kernel(ranges, qa, ka, vt, mixed, exact, qb, total, peak):
    step = pl.program_id(0)
    peak[...] = jnp.full((HEADS, 8, BLOCK), -3e38, f32)
    total[...] = jnp.zeros_like(total)

    def body(n, carry):
        rows = block(key_block(ranges, step, n))
        scores = [dot(ka[h, rows, :], qa[h], NT) for h in range(HEADS)]
        weights = []
        for h in range(HEADS):
            old = peak[h][:1]
            new = jnp.maximum(old, jnp.max(scores[h], axis=0, keepdims=True))
            weights.append((jnp.exp(scores[h] - new).astype(bf16), jnp.exp(old - new)))
            peak[h] = jnp.broadcast_to(new, (8, BLOCK))
        for h in range(HEADS):
            weight, shrink = weights[h]
            total[h] = total[h] * shrink + dot(vt[h, :, rows], weight, NN)
        return carry

    lax.fori_loop(0, ranges[3, step], body, 0)
    terms = []
    for h in range(HEADS):
        bottom = total[h][HD : HD + 1]
        terms.append(total[h][:HD] / bottom)
        logs = -(peak[h][:1] + jnp.log(bottom))
        for piece in split_three(logs):
            terms.append(piece.astype(f32))
    for pair in range(HEADS // 2):
        spots = (SPOT[2 * pair], SPOT[2 * pair + 1])
        both = jnp.concatenate([terms[4 * spot] for spot in spots], axis=0).T
        mixed[:, pair * LANES : (pair + 1) * LANES] = both.astype(bf16)
        exact[:, pair * LANES : (pair + 1) * LANES] = both
    pieces = [terms[4 * h + 1 + i] for h in range(HEADS) for i in range(3)]
    table = jnp.concatenate(
        [jnp.zeros((HD + 8, BLOCK), f32)]
        + pieces
        + [jnp.zeros((LANES - HD - 8 - 3 * HEADS, BLOCK), f32)],
        axis=0,
    ).T
    lane = lax.broadcasted_iota(jnp.int32, (BLOCK, LANES), 1)
    for h in range(HEADS):
        start = HD + 8 + 3 * h
        qb[h] = jnp.where(
            (lane >= start) & (lane < start + 3), table, qa[h].astype(f32)
        ).astype(bf16)


def attend(ranges, qa, ka, vt):
    heads, length, _ = qa.shape
    whole = ka.shape[1]
    return pl.pallas_call(
        attend_kernel,
        out_shape=[
            jax.ShapeDtypeStruct((length, D), bf16),
            jax.ShapeDtypeStruct((length, D), f32),
            jax.ShapeDtypeStruct(qa.shape, bf16),
        ],
        grid_spec=pltpu.PrefetchScalarGridSpec(
            num_scalar_prefetch=1,
            grid=(length // BLOCK,),
            in_specs=[
                pl.BlockSpec((heads, BLOCK, LANES), lambda i, *_: (0, i, 0)),
                pl.BlockSpec((heads, whole, LANES), lambda i, *_: (0, 0, 0)),
                pl.BlockSpec((heads, HD + 8, whole), lambda i, *_: (0, 0, 0)),
            ],
            out_specs=[
                pl.BlockSpec((BLOCK, D), lambda i, *_: (i, 0)),
                pl.BlockSpec((BLOCK, D), lambda i, *_: (i, 0)),
                pl.BlockSpec((heads, BLOCK, LANES), lambda i, *_: (0, i, 0)),
            ],
            scratch_shapes=[
                pltpu.VMEM((heads, HD + 8, BLOCK), f32),
                pltpu.VMEM((heads, 8, BLOCK), f32),
            ],
        ),
        compiler_params=pltpu.CompilerParams(vmem_limit_bytes=VMEM_LIMIT),
        cost_estimate=cost(12 * 10**9, 12 * 2**20),
        name="attend",
    )(ranges, qa, ka, vt)


def attend_back_kernel(ranges, qb, ka, da, va, kt, *refs):
    dq, own, there, sums, acc = refs[-5:]
    step = pl.program_id(0)
    heads = qb.shape[0]

    @pl.when(step == 0)
    def _():
        sums[...] = jnp.zeros_like(sums)

    acc[...] = jnp.zeros_like(acc)
    zero = jnp.zeros((BLOCK, HD), bf16)

    def body(n, carry):
        rows = block(key_block(ranges, step, n))
        first = [
            (dot(ka[h, rows, :], qb[h], NT), dot(va[h, rows, :], da[h], NT)) for h in range(heads)
        ]
        second = []
        for scores, grads in first:
            probs = jnp.exp(scores)
            second.append((probs.astype(bf16), (probs * grads).astype(bf16)))
        for h in range(heads):
            probs_low, grads_low = second[h]
            grad_side = jnp.concatenate([da[h][:, :HD], zero], axis=1)
            query_side = jnp.concatenate([zero, qb[h][:, :HD]], axis=1)
            sums[h, rows, :] += dot(probs_low, grad_side, NN) + dot(grads_low, query_side, NN)
            acc[h] += dot(kt[h, :, rows], grads_low, NN)
        return carry

    lax.fori_loop(0, ranges[3, step], body, 0)
    dq[...] = acc[...]

    @pl.when(step == pl.num_programs(0) - 1)
    def _():
        length = own.shape[1]
        own[...] = sums[:, :length, :]
        there[...] = sums[:, length:, :].astype(bf16)


def attend_back(heads, group, ranges, qb, ka, da, va, kt, waits):
    length, whole = qb.shape[1], ka.shape[1]
    return pl.pallas_call(
        attend_back_kernel,
        out_shape=[
            jax.ShapeDtypeStruct((heads, HD, length), f32),
            jax.ShapeDtypeStruct((heads, length, LANES), f32),
            jax.ShapeDtypeStruct((heads, whole - length, LANES), bf16),
        ],
        grid_spec=pltpu.PrefetchScalarGridSpec(
            num_scalar_prefetch=1,
            grid=(length // BLOCK,),
            in_specs=[
                pl.BlockSpec((heads, BLOCK, LANES), lambda i, *_: (group, i, 0)),
                pl.BlockSpec((heads, whole, LANES), lambda i, *_: (group, 0, 0)),
                pl.BlockSpec((heads, BLOCK, LANES), lambda i, *_: (group, i, 0)),
                pl.BlockSpec((heads, whole, LANES), lambda i, *_: (group, 0, 0)),
                pl.BlockSpec((heads, HD, whole), lambda i, *_: (group, 0, 0)),
            ]
            + [pl.BlockSpec(memory_space=pl.ANY)] * len(waits),
            out_specs=[
                pl.BlockSpec((heads, HD, BLOCK), lambda i, *_: (0, 0, i)),
                pl.BlockSpec((heads, length, LANES), lambda i, *_: (0, 0, 0)),
                pl.BlockSpec((heads, whole - length, LANES), lambda i, *_: (0, 0, 0)),
            ],
            scratch_shapes=[
                pltpu.VMEM((heads, whole, LANES), f32),
                pltpu.VMEM((heads, HD, BLOCK), f32),
            ],
        ),
        compiler_params=pltpu.CompilerParams(vmem_limit_bytes=VMEM_LIMIT),
        cost_estimate=cost(12 * 10**9, 8 * 2**20),
        name="attend_back",
    )(ranges, qb, ka, da, va, kt, *waits)


def feed_kernel(fused, own, mixed, exact, cotangent, query_aux, gains, *refs):
    if fused:
        where, mine, other = refs[:3]
        result, grad_middle, da, sums, give = refs[3:8]
        normed_all, low_all, hidden_all, up_all, middle_all, wo, wgu, wd, stage, g_gain = refs[8:-1]
    else:
        wo, wgu, wd = refs[:3]
        result, grad_middle, da, g_out, g_gate_up, g_down, g_gain = refs[3:10]
        normed_all, low_all, hidden_all, up_all, middle_all = refs[10:-1]
    step = pl.program_id(0)
    steps = pl.num_programs(0)
    gain = gains[1:2, :]

    @pl.when(step == 0)
    def _():
        g_gain[...] = jnp.zeros_like(g_gain)
        if fused:
            unpack(*fused, where, mine, other, stage, wd)
            for i in range(3):
                wo[:, i * LANES : (i + 1) * LANES] = stage[i].astype(bf16)
            for i in range(16):
                wgu[:, i * LANES : (i + 1) * LANES] = stage[3 + i].astype(bf16)

    chunks = FF // BLOCK
    lane = lax.broadcasted_iota(jnp.int32, (BLOCK, LANES), 1)

    rows = block(step)
    x = own[...].astype(f32)
    middle = x + dot(mixed[...], wo[...], NN)
    scale = row_scale(middle)
    normed = (middle * scale * gain).astype(bf16)
    normed_all[rows, :] = normed
    kept = query_aux[...].astype(f32)[:, KEEP_LANE : KEEP_LANE + 1]
    upstream = cotangent[...].astype(f32) * kept
    up_low = upstream.astype(bf16)
    up_all[rows, :] = up_low
    gates = [dot(normed, wgu[:, c * BLOCK : (c + 1) * BLOCK], NN) for c in range(chunks)]
    ups = [dot(normed, wgu[:, FF + c * BLOCK : FF + (c + 1) * BLOCK], NN) for c in range(chunks)]
    hiddens = [dot(up_low, wd[c * BLOCK : (c + 1) * BLOCK, :], NT) for c in range(chunks)]
    for c in range(chunks):
        gate, up, grad_hidden = gates[c], ups[c], hiddens[c]
        sig = 1.0 / (1.0 + jnp.exp(-gate))
        silu = gate * sig
        hidden_all[rows, c * BLOCK : (c + 1) * BLOCK] = (silu * up).astype(bf16)
        low_all[rows, FF + c * BLOCK : FF + (c + 1) * BLOCK] = (grad_hidden * silu).astype(bf16)
        low_all[rows, c * BLOCK : (c + 1) * BLOCK] = (
            grad_hidden * up * (sig + silu * (1.0 - sig))
        ).astype(bf16)
    ffn = dot(hidden_all[rows, :], wd[...], NN)
    grad_normed = dot(low_all[rows, :], wgu[...], NT)
    result[...] = (kept * (middle + ffn)).astype(bf16)
    g_gain[0:1, :] += jnp.sum(grad_normed * middle * scale, axis=0, keepdims=True)
    grad = upstream + norm_back(grad_normed * gain, middle, scale)
    grad_middle[...] = grad
    low = grad.astype(bf16)
    middle_all[rows, :] = low
    grad_mixed = dot(low, wo[...], NT).astype(bf16).astype(f32)
    products = grad_mixed * exact[...]
    for h in range(HEADS):
        pair = h // 2
        head = grad_mixed[:, pair * LANES : (pair + 1) * LANES]
        product = products[:, pair * LANES : (pair + 1) * LANES]
        mine_lanes = (lane < HD) if h % 2 == 0 else (lane >= HD)
        delta = -jnp.sum(jnp.where(mine_lanes, product, 0.0), axis=1, keepdims=True)
        if h % 2:
            head = pltpu.roll(head, HD, 1)
        high, mid, last = split_three(delta)
        extra = jnp.where(
            lane == HD,
            high.astype(f32),
            jnp.where(
                lane == HD + 1,
                mid.astype(f32),
                jnp.where(lane == HD + 2, last.astype(f32), 0.0),
            ),
        )
        da[SPOT[h]] = jnp.where(lane < HD, head, extra).astype(bf16)

    mixed_all = refs[-1]
    mixed_all[rows, :] = mixed[...]

    @pl.when(step == steps - 1)
    def _():
        if not fused:
            g_out[...] = dot(mixed_all[...], middle_all[...], TN)
            for c in range(2 * FF // 512):
                g_gate_up[:, c * 512 : (c + 1) * 512] = dot(
                    normed_all[...], low_all[:, c * 512 : (c + 1) * 512], TN
                )
            for c in range(chunks):
                g_down[c * BLOCK : (c + 1) * BLOCK, :] = dot(
                    hidden_all[:, c * BLOCK : (c + 1) * BLOCK], up_all[...], TN
                )
            return
        count, number, shard, down = fused
        core = where[0]

        def put(at, value):
            for i in range(value.shape[1] // LANES):
                put_slab(sums, core, number, shard, at + i, value[:, i * LANES : (i + 1) * LANES])

        put(0, dot(mixed_all[...], middle_all[...], TN))
        for c in range(2 * FF // 512):
            put(3 + 4 * c, dot(normed_all[...], low_all[:, c * 512 : (c + 1) * 512], TN))
        put(19, gain_column(g_gain[...]))
        for c in range(chunks):
            value = dot(hidden_all[:, c * BLOCK : (c + 1) * BLOCK], up_all[...], TN)
            for i in range(3):
                put_down(
                    sums, core, number, shard, down, i,
                    value[:, i * LANES : (i + 1) * LANES], c * BLOCK // (2 * down),
                )
        give[...] = sums[1].astype(bf16)


def feed(own, mixed, exact, cotangent, query_aux, gains, weights, fused):
    length = own.shape[0]
    spec = pl.BlockSpec(memory_space=pltpu.VMEM)
    scratch = [
        pltpu.VMEM((length, D), bf16),
        pltpu.VMEM((length, 2 * FF), bf16),
        pltpu.VMEM((length, FF), bf16),
        pltpu.VMEM((length, D), bf16),
        pltpu.VMEM((length, D), bf16),
    ]
    rows_of = lambda i: (i, 0)
    out_shape = [
        jax.ShapeDtypeStruct((length, D), bf16),
        jax.ShapeDtypeStruct((length, D), f32),
        jax.ShapeDtypeStruct((HEADS, length, LANES), bf16),
    ]
    out_specs = [
        pl.BlockSpec((BLOCK, D), rows_of),
        pl.BlockSpec((BLOCK, D), rows_of),
        pl.BlockSpec((HEADS, BLOCK, LANES), lambda i: (0, i, 0)),
    ]
    if fused:
        count, number, shard, down = fused
        rows = number * shard + 3 * down
        weight_specs = [pl.BlockSpec(memory_space=pltpu.SMEM), spec, spec]
        out_shape += [
            jax.ShapeDtypeStruct((2, count, rows, LANES), f32),
            jax.ShapeDtypeStruct((count, rows, LANES), bf16),
        ]
        out_specs += [spec, spec]
        scratch += [
            pltpu.VMEM((D, D), bf16),
            pltpu.VMEM((D, 2 * FF), bf16),
            pltpu.VMEM((FF, D), bf16),
            pltpu.VMEM((2 * number, D, LANES), f32),
            pltpu.VMEM((8, D), f32),
        ]
    else:
        weight_specs = [spec] * 3
        out_shape += [
            jax.ShapeDtypeStruct((D, D), f32),
            jax.ShapeDtypeStruct((D, 2 * FF), f32),
            jax.ShapeDtypeStruct((FF, D), f32),
            jax.ShapeDtypeStruct((8, D), f32),
        ]
        out_specs += [spec] * 4
    scratch.append(pltpu.VMEM((length, D), bf16))
    return pl.pallas_call(
        partial(feed_kernel, fused),
        out_shape=out_shape,
        grid=(length // BLOCK,),
        in_specs=[
            pl.BlockSpec((BLOCK, D), rows_of),
            pl.BlockSpec((BLOCK, D), rows_of),
            pl.BlockSpec((BLOCK, D), rows_of),
            pl.BlockSpec((BLOCK, D), rows_of),
            pl.BlockSpec((BLOCK, LANES), rows_of),
            pl.BlockSpec((8, D), lambda i: (0, 0)),
        ]
        + weight_specs,
        out_specs=out_specs,
        scratch_shapes=scratch,
        compiler_params=pltpu.CompilerParams(vmem_limit_bytes=VMEM_LIMIT),
        cost_estimate=cost(14 * 10**9, 16 * 2**20),
        name="feed",
    )(own, mixed, exact, cotangent, query_aux, gains, *weights)


PARTS = ((0, 1, 2, 3, 6), (4, 5, 7, 8))


def runs(part):
    found = []
    for at, slab in enumerate(part):
        if found and slab == found[-1][0] + found[-1][1]:
            found[-1][1] += 1
        else:
            found.append([slab, 1, at])
    return found


def project_back_kernel(number, fused, own, cosine, sine, w, gains, *refs):
    part = PARTS[number]
    step = pl.program_id(0)
    rows = block(step)
    cos, sin = cosine[...], -sine[...]
    low = lax.broadcasted_iota(jnp.int32, (BLOCK, LANES), 1) < HD
    if number == 0:
        dqs, (kept, got) = refs[:2], refs[2:4]
        partial_sum, grads, normed_all, low_all = refs[-4:]
    else:
        kept, got, grad_middle, before, grads_before = refs[:5]
        if fused:
            where = refs[5]
            grad_tokens, sums, give, g_gain, normed_all, low_all = refs[-6:]
        else:
            grad_tokens, grads, g_gain, normed_all, low_all = refs[-5:]
    x = own[...].astype(f32)
    scale = row_scale(x)
    gain = gains[0:1, :]
    normed_all[rows, :] = (x * scale * gain).astype(bf16)
    for at, slab in enumerate(part):
        kind, pair = divmod(slab, 3)
        if kind == 0:
            source, first = (dqs[0], 0) if pair == 0 else (dqs[1], 2 * pair - 2)
            z = jnp.concatenate([source[first], source[first + 1]], axis=0).T * HD**-0.5
        else:
            first = 0 if pair == 0 else 2 * pair - 2
            one, two = [kept[i] + got[i].astype(f32) for i in (first, first + 1)]
            if kind == 1:
                z = jnp.where(low, pltpu.roll(one, HD, 1), two)
            else:
                z = jnp.where(low, one, pltpu.roll(two, HD, 1))
        if kind < 2:
            z = z * cos + swap_halves(z) * sin
        low_all[rows, at * LANES : (at + 1) * LANES] = z.astype(bf16)
    grad_normed = sum(
        dot(
            low_all[rows, at * LANES : (at + many) * LANES],
            w[:, slab * LANES : (slab + many) * LANES],
            NT,
        )
        for slab, many, at in runs(part)
    )
    if number == 0:
        partial_sum[...] = grad_normed
    else:
        grad_normed = grad_normed + before[...]
        gain_sum = jnp.sum(grad_normed * x * scale, axis=0, keepdims=True)

        @pl.when(step == 0)
        def _():
            g_gain[...] = jnp.zeros_like(g_gain)

        g_gain[0:1, :] += gain_sum
        grad_tokens[...] = (
            grad_middle[...] + norm_back(grad_normed * gain, x, scale)
        ).astype(bf16)

    @pl.when(step == pl.num_programs(0) - 1)
    def _():
        value = dot(normed_all[...], low_all[...], TN)
        if number == 0 or not fused:
            grads[...] = value
            return
        core = where[0]
        for done, source in ((PARTS[0], grads_before), (PARTS[1], value)):
            for at, slab in enumerate(done):
                put_slab(sums, core, *fused, slab, source[:, at * LANES : (at + 1) * LANES])
        put_slab(sums, core, *fused, 9, gain_column(g_gain[...]))
        give[...] = sums[1].astype(bf16)


def project_back(number, fused, where, tables, arrays, waits):
    own, cosine, sine, w, gains = tables
    length = own.shape[0]
    columns = len(PARTS[number]) * LANES
    whole = pl.BlockSpec(memory_space=pltpu.VMEM)
    rows_of = lambda i: (i, 0)
    wide = pl.BlockSpec((BLOCK, D), rows_of)
    narrow = pl.BlockSpec((BLOCK, LANES), rows_of)
    scratch = [pltpu.VMEM((length, D), bf16), pltpu.VMEM((length, columns), bf16)]

    def heads(array, turned):
        if turned:
            return pl.BlockSpec((array.shape[0], HD, BLOCK), lambda i: (0, 0, i))
        return pl.BlockSpec((array.shape[0], BLOCK, LANES), lambda i: (0, i, 0))

    if number == 0:
        specs = [heads(arrays[0], True), heads(arrays[1], True)]
        specs += [heads(arrays[2], False), heads(arrays[3], False)]
        shapes = [((length, D), f32), ((D, columns), f32)]
        out_specs = [wide, whole]
    else:
        specs = [heads(arrays[0], False), heads(arrays[1], False), wide, wide, whole]
        if fused:
            size, shard = fused
            chunk = (D // shard, size * shard, LANES)
            specs.append(pl.BlockSpec(memory_space=pltpu.SMEM))
            arrays = [*arrays, where]
            shapes = [((length, D), bf16), ((2,) + chunk, f32), (chunk, bf16)]
            out_specs = [wide, whole, whole]
            scratch = [pltpu.VMEM((8, D), f32)] + scratch
        else:
            shapes = [((length, D), bf16), ((D, columns), f32), ((8, D), f32)]
            out_specs = [wide, whole, whole]
    return pl.pallas_call(
        partial(project_back_kernel, number, fused),
        out_shape=[jax.ShapeDtypeStruct(*item) for item in shapes],
        grid=(length // BLOCK,),
        in_specs=[
            wide,
            narrow,
            narrow,
            pl.BlockSpec((D, 3 * D), lambda i: (0, 0)),
            pl.BlockSpec((8, D), lambda i: (0, 0)),
        ]
        + specs
        + [pl.BlockSpec(memory_space=pl.ANY)] * len(waits),
        out_specs=out_specs,
        scratch_shapes=scratch,
        compiler_params=pltpu.CompilerParams(vmem_limit_bytes=VMEM_LIMIT),
        cost_estimate=cost(4 * 10**9, 8 * 2**20),
        name="project_back",
    )(own, cosine, sine, w, gains, *arrays, *waits)


def update_kernel(shard, down, where, total, sums, there, *refs):
    core = where[0]
    masters, firsts, seconds = refs[:5], refs[5:10], refs[10:15]
    norm = refs[15]
    outs = [refs[16 + 5 * i : 21 + 5 * i] for i in range(4)]
    low, high, square = refs[36:]

    @pl.when(core == 0)
    def _():
        low[...] = sums[...]
        high[...] = there[...]

    @pl.when(core == 1)
    def _():
        low[...] = there[...]
        high[...] = sums[...]

    length = jnp.sqrt(total[...])
    norm[...] = length
    factor = clip_limit / jnp.maximum(length, clip_limit)
    halves = (low, high)

    def step(which, grad, rows, columns, rate, decay):
        at = (rows, columns)
        new = adam_update(
            masters[which][at], factor * grad, firsts[which][at], seconds[which][at], rate, decay
        )
        outs[0][which][at] = new[0]
        outs[1][which][at] = new[1]
        outs[2][which][at] = new[2]
        outs[3][which][at] = new[2].astype(bf16)

    every = slice(None)
    places = [(0, i, i // 5, (i % 5) * shard) for i in range(9)]
    for i in range(19):
        which, column = (1, i) if i < 3 else (2, i - 3)
        places.append((which, column, i // 10, (5 + i % 10) * shard))
    for which, column, half, row in places:
        rate = 4.0 * D**-0.5 if which == 1 else D**-0.5
        grad = halves[half][row : row + shard, :]
        step(which, grad, every, slice(column * LANES, (column + 1) * LANES), rate, decay_rate)
    for half in range(2):
        for i in range(3):
            row = 15 * shard + i * down
            step(
                3, halves[half][row : row + down, :], slice(half * down, (half + 1) * down),
                slice(i * LANES, (i + 1) * LANES), FF**-0.5, decay_rate,
            )
    gain_rows = []
    for row in (4 * shard, 14 * shard):
        square[...] = jnp.zeros_like(square)
        square[0:shard, :] = high[row : row + shard, :]
        gain_rows.append(square[...].T[0:1, :shard])
    for i in range(2):
        step(4, gain_rows[i], slice(i, i + 1), every, 0.5, 0.0)


def update(where, total, sums, there, masters, firsts, seconds):
    shard, down = masters[0].shape[0], masters[3].shape[0] // 2
    spec = pl.BlockSpec(memory_space=pltpu.VMEM)
    shapes = [item.shape for item in masters]
    outs = pl.pallas_call(
        partial(update_kernel, shard, down),
        out_shape=[jax.ShapeDtypeStruct((1, 1), f32)]
        + [jax.ShapeDtypeStruct(shape, f32) for _ in range(3) for shape in shapes]
        + [jax.ShapeDtypeStruct(shape, bf16) for shape in shapes],
        in_specs=[pl.BlockSpec(memory_space=pltpu.SMEM)] + [spec] * 18,
        out_specs=[spec] * 21,
        scratch_shapes=[
            pltpu.VMEM(sums.shape, f32),
            pltpu.VMEM(sums.shape, f32),
            pltpu.VMEM((LANES, LANES), f32),
        ],
        compiler_params=pltpu.CompilerParams(vmem_limit_bytes=VMEM_LIMIT),
        name="update",
    )(where, total, sums, there, *masters, *firsts, *seconds)
    return outs[0][0, 0], outs[1:6], outs[6:11], outs[11:16], outs[16:21]


def update_plain(core, total, sums, there, masters, firsts, seconds):
    shard, down = masters[0].shape[0], masters[3].shape[0] // 2
    low = jnp.where(core == 0, sums, there)
    high = jnp.where(core == 0, there, sums)
    five, fifteen = 5 * shard, 15 * shard
    first_shard = jnp.concatenate([low[:five], high[:five]]).reshape(10, shard, LANES)
    second_shard = jnp.concatenate([low[five:fifteen], high[five:fifteen]])
    second_shard = second_shard.reshape(20, shard, LANES)
    down_shard = jnp.stack(
        [item[fifteen:].reshape(3, down, LANES) for item in (low, high)], axis=1
    ).reshape(3, 2 * down, LANES)
    shard_grads = (
        unslab(first_shard[:9]),
        unslab(second_shard[:3]),
        unslab(second_shard[3:19]),
        unslab(down_shard),
        jnp.stack([first_shard[9, :, 0], second_shard[19, :, 0]]),
    )
    grad_norm = jnp.sqrt(total[0, 0])
    factor = clip_limit / jnp.maximum(grad_norm, clip_limit)
    rates = (D ** (-0.5), 4.0 * D ** (-0.5), D ** (-0.5), FF ** (-0.5), 0.5)
    decays = (decay_rate, decay_rate, decay_rate, decay_rate, 0.0)
    updates = [
        adam_update(
            masters[i], factor * shard_grads[i], firsts[i], seconds[i], rates[i], decays[i]
        )
        for i in range(5)
    ]
    new_first, new_second, new_master = zip(*updates)
    return grad_norm, new_first, new_second, new_master, [item.astype(bf16) for item in new_master]


def per_device(
    count,
    tokens,
    cotangent,
    sample_ids,
    pad_flags,
    offsets,
    w_qkv,
    w_out,
    w_gate_up,
    w_down,
    gains,
    m_qkv,
    m_out,
    m_gate_up,
    m_down,
    m_gains,
    v_qkv,
    v_out,
    v_gate_up,
    v_down,
    v_gains,
):
    owner = lax.axis_index("batch")
    core = lax.axis_index("tm")
    where = jnp.stack([core, owner]).astype(jnp.int32)
    shard = w_qkv.shape[0]
    down = w_down.shape[0] // 2
    own = tokens[0]
    fuse_in = can_unpack(shard, down)
    masters = (w_qkv, w_out, w_gate_up, w_down, gains)

    first, second = send_chunks(where, *masters)
    cosine, sine, key_aux, query_aux, ranges = tables(where, sample_ids, pad_flags, offsets)
    first_steps = gather_steps(first, count, first_after=query_aux)
    first_held = first_steps[-1]
    second_steps = gather_steps(second, count, first_steps)
    there = swap_tm(own)

    def gathered(held, number, down):
        other = swap_tm(held)
        if fuse_in:
            return (where, held, other), (count, number, shard, down)
        return unpack_plain(count, number, shard, down, where, held, other), None

    weights, fused = gathered(first_held, 5, 0)
    waits = second_steps[-2:-1] if len(second_steps) > 1 else []
    qa, ka, va, kt, vt, attn_in, gain_pair = project(
        own, there, cosine, sine, key_aux, query_aux, weights, fused, waits
    )
    second_held = tie(second_steps[-1], gain_pair)
    mixed, exact, qb = attend(ranges, qa, ka, vt)
    weights, fused = gathered(second_held, 10, down)
    result, grad_middle, da, *grads = feed(
        own, mixed, exact, cotangent[0], query_aux, gain_pair, weights, fused
    )
    if not fused:
        grads = pack_plain(count, core, grads, 10, shard, down)
    kept, given = grads
    second_total = kept[0] + swap_tm(given).astype(f32)
    second_sums = scatter_steps(second_total, count, owner)

    dqs, owns, recvs = [], [], []
    for group, waits in zip(GROUPS, ([given], [second_total])):
        dq, kept, part = attend_back(*group, ranges, qb, ka, da, va, kt, waits)
        dqs.append(dq)
        owns.append(kept)
        recvs.append(swap_tm(part))
    fused = (5, shard) if fuse_in else None
    shared = (own, cosine, sine, attn_in, gain_pair)
    several = len(second_sums) > 1
    before, grads_before = project_back(
        0, fused, where, shared, [*dqs, owns[0], recvs[0]], second_sums[:1] if several else []
    )
    grad_tokens, *grads = project_back(
        1, fused, where, shared, [owns[1], recvs[1], grad_middle, before, grads_before],
        second_sums[1:2] if several else [],
    )
    if not fused:
        order = [(PARTS[0] + PARTS[1]).index(i) for i in range(9)]
        both = jnp.concatenate([slabs(grads_before), slabs(grads[0])])
        grads = pack_plain(count, core, [unslab(both[jnp.array(order)]), grads[1]], 5, shard, 0)
    kept, given = grads
    first_total = kept[0] + swap_tm(given).astype(f32)
    first_sum = scatter_steps(first_total, count, owner)[-1].reshape(-1, LANES)
    second_sum = second_sums[-1].reshape(-1, LANES)

    sums = jnp.concatenate([first_sum, second_sum], axis=0)
    sums_there = swap_tm(sums)
    squares = jnp.sum(sums * sums) + jnp.sum(sums_there * sums_there)
    total = sum_batch(squares.reshape(1, 1), count)
    firsts = (m_qkv, m_out, m_gate_up, m_down, m_gains)
    seconds = (v_qkv, v_out, v_gate_up, v_down, v_gains)
    if fuse_in:
        updates = update(where, total, sums, sums_there, masters, firsts, seconds)
    else:
        updates = update_plain(core, total, sums, sums_there, masters, firsts, seconds)
    grad_norm, new_first, new_second, new_master, copies = updates
    return (
        result[None],
        grad_tokens[None],
        grad_norm,
        *new_first,
        *new_second,
        *new_master,
        *copies,
    )


def solution(mesh):
    in_specs = (
        P("batch", "tm", None),
        P("batch", "tm", None),
        P("batch", None),
        P("batch", None),
        P("batch", None),
        P("batch", None),
        P("batch", None),
        P("batch", None),
        P("batch", None),
        P(None, "batch"),
        P("batch", None),
        P("batch", None),
        P("batch", None),
        P("batch", None),
        P(None, "batch"),
        P("batch", None),
        P("batch", None),
        P("batch", None),
        P("batch", None),
        P(None, "batch"),
    )
    out_specs = (
        P("batch", "tm", None),
        P("batch", "tm", None),
        P(),
        P("batch", None),
        P("batch", None),
        P("batch", None),
        P("batch", None),
        P(None, "batch"),
        P("batch", None),
        P("batch", None),
        P("batch", None),
        P("batch", None),
        P(None, "batch"),
        P("batch", None),
        P("batch", None),
        P("batch", None),
        P("batch", None),
        P(None, "batch"),
        P("batch", None),
        P("batch", None),
        P("batch", None),
        P("batch", None),
        P(None, "batch"),
    )
    return jax.shard_map(
        partial(per_device, mesh.shape["batch"]), mesh=mesh, in_specs=in_specs, out_specs=out_specs, check_vma=False
    )
```

```python
import math
from functools import partial

import jax
import jax.numpy as jnp
from jax import lax
from jax.experimental import pallas as pl
from jax.experimental.pallas import tpu as pltpu
from jax.sharding import PartitionSpec as P

D = 384
FF = 1024
HEADS = 6
HD = 64
STEP = 3


norm_eps = 1e-06
beta_one = 0.5
beta_two = 0.5
adam_eps = 1e-08
decay_rate = 0.1
clip_limit = 1.0
masked_score = -1e30


def adam_update(master, grad, first, second, rate, decay):
    first_new = beta_one * first + (1.0 - beta_one) * grad
    second_new = beta_two * second + (1.0 - beta_two) * grad * grad
    direction = (
        first_new
        / (1.0 - beta_one**STEP)
        / (jnp.sqrt(second_new / (1.0 - beta_two**STEP)) + adam_eps)
    )
    return (first_new, second_new, master - rate * (direction + decay * master))


def bit_groups(count):
    groups = []
    low, bits = 0, count.bit_length() - 1
    while low < bits:
        width = min(2, bits - low)
        groups.append((low, width))
        low += width
    return groups


def permute_batch(value, flip, count):
    return lax.ppermute(value, "batch", [(i, i ^ flip) for i in range(count)])


def swap_tm(value):
    return lax.ppermute(value, "tm", [(0, 1), (1, 0)])


def slabs(matrix):
    rows, columns = matrix.shape
    return matrix.reshape(rows, columns // 128, 128).transpose(1, 0, 2)


def unslab(stack):
    count, rows, _ = stack.shape
    return stack.transpose(1, 0, 2).reshape(rows, count * 128)


bf16 = jnp.bfloat16
f32 = jnp.float32
BLOCK = 256
LANES = 128
KEEP_LANE = 96
STORED = (2, 3, 4, 5, 0, 1)
SPOT = tuple(STORED.index(head) for head in range(HEADS))
GROUPS = ((2, 2), (4, 0))
VMEM_LIMIT = 58 * 2**20
NN = (((1,), (0,)), ((), ()))
NT = (((1,), (1,)), ((), ()))
TN = (((0,), (0,)), ((), ()))


def dot(left, right, dims):
    return lax.dot_general(left, right, dims, preferred_element_type=f32)


def cost(flops, moved):
    return pl.CostEstimate(flops=flops, bytes_accessed=moved, transcendentals=0)


def block(start, size=BLOCK):
    return pl.ds(pl.multiple_of(start * size, size), size)


def sum_batch(value, count):
    value = jnp.broadcast_to(value[:, None], (count, 1, LANES))
    value = lax.all_to_all(value, "batch", 0, 0, tiled=True)
    return jnp.sum(value, axis=0)


def row_scale(values):
    return lax.rsqrt(jnp.mean(values * values, axis=-1, keepdims=True) + norm_eps)


def norm_back(grad_normed, values, scale):
    return scale * grad_normed - values * scale * scale * scale * jnp.mean(
        grad_normed * values, axis=-1, keepdims=True
    )


def split_three(values):
    high = values.astype(bf16)
    rest = values - high.astype(f32)
    middle = rest.astype(bf16)
    return high, middle, (rest - middle.astype(f32)).astype(bf16)


def swap_halves(pair):
    lane = lax.broadcasted_iota(jnp.int32, pair.shape, 1)
    return jnp.where(lane % HD < HD // 2, pltpu.roll(pair, 96, 1), pltpu.roll(pair, 32, 1))


def relative_place(device, owner, count):
    flips = device ^ owner
    place, scale = 0, 1
    for low, width in reversed(bit_groups(count)):
        place = place + ((flips >> low) & ((1 << width) - 1)) * scale
        scale <<= width
    return place


def exchange_all(held, low, width, count):
    return [held] + [permute_batch(held, k << low, count) for k in range(1, 1 << width)]


def hold(values, waits):
    spec = pl.BlockSpec(memory_space=pl.ANY)
    number = len(values)
    return pl.pallas_call(
        lambda *refs: None,
        out_shape=[jax.ShapeDtypeStruct(item.shape, item.dtype) for item in values],
        in_specs=[spec] * (number + len(waits)),
        out_specs=[spec] * number,
        input_output_aliases={i: i for i in range(number)},
        name="hold",
    )(*values, *waits)


def send_kernel(shard, plan, down, where, *refs):
    sources, (target, stage, square) = refs[: len(refs) - 3], refs[len(refs) - 3 :]
    number = len(plan) // 2
    core = where[0]
    stage[...] = jnp.zeros_like(stage)
    gain_at = [i for i, item in enumerate(plan) if item == "gain"]
    if gain_at:
        square[...] = jnp.zeros_like(square)
        square[0:2, 0:shard] = sources[-1][...]
        column = square[...].T

    def fill(half):
        for i in range(number):
            item = plan[half * number + i]
            rows = slice(i * shard, (i + 1) * shard)
            if item == "gain":
                stage[rows, :] = column[:shard]
            elif item is not None:
                which, at = item
                stage[rows, :] = sources[which][:, at * LANES : (at + 1) * LANES]
        for i in range(3 if down else 0):
            start = number * shard + i * down
            stage[start : start + down, :] = sources[2][
                half * down : (half + 1) * down, i * LANES : (i + 1) * LANES
            ]

    @pl.when(core == 0)
    def _():
        fill(0)

    @pl.when(core == 1)
    def _():
        fill(1)

    target[...] = stage[...].astype(bf16)


def send_chunk(where, plan, down, sources, waits):
    shard = sources[0].shape[0]
    rows = len(plan) // 2 * shard + 3 * down
    rows = -(-rows // 16) * 16
    core = where[0]
    if shard % 8 == 0 and down % 8 == 0:
        spec = pl.BlockSpec(memory_space=pltpu.VMEM)

        def kernel(where, *refs):
            kept = refs[: len(sources)] + refs[len(sources) + len(waits) :]
            send_kernel(shard, plan, down, where, *kept)

        return pl.pallas_call(
            kernel,
            out_shape=jax.ShapeDtypeStruct((rows, LANES), bf16),
            in_specs=[pl.BlockSpec(memory_space=pltpu.SMEM)]
            + [spec] * len(sources)
            + [pl.BlockSpec(memory_space=pl.ANY)] * len(waits),
            out_specs=spec,
            scratch_shapes=[pltpu.VMEM((rows, LANES), f32), pltpu.VMEM((LANES, LANES), f32)],
            compiler_params=pltpu.CompilerParams(vmem_limit_bytes=VMEM_LIMIT),
            name="send_chunk",
        )(where, *sources, *waits)
    stacks = {i: slabs(item) for i, item in enumerate(sources) if item.shape[1] % LANES == 0}
    pieces = []
    for item in plan:
        if item == "gain":
            pieces.append(jnp.pad(sources[-1].T, ((0, 0), (0, LANES - 2))))
        elif item is None:
            pieces.append(jnp.zeros((shard, LANES), f32))
        else:
            pieces.append(stacks[item[0]][item[1]])
    half = len(plan) // 2
    halves = [jnp.concatenate(pieces[:half]), jnp.concatenate(pieces[half:])]
    if down:
        for i in range(2):
            part = stacks[2][:, i * down : (i + 1) * down].reshape(3 * down, LANES)
            halves[i] = jnp.concatenate([halves[i], part])
    chunk = jnp.where(core == 0, halves[0], halves[1]).astype(bf16)
    return jnp.pad(chunk, ((0, rows - chunk.shape[0]), (0, 0)))


FIRST_PLAN = tuple((0, i) for i in range(9)) + ("gain",)
SECOND_PLAN = tuple((0, i) for i in range(3)) + tuple((1, i) for i in range(16)) + (None,)


def gather(chunk, count, waits):
    held = chunk[None]
    groups = bit_groups(count)[::-1]
    for n, (low, width) in enumerate(groups):
        pieces = exchange_all(held, low, width, count)
        if n == 0:
            pieces[1:] = hold(pieces[1:], waits)
        if n + 1 < len(groups):
            held = jnp.concatenate(pieces, axis=0)
    return held, pieces


def unpack(count, number, shard, down, where, pieces, others, stage, w_down):
    core, owner = where[0], where[1]
    last = bit_groups(count)[0][1]
    for sources, half in ((pieces, core), (others, 1 - core)):
        for flip, source in enumerate(sources):

            def one(n, carry, source=source, half=half, flip=flip):
                inner = n // (count >> last)
                device = owner ^ (flip + inner) ^ (relative_flips(n % (count >> last), count) << last)
                chunk = source[n].astype(f32)
                for i in range(number):
                    rows = pl.ds(pl.multiple_of(device * shard, 8), shard)
                    stage[half * number + i, rows, :] = chunk[i * shard : (i + 1) * shard]
                for i in range(3 if down else 0):
                    start = number * shard + i * down
                    rows = pl.ds(pl.multiple_of((device * 2 + half) * down, 16), down)
                    w_down[rows, i * LANES : (i + 1) * LANES] = chunk[start : start + down].astype(
                        bf16
                    )
                return carry

            lax.fori_loop(0, source.shape[0], one, 0, unroll=True)


def relative_flips(place, count):
    last = bit_groups(count)[0][1]
    flips, scale = 0, 1
    for low, width in reversed(bit_groups(count)[1:]):
        flips = flips + (((place // scale) & ((1 << width) - 1)) << (low - last))
        scale <<= width
    return flips


def can_unpack(shard, down):
    return shard % 8 == 0 and down % 16 == 0


def unpack_plain(count, number, shard, down, where, mine, other):
    core, owner = where[0], where[1]
    places = relative_place(jnp.arange(count, dtype=jnp.int32), owner, count)
    mine, other = jnp.concatenate(mine), jnp.concatenate(other)
    low = jnp.take(jnp.where(core == 0, mine, other), places, axis=0)
    high = jnp.take(jnp.where(core == 0, other, mine), places, axis=0)

    def part(source):
        return (
            source[:, : number * shard]
            .reshape(count, number, shard, LANES)
            .transpose(1, 0, 2, 3)
            .reshape(number, D, LANES)
        )

    stack = jnp.concatenate([part(low), part(high)], axis=0)
    if number == 5:
        return unslab(stack[:9]), stack[9].T[:8].astype(f32)
    downs = [
        item[:, number * shard : number * shard + 3 * down].reshape(count, 3, down, LANES)
        for item in (low, high)
    ]
    w_down = jnp.stack(downs, axis=1).transpose(0, 1, 3, 2, 4).reshape(FF, D)
    return unslab(stack[:3]), unslab(stack[3:19]), w_down


def put_slab(stage, core, number, shard, at, slab):
    half, row = at // number, (at % number) * shard
    slot = core if half == 0 else 1 - core
    stage[slot, :, row : row + shard, :] = slab.reshape(-1, shard, LANES)


def put_down(stage, core, number, shard, down, column, slab, first):
    parts = slab.reshape(-1, 2, down, LANES)
    row = number * shard + column * down
    devices = slice(first, first + parts.shape[0])
    stage[core, devices, row : row + down, :] = parts[:, 0]
    stage[1 - core, devices, row : row + down, :] = parts[:, 1]


def gain_column(row):
    return jnp.concatenate([row, jnp.zeros((LANES - 8, D), f32)], axis=0).T


def pack_plain(count, core, grads, number, shard, down):
    column = jnp.pad(grads[-1][:1].T, ((0, 0), (0, LANES - 1)))[None]
    stack = jnp.concatenate([slabs(item) for item in (grads[:2] if down else grads[:1])] + [column])

    def by_device(part):
        return (
            part.reshape(number, count, shard, LANES)
            .transpose(1, 0, 2, 3)
            .reshape(count, number * shard, LANES)
        )

    halves = [by_device(stack[:number]), by_device(stack[number:])]
    if down:
        downs = (
            slabs(grads[2])
            .reshape(3, count, 2, down, LANES)
            .transpose(2, 1, 0, 3, 4)
            .reshape(2, count, 3 * down, LANES)
        )
        halves = [jnp.concatenate([halves[i], downs[i]], axis=1) for i in range(2)]
    return (
        jnp.where(core == 0, jnp.stack(halves), jnp.stack(halves[::-1])),
        jnp.where(core == 0, halves[1], halves[0]).astype(bf16),
    )


def scatter_steps(parts, count, owner):
    held, steps = parts, []
    rest = parts.shape[1:]
    for low, width in bit_groups(count):
        fan = 1 << width
        view = held.reshape((-1, fan) + rest)
        mine = (owner >> low) & (fan - 1)
        total = lax.dynamic_index_in_dim(view, mine, 1, keepdims=False).astype(f32)
        got = []
        for k in range(1, fan):
            piece = lax.dynamic_index_in_dim(view, mine ^ k, 1, keepdims=False)
            got.append(permute_batch(piece.astype(bf16), k << low, count))
        for item in got:
            total = total + item.astype(f32)
        held = total
        steps.append(held)
    return steps


def tables_kernel(length, where, ids, pads, offsets, *refs):
    cosine, sine, key_aux, query_aux, ranges = refs[-5:]
    core = where[0]
    whole = 2 * length

    def turn(row):
        low, high = row[:, :length], row[:, length:]
        return jnp.concatenate(
            [jnp.where(core == 0, low, high), jnp.where(core == 0, high, low)], axis=1
        )

    classes = (2 * ids[...] + pads[...]).astype(f32)
    spot = lax.broadcasted_iota(jnp.int32, (1, whole), 1)
    position = (turn(spot) + turn(offsets[...])).astype(f32)
    turned = turn(classes)
    index = lax.broadcasted_iota(jnp.int32, (HD // 2, whole), 0).astype(f32)
    angle = position * jnp.exp(index * (-2.0 * math.log(10000.0) / HD))
    cos, sin = jnp.cos(angle), jnp.sin(angle)
    cosine[...] = jnp.concatenate([cos, cos, cos, cos], axis=0).T
    sine[...] = jnp.concatenate([-sin, sin, -sin, sin], axis=0).T
    at = lax.broadcasted_iota(jnp.int32, (LANES, whole), 0)
    is_class = (at >= HD) & (at < HD + 8)
    same = (at - HD).astype(f32) == turned
    is_log = (at >= HD + 8) & (at < HD + 8 + 3 * HEADS)
    key_aux[...] = jnp.where((is_class & same) | is_log, 1.0, 0.0).T.astype(bf16)
    own = turned[:, :length]
    kept = jnp.where(turn(pads[...])[:, :length] == 0, 1.0, 0.0)
    extra = jnp.where(is_class & ~same, masked_score, 0.0)[:, :length]
    query_aux[...] = jnp.where(at[:, :length] == KEEP_LANE, kept, extra).T.astype(bf16)
    starts = (core * length, (1 - core) * length)
    for n in range(length // BLOCK):
        mine = own[:, n * BLOCK : (n + 1) * BLOCK]
        first = jnp.min(mine)
        last = jnp.max(mine)
        low_key = jnp.sum(jnp.where(classes < first, 1.0, 0.0)).astype(jnp.int32)
        high_key = jnp.sum(jnp.where(classes <= last, 1.0, 0.0)).astype(jnp.int32)
        bounds = []
        for start in starts:
            low_part = jnp.clip(low_key - start, 0, length)
            high_part = jnp.clip(high_key - start, 0, length)
            low_block = low_part // BLOCK
            bounds.append((low_block, jnp.maximum((high_part + BLOCK - 1) // BLOCK - low_block, 0)))
        ranges[0, n] = bounds[0][0]
        ranges[1, n] = bounds[0][1]
        ranges[2, n] = bounds[1][0] + length // BLOCK - bounds[0][1]
        ranges[3, n] = bounds[0][1] + bounds[1][1]


def tables(where, ids, pads, offsets, waits):
    whole = ids.shape[1]
    length = whole // 2
    spec = pl.BlockSpec(memory_space=pltpu.VMEM)
    smem = pl.BlockSpec(memory_space=pltpu.SMEM)
    return pl.pallas_call(
        partial(tables_kernel, length),
        out_shape=[
            jax.ShapeDtypeStruct((whole, LANES), f32),
            jax.ShapeDtypeStruct((whole, LANES), f32),
            jax.ShapeDtypeStruct((whole, LANES), bf16),
            jax.ShapeDtypeStruct((length, LANES), bf16),
            jax.ShapeDtypeStruct((4, length // BLOCK), jnp.int32),
        ],
        in_specs=[smem, spec, spec, spec] + [pl.BlockSpec(memory_space=pl.ANY)] * len(waits),
        out_specs=[spec] * 4 + [smem],
        compiler_params=pltpu.CompilerParams(vmem_limit_bytes=VMEM_LIMIT),
        cost_estimate=cost(3 * 10**9, 4 * 2**20),
        name="tables",
    )(where, ids, pads, offsets, *waits)


def project_kernel(
    fused, own, there, cosine, sine, key_aux, query_aux, *refs
):
    if fused:
        where, (qa, ka, va, kt, vt, w, gains, stage) = refs[0], refs[-8:]
        mine, other = refs[1:2], refs[2:3]
    else:
        w_in, gains_in, qa, ka, va, kt, vt, w, gains = refs[:2] + refs[-7:]

    @pl.when(pl.program_id(0) == 0)
    def _():
        if fused:
            unpack(*fused, where, mine, other, stage, None)
            for i in range(9):
                w[:, i * LANES : (i + 1) * LANES] = stage[i].astype(bf16)
            gains[...] = stage[9].T[:8]
        else:
            w[...] = w_in[...]
            gains[...] = gains_in[...]

    step = pl.program_id(0)
    is_own = step < pl.num_programs(0) // 2
    x = jnp.where(is_own, own[...], there[...]).astype(f32)
    normed = (x * row_scale(x) * gains[0:1, :]).astype(bf16)
    cos, sin = cosine[...], sine[...]
    low = lax.broadcasted_iota(jnp.int32, (BLOCK, LANES), 1) < HD
    products = [dot(normed, w[:, i * LANES : (i + 1) * LANES], NN) for i in range(3, 9)]
    key_extra = key_aux[...].astype(f32)
    query_extra = query_aux[...].astype(f32)
    lane = lax.broadcasted_iota(jnp.int32, (BLOCK, LANES), 1)
    value_extra = jnp.where((lane >= HD) & (lane < HD + 3), 1.0, 0.0)
    ones = jnp.ones((8, BLOCK), bf16)

    @pl.when(is_own)
    def _():
        for pair in range(HEADS // 2):
            z = dot(normed, w[:, pair * LANES : (pair + 1) * LANES], NN)
            z = (z * cos + swap_halves(z) * sin).astype(bf16).astype(f32) * HD**-0.5
            qa[SPOT[2 * pair]] = jnp.where(low, z, query_extra).astype(bf16)
            qa[SPOT[2 * pair + 1]] = jnp.where(low, pltpu.roll(z, HD, 1), query_extra).astype(bf16)

    for pair in range(HEADS // 2):
        z = products[pair]
        z = z * cos + swap_halves(z) * sin
        ka[SPOT[2 * pair]] = jnp.where(low, z, key_extra).astype(bf16)
        ka[SPOT[2 * pair + 1]] = jnp.where(low, pltpu.roll(z, HD, 1), key_extra).astype(bf16)
        turned = z.T.astype(bf16)
        kt[SPOT[2 * pair]] = turned[:HD]
        kt[SPOT[2 * pair + 1]] = turned[HD:]
    for pair in range(HEADS // 2):
        z = products[3 + pair]
        va[SPOT[2 * pair]] = jnp.where(low, z, value_extra).astype(bf16)
        va[SPOT[2 * pair + 1]] = jnp.where(low, pltpu.roll(z, HD, 1), value_extra).astype(bf16)
        turned = z.T.astype(bf16)
        vt[SPOT[2 * pair], :HD] = turned[:HD]
        vt[SPOT[2 * pair + 1], :HD] = turned[HD:]
        vt[SPOT[2 * pair], HD:] = ones
        vt[SPOT[2 * pair + 1], HD:] = ones


def project(own, there, cosine, sine, key_aux, query_aux, weights, fused, waits):
    length = own.shape[0]
    steps = length // BLOCK
    whole = 2 * length
    first = lambda i: (jnp.minimum(i, steps - 1), 0)
    last = lambda i: (jnp.maximum(i - steps, 0), 0)
    spec = pl.BlockSpec(memory_space=pltpu.VMEM)
    if fused:
        weight_specs = [pl.BlockSpec(memory_space=pltpu.SMEM)] + [spec] * (len(weights) - 1)
    else:
        weight_specs = [spec, spec]
    return pl.pallas_call(
        partial(project_kernel, fused),
        out_shape=[
            jax.ShapeDtypeStruct((HEADS, length, LANES), bf16),
            jax.ShapeDtypeStruct((HEADS, whole, LANES), bf16),
            jax.ShapeDtypeStruct((HEADS, whole, LANES), bf16),
            jax.ShapeDtypeStruct((HEADS, HD, whole), bf16),
            jax.ShapeDtypeStruct((HEADS, HD + 8, whole), bf16),
            jax.ShapeDtypeStruct((D, 3 * D), bf16),
            jax.ShapeDtypeStruct((8, D), f32),
        ],
        grid=(2 * steps,),
        in_specs=[
            pl.BlockSpec((BLOCK, D), first),
            pl.BlockSpec((BLOCK, D), last),
            pl.BlockSpec((BLOCK, LANES), lambda i: (i, 0)),
            pl.BlockSpec((BLOCK, LANES), lambda i: (i, 0)),
            pl.BlockSpec((BLOCK, LANES), lambda i: (i, 0)),
            pl.BlockSpec((BLOCK, LANES), first),
        ]
        + weight_specs
        + [pl.BlockSpec(memory_space=pl.ANY)] * len(waits),
        out_specs=[
            pl.BlockSpec((HEADS, BLOCK, LANES), lambda i: (0, jnp.minimum(i, steps - 1), 0)),
            pl.BlockSpec((HEADS, BLOCK, LANES), lambda i: (0, i, 0)),
            pl.BlockSpec((HEADS, BLOCK, LANES), lambda i: (0, i, 0)),
            pl.BlockSpec((HEADS, HD, BLOCK), lambda i: (0, 0, i)),
            pl.BlockSpec((HEADS, HD + 8, BLOCK), lambda i: (0, 0, i)),
            pl.BlockSpec((D, 3 * D), lambda i: (0, 0)),
            pl.BlockSpec((8, D), lambda i: (0, 0)),
        ],
        scratch_shapes=[pltpu.VMEM((10, D, LANES), f32)] if fused else [],
        compiler_params=pltpu.CompilerParams(vmem_limit_bytes=VMEM_LIMIT),
        cost_estimate=cost(9 * 10**9, 16 * 2**20),
        name="project",
    )(own, there, cosine, sine, key_aux, query_aux, *weights, *waits)


def key_block(ranges, step, n):
    return jnp.where(n < ranges[1, step], ranges[0, step] + n, ranges[2, step] + n)


def attend_kernel(ranges, qa, ka, vt, *refs):
    mixed, exact, qb, total, peak = refs[-5:]
    step = pl.program_id(0)
    peak[...] = jnp.full((HEADS, 8, BLOCK), -3e38, f32)
    total[...] = jnp.zeros_like(total)

    def body(n, carry):
        rows = block(key_block(ranges, step, n))
        scores = [dot(ka[h, rows, :], qa[h], NT) for h in range(HEADS)]
        weights = []
        for h in range(HEADS):
            old = peak[h][:1]
            new = jnp.maximum(old, jnp.max(scores[h], axis=0, keepdims=True))
            weights.append((jnp.exp(scores[h] - new).astype(bf16), jnp.exp(old - new)))
            peak[h] = jnp.broadcast_to(new, (8, BLOCK))
        for h in range(HEADS):
            weight, shrink = weights[h]
            total[h] = total[h] * shrink + dot(vt[h, :, rows], weight, NN)
        return carry

    lax.fori_loop(0, ranges[3, step], body, 0)
    terms = []
    for h in range(HEADS):
        bottom = total[h][HD : HD + 1]
        terms.append(total[h][:HD] / bottom)
        logs = -(peak[h][:1] + jnp.log(bottom))
        for piece in split_three(logs):
            terms.append(piece.astype(f32))
    for pair in range(HEADS // 2):
        spots = (SPOT[2 * pair], SPOT[2 * pair + 1])
        both = jnp.concatenate([terms[4 * spot] for spot in spots], axis=0).T
        mixed[:, pair * LANES : (pair + 1) * LANES] = both.astype(bf16)
        exact[:, pair * LANES : (pair + 1) * LANES] = both
    pieces = [terms[4 * h + 1 + i] for h in range(HEADS) for i in range(3)]
    table = jnp.concatenate(
        [jnp.zeros((HD + 8, BLOCK), f32)]
        + pieces
        + [jnp.zeros((LANES - HD - 8 - 3 * HEADS, BLOCK), f32)],
        axis=0,
    ).T
    lane = lax.broadcasted_iota(jnp.int32, (BLOCK, LANES), 1)
    for h in range(HEADS):
        start = HD + 8 + 3 * h
        qb[h] = jnp.where(
            (lane >= start) & (lane < start + 3), table, qa[h].astype(f32)
        ).astype(bf16)


def attend(ranges, qa, ka, vt, waits):
    heads, length, _ = qa.shape
    whole = ka.shape[1]
    return pl.pallas_call(
        attend_kernel,
        out_shape=[
            jax.ShapeDtypeStruct((length, D), bf16),
            jax.ShapeDtypeStruct((length, D), f32),
            jax.ShapeDtypeStruct(qa.shape, bf16),
        ],
        grid_spec=pltpu.PrefetchScalarGridSpec(
            num_scalar_prefetch=1,
            grid=(length // BLOCK,),
            in_specs=[
                pl.BlockSpec((heads, BLOCK, LANES), lambda i, *_: (0, i, 0)),
                pl.BlockSpec((heads, whole, LANES), lambda i, *_: (0, 0, 0)),
                pl.BlockSpec((heads, HD + 8, whole), lambda i, *_: (0, 0, 0)),
            ]
            + [pl.BlockSpec(memory_space=pl.ANY)] * len(waits),
            out_specs=[
                pl.BlockSpec((BLOCK, D), lambda i, *_: (i, 0)),
                pl.BlockSpec((BLOCK, D), lambda i, *_: (i, 0)),
                pl.BlockSpec((heads, BLOCK, LANES), lambda i, *_: (0, i, 0)),
            ],
            scratch_shapes=[
                pltpu.VMEM((heads, HD + 8, BLOCK), f32),
                pltpu.VMEM((heads, 8, BLOCK), f32),
            ],
        ),
        compiler_params=pltpu.CompilerParams(vmem_limit_bytes=VMEM_LIMIT),
        cost_estimate=cost(12 * 10**9, 12 * 2**20),
        name="attend",
    )(ranges, qa, ka, vt, *waits)


def attend_back_kernel(ranges, qb, ka, da, va, kt, *refs):
    dq, own, there, sums, acc = refs[-5:]
    step = pl.program_id(0)
    heads = qb.shape[0]

    @pl.when(step == 0)
    def _():
        sums[...] = jnp.zeros_like(sums)

    acc[...] = jnp.zeros_like(acc)
    zero = jnp.zeros((BLOCK, HD), bf16)

    def body(n, carry):
        rows = block(key_block(ranges, step, n))
        first = [
            (dot(ka[h, rows, :], qb[h], NT), dot(va[h, rows, :], da[h], NT)) for h in range(heads)
        ]
        second = []
        for scores, grads in first:
            probs = jnp.exp(scores)
            second.append((probs.astype(bf16), (probs * grads).astype(bf16)))
        for h in range(heads):
            probs_low, grads_low = second[h]
            grad_side = jnp.concatenate([da[h][:, :HD], zero], axis=1)
            query_side = jnp.concatenate([zero, qb[h][:, :HD]], axis=1)
            sums[h, rows, :] += dot(probs_low, grad_side, NN) + dot(grads_low, query_side, NN)
            acc[h] += dot(kt[h, :, rows], grads_low, NN)
        return carry

    lax.fori_loop(0, ranges[3, step], body, 0)
    dq[...] = acc[...]

    @pl.when(step == pl.num_programs(0) - 1)
    def _():
        length = own.shape[1]
        own[...] = sums[:, :length, :]
        there[...] = sums[:, length:, :].astype(bf16)


def attend_back(heads, group, ranges, qb, ka, da, va, kt, waits):
    length, whole = qb.shape[1], ka.shape[1]
    return pl.pallas_call(
        attend_back_kernel,
        out_shape=[
            jax.ShapeDtypeStruct((heads, HD, length), f32),
            jax.ShapeDtypeStruct((heads, length, LANES), f32),
            jax.ShapeDtypeStruct((heads, whole - length, LANES), bf16),
        ],
        grid_spec=pltpu.PrefetchScalarGridSpec(
            num_scalar_prefetch=1,
            grid=(length // BLOCK,),
            in_specs=[
                pl.BlockSpec((heads, BLOCK, LANES), lambda i, *_: (group, i, 0)),
                pl.BlockSpec((heads, whole, LANES), lambda i, *_: (group, 0, 0)),
                pl.BlockSpec((heads, BLOCK, LANES), lambda i, *_: (group, i, 0)),
                pl.BlockSpec((heads, whole, LANES), lambda i, *_: (group, 0, 0)),
                pl.BlockSpec((heads, HD, whole), lambda i, *_: (group, 0, 0)),
            ]
            + [pl.BlockSpec(memory_space=pl.ANY)] * len(waits),
            out_specs=[
                pl.BlockSpec((heads, HD, BLOCK), lambda i, *_: (0, 0, i)),
                pl.BlockSpec((heads, length, LANES), lambda i, *_: (0, 0, 0)),
                pl.BlockSpec((heads, whole - length, LANES), lambda i, *_: (0, 0, 0)),
            ],
            scratch_shapes=[
                pltpu.VMEM((heads, whole, LANES), f32),
                pltpu.VMEM((heads, HD, BLOCK), f32),
            ],
        ),
        compiler_params=pltpu.CompilerParams(vmem_limit_bytes=VMEM_LIMIT),
        cost_estimate=cost(12 * 10**9, 8 * 2**20),
        name="attend_back",
    )(ranges, qb, ka, da, va, kt, *waits)


def feed_kernel(fused, own, mixed, exact, cotangent, query_aux, gains, *refs):
    if fused:
        pieces = 1 << bit_groups(fused[0])[0][1]
        where, mine, other = refs[0], refs[1 : 1 + pieces], refs[1 + pieces : 1 + 2 * pieces]
        result, grad_middle, da, sums, give = refs[1 + 2 * pieces : 6 + 2 * pieces]
        normed_all, low_all, hidden_all, up_all, middle_all, wo, wgu, wd, stage, g_gain = refs[
            6 + 2 * pieces : -1
        ]
    else:
        wo, wgu, wd = refs[:3]
        result, grad_middle, da, g_out, g_gate_up, g_down, g_gain = refs[3:10]
        normed_all, low_all, hidden_all, up_all, middle_all = refs[10:-1]
    step = pl.program_id(0)
    steps = pl.num_programs(0)
    gain = gains[1:2, :]

    @pl.when(step == 0)
    def _():
        g_gain[...] = jnp.zeros_like(g_gain)
        if fused:
            unpack(*fused, where, mine, other, stage, wd)
            for i in range(3):
                wo[:, i * LANES : (i + 1) * LANES] = stage[i].astype(bf16)
            for i in range(16):
                wgu[:, i * LANES : (i + 1) * LANES] = stage[3 + i].astype(bf16)

    chunks = FF // BLOCK
    lane = lax.broadcasted_iota(jnp.int32, (BLOCK, LANES), 1)

    rows = block(step)
    x = own[...].astype(f32)
    middle = x + dot(mixed[...], wo[...], NN)
    scale = row_scale(middle)
    normed = (middle * scale * gain).astype(bf16)
    normed_all[rows, :] = normed
    kept = query_aux[...].astype(f32)[:, KEEP_LANE : KEEP_LANE + 1]
    upstream = cotangent[...].astype(f32) * kept
    up_low = upstream.astype(bf16)
    up_all[rows, :] = up_low
    gates = [dot(normed, wgu[:, c * BLOCK : (c + 1) * BLOCK], NN) for c in range(chunks)]
    ups = [dot(normed, wgu[:, FF + c * BLOCK : FF + (c + 1) * BLOCK], NN) for c in range(chunks)]
    hiddens = [dot(up_low, wd[c * BLOCK : (c + 1) * BLOCK, :], NT) for c in range(chunks)]
    for c in range(chunks):
        gate, up, grad_hidden = gates[c], ups[c], hiddens[c]
        sig = 1.0 / (1.0 + jnp.exp(-gate))
        silu = gate * sig
        hidden_all[rows, c * BLOCK : (c + 1) * BLOCK] = (silu * up).astype(bf16)
        low_all[rows, FF + c * BLOCK : FF + (c + 1) * BLOCK] = (grad_hidden * silu).astype(bf16)
        low_all[rows, c * BLOCK : (c + 1) * BLOCK] = (
            grad_hidden * up * (sig + silu * (1.0 - sig))
        ).astype(bf16)
    ffn = dot(hidden_all[rows, :], wd[...], NN)
    grad_normed = dot(low_all[rows, :], wgu[...], NT)
    result[...] = (kept * (middle + ffn)).astype(bf16)
    g_gain[0:1, :] += jnp.sum(grad_normed * middle * scale, axis=0, keepdims=True)
    grad = upstream + norm_back(grad_normed * gain, middle, scale)
    grad_middle[...] = grad
    low = grad.astype(bf16)
    middle_all[rows, :] = low
    grad_mixed = dot(low, wo[...], NT).astype(bf16).astype(f32)
    products = grad_mixed * exact[...]
    for h in range(HEADS):
        pair = h // 2
        head = grad_mixed[:, pair * LANES : (pair + 1) * LANES]
        product = products[:, pair * LANES : (pair + 1) * LANES]
        mine_lanes = (lane < HD) if h % 2 == 0 else (lane >= HD)
        delta = -jnp.sum(jnp.where(mine_lanes, product, 0.0), axis=1, keepdims=True)
        if h % 2:
            head = pltpu.roll(head, HD, 1)
        high, mid, last = split_three(delta)
        extra = jnp.where(
            lane == HD,
            high.astype(f32),
            jnp.where(
                lane == HD + 1,
                mid.astype(f32),
                jnp.where(lane == HD + 2, last.astype(f32), 0.0),
            ),
        )
        da[SPOT[h]] = jnp.where(lane < HD, head, extra).astype(bf16)

    mixed_all = refs[-1]
    mixed_all[rows, :] = mixed[...]

    @pl.when(step == steps - 1)
    def _():
        if not fused:
            g_out[...] = dot(mixed_all[...], middle_all[...], TN)
            for c in range(2 * FF // 512):
                g_gate_up[:, c * 512 : (c + 1) * 512] = dot(
                    normed_all[...], low_all[:, c * 512 : (c + 1) * 512], TN
                )
            for c in range(chunks):
                g_down[c * BLOCK : (c + 1) * BLOCK, :] = dot(
                    hidden_all[:, c * BLOCK : (c + 1) * BLOCK], up_all[...], TN
                )
            return
        count, number, shard, down = fused
        core = where[0]

        def put(at, value):
            for i in range(value.shape[1] // LANES):
                put_slab(sums, core, number, shard, at + i, value[:, i * LANES : (i + 1) * LANES])

        put(0, dot(mixed_all[...], middle_all[...], TN))
        for c in range(2 * FF // 512):
            put(3 + 4 * c, dot(normed_all[...], low_all[:, c * 512 : (c + 1) * 512], TN))
        put(19, gain_column(g_gain[...]))
        for c in range(chunks):
            value = dot(hidden_all[:, c * BLOCK : (c + 1) * BLOCK], up_all[...], TN)
            for i in range(3):
                put_down(
                    sums, core, number, shard, down, i,
                    value[:, i * LANES : (i + 1) * LANES], c * BLOCK // (2 * down),
                )
        give[...] = sums[1].astype(bf16)


def feed(own, mixed, exact, cotangent, query_aux, gains, weights, fused):
    length = own.shape[0]
    spec = pl.BlockSpec(memory_space=pltpu.VMEM)
    scratch = [
        pltpu.VMEM((length, D), bf16),
        pltpu.VMEM((length, 2 * FF), bf16),
        pltpu.VMEM((length, FF), bf16),
        pltpu.VMEM((length, D), bf16),
        pltpu.VMEM((length, D), bf16),
    ]
    rows_of = lambda i: (i, 0)
    out_shape = [
        jax.ShapeDtypeStruct((length, D), bf16),
        jax.ShapeDtypeStruct((length, D), f32),
        jax.ShapeDtypeStruct((HEADS, length, LANES), bf16),
    ]
    out_specs = [
        pl.BlockSpec((BLOCK, D), rows_of),
        pl.BlockSpec((BLOCK, D), rows_of),
        pl.BlockSpec((HEADS, BLOCK, LANES), lambda i: (0, i, 0)),
    ]
    if fused:
        count, number, shard, down = fused
        rows = number * shard + 3 * down
        weight_specs = [pl.BlockSpec(memory_space=pltpu.SMEM)] + [spec] * (len(weights) - 1)
        out_shape += [
            jax.ShapeDtypeStruct((2, count, rows, LANES), f32),
            jax.ShapeDtypeStruct((count, rows, LANES), bf16),
        ]
        out_specs += [spec, spec]
        scratch += [
            pltpu.VMEM((D, D), bf16),
            pltpu.VMEM((D, 2 * FF), bf16),
            pltpu.VMEM((FF, D), bf16),
            pltpu.VMEM((2 * number, D, LANES), f32),
            pltpu.VMEM((8, D), f32),
        ]
    else:
        weight_specs = [spec] * 3
        out_shape += [
            jax.ShapeDtypeStruct((D, D), f32),
            jax.ShapeDtypeStruct((D, 2 * FF), f32),
            jax.ShapeDtypeStruct((FF, D), f32),
            jax.ShapeDtypeStruct((8, D), f32),
        ]
        out_specs += [spec] * 4
    scratch.append(pltpu.VMEM((length, D), bf16))
    return pl.pallas_call(
        partial(feed_kernel, fused),
        out_shape=out_shape,
        grid=(length // BLOCK,),
        in_specs=[
            pl.BlockSpec((BLOCK, D), rows_of),
            pl.BlockSpec((BLOCK, D), rows_of),
            pl.BlockSpec((BLOCK, D), rows_of),
            pl.BlockSpec((BLOCK, D), rows_of),
            pl.BlockSpec((BLOCK, LANES), rows_of),
            pl.BlockSpec((8, D), lambda i: (0, 0)),
        ]
        + weight_specs,
        out_specs=out_specs,
        scratch_shapes=scratch,
        compiler_params=pltpu.CompilerParams(vmem_limit_bytes=VMEM_LIMIT),
        cost_estimate=cost(14 * 10**9, 16 * 2**20),
        name="feed",
    )(own, mixed, exact, cotangent, query_aux, gains, *weights)


PARTS = ((0, 1, 2, 3, 6), (4, 5, 7, 8))


def runs(part):
    found = []
    for at, slab in enumerate(part):
        if found and slab == found[-1][0] + found[-1][1]:
            found[-1][1] += 1
        else:
            found.append([slab, 1, at])
    return found


def project_back_kernel(number, fused, own, cosine, sine, w, gains, *refs):
    part = PARTS[number]
    step = pl.program_id(0)
    rows = block(step)
    cos, sin = cosine[...], -sine[...]
    low = lax.broadcasted_iota(jnp.int32, (BLOCK, LANES), 1) < HD
    if number == 0:
        dqs, (kept, got) = refs[:2], refs[2:4]
        partial_sum, grads, normed_all, low_all = refs[-4:]
    else:
        kept, got, grad_middle, before, grads_before = refs[:5]
        if fused:
            where = refs[5]
            grad_tokens, sums, give, g_gain, normed_all, low_all = refs[-6:]
        else:
            grad_tokens, grads, g_gain, normed_all, low_all = refs[-5:]
    x = own[...].astype(f32)
    scale = row_scale(x)
    gain = gains[0:1, :]
    normed_all[rows, :] = (x * scale * gain).astype(bf16)
    for at, slab in enumerate(part):
        kind, pair = divmod(slab, 3)
        if kind == 0:
            source, first = (dqs[0], 0) if pair == 0 else (dqs[1], 2 * pair - 2)
            z = jnp.concatenate([source[first], source[first + 1]], axis=0).T * HD**-0.5
        else:
            first = 0 if pair == 0 else 2 * pair - 2
            one, two = [kept[i] + got[i].astype(f32) for i in (first, first + 1)]
            if kind == 1:
                z = jnp.where(low, pltpu.roll(one, HD, 1), two)
            else:
                z = jnp.where(low, one, pltpu.roll(two, HD, 1))
        if kind < 2:
            z = z * cos + swap_halves(z) * sin
        low_all[rows, at * LANES : (at + 1) * LANES] = z.astype(bf16)
    grad_normed = sum(
        dot(
            low_all[rows, at * LANES : (at + many) * LANES],
            w[:, slab * LANES : (slab + many) * LANES],
            NT,
        )
        for slab, many, at in runs(part)
    )
    if number == 0:
        partial_sum[...] = grad_normed
    else:
        grad_normed = grad_normed + before[...]
        gain_sum = jnp.sum(grad_normed * x * scale, axis=0, keepdims=True)

        @pl.when(step == 0)
        def _():
            g_gain[...] = jnp.zeros_like(g_gain)

        g_gain[0:1, :] += gain_sum
        grad_tokens[...] = (
            grad_middle[...] + norm_back(grad_normed * gain, x, scale)
        ).astype(bf16)

    @pl.when(step == pl.num_programs(0) - 1)
    def _():
        value = dot(normed_all[...], low_all[...], TN)
        if number == 0 or not fused:
            grads[...] = value
            return
        core = where[0]
        for done, source in ((PARTS[0], grads_before), (PARTS[1], value)):
            for at, slab in enumerate(done):
                put_slab(sums, core, *fused, slab, source[:, at * LANES : (at + 1) * LANES])
        put_slab(sums, core, *fused, 9, gain_column(g_gain[...]))
        give[...] = sums[1].astype(bf16)


def project_back(number, fused, where, tables, arrays, waits):
    own, cosine, sine, w, gains = tables
    length = own.shape[0]
    columns = len(PARTS[number]) * LANES
    whole = pl.BlockSpec(memory_space=pltpu.VMEM)
    rows_of = lambda i: (i, 0)
    wide = pl.BlockSpec((BLOCK, D), rows_of)
    narrow = pl.BlockSpec((BLOCK, LANES), rows_of)
    scratch = [pltpu.VMEM((length, D), bf16), pltpu.VMEM((length, columns), bf16)]

    def heads(array, turned):
        if turned:
            return pl.BlockSpec((array.shape[0], HD, BLOCK), lambda i: (0, 0, i))
        return pl.BlockSpec((array.shape[0], BLOCK, LANES), lambda i: (0, i, 0))

    if number == 0:
        specs = [heads(arrays[0], True), heads(arrays[1], True)]
        specs += [heads(arrays[2], False), heads(arrays[3], False)]
        shapes = [((length, D), f32), ((D, columns), f32)]
        out_specs = [wide, whole]
    else:
        specs = [heads(arrays[0], False), heads(arrays[1], False), wide, wide, whole]
        if fused:
            size, shard = fused
            chunk = (D // shard, size * shard, LANES)
            specs.append(pl.BlockSpec(memory_space=pltpu.SMEM))
            arrays = [*arrays, where]
            shapes = [((length, D), bf16), ((2,) + chunk, f32), (chunk, bf16)]
            out_specs = [wide, whole, whole]
            scratch = [pltpu.VMEM((8, D), f32)] + scratch
        else:
            shapes = [((length, D), bf16), ((D, columns), f32), ((8, D), f32)]
            out_specs = [wide, whole, whole]
    return pl.pallas_call(
        partial(project_back_kernel, number, fused),
        out_shape=[jax.ShapeDtypeStruct(*item) for item in shapes],
        grid=(length // BLOCK,),
        in_specs=[
            wide,
            narrow,
            narrow,
            pl.BlockSpec((D, 3 * D), lambda i: (0, 0)),
            pl.BlockSpec((8, D), lambda i: (0, 0)),
        ]
        + specs
        + [pl.BlockSpec(memory_space=pl.ANY)] * len(waits),
        out_specs=out_specs,
        scratch_shapes=scratch,
        compiler_params=pltpu.CompilerParams(vmem_limit_bytes=VMEM_LIMIT),
        cost_estimate=cost(4 * 10**9, 8 * 2**20),
        name="project_back",
    )(own, cosine, sine, w, gains, *arrays, *waits)


def squares_kernel(*refs):
    total = sum(jnp.sum(ref[...] * ref[...]) for ref in refs[0:4:2]) + 0.0
    other = sum(jnp.sum(ref[...] * ref[...]) for ref in refs[1:4:2]) + 0.0
    refs[4][...] = jnp.full((1, LANES), total + other, f32)


def squares(sums):
    spec = pl.BlockSpec(memory_space=pltpu.VMEM)
    return pl.pallas_call(
        squares_kernel,
        out_shape=jax.ShapeDtypeStruct((1, LANES), f32),
        in_specs=[spec] * 4,
        out_specs=spec,
        compiler_params=pltpu.CompilerParams(vmem_limit_bytes=VMEM_LIMIT),
        name="squares",
    )(*sums)


def update_kernel(shard, down, where, total, *refs):
    core = where[0]
    chunks, masters, firsts, seconds = refs[:4], refs[4:9], refs[9:14], refs[14:19]
    norm = refs[19]
    outs = [refs[20 + 5 * i : 25 + 5 * i] for i in range(4)]
    low, high, square = refs[40:]
    split = 5 * shard

    @pl.when(core == 0)
    def _():
        for i, target in ((0, low), (1, high)):
            target[:split] = chunks[i][...]
            target[split:] = chunks[2 + i][...]

    @pl.when(core == 1)
    def _():
        for i, target in ((0, high), (1, low)):
            target[:split] = chunks[i][...]
            target[split:] = chunks[2 + i][...]

    length = jnp.sqrt(total[0:1, 0:1])
    norm[...] = length
    factor = clip_limit / jnp.maximum(length, clip_limit)
    halves = (low, high)

    def step(which, grad, rows, columns, rate, decay):
        at = (rows, columns)
        new = adam_update(
            masters[which][at], factor * grad, firsts[which][at], seconds[which][at], rate, decay
        )
        outs[0][which][at] = new[0]
        outs[1][which][at] = new[1]
        outs[2][which][at] = new[2]
        outs[3][which][at] = new[2].astype(bf16)

    every = slice(None)
    places = [(0, i, i // 5, (i % 5) * shard) for i in range(9)]
    for i in range(19):
        which, column = (1, i) if i < 3 else (2, i - 3)
        places.append((which, column, i // 10, (5 + i % 10) * shard))
    for which, column, half, row in places:
        rate = 4.0 * D**-0.5 if which == 1 else D**-0.5
        grad = halves[half][row : row + shard, :]
        step(which, grad, every, slice(column * LANES, (column + 1) * LANES), rate, decay_rate)
    for half in range(2):
        for i in range(3):
            row = 15 * shard + i * down
            step(
                3, halves[half][row : row + down, :], slice(half * down, (half + 1) * down),
                slice(i * LANES, (i + 1) * LANES), FF**-0.5, decay_rate,
            )
    gain_rows = []
    for row in (4 * shard, 14 * shard):
        square[...] = jnp.zeros_like(square)
        square[0:shard, :] = high[row : row + shard, :]
        gain_rows.append(square[...].T[0:1, :shard])
    for i in range(2):
        step(4, gain_rows[i], slice(i, i + 1), every, 0.5, 0.0)


def update(where, total, sums, masters, firsts, seconds):
    shard, down = masters[0].shape[0], masters[3].shape[0] // 2
    spec = pl.BlockSpec(memory_space=pltpu.VMEM)
    shapes = [item.shape for item in masters]
    outs = pl.pallas_call(
        partial(update_kernel, shard, down),
        out_shape=[jax.ShapeDtypeStruct((1, 1), f32)]
        + [jax.ShapeDtypeStruct(shape, f32) for _ in range(3) for shape in shapes]
        + [jax.ShapeDtypeStruct(shape, bf16) for shape in shapes],
        in_specs=[pl.BlockSpec(memory_space=pltpu.SMEM)] + [spec] * 20,
        out_specs=[spec] * 21,
        scratch_shapes=[
            pltpu.VMEM((15 * shard + 3 * down, LANES), f32),
            pltpu.VMEM((15 * shard + 3 * down, LANES), f32),
            pltpu.VMEM((LANES, LANES), f32),
        ],
        compiler_params=pltpu.CompilerParams(vmem_limit_bytes=VMEM_LIMIT),
        name="update",
    )(where, total, *sums, *masters, *firsts, *seconds)
    return outs[0][0, 0], outs[1:6], outs[6:11], outs[11:16], outs[16:21]


def update_plain(core, total, sums, masters, firsts, seconds):
    shard, down = masters[0].shape[0], masters[3].shape[0] // 2
    mine = jnp.concatenate([sums[0], sums[2]])
    there = jnp.concatenate([sums[1], sums[3]])
    low = jnp.where(core == 0, mine, there)
    high = jnp.where(core == 0, there, mine)
    five, fifteen = 5 * shard, 15 * shard
    first_shard = jnp.concatenate([low[:five], high[:five]]).reshape(10, shard, LANES)
    second_shard = jnp.concatenate([low[five:fifteen], high[five:fifteen]])
    second_shard = second_shard.reshape(20, shard, LANES)
    down_shard = jnp.stack(
        [item[fifteen:].reshape(3, down, LANES) for item in (low, high)], axis=1
    ).reshape(3, 2 * down, LANES)
    shard_grads = (
        unslab(first_shard[:9]),
        unslab(second_shard[:3]),
        unslab(second_shard[3:19]),
        unslab(down_shard),
        jnp.stack([first_shard[9, :, 0], second_shard[19, :, 0]]),
    )
    grad_norm = jnp.sqrt(total[0, 0])
    factor = clip_limit / jnp.maximum(grad_norm, clip_limit)
    rates = (D ** (-0.5), 4.0 * D ** (-0.5), D ** (-0.5), FF ** (-0.5), 0.5)
    decays = (decay_rate, decay_rate, decay_rate, decay_rate, 0.0)
    updates = [
        adam_update(
            masters[i], factor * shard_grads[i], firsts[i], seconds[i], rates[i], decays[i]
        )
        for i in range(5)
    ]
    new_first, new_second, new_master = zip(*updates)
    return grad_norm, new_first, new_second, new_master, [item.astype(bf16) for item in new_master]


def per_device(
    count,
    tokens,
    cotangent,
    sample_ids,
    pad_flags,
    offsets,
    w_qkv,
    w_out,
    w_gate_up,
    w_down,
    gains,
    m_qkv,
    m_out,
    m_gate_up,
    m_down,
    m_gains,
    v_qkv,
    v_out,
    v_gate_up,
    v_down,
    v_gains,
):
    owner = lax.axis_index("batch")
    core = lax.axis_index("tm")
    where = jnp.stack([core, owner]).astype(jnp.int32)
    shard = w_qkv.shape[0]
    down = w_down.shape[0] // 2
    own = tokens[0]
    fuse_in = can_unpack(shard, down)
    masters = (w_qkv, w_out, w_gate_up, w_down, gains)

    first = send_chunk(where, FIRST_PLAN, 0, [w_qkv, gains], [])
    there = swap_tm(own)
    cosine, sine, key_aux, query_aux, ranges = tables(
        where, sample_ids, pad_flags, offsets, [there]
    )
    first_held, first_pieces = gather(first, count, [query_aux])
    second = send_chunk(where, SECOND_PLAN, down, [w_out, w_gate_up, w_down], [first_held])

    def gathered(pieces, number, down):
        others = [swap_tm(piece) for piece in pieces]
        if fuse_in:
            return (where, *pieces, *others), (count, number, shard, down)
        return unpack_plain(count, number, shard, down, where, pieces, others), None

    weights, fused = gathered([jnp.concatenate(first_pieces)], 5, 0)
    qa, ka, va, kt, vt, attn_in, gain_pair = project(
        own, there, cosine, sine, key_aux, query_aux, weights, fused, []
    )
    second_held, second_pieces = gather(second, count, [gain_pair])
    mixed, exact, qb = attend(ranges, qa, ka, vt, [second_held])
    second_pieces[1:] = hold(second_pieces[1:], [mixed])
    weights, fused = gathered(second_pieces, 10, down)
    result, grad_middle, da, *grads = feed(
        own, mixed, exact, cotangent[0], query_aux, gain_pair, weights, fused
    )
    if not fused:
        grads = pack_plain(count, core, grads, 10, shard, down)
    kept, given = grads
    second_total = kept[0] + swap_tm(given).astype(f32)
    second_sums = scatter_steps(second_total, count, owner)

    dqs, owns, recvs = [], [], []
    for group, waits in zip(GROUPS, ([given], [second_total])):
        dq, kept, part = attend_back(*group, ranges, qb, ka, da, va, kt, waits)
        dqs.append(dq)
        owns.append(kept)
        recvs.append(swap_tm(part))
    fused = (5, shard) if fuse_in else None
    shared = (own, cosine, sine, attn_in, gain_pair)
    several = len(second_sums) > 1
    before, grads_before = project_back(
        0, fused, where, shared, [*dqs, owns[0], recvs[0]], second_sums[:1] if several else []
    )
    grad_tokens, *grads = project_back(
        1, fused, where, shared, [owns[1], recvs[1], grad_middle, before, grads_before],
        second_sums[1:2] if several else [],
    )
    if not fused:
        order = [(PARTS[0] + PARTS[1]).index(i) for i in range(9)]
        both = jnp.concatenate([slabs(grads_before), slabs(grads[0])])
        grads = pack_plain(count, core, [unslab(both[jnp.array(order)]), grads[1]], 5, shard, 0)
    kept, given = grads
    first_total = kept[0] + swap_tm(given).astype(f32)
    first_sum = scatter_steps(first_total, count, owner)[-1].reshape(-1, LANES)
    second_sum = second_sums[-1].reshape(-1, LANES)

    sums = (first_sum, swap_tm(first_sum), second_sum, swap_tm(second_sum))
    total = sum_batch(squares(sums), count)
    firsts = (m_qkv, m_out, m_gate_up, m_down, m_gains)
    seconds = (v_qkv, v_out, v_gate_up, v_down, v_gains)
    if fuse_in:
        updates = update(where, total, sums, masters, firsts, seconds)
    else:
        updates = update_plain(core, total, sums, masters, firsts, seconds)
    grad_norm, new_first, new_second, new_master, copies = updates
    return (
        result[None],
        grad_tokens[None],
        grad_norm,
        *new_first,
        *new_second,
        *new_master,
        *copies,
    )


def solution(mesh):
    in_specs = (
        P("batch", "tm", None),
        P("batch", "tm", None),
        P("batch", None),
        P("batch", None),
        P("batch", None),
        P("batch", None),
        P("batch", None),
        P("batch", None),
        P("batch", None),
        P(None, "batch"),
        P("batch", None),
        P("batch", None),
        P("batch", None),
        P("batch", None),
        P(None, "batch"),
        P("batch", None),
        P("batch", None),
        P("batch", None),
        P("batch", None),
        P(None, "batch"),
    )
    out_specs = (
        P("batch", "tm", None),
        P("batch", "tm", None),
        P(),
        P("batch", None),
        P("batch", None),
        P("batch", None),
        P("batch", None),
        P(None, "batch"),
        P("batch", None),
        P("batch", None),
        P("batch", None),
        P("batch", None),
        P(None, "batch"),
        P("batch", None),
        P("batch", None),
        P("batch", None),
        P("batch", None),
        P(None, "batch"),
        P("batch", None),
        P("batch", None),
        P("batch", None),
        P("batch", None),
        P(None, "batch"),
    )
    return jax.shard_map(
        partial(per_device, mesh.shape["batch"]), mesh=mesh, in_specs=in_specs, out_specs=out_specs, check_vma=False
    )
```

```python
import math
from functools import partial

import jax
import jax.numpy as jnp
from jax import lax
from jax.experimental import pallas as pl
from jax.experimental.pallas import tpu as pltpu
from jax.sharding import PartitionSpec as P

D = 384
FF = 1024
HEADS = 6
HD = 64
STEP = 3


norm_eps = 1e-06
beta_one = 0.5
beta_two = 0.5
adam_eps = 1e-08
decay_rate = 0.1
clip_limit = 1.0
masked_score = -1e30


def adam_update(master, grad, first, second, rate, decay):
    first_new = beta_one * first + (1.0 - beta_one) * grad
    second_new = beta_two * second + (1.0 - beta_two) * grad * grad
    direction = (
        first_new
        / (1.0 - beta_one**STEP)
        / (jnp.sqrt(second_new / (1.0 - beta_two**STEP)) + adam_eps)
    )
    return (first_new, second_new, master - rate * (direction + decay * master))


def bit_groups(count):
    groups = []
    low, bits = 0, count.bit_length() - 1
    while low < bits:
        width = min(2, bits - low)
        groups.append((low, width))
        low += width
    return groups


def permute_batch(value, flip, count):
    return lax.ppermute(value, "batch", [(i, i ^ flip) for i in range(count)])


def swap_tm(value):
    return lax.ppermute(value, "tm", [(0, 1), (1, 0)])


def slabs(matrix):
    rows, columns = matrix.shape
    return matrix.reshape(rows, columns // 128, 128).transpose(1, 0, 2)


def unslab(stack):
    count, rows, _ = stack.shape
    return stack.transpose(1, 0, 2).reshape(rows, count * 128)


bf16 = jnp.bfloat16
f32 = jnp.float32
BLOCK = 256
LANES = 128
KEEP_LANE = 96
LIMITS = (12, 12, 12, 34, 12, 12, 12)
NN = (((1,), (0,)), ((), ()))
NT = (((1,), (1,)), ((), ()))
TN = (((0,), (0,)), ((), ()))


def dot(left, right, dims):
    return lax.dot_general(left, right, dims, preferred_element_type=f32)


def cost(flops, moved):
    return pl.CostEstimate(flops=flops, bytes_accessed=moved, transcendentals=0)


def in_vmem(shape, dtype):
    return pltpu.VMEM(tuple(shape), dtype)


VMEM = pl.BlockSpec(memory_space=pltpu.VMEM)
SMEM = pl.BlockSpec(memory_space=pltpu.SMEM)
ANY = pl.BlockSpec(memory_space=pl.ANY)
HBM = pl.BlockSpec(memory_space=pltpu.HBM)


def fetch(sources, targets, semaphores):
    copies = [
        pltpu.make_async_copy(source, target, semaphores.at[i])
        for i, (source, target) in enumerate(zip(sources, targets))
    ]
    for copy in copies:
        copy.start()
    return copies


def landing(arrays):
    return [pltpu.VMEM(item.shape, item.dtype) for item in arrays] + [
        pltpu.SemaphoreType.DMA((len(arrays),))
    ]


def arrive(copies):
    for copy in copies:
        copy.wait()


def limit(mebibytes):
    return pltpu.CompilerParams(vmem_limit_bytes=mebibytes * 2**20)


def block(start, size=BLOCK):
    return pl.ds(pl.multiple_of(start * size, size), size)


def sum_batch(value, count):
    value = jnp.broadcast_to(value[:, None], (count, 1, LANES))
    value = lax.all_to_all(value, "batch", 0, 0, tiled=True)
    return jnp.sum(value, axis=0)


def row_scale(values):
    return lax.rsqrt(jnp.mean(values * values, axis=-1, keepdims=True) + norm_eps)


def norm_back(grad_normed, values, scale):
    return scale * grad_normed - values * scale * scale * scale * jnp.mean(
        grad_normed * values, axis=-1, keepdims=True
    )


def split_three(values):
    high = values.astype(bf16)
    rest = values - high.astype(f32)
    middle = rest.astype(bf16)
    return high, middle, (rest - middle.astype(f32)).astype(bf16)


def swap_halves(pair):
    lane = lax.broadcasted_iota(jnp.int32, pair.shape, 1)
    return jnp.where(lane % HD < HD // 2, pltpu.roll(pair, 96, 1), pltpu.roll(pair, 32, 1))


def relative_place(device, owner, count):
    flips = device ^ owner
    place, scale = 0, 1
    for low, width in reversed(bit_groups(count)):
        place = place + ((flips >> low) & ((1 << width) - 1)) * scale
        scale <<= width
    return place


def exchange_all(held, low, width, count):
    return [held] + [permute_batch(held, k << low, count) for k in range(1, 1 << width)]


def in_hbm(arrays):
    return [pltpu.with_memory_space_constraint(item, pltpu.HBM) for item in arrays]


def join_kernel(number, *refs):
    out = refs[-1]
    size = refs[0].shape[0]
    for i in range(number):
        out[i * size : (i + 1) * size] = refs[i][...]


def join(pieces, waits=()):
    first = pieces[0]
    shape = (len(pieces) * first.shape[0],) + first.shape[1:]
    return pl.pallas_call(
        partial(join_kernel, len(pieces)),
        out_shape=jax.ShapeDtypeStruct(shape, first.dtype),
        in_specs=[VMEM] * len(pieces) + [ANY] * len(waits),
        out_specs=VMEM,
        compiler_params=limit(4),
        name="join",
    )(*pieces, *waits)


def combine_kernel(number, split, where, *refs):
    items, outs = refs[:number], refs[-len(refs) + number :]
    outs = outs[-(split[1] if split else 1) :]

    def total(index):
        return sum(item[index].astype(f32) for item in items[1:]) + items[0][index].astype(f32)

    if not split:
        outs[0][...] = total(slice(None))
        return
    upper, fan, lower, which, low = split
    mine = (where[which] >> low) & (fan - 1)
    for a in range(upper):
        for b in range(lower):
            for flip in range(fan):
                index = (a * fan + (mine ^ flip)) * lower + b
                outs[flip][a * lower + b] = total(index).astype(outs[flip].dtype)


def combine(where, items, split, waits=()):
    count, rows, _ = items[0].shape
    if split:
        fan = split[1]
        shapes = [
            jax.ShapeDtypeStruct((count // fan, rows, LANES), bf16 if flip else f32)
            for flip in range(fan)
        ]
    else:
        shapes = [jax.ShapeDtypeStruct((count, rows, LANES), f32)]
    return pl.pallas_call(
        partial(combine_kernel, len(items), split),
        out_shape=shapes,
        in_specs=[SMEM] + [VMEM] * len(items) + [ANY] * len(waits),
        out_specs=[VMEM] * len(shapes),
        compiler_params=limit(12),
        name="combine",
    )(where, *items, *waits)


def scatter_parts(where, parts, count, groups, waits=None):
    for n, (low, width) in enumerate(groups):
        got = [permute_batch(item, k << low, count) for k, item in enumerate(parts) if k]
        if waits and n == 0:
            got = hold(got, waits)
        split = None
        if n + 1 < len(groups):
            fan = 1 << groups[n + 1][1]
            split = (parts[0].shape[0] // fan, fan, 1, 1, groups[n + 1][0])
        parts = combine(where, [parts[0], *got], split)
    return parts[0]


def hold(values, waits):
    spec = pl.BlockSpec(memory_space=pl.ANY)
    number = len(values)
    return pl.pallas_call(
        lambda *refs: None,
        out_shape=[jax.ShapeDtypeStruct(item.shape, item.dtype) for item in values],
        in_specs=[spec] * (number + len(waits)),
        out_specs=[spec] * number,
        input_output_aliases={i: i for i in range(number)},
        compiler_params=limit(1),
        name="hold",
    )(*values, *waits)


def send_kernel(shard, plan, down, where, *refs):
    number = (len(refs) - 4) // 2
    target, stage, square = refs[number : number + 3]
    sources = refs[number + 3 : -1]
    arrive(fetch(refs[:number], sources, refs[-1]))
    number = len(plan) // 2
    core = where[0]
    stage[...] = jnp.zeros_like(stage)
    gain_at = [i for i, item in enumerate(plan) if item == "gain"]
    if gain_at:
        square[...] = jnp.zeros_like(square)
        square[0:2, 0:shard] = sources[-1][...]
        column = square[...].T

    def fill(half):
        for i in range(number):
            item = plan[half * number + i]
            rows = slice(i * shard, (i + 1) * shard)
            if item == "gain":
                stage[rows, :] = column[:shard]
            elif item is not None:
                which, at = item
                stage[rows, :] = sources[which][:, at * LANES : (at + 1) * LANES]
        for i in range(3 if down else 0):
            start = number * shard + i * down
            stage[start : start + down, :] = sources[2][
                half * down : (half + 1) * down, i * LANES : (i + 1) * LANES
            ]

    @pl.when(core == 0)
    def _():
        fill(0)

    @pl.when(core == 1)
    def _():
        fill(1)

    target[...] = stage[...].astype(bf16)


def send_chunk(where, plan, down, sources, waits):
    shard = sources[0].shape[0]
    rows = len(plan) // 2 * shard + 3 * down
    rows = -(-rows // 16) * 16
    core = where[0]
    if shard % 8 == 0 and down % 8 == 0:
        spec = VMEM

        def kernel(where, *refs):
            kept = refs[: len(sources)] + refs[len(sources) + len(waits) :]
            send_kernel(shard, plan, down, where, *kept)

        return pl.pallas_call(
            kernel,
            out_shape=jax.ShapeDtypeStruct((rows, LANES), bf16),
            in_specs=[SMEM] + [HBM] * len(sources) + [ANY] * len(waits),
            out_specs=spec,
            scratch_shapes=[pltpu.VMEM((rows, LANES), f32), pltpu.VMEM((LANES, LANES), f32)]
            + landing(sources),
            compiler_params=limit(6),
            name="send_chunk",
        )(where, *in_hbm(sources), *waits)
    stacks = {i: slabs(item) for i, item in enumerate(sources) if item.shape[1] % LANES == 0}
    pieces = []
    for item in plan:
        if item == "gain":
            pieces.append(jnp.pad(sources[-1].T, ((0, 0), (0, LANES - 2))))
        elif item is None:
            pieces.append(jnp.zeros((shard, LANES), f32))
        else:
            pieces.append(stacks[item[0]][item[1]])
    half = len(plan) // 2
    halves = [jnp.concatenate(pieces[:half]), jnp.concatenate(pieces[half:])]
    if down:
        for i in range(2):
            part = stacks[2][:, i * down : (i + 1) * down].reshape(3 * down, LANES)
            halves[i] = jnp.concatenate([halves[i], part])
    chunk = jnp.where(core == 0, halves[0], halves[1]).astype(bf16)
    return jnp.pad(chunk, ((0, rows - chunk.shape[0]), (0, 0)))


FIRST_PLAN = tuple((0, i) for i in range(9)) + ("gain",)
SECOND_PLAN = tuple((0, i) for i in range(3)) + tuple((1, i) for i in range(16)) + (None,)


def gather(chunk, count, waits):
    held = chunk[None]
    groups = bit_groups(count)[::-1]
    for n, (low, width) in enumerate(groups):
        pieces = exchange_all(held, low, width, count)
        if n + 1 < len(groups):
            held = join(pieces, () if n else waits)
    return held, pieces


def unpack(count, number, shard, down, where, pieces, others, stage, w_down):
    core, owner = where[0], where[1]
    last = bit_groups(count)[0][1]
    for sources, half in ((pieces, core), (others, 1 - core)):
        for flip, source in enumerate(sources):

            def one(n, carry, source=source, half=half, flip=flip):
                device = owner ^ flip ^ (relative_flips(n, count) << last)
                chunk = source[n].astype(f32)
                for i in range(number):
                    rows = pl.ds(pl.multiple_of(device * shard, 8), shard)
                    stage[half * number + i, rows, :] = chunk[i * shard : (i + 1) * shard]
                for i in range(3 if down else 0):
                    start = number * shard + i * down
                    rows = pl.ds(pl.multiple_of((device * 2 + half) * down, 16), down)
                    w_down[rows, i * LANES : (i + 1) * LANES] = chunk[start : start + down].astype(
                        bf16
                    )
                return carry

            lax.fori_loop(0, source.shape[0], one, 0, unroll=True)


def relative_flips(place, count):
    last = bit_groups(count)[0][1]
    flips, scale = 0, 1
    for low, width in reversed(bit_groups(count)[1:]):
        flips = flips + (((place // scale) & ((1 << width) - 1)) << (low - last))
        scale <<= width
    return flips


def can_unpack(shard, down):
    return shard % 8 == 0 and down % 16 == 0


def unpack_plain(count, number, shard, down, where, mine, other):
    core, owner = where[0], where[1]
    places = relative_place(jnp.arange(count, dtype=jnp.int32), owner, count)
    mine, other = jnp.concatenate(mine), jnp.concatenate(other)
    low = jnp.take(jnp.where(core == 0, mine, other), places, axis=0)
    high = jnp.take(jnp.where(core == 0, other, mine), places, axis=0)

    def part(source):
        return (
            source[:, : number * shard]
            .reshape(count, number, shard, LANES)
            .transpose(1, 0, 2, 3)
            .reshape(number, D, LANES)
        )

    stack = jnp.concatenate([part(low), part(high)], axis=0)
    if number == 5:
        return unslab(stack[:9]), stack[9].T[:8].astype(f32)
    downs = [
        item[:, number * shard : number * shard + 3 * down].reshape(count, 3, down, LANES)
        for item in (low, high)
    ]
    w_down = jnp.stack(downs, axis=1).transpose(0, 1, 3, 2, 4).reshape(FF, D)
    return unslab(stack[:3]), unslab(stack[3:19]), w_down


def put_slab(stage, core, number, shard, at, slab):
    half, row = at // number, (at % number) * shard
    slot = core if half == 0 else 1 - core
    stage[slot, :, row : row + shard, :] = slab.reshape(-1, shard, LANES)


def put_down(stage, core, number, shard, down, column, slab, first):
    parts = slab.reshape(-1, 2, down, LANES)
    row = number * shard + column * down
    devices = slice(first, first + parts.shape[0])
    stage[core, devices, row : row + down, :] = parts[:, 0]
    stage[1 - core, devices, row : row + down, :] = parts[:, 1]


def gain_column(row):
    return jnp.concatenate([row, jnp.zeros((LANES - 8, D), f32)], axis=0).T


def pack_plain(count, core, grads, number, shard, down):
    column = jnp.pad(grads[-1][:1].T, ((0, 0), (0, LANES - 1)))[None]
    stack = jnp.concatenate([slabs(item) for item in (grads[:2] if down else grads[:1])] + [column])

    def by_device(part):
        return (
            part.reshape(number, count, shard, LANES)
            .transpose(1, 0, 2, 3)
            .reshape(count, number * shard, LANES)
        )

    halves = [by_device(stack[:number]), by_device(stack[number:])]
    if down:
        downs = (
            slabs(grads[2])
            .reshape(3, count, 2, down, LANES)
            .transpose(2, 1, 0, 3, 4)
            .reshape(2, count, 3 * down, LANES)
        )
        halves = [jnp.concatenate([halves[i], downs[i]], axis=1) for i in range(2)]
    return jnp.stack(halves)


def tables_kernel(length, where, ids, pads, offsets, *refs):
    cosine, sine, key_aux, query_aux, ranges = refs[-5:]
    core = where[0]
    whole = 2 * length

    def turn(row):
        low, high = row[:, :length], row[:, length:]
        return jnp.concatenate(
            [jnp.where(core == 0, low, high), jnp.where(core == 0, high, low)], axis=1
        )

    classes = (2 * ids[...] + pads[...]).astype(f32)
    spot = lax.broadcasted_iota(jnp.int32, (1, whole), 1)
    position = (turn(spot) + turn(offsets[...])).astype(f32)
    turned = turn(classes)
    index = lax.broadcasted_iota(jnp.int32, (HD // 2, whole), 0).astype(f32)
    angle = position * jnp.exp(index * (-2.0 * math.log(10000.0) / HD))
    cos, sin = jnp.cos(angle), jnp.sin(angle)
    cosine[...] = jnp.concatenate([cos, cos, cos, cos], axis=0).T
    sine[...] = jnp.concatenate([-sin, sin, -sin, sin], axis=0).T
    at = lax.broadcasted_iota(jnp.int32, (LANES, whole), 0)
    is_class = (at >= HD) & (at < HD + 8)
    same = (at - HD).astype(f32) == turned
    is_log = (at >= HD + 8) & (at < HD + 8 + 3 * HEADS)
    key_aux[...] = jnp.where((is_class & same) | is_log, 1.0, 0.0).T.astype(bf16)
    own = turned[:, :length]
    kept = jnp.where(turn(pads[...])[:, :length] == 0, 1.0, 0.0)
    extra = jnp.where(is_class & ~same, masked_score, 0.0)[:, :length]
    query_aux[...] = jnp.where(at[:, :length] == KEEP_LANE, kept, extra).T.astype(bf16)
    starts = (core * length, (1 - core) * length)
    for n in range(length // BLOCK):
        mine = own[:, n * BLOCK : (n + 1) * BLOCK]
        first = jnp.min(mine)
        last = jnp.max(mine)
        low_key = jnp.sum(jnp.where(classes < first, 1.0, 0.0)).astype(jnp.int32)
        high_key = jnp.sum(jnp.where(classes <= last, 1.0, 0.0)).astype(jnp.int32)
        bounds = []
        for start in starts:
            low_part = jnp.clip(low_key - start, 0, length)
            high_part = jnp.clip(high_key - start, 0, length)
            low_block = low_part // BLOCK
            bounds.append((low_block, jnp.maximum((high_part + BLOCK - 1) // BLOCK - low_block, 0)))
        ranges[0, n] = bounds[0][0]
        ranges[1, n] = bounds[0][1]
        ranges[2, n] = bounds[1][0] + length // BLOCK - bounds[0][1]
        ranges[3, n] = bounds[0][1] + bounds[1][1]


def tables(where, ids, pads, offsets, waits):
    whole = ids.shape[1]
    length = whole // 2
    spec = pl.BlockSpec(memory_space=pltpu.VMEM)
    smem = pl.BlockSpec(memory_space=pltpu.SMEM)
    return pl.pallas_call(
        partial(tables_kernel, length),
        out_shape=[
            in_vmem((whole, LANES), f32),
            in_vmem((whole, LANES), f32),
            in_vmem((whole, LANES), bf16),
            in_vmem((length, LANES), bf16),
            jax.ShapeDtypeStruct((4, length // BLOCK), jnp.int32),
        ],
        in_specs=[smem, spec, spec, spec] + [pl.BlockSpec(memory_space=pl.ANY)] * len(waits),
        out_specs=[spec] * 4 + [smem],
        compiler_params=limit(LIMITS[0]),
        cost_estimate=cost(3 * 10**9, 4 * 2**20),
        name="tables",
    )(where, ids, pads, offsets, *waits)


def project_kernel(fused, own, there, cosine, sine, key_aux, query_aux, *refs):
    if fused:
        pieces = 1 << bit_groups(fused[0])[0][1]
        where, scratch = refs[0], refs[-2 * pieces - 3 : -1]
        qa, ka, va, kt, vt, w, gains, stage = refs[-2 * pieces - 11 : -2 * pieces - 3]
        copies = fetch((*refs[1 : 1 + 2 * pieces], own, there), scratch, refs[-1])
        mine, other, (own, there) = (
            scratch[:pieces], scratch[pieces : 2 * pieces], scratch[2 * pieces :]
        )
        arrive(copies)
        unpack(*fused, where, mine, other, stage, None)
        for i in range(9):
            w[:, i * LANES : (i + 1) * LANES] = stage[i].astype(bf16)
        gains[...] = stage[9].T[:8]
    else:
        w_in, gains_in, (qa, ka, va, kt, vt, w, gains) = *refs[:2], refs[-7:]
        w[...] = w_in[...]
        gains[...] = gains_in[...]
    low = lax.broadcasted_iota(jnp.int32, (BLOCK, LANES), 1) < HD
    lane = lax.broadcasted_iota(jnp.int32, (BLOCK, LANES), 1)
    value_extra = jnp.where((lane >= HD) & (lane < HD + 3), 1.0, 0.0)
    ones = jnp.ones((8, BLOCK), bf16)
    blocks = own.shape[0] // BLOCK

    def body(step, carry, source, base):
        rows, keys = block(step), block(base + step)
        x = source[rows, :].astype(f32)
        normed = (x * row_scale(x) * gains[0:1, :]).astype(bf16)
        cos, sin = cosine[keys, :], sine[keys, :]
        first = 0 if base == 0 else D
        products = dot(normed, w[:, first:], NN)
        products = [
            products[:, i * LANES - first : (i + 1) * LANES - first]
            for i in range(first // LANES, 9)
        ]
        if base == 0:
            query_extra = query_aux[rows, :].astype(f32)
            for pair in range(HEADS // 2):
                z = products[pair]
                z = (z * cos + swap_halves(z) * sin).astype(bf16).astype(f32) * HD**-0.5
                qa[2 * pair, rows, :] = jnp.where(low, z, query_extra).astype(bf16)
                qa[2 * pair + 1, rows, :] = jnp.where(
                    low, pltpu.roll(z, HD, 1), query_extra
                ).astype(bf16)
        key_extra = key_aux[keys, :].astype(f32)
        for pair in range(HEADS // 2):
            z = products[pair - 6]
            z = z * cos + swap_halves(z) * sin
            ka[2 * pair, keys, :] = jnp.where(low, z, key_extra).astype(bf16)
            ka[2 * pair + 1, keys, :] = jnp.where(
                low, pltpu.roll(z, HD, 1), key_extra
            ).astype(bf16)
            turned = z.T.astype(bf16)
            kt[2 * pair, :, keys] = turned[:HD]
            kt[2 * pair + 1, :, keys] = turned[HD:]
        for pair in range(HEADS // 2):
            z = products[pair - 3]
            va[2 * pair, keys, :] = jnp.where(low, z, value_extra).astype(bf16)
            va[2 * pair + 1, keys, :] = jnp.where(
                low, pltpu.roll(z, HD, 1), value_extra
            ).astype(bf16)
            turned = z.T.astype(bf16)
            for i in range(2):
                vt[2 * pair + i, :HD, keys] = turned[i * HD : (i + 1) * HD]
                vt[2 * pair + i, HD:, keys] = ones
        return carry

    lax.fori_loop(0, blocks, partial(body, source=own, base=0), 0)
    lax.fori_loop(0, blocks, partial(body, source=there, base=blocks), 0)


def project(own, there, cosine, sine, key_aux, query_aux, weights, fused, waits):
    length = own.shape[0]
    whole = 2 * length
    scratch, specs = [], [VMEM] * 6
    weight_specs = [VMEM] * 2
    if fused:
        specs = [HBM, ANY] + [VMEM] * 4
        weight_specs = [SMEM] + [ANY] * (len(weights) - 1)
        scratch = [pltpu.VMEM((10, D, LANES), f32)] + landing([*weights[1:], own, there])
    if fused:
        (own,) = in_hbm([own])
    return pl.pallas_call(
        partial(project_kernel, fused),
        out_shape=[
            in_vmem((HEADS, length, LANES), bf16),
            in_vmem((HEADS, whole, LANES), bf16),
            in_vmem((HEADS, whole, LANES), bf16),
            in_vmem((HEADS, HD, whole), bf16),
            in_vmem((HEADS, HD + 8, whole), bf16),
            in_vmem((D, 3 * D), bf16),
            in_vmem((8, D), f32),
        ],
        in_specs=specs + weight_specs + [ANY] * len(waits),
        out_specs=[VMEM] * 7,
        scratch_shapes=scratch,
        compiler_params=limit(LIMITS[1]),
        cost_estimate=cost(9 * 10**9, 16 * 2**20),
        name="project",
    )(own, there, cosine, sine, key_aux, query_aux, *weights, *waits)


def key_block(ranges, step, n):
    return jnp.where(n < ranges[1, step], ranges[0, step] + n, ranges[2, step] + n)


def attend_kernel(ranges, qa, ka, vt, *refs):
    mixed, exact, qb, total, peak = refs[-5:]
    lane = lax.broadcasted_iota(jnp.int32, (BLOCK, LANES), 1)

    def one(step, carry):
        queries = block(step)
        peak[...] = jnp.full((HEADS, 8, BLOCK), -3e38, f32)
        total[...] = jnp.zeros_like(total)

        def body(n, carry):
            rows = block(key_block(ranges, step, n))
            scores = [dot(ka[h, rows, :], qa[h, queries, :], NT) for h in range(HEADS)]
            weights = []
            for h in range(HEADS):
                old = peak[h][:1]
                new = jnp.maximum(old, jnp.max(scores[h], axis=0, keepdims=True))
                weights.append((jnp.exp(scores[h] - new).astype(bf16), jnp.exp(old - new)))
                peak[h] = jnp.broadcast_to(new, (8, BLOCK))
            for h in range(HEADS):
                weight, shrink = weights[h]
                total[h] = total[h] * shrink + dot(vt[h, :, rows], weight, NN)
            return carry

        lax.fori_loop(0, ranges[3, step], body, 0)
        means, pieces = [], []
        for h in range(HEADS):
            bottom = total[h][HD : HD + 1]
            means.append(total[h][:HD] / bottom)
            logs = -(peak[h][:1] + jnp.log(bottom))
            pieces.extend(piece.astype(f32) for piece in split_three(logs))
        for pair in range(HEADS // 2):
            both = jnp.concatenate(means[2 * pair : 2 * pair + 2], axis=0).T
            mixed[queries, pair * LANES : (pair + 1) * LANES] = both.astype(bf16)
            exact[queries, pair * LANES : (pair + 1) * LANES] = both
        table = jnp.concatenate(
            [jnp.zeros((HD + 8, BLOCK), f32)]
            + pieces
            + [jnp.zeros((LANES - HD - 8 - 3 * HEADS, BLOCK), f32)],
            axis=0,
        ).T
        for h in range(HEADS):
            start = HD + 8 + 3 * h
            qb[h, queries, :] = jnp.where(
                (lane >= start) & (lane < start + 3), table, qa[h, queries, :].astype(f32)
            ).astype(bf16)
        return carry

    lax.fori_loop(0, qa.shape[1] // BLOCK, one, 0)


def attend(ranges, qa, ka, vt, waits):
    heads, length, _ = qa.shape
    return pl.pallas_call(
        attend_kernel,
        out_shape=[
            in_vmem((length, D), bf16),
            in_vmem((length, D), f32),
            in_vmem(qa.shape, bf16),
        ],
        in_specs=[SMEM] + [VMEM] * 3 + [ANY] * len(waits),
        out_specs=[VMEM] * 3,
        scratch_shapes=[
            pltpu.VMEM((heads, HD + 8, BLOCK), f32),
            pltpu.VMEM((heads, 8, BLOCK), f32),
        ],
        compiler_params=limit(LIMITS[2]),
        cost_estimate=cost(18 * 10**9, 12 * 2**20),
        name="attend",
    )(ranges, qa, ka, vt, *waits)


def attend_back_kernel(ranges, qb, ka, da, va, kt, *refs):
    dq, sums, there, acc = refs[-4:]
    sums[...] = jnp.zeros_like(sums)
    zero = jnp.zeros((BLOCK, HD), bf16)

    def one(step, carry):
        queries = block(step)
        acc[...] = jnp.zeros_like(acc)

        def body(n, carry):
            rows = block(key_block(ranges, step, n))
            first = [
                (
                    dot(ka[h, rows, :], qb[h, queries, :], NT),
                    dot(va[h, rows, :], da[h, queries, :], NT),
                )
                for h in range(HEADS)
            ]
            second = []
            for scores, grads in first:
                probs = jnp.exp(scores)
                second.append((probs.astype(bf16), (probs * grads).astype(bf16)))
            for h in range(HEADS):
                probs_low, grads_low = second[h]
                grad_side = jnp.concatenate([da[h, queries, :HD], zero], axis=1)
                query_side = jnp.concatenate([zero, qb[h, queries, :HD]], axis=1)
                sums[h, rows, :] += dot(probs_low, grad_side, NN) + dot(grads_low, query_side, NN)
                acc[h] += dot(kt[h, :, rows], grads_low, NN)
            return carry

        lax.fori_loop(0, ranges[3, step], body, 0)
        for h in range(HEADS):
            dq[h, :, queries] = acc[h]
        return carry

    length = qb.shape[1]
    lax.fori_loop(0, length // BLOCK, one, 0)
    there[...] = sums[:, length:, :].astype(bf16)


def attend_back(ranges, qb, ka, da, va, kt, waits):
    heads, length, _ = qb.shape
    whole = ka.shape[1]
    return pl.pallas_call(
        attend_back_kernel,
        out_shape=[
            in_vmem((heads, HD, length), f32),
            in_vmem((heads, whole, LANES), f32),
            jax.ShapeDtypeStruct((heads, whole - length, LANES), bf16),
        ],
        in_specs=[SMEM] + [VMEM] * 5 + [ANY] * len(waits),
        out_specs=[VMEM] * 3,
        scratch_shapes=[pltpu.VMEM((heads, HD, BLOCK), f32)],
        compiler_params=limit(LIMITS[4]),
        cost_estimate=cost(34 * 10**9, 8 * 2**20),
        name="attend_back",
    )(ranges, qb, ka, da, va, kt, *waits)


FEED = 512


def feed_kernel(fused, own, mixed, exact, cotangent, query_aux, gains, *refs):
    if fused:
        pieces = fan = 1 << bit_groups(fused[0])[0][1]
        where, mine, other = refs[0], refs[1 : 1 + pieces], refs[1 + pieces : 1 + 2 * pieces]
        refs = refs[1 + 2 * pieces :]
        result, grad_middle, da, gives = *refs[:3], refs[3 : 3 + fan]
        normed_all, low_all, hidden_all, up_all, middle_all, wo, wgu, wd, stage, g_gain, sums = (
            refs[3 + fan : 14 + fan]
        )
        scratch = refs[14 + fan : -1]
        copies = fetch((*mine, *other, own, cotangent), scratch, refs[-1])
        mine, other, (own, cotangent) = (
            scratch[:pieces], scratch[pieces : 2 * pieces], scratch[2 * pieces :]
        )
        arrive(copies)
    else:
        wo, wgu, wd = refs[:3]
        result, grad_middle, da, g_out, g_gate_up, g_down, g_gain = refs[3:10]
        normed_all, low_all, hidden_all, up_all, middle_all = refs[10:]
    gain = gains[1:2, :]
    g_gain[...] = jnp.zeros_like(g_gain)
    if fused:
        unpack(*fused, where, mine, other, stage, wd)
        for i in range(3):
            wo[:, i * LANES : (i + 1) * LANES] = stage[i].astype(bf16)
        for i in range(16):
            wgu[:, i * LANES : (i + 1) * LANES] = stage[3 + i].astype(bf16)

    chunks = FF // BLOCK
    lane = lax.broadcasted_iota(jnp.int32, (FEED, LANES), 1)

    def body(step, carry):
        rows = block(step, FEED)
        x = own[rows, :].astype(f32)
        middle = x + dot(mixed[rows, :], wo[...], NN)
        scale = row_scale(middle)
        normed = (middle * scale * gain).astype(bf16)
        normed_all[rows, :] = normed
        kept = query_aux[rows, :].astype(f32)[:, KEEP_LANE : KEEP_LANE + 1]
        upstream = cotangent[rows, :].astype(f32) * kept
        up_low = upstream.astype(bf16)
        up_all[rows, :] = up_low
        gates = [dot(normed, wgu[:, c * BLOCK : (c + 1) * BLOCK], NN) for c in range(chunks)]
        ups = [dot(normed, wgu[:, FF + c * BLOCK : FF + (c + 1) * BLOCK], NN) for c in range(chunks)]
        hiddens = [dot(up_low, wd[c * BLOCK : (c + 1) * BLOCK, :], NT) for c in range(chunks)]
        for c in range(chunks):
            gate, up, grad_hidden = gates[c], ups[c], hiddens[c]
            sig = 1.0 / (1.0 + jnp.exp(-gate))
            silu = gate * sig
            hidden_all[rows, c * BLOCK : (c + 1) * BLOCK] = (silu * up).astype(bf16)
            low_all[rows, FF + c * BLOCK : FF + (c + 1) * BLOCK] = (grad_hidden * silu).astype(bf16)
            low_all[rows, c * BLOCK : (c + 1) * BLOCK] = (
                grad_hidden * up * (sig + silu * (1.0 - sig))
            ).astype(bf16)
        ffn = dot(hidden_all[rows, :], wd[...], NN)
        grad_normed = dot(low_all[rows, :], wgu[...], NT)
        result[rows, :] = (kept * (middle + ffn)).astype(bf16)
        g_gain[0:1, :] += jnp.sum(grad_normed * middle * scale, axis=0, keepdims=True)
        grad = upstream + norm_back(grad_normed * gain, middle, scale)
        grad_middle[rows, :] = grad
        low = grad.astype(bf16)
        middle_all[rows, :] = low
        grad_mixed = dot(low, wo[...], NT).astype(bf16).astype(f32)
        products = grad_mixed * exact[rows, :]
        for h in range(HEADS):
            pair = h // 2
            head = grad_mixed[:, pair * LANES : (pair + 1) * LANES]
            product = products[:, pair * LANES : (pair + 1) * LANES]
            mine_lanes = (lane < HD) if h % 2 == 0 else (lane >= HD)
            delta = -jnp.sum(jnp.where(mine_lanes, product, 0.0), axis=1, keepdims=True)
            if h % 2:
                head = pltpu.roll(head, HD, 1)
            high, mid, last = split_three(delta)
            extra = jnp.where(
                lane == HD,
                high.astype(f32),
                jnp.where(
                    lane == HD + 1,
                    mid.astype(f32),
                    jnp.where(lane == HD + 2, last.astype(f32), 0.0),
                ),
            )
            da[h, rows, :] = jnp.where(lane < HD, head, extra).astype(bf16)
        return carry

    lax.fori_loop(0, own.shape[0] // FEED, body, 0)
    if not fused:
        g_out[...] = dot(mixed[...], middle_all[...], TN)
        for c in range(2 * FF // 512):
            g_gate_up[:, c * 512 : (c + 1) * 512] = dot(
                normed_all[...], low_all[:, c * 512 : (c + 1) * 512], TN
            )
        for c in range(chunks):
            g_down[c * BLOCK : (c + 1) * BLOCK, :] = dot(
                hidden_all[:, c * BLOCK : (c + 1) * BLOCK], up_all[...], TN
            )
        return
    count, number, shard, down = fused

    def put(at, value):
        for i in range(value.shape[1] // LANES):
            put_slab(sums, 0, number, shard, at + i, value[:, i * LANES : (i + 1) * LANES])

    put(0, dot(mixed[...], middle_all[...], TN))
    for c in range(2 * FF // 512):
        put(3 + 4 * c, dot(normed_all[...], low_all[:, c * 512 : (c + 1) * 512], TN))
    put(19, gain_column(g_gain[...]))
    for c in range(chunks):
        value = dot(hidden_all[:, c * BLOCK : (c + 1) * BLOCK], up_all[...], TN)
        for i in range(3):
            put_down(
                sums, 0, number, shard, down, i,
                value[:, i * LANES : (i + 1) * LANES], c * BLOCK // (2 * down),
            )
    me = where[1] & (fan - 1)
    for high in range(count // fan):
        for flip in range(fan):
            for half in range(2):
                gives[flip][half * (count // fan) + high] = sums[
                    half, high * fan + (me ^ flip)
                ].astype(gives[flip].dtype)


def feed(own, mixed, exact, cotangent, query_aux, gains, weights, fused):
    length = own.shape[0]
    scratch = [
        pltpu.VMEM((length, D), bf16),
        pltpu.VMEM((length, 2 * FF), bf16),
        pltpu.VMEM((length, FF), bf16),
        pltpu.VMEM((length, D), bf16),
        pltpu.VMEM((length, D), bf16),
    ]
    out_shape = [
        jax.ShapeDtypeStruct((length, D), bf16),
        in_vmem((length, D), f32),
        in_vmem((HEADS, length, LANES), bf16),
    ]
    if fused:
        count, number, shard, down = fused
        rows = number * shard + 3 * down
        fan = 1 << bit_groups(count)[0][1]
        weight_specs = [SMEM] + [ANY] * (len(weights) - 1)
        specs = [HBM, VMEM, VMEM, HBM, VMEM, VMEM]
        out_shape += [
            jax.ShapeDtypeStruct((2 * count // fan, rows, LANES), bf16 if flip else f32)
            for flip in range(fan)
        ]
        scratch += [
            pltpu.VMEM((D, D), bf16),
            pltpu.VMEM((D, 2 * FF), bf16),
            pltpu.VMEM((FF, D), bf16),
            pltpu.VMEM((2 * number, D, LANES), f32),
            pltpu.VMEM((8, D), f32),
            pltpu.VMEM((2, count, rows, LANES), f32),
        ]
        scratch += landing([*weights[1:], own, cotangent])
    else:
        weight_specs = [VMEM] * 3
        specs = [VMEM] * 6
        out_shape += [
            jax.ShapeDtypeStruct((D, D), f32),
            jax.ShapeDtypeStruct((D, 2 * FF), f32),
            jax.ShapeDtypeStruct((FF, D), f32),
            jax.ShapeDtypeStruct((8, D), f32),
        ]
    if fused:
        own, cotangent = in_hbm([own, cotangent])
    return pl.pallas_call(
        partial(feed_kernel, fused),
        out_shape=out_shape,
        in_specs=specs + weight_specs,
        out_specs=[VMEM] * len(out_shape),
        scratch_shapes=scratch,
        compiler_params=limit(LIMITS[3]),
        cost_estimate=cost(14 * 10**9, 16 * 2**20),
        name="feed",
    )(own, mixed, exact, cotangent, query_aux, gains, *weights)


PARTS = ((0, 1, 2), (3, 4, 5, 6, 7, 8))


def project_back_kernel(number, fused, own, cosine, sine, w, gains, *refs):
    part = PARTS[number]
    low = lax.broadcasted_iota(jnp.int32, (BLOCK, LANES), 1) < HD
    gain = gains[0:1, :]
    if number == 0:
        dq = refs[0]
        partial_sum, grads, normed_all, low_all = refs[-6:-2]
        copies = fetch((own,), refs[-2:-1], refs[-1])
        own = refs[-2]
    else:
        kept, got, grad_middle, before, grads_before = refs[:5]
        if fused:
            where = refs[5]
            grad_tokens, keep, give, sums, g_gain, normed_all, low_all = refs[-10:-3]
        else:
            grad_tokens, grads, g_gain, normed_all, low_all = refs[-8:-3]
        g_gain[...] = jnp.zeros_like(g_gain)
        copies = fetch((own, got), refs[-3:-1], refs[-1])
        own, got = refs[-3:-1]
    arrive(copies)

    def body(step, carry):
        rows = block(step)
        cos, sin = cosine[rows, :], -sine[rows, :]
        x = own[rows, :].astype(f32)
        scale = row_scale(x)
        normed_all[rows, :] = (x * scale * gain).astype(bf16)
        for at, slab in enumerate(part):
            kind, pair = divmod(slab, 3)
            heads = (2 * pair, 2 * pair + 1)
            if kind == 0:
                z = jnp.concatenate([dq[h, :, rows] for h in heads], axis=0).T * HD**-0.5
            else:
                one, two = [kept[h, rows, :] + got[h, rows, :].astype(f32) for h in heads]
                if kind == 1:
                    z = jnp.where(low, pltpu.roll(one, HD, 1), two)
                else:
                    z = jnp.where(low, one, pltpu.roll(two, HD, 1))
            if kind < 2:
                z = z * cos + swap_halves(z) * sin
            low_all[rows, at * LANES : (at + 1) * LANES] = z.astype(bf16)
        first = part[0] * LANES
        grad_normed = dot(
            low_all[rows, :], w[:, first : first + len(part) * LANES], NT
        )
        if number == 0:
            partial_sum[rows, :] = grad_normed
        else:
            grad_normed = grad_normed + before[rows, :]
            g_gain[0:1, :] += jnp.sum(grad_normed * x * scale, axis=0, keepdims=True)
            grad_tokens[rows, :] = (
                grad_middle[rows, :] + norm_back(grad_normed * gain, x, scale)
            ).astype(bf16)
        return carry

    lax.fori_loop(0, own.shape[0] // BLOCK, body, 0)
    value = dot(normed_all[...], low_all[...], TN)
    if number == 0 or not fused:
        grads[...] = value
        return
    core = where[0]
    for done, source in ((PARTS[0], grads_before), (PARTS[1], value)):
        for at, slab in enumerate(done):
            put_slab(sums, core, *fused, slab, source[:, at * LANES : (at + 1) * LANES])
    put_slab(sums, core, *fused, 9, gain_column(g_gain[...]))
    keep[...] = sums[0]
    give[...] = sums[1].astype(bf16)


def project_back(number, fused, where, shared, arrays, waits):
    own, cosine, sine, w, gains = shared
    length = own.shape[0]
    columns = len(PARTS[number]) * LANES
    scratch = [pltpu.VMEM((length, D), bf16), pltpu.VMEM((length, columns), bf16)]
    specs = [VMEM] * len(arrays)
    if number:
        specs[1] = ANY
    scratch += landing([own] + list(arrays[1:2]))
    if number == 0:
        out_shape = [in_vmem((length, D), f32), in_vmem((D, columns), f32)]
    elif fused:
        size, shard = fused
        chunk = (D // shard, size * shard, LANES)
        specs.append(SMEM)
        arrays = [*arrays, where]
        out_shape = [
            jax.ShapeDtypeStruct((length, D), bf16),
            jax.ShapeDtypeStruct(chunk, f32),
            jax.ShapeDtypeStruct(chunk, bf16),
        ]
        scratch = [pltpu.VMEM((2,) + chunk, f32), pltpu.VMEM((8, D), f32)] + scratch
    else:
        out_shape = [
            jax.ShapeDtypeStruct((length, D), bf16),
            jax.ShapeDtypeStruct((D, columns), f32),
            jax.ShapeDtypeStruct((8, D), f32),
        ]
    (own,) = in_hbm([own])
    return pl.pallas_call(
        partial(project_back_kernel, number, fused),
        out_shape=out_shape,
        in_specs=[HBM] + [VMEM] * 4 + specs + [ANY] * len(waits),
        out_specs=[VMEM] * len(out_shape),
        scratch_shapes=scratch,
        compiler_params=limit(LIMITS[5]),
        cost_estimate=cost((40 if number == 0 else 4) * 10**9, 8 * 2**20),
        name="project_back",
    )(own, cosine, sine, w, gains, *arrays, *waits)


def squares_kernel(*refs):
    total = sum(jnp.sum(ref[...] * ref[...]) for ref in refs[0:4:2]) + 0.0
    other = sum(jnp.sum(ref[...] * ref[...]) for ref in refs[1:4:2]) + 0.0
    refs[4][...] = jnp.full((1, LANES), total + other, f32)


def squares(sums):
    spec = pl.BlockSpec(memory_space=pltpu.VMEM)
    return pl.pallas_call(
        squares_kernel,
        out_shape=jax.ShapeDtypeStruct((1, LANES), f32),
        in_specs=[spec] * 4,
        out_specs=spec,
        compiler_params=limit(16),
        name="squares",
    )(*sums)


def update_kernel(shard, down, where, total, *refs):
    core = where[0]
    chunks = refs[:4]
    norm = refs[19]
    outs = [refs[20 + 5 * i : 25 + 5 * i] for i in range(4)]
    low, high, square = refs[40:43]
    copies = fetch(refs[4:19], refs[43:58], refs[58])
    masters, firsts, seconds = refs[43:48], refs[48:53], refs[53:58]
    split = 5 * shard

    @pl.when(core == 0)
    def _():
        for i, target in ((0, low), (1, high)):
            target[:split] = chunks[i][...]
            target[split:] = chunks[2 + i][...]

    @pl.when(core == 1)
    def _():
        for i, target in ((0, high), (1, low)):
            target[:split] = chunks[i][...]
            target[split:] = chunks[2 + i][...]

    arrive(copies)
    length = jnp.sqrt(total[0:1, 0:1])
    norm[...] = length
    factor = clip_limit / jnp.maximum(length, clip_limit)
    halves = (low, high)

    def step(which, grad, rows, columns, rate, decay):
        at = (rows, columns)
        new = adam_update(
            masters[which][at], factor * grad, firsts[which][at], seconds[which][at], rate, decay
        )
        outs[0][which][at] = new[0]
        outs[1][which][at] = new[1]
        outs[2][which][at] = new[2]
        outs[3][which][at] = new[2].astype(bf16)

    every = slice(None)
    places = [(0, i, i // 5, (i % 5) * shard) for i in range(9)]
    for i in range(19):
        which, column = (1, i) if i < 3 else (2, i - 3)
        places.append((which, column, i // 10, (5 + i % 10) * shard))
    for which, column, half, row in places:
        rate = 4.0 * D**-0.5 if which == 1 else D**-0.5
        grad = halves[half][row : row + shard, :]
        step(which, grad, every, slice(column * LANES, (column + 1) * LANES), rate, decay_rate)
    for half in range(2):
        for i in range(3):
            row = 15 * shard + i * down
            step(
                3, halves[half][row : row + down, :], slice(half * down, (half + 1) * down),
                slice(i * LANES, (i + 1) * LANES), FF**-0.5, decay_rate,
            )
    gain_rows = []
    for row in (4 * shard, 14 * shard):
        square[...] = jnp.zeros_like(square)
        square[0:shard, :] = high[row : row + shard, :]
        gain_rows.append(square[...].T[0:1, :shard])
    for i in range(2):
        step(4, gain_rows[i], slice(i, i + 1), every, 0.5, 0.0)


def update(where, total, sums, masters, firsts, seconds):
    shard, down = masters[0].shape[0], masters[3].shape[0] // 2
    spec = pl.BlockSpec(memory_space=pltpu.VMEM)
    shapes = [item.shape for item in masters]
    outs = pl.pallas_call(
        partial(update_kernel, shard, down),
        out_shape=[jax.ShapeDtypeStruct((1, 1), f32)]
        + [jax.ShapeDtypeStruct(shape, f32) for _ in range(3) for shape in shapes]
        + [jax.ShapeDtypeStruct(shape, bf16) for shape in shapes],
        in_specs=[pl.BlockSpec(memory_space=pltpu.SMEM)] + [VMEM] * 5 + [HBM] * 15,
        out_specs=[spec] * 21,
        scratch_shapes=[
            pltpu.VMEM((15 * shard + 3 * down, LANES), f32),
            pltpu.VMEM((15 * shard + 3 * down, LANES), f32),
            pltpu.VMEM((LANES, LANES), f32),
        ]
        + landing([*masters, *firsts, *seconds]),
        compiler_params=limit(LIMITS[6]),
        name="update",
    )(where, total, *sums, *in_hbm([*masters, *firsts, *seconds]))
    return outs[0][0, 0], outs[1:6], outs[6:11], outs[11:16], outs[16:21]


def update_plain(core, total, sums, masters, firsts, seconds):
    shard, down = masters[0].shape[0], masters[3].shape[0] // 2
    mine = jnp.concatenate([sums[0], sums[2]])
    there = jnp.concatenate([sums[1], sums[3]])
    low = jnp.where(core == 0, mine, there)
    high = jnp.where(core == 0, there, mine)
    five, fifteen = 5 * shard, 15 * shard
    first_shard = jnp.concatenate([low[:five], high[:five]]).reshape(10, shard, LANES)
    second_shard = jnp.concatenate([low[five:fifteen], high[five:fifteen]])
    second_shard = second_shard.reshape(20, shard, LANES)
    down_shard = jnp.stack(
        [item[fifteen:].reshape(3, down, LANES) for item in (low, high)], axis=1
    ).reshape(3, 2 * down, LANES)
    shard_grads = (
        unslab(first_shard[:9]),
        unslab(second_shard[:3]),
        unslab(second_shard[3:19]),
        unslab(down_shard),
        jnp.stack([first_shard[9, :, 0], second_shard[19, :, 0]]),
    )
    grad_norm = jnp.sqrt(total[0, 0])
    factor = clip_limit / jnp.maximum(grad_norm, clip_limit)
    rates = (D ** (-0.5), 4.0 * D ** (-0.5), D ** (-0.5), FF ** (-0.5), 0.5)
    decays = (decay_rate, decay_rate, decay_rate, decay_rate, 0.0)
    updates = [
        adam_update(
            masters[i], factor * shard_grads[i], firsts[i], seconds[i], rates[i], decays[i]
        )
        for i in range(5)
    ]
    new_first, new_second, new_master = zip(*updates)
    return grad_norm, new_first, new_second, new_master, [item.astype(bf16) for item in new_master]


def per_device(
    count,
    tokens,
    cotangent,
    sample_ids,
    pad_flags,
    offsets,
    w_qkv,
    w_out,
    w_gate_up,
    w_down,
    gains,
    m_qkv,
    m_out,
    m_gate_up,
    m_down,
    m_gains,
    v_qkv,
    v_out,
    v_gate_up,
    v_down,
    v_gains,
):
    owner = lax.axis_index("batch")
    core = lax.axis_index("tm")
    where = jnp.stack([core, owner]).astype(jnp.int32)
    shard = w_qkv.shape[0]
    down = w_down.shape[0] // 2
    own = tokens[0]
    fuse_in = can_unpack(shard, down)
    masters = (w_qkv, w_out, w_gate_up, w_down, gains)

    first = send_chunk(where, FIRST_PLAN, 0, [w_qkv, gains], [])
    there = swap_tm(own)
    cosine, sine, key_aux, query_aux, ranges = tables(
        where, sample_ids, pad_flags, offsets, [there]
    )
    first_held, first_pieces = gather(first, count, [query_aux])
    second = send_chunk(where, SECOND_PLAN, down, [w_out, w_gate_up, w_down], [first_held])

    def gathered(pieces, number, down):
        others = [swap_tm(piece) for piece in pieces]
        if fuse_in:
            return (where, *pieces, *others), (count, number, shard, down)
        return unpack_plain(count, number, shard, down, where, pieces, others), None

    weights, fused = gathered(first_pieces, 5, 0)
    qa, ka, va, kt, vt, attn_in, gain_pair = project(
        own, there, cosine, sine, key_aux, query_aux, weights, fused, []
    )
    second_held, second_pieces = gather(second, count, [gain_pair])
    mixed, exact, qb = attend(ranges, qa, ka, vt, [second_held])
    second_pieces[1:] = hold(second_pieces[1:], [mixed])
    weights, fused = gathered(second_pieces, 10, down)
    result, grad_middle, da, *grads = feed(
        own, mixed, exact, cotangent[0], query_aux, gain_pair, weights, fused
    )
    groups = bit_groups(count)
    fan = 1 << groups[0][1]

    def flips(halves):
        halves = halves.reshape((-1, fan) + halves.shape[-2:])
        mine = owner & (fan - 1)
        parts = [lax.dynamic_index_in_dim(halves, mine ^ k, 1, keepdims=False) for k in range(fan)]
        return [parts[0]] + [item.astype(bf16) for item in parts[1:]]

    if not fused:
        grads = flips(pack_plain(count, core, grads, 10, shard, down))
    got = [permute_batch(grads[k], k, count) for k in range(1, fan)]
    dq, kept, part = attend_back(ranges, qb, ka, da, va, kt, [])
    got = hold(got, [part])
    part_there = swap_tm(part)
    left = count // fan
    keep, give = combine(where, [grads[0], *got], (1, 2, left, 0, 0))
    split = None
    if len(groups) > 1:
        split = (left >> groups[1][1], 1 << groups[1][1], 1, 1, groups[1][0])
    parts = combine(where, [keep, swap_tm(give)], split)
    fused = (5, shard) if fuse_in else None
    shared = (own, cosine, sine, attn_in, gain_pair)
    before, grads_before = project_back(0, fused, where, shared, [dq], [parts[0]])
    if split:
        parts = [scatter_parts(where, parts, count, groups[1:], [grads_before])]
    second_sum = parts[0].reshape(-1, LANES)
    grad_tokens, *grads = project_back(
        1, fused, where, shared, [kept, part_there, grad_middle, before, grads_before], [parts[0]]
    )
    if fused:
        kept, given = grads
    else:
        grads = [jnp.concatenate([grads_before, grads[0]], axis=1), grads[1]]
        halves = pack_plain(count, core, grads, 5, shard, 0)
        kept = jnp.where(core == 0, halves[0], halves[1])
        given = jnp.where(core == 0, halves[1], halves[0]).astype(bf16)
    parts = combine(where, [kept, swap_tm(given)], (left, fan, 1, 1, 0))
    first_sum = scatter_parts(where, parts, count, groups).reshape(-1, LANES)
    sums = (first_sum, swap_tm(first_sum), second_sum, swap_tm(second_sum))
    total = sum_batch(squares(sums), count)
    firsts = (m_qkv, m_out, m_gate_up, m_down, m_gains)
    seconds = (v_qkv, v_out, v_gate_up, v_down, v_gains)
    if fuse_in:
        updates = update(where, total, sums, masters, firsts, seconds)
    else:
        updates = update_plain(core, total, sums, masters, firsts, seconds)
    grad_norm, new_first, new_second, new_master, copies = updates
    return (
        result[None],
        grad_tokens[None],
        grad_norm,
        *new_first,
        *new_second,
        *new_master,
        *copies,
    )


def solution(mesh):
    in_specs = (
        P("batch", "tm", None),
        P("batch", "tm", None),
        P("batch", None),
        P("batch", None),
        P("batch", None),
        P("batch", None),
        P("batch", None),
        P("batch", None),
        P("batch", None),
        P(None, "batch"),
        P("batch", None),
        P("batch", None),
        P("batch", None),
        P("batch", None),
        P(None, "batch"),
        P("batch", None),
        P("batch", None),
        P("batch", None),
        P("batch", None),
        P(None, "batch"),
    )
    out_specs = (
        P("batch", "tm", None),
        P("batch", "tm", None),
        P(),
        P("batch", None),
        P("batch", None),
        P("batch", None),
        P("batch", None),
        P(None, "batch"),
        P("batch", None),
        P("batch", None),
        P("batch", None),
        P("batch", None),
        P(None, "batch"),
        P("batch", None),
        P("batch", None),
        P("batch", None),
        P("batch", None),
        P(None, "batch"),
        P("batch", None),
        P("batch", None),
        P("batch", None),
        P("batch", None),
        P(None, "batch"),
    )
    return jax.shard_map(
        partial(per_device, mesh.shape["batch"]), mesh=mesh, in_specs=in_specs, out_specs=out_specs, check_vma=False
    )
```

```python
import math
from functools import partial

import jax
import jax.numpy as jnp
from jax import lax
from jax.experimental import pallas as pl
from jax.experimental.pallas import tpu as pltpu
from jax.sharding import PartitionSpec as P

D = 384
FF = 1024
HEADS = 6
HD = 64
STEP = 3


norm_eps = 1e-06
beta_one = 0.5
beta_two = 0.5
adam_eps = 1e-08
decay_rate = 0.1
clip_limit = 1.0
masked_score = -1e30


def adam_update(master, grad, first, second, rate, decay):
    first_new = beta_one * first + (1.0 - beta_one) * grad
    second_new = beta_two * second + (1.0 - beta_two) * grad * grad
    direction = (
        first_new
        / (1.0 - beta_one**STEP)
        / (jnp.sqrt(second_new / (1.0 - beta_two**STEP)) + adam_eps)
    )
    return (first_new, second_new, master - rate * (direction + decay * master))


def bit_groups(count):
    groups = []
    low, bits = 0, count.bit_length() - 1
    while low < bits:
        width = min(2, bits - low)
        groups.append((low, width))
        low += width
    return groups


def permute_batch(value, flip, count):
    return lax.ppermute(value, "batch", [(i, i ^ flip) for i in range(count)])


def swap_tm(value):
    return lax.ppermute(value, "tm", [(0, 1), (1, 0)])


def slabs(matrix):
    rows, columns = matrix.shape
    return matrix.reshape(rows, columns // 128, 128).transpose(1, 0, 2)


def unslab(stack):
    count, rows, _ = stack.shape
    return stack.transpose(1, 0, 2).reshape(rows, count * 128)


bf16 = jnp.bfloat16
f32 = jnp.float32
BLOCK = 256
LANES = 128
KEEP_LANE = 96
LIMITS = (12, 12, 12, 34, 12, 12, 12)
NN = (((1,), (0,)), ((), ()))
NT = (((1,), (1,)), ((), ()))
TN = (((0,), (0,)), ((), ()))


def dot(left, right, dims):
    return lax.dot_general(left, right, dims, preferred_element_type=f32)


def cost(flops, moved):
    return pl.CostEstimate(flops=flops, bytes_accessed=moved, transcendentals=0)


def in_vmem(shape, dtype):
    return pltpu.VMEM(tuple(shape), dtype)


VMEM = pl.BlockSpec(memory_space=pltpu.VMEM)
SMEM = pl.BlockSpec(memory_space=pltpu.SMEM)
ANY = pl.BlockSpec(memory_space=pl.ANY)
HBM = pl.BlockSpec(memory_space=pltpu.HBM)


def fetch(sources, targets, semaphores):
    copies = [
        pltpu.make_async_copy(source, target, semaphores.at[i])
        for i, (source, target) in enumerate(zip(sources, targets))
    ]
    for copy in copies:
        copy.start()
    return copies


def landing(arrays):
    return [pltpu.VMEM(item.shape, item.dtype) for item in arrays] + [
        pltpu.SemaphoreType.DMA((len(arrays),))
    ]


def arrive(copies):
    for copy in copies:
        copy.wait()


def limit(mebibytes):
    return pltpu.CompilerParams(vmem_limit_bytes=mebibytes * 2**20)


def block(start, size=BLOCK):
    return pl.ds(pl.multiple_of(start * size, size), size)


def sum_batch(value, count):
    value = jnp.broadcast_to(value[:, None], (count, 1, LANES))
    value = lax.all_to_all(value, "batch", 0, 0, tiled=True)
    return jnp.sum(value, axis=0)


def row_scale(values):
    return lax.rsqrt(jnp.mean(values * values, axis=-1, keepdims=True) + norm_eps)


def norm_back(grad_normed, values, scale):
    return scale * grad_normed - values * scale * scale * scale * jnp.mean(
        grad_normed * values, axis=-1, keepdims=True
    )


def split_three(values):
    high = values.astype(bf16)
    rest = values - high.astype(f32)
    middle = rest.astype(bf16)
    return high, middle, (rest - middle.astype(f32)).astype(bf16)


def swap_halves(pair):
    lane = lax.broadcasted_iota(jnp.int32, pair.shape, 1)
    return jnp.where(lane % HD < HD // 2, pltpu.roll(pair, 96, 1), pltpu.roll(pair, 32, 1))


def relative_place(device, owner, count):
    flips = device ^ owner
    place, scale = 0, 1
    for low, width in reversed(bit_groups(count)):
        place = place + ((flips >> low) & ((1 << width) - 1)) * scale
        scale <<= width
    return place


def exchange_all(held, low, width, count):
    return [held] + [permute_batch(held, k << low, count) for k in range(1, 1 << width)]


def in_hbm(arrays):
    return [pltpu.with_memory_space_constraint(item, pltpu.HBM) for item in arrays]


def join_kernel(number, *refs):
    out = refs[-1]
    size = refs[0].shape[0]
    for i in range(number):
        out[i * size : (i + 1) * size] = refs[i][...]


def join(pieces, waits=()):
    first = pieces[0]
    shape = (len(pieces) * first.shape[0],) + first.shape[1:]
    return pl.pallas_call(
        partial(join_kernel, len(pieces)),
        out_shape=jax.ShapeDtypeStruct(shape, first.dtype),
        in_specs=[VMEM] * len(pieces) + [ANY] * len(waits),
        out_specs=VMEM,
        compiler_params=limit(4),
        name="join",
    )(*pieces, *waits)


def combine_kernel(number, split, where, *refs):
    items, outs = refs[:number], refs[-len(refs) + number :]
    outs = outs[-(split[1] if split else 1) :]

    def total(index):
        return sum(item[index].astype(f32) for item in items[1:]) + items[0][index].astype(f32)

    if not split:
        outs[0][...] = total(slice(None))
        return
    upper, fan, lower, which, low = split
    mine = (where[which] >> low) & (fan - 1)
    for a in range(upper):
        for b in range(lower):
            for flip in range(fan):
                index = (a * fan + (mine ^ flip)) * lower + b
                outs[flip][a * lower + b] = total(index).astype(outs[flip].dtype)


def combine(where, items, split, waits=()):
    count, rows, _ = items[0].shape
    if split:
        fan = split[1]
        shapes = [
            jax.ShapeDtypeStruct((count // fan, rows, LANES), bf16 if flip else f32)
            for flip in range(fan)
        ]
    else:
        shapes = [jax.ShapeDtypeStruct((count, rows, LANES), f32)]
    return pl.pallas_call(
        partial(combine_kernel, len(items), split),
        out_shape=shapes,
        in_specs=[SMEM] + [VMEM] * len(items) + [ANY] * len(waits),
        out_specs=[VMEM] * len(shapes),
        compiler_params=limit(12),
        name="combine",
    )(where, *items, *waits)


def scatter_parts(where, parts, count, groups, waits=None):
    for n, (low, width) in enumerate(groups):
        got = [permute_batch(item, k << low, count) for k, item in enumerate(parts) if k]
        if waits and n == 0:
            got = hold(got, waits)
        split = None
        if n + 1 < len(groups):
            fan = 1 << groups[n + 1][1]
            split = (parts[0].shape[0] // fan, fan, 1, 1, groups[n + 1][0])
        parts = combine(where, [parts[0], *got], split)
    return parts[0]


def hold(values, waits):
    spec = pl.BlockSpec(memory_space=pl.ANY)
    number = len(values)
    return pl.pallas_call(
        lambda *refs: None,
        out_shape=[jax.ShapeDtypeStruct(item.shape, item.dtype) for item in values],
        in_specs=[spec] * (number + len(waits)),
        out_specs=[spec] * number,
        input_output_aliases={i: i for i in range(number)},
        compiler_params=limit(1),
        name="hold",
    )(*values, *waits)


def send_kernel(shard, plan, down, where, *refs):
    number = (len(refs) - 4) // 2
    target, stage, square = refs[number : number + 3]
    sources = refs[number + 3 : -1]
    arrive(fetch(refs[:number], sources, refs[-1]))
    number = len(plan) // 2
    core = where[0]
    stage[...] = jnp.zeros_like(stage)
    gain_at = [i for i, item in enumerate(plan) if item == "gain"]
    if gain_at:
        square[...] = jnp.zeros_like(square)
        square[0:2, 0:shard] = sources[-1][...]
        column = square[...].T

    def fill(half):
        for i in range(number):
            item = plan[half * number + i]
            rows = slice(i * shard, (i + 1) * shard)
            if item == "gain":
                stage[rows, :] = column[:shard]
            elif item is not None:
                which, at = item
                stage[rows, :] = sources[which][:, at * LANES : (at + 1) * LANES]
        for i in range(3 if down else 0):
            start = number * shard + i * down
            stage[start : start + down, :] = sources[2][
                half * down : (half + 1) * down, i * LANES : (i + 1) * LANES
            ]

    @pl.when(core == 0)
    def _():
        fill(0)

    @pl.when(core == 1)
    def _():
        fill(1)

    target[...] = stage[...].astype(bf16)


def send_chunk(where, plan, down, sources, waits):
    shard = sources[0].shape[0]
    rows = len(plan) // 2 * shard + 3 * down
    rows = -(-rows // 16) * 16
    core = where[0]
    if shard % 8 == 0 and down % 8 == 0:
        spec = VMEM

        def kernel(where, *refs):
            kept = refs[: len(sources)] + refs[len(sources) + len(waits) :]
            send_kernel(shard, plan, down, where, *kept)

        return pl.pallas_call(
            kernel,
            out_shape=jax.ShapeDtypeStruct((rows, LANES), bf16),
            in_specs=[SMEM] + [HBM] * len(sources) + [ANY] * len(waits),
            out_specs=spec,
            scratch_shapes=[pltpu.VMEM((rows, LANES), f32), pltpu.VMEM((LANES, LANES), f32)]
            + landing(sources),
            compiler_params=limit(6),
            name="send_chunk",
        )(where, *in_hbm(sources), *waits)
    stacks = {i: slabs(item) for i, item in enumerate(sources) if item.shape[1] % LANES == 0}
    pieces = []
    for item in plan:
        if item == "gain":
            pieces.append(jnp.pad(sources[-1].T, ((0, 0), (0, LANES - 2))))
        elif item is None:
            pieces.append(jnp.zeros((shard, LANES), f32))
        else:
            pieces.append(stacks[item[0]][item[1]])
    half = len(plan) // 2
    halves = [jnp.concatenate(pieces[:half]), jnp.concatenate(pieces[half:])]
    if down:
        for i in range(2):
            part = stacks[2][:, i * down : (i + 1) * down].reshape(3 * down, LANES)
            halves[i] = jnp.concatenate([halves[i], part])
    chunk = jnp.where(core == 0, halves[0], halves[1]).astype(bf16)
    return jnp.pad(chunk, ((0, rows - chunk.shape[0]), (0, 0)))


FIRST_PLAN = tuple((0, i) for i in range(9)) + ("gain",)
SECOND_PLAN = tuple((0, i) for i in range(3)) + tuple((1, i) for i in range(16)) + (None,)


def gather(chunk, count, waits):
    held = chunk[None]
    groups = bit_groups(count)[::-1]
    for n, (low, width) in enumerate(groups):
        pieces = exchange_all(held, low, width, count)
        if n + 1 < len(groups):
            held = join(pieces, () if n else waits)
    return held, pieces


def unpack(count, number, shard, down, where, pieces, others, stage, w_down):
    core, owner = where[0], where[1]
    last = bit_groups(count)[0][1]
    for sources, half in ((pieces, core), (others, 1 - core)):
        for flip, source in enumerate(sources):

            def one(n, carry, source=source, half=half, flip=flip):
                device = owner ^ flip ^ (relative_flips(n, count) << last)
                chunk = source[n].astype(f32)
                for i in range(number):
                    rows = pl.ds(pl.multiple_of(device * shard, 8), shard)
                    stage[half * number + i, rows, :] = chunk[i * shard : (i + 1) * shard]
                for i in range(3 if down else 0):
                    start = number * shard + i * down
                    rows = pl.ds(pl.multiple_of((device * 2 + half) * down, 16), down)
                    w_down[rows, i * LANES : (i + 1) * LANES] = chunk[start : start + down].astype(
                        bf16
                    )
                return carry

            lax.fori_loop(0, source.shape[0], one, 0, unroll=True)


def relative_flips(place, count):
    last = bit_groups(count)[0][1]
    flips, scale = 0, 1
    for low, width in reversed(bit_groups(count)[1:]):
        flips = flips + (((place // scale) & ((1 << width) - 1)) << (low - last))
        scale <<= width
    return flips


def can_unpack(shard, down):
    return shard % 8 == 0 and down % 16 == 0


def unpack_plain(count, number, shard, down, where, mine, other):
    core, owner = where[0], where[1]
    places = relative_place(jnp.arange(count, dtype=jnp.int32), owner, count)
    mine, other = jnp.concatenate(mine), jnp.concatenate(other)
    low = jnp.take(jnp.where(core == 0, mine, other), places, axis=0)
    high = jnp.take(jnp.where(core == 0, other, mine), places, axis=0)

    def part(source):
        return (
            source[:, : number * shard]
            .reshape(count, number, shard, LANES)
            .transpose(1, 0, 2, 3)
            .reshape(number, D, LANES)
        )

    stack = jnp.concatenate([part(low), part(high)], axis=0)
    if number == 5:
        return unslab(stack[:9]), stack[9].T[:8].astype(f32)
    downs = [
        item[:, number * shard : number * shard + 3 * down].reshape(count, 3, down, LANES)
        for item in (low, high)
    ]
    w_down = jnp.stack(downs, axis=1).transpose(0, 1, 3, 2, 4).reshape(FF, D)
    return unslab(stack[:3]), unslab(stack[3:19]), w_down


def put_slab(stage, core, number, shard, at, slab):
    half, row = at // number, (at % number) * shard
    slot = core if half == 0 else 1 - core
    stage[slot, :, row : row + shard, :] = slab.reshape(-1, shard, LANES)


def put_down(stage, core, number, shard, down, column, slab, first):
    parts = slab.reshape(-1, 2, down, LANES)
    row = number * shard + column * down
    devices = slice(first, first + parts.shape[0])
    stage[core, devices, row : row + down, :] = parts[:, 0]
    stage[1 - core, devices, row : row + down, :] = parts[:, 1]


def gain_column(row):
    return jnp.concatenate([row, jnp.zeros((LANES - 8, D), f32)], axis=0).T


def pack_plain(count, core, grads, number, shard, down):
    column = jnp.pad(grads[-1][:1].T, ((0, 0), (0, LANES - 1)))[None]
    stack = jnp.concatenate([slabs(item) for item in (grads[:2] if down else grads[:1])] + [column])

    def by_device(part):
        return (
            part.reshape(number, count, shard, LANES)
            .transpose(1, 0, 2, 3)
            .reshape(count, number * shard, LANES)
        )

    halves = [by_device(stack[:number]), by_device(stack[number:])]
    if down:
        downs = (
            slabs(grads[2])
            .reshape(3, count, 2, down, LANES)
            .transpose(2, 1, 0, 3, 4)
            .reshape(2, count, 3 * down, LANES)
        )
        halves = [jnp.concatenate([halves[i], downs[i]], axis=1) for i in range(2)]
    return jnp.stack(halves)


def tables_kernel(length, where, ids, pads, offsets, *refs):
    cosine, sine, key_aux, query_aux, ranges = refs[-5:]
    core = where[0]
    whole = 2 * length

    def turn(row):
        low, high = row[:, :length], row[:, length:]
        return jnp.concatenate(
            [jnp.where(core == 0, low, high), jnp.where(core == 0, high, low)], axis=1
        )

    classes = (2 * ids[...] + pads[...]).astype(f32)
    spot = lax.broadcasted_iota(jnp.int32, (1, whole), 1)
    position = (turn(spot) + turn(offsets[...])).astype(f32)
    turned = turn(classes)
    index = lax.broadcasted_iota(jnp.int32, (HD // 2, whole), 0).astype(f32)
    angle = position * jnp.exp(index * (-2.0 * math.log(10000.0) / HD))
    cos, sin = jnp.cos(angle), jnp.sin(angle)
    cosine[...] = jnp.concatenate([cos, cos, cos, cos], axis=0).T
    sine[...] = jnp.concatenate([-sin, sin, -sin, sin], axis=0).T
    at = lax.broadcasted_iota(jnp.int32, (LANES, whole), 0)
    is_class = (at >= HD) & (at < HD + 8)
    same = (at - HD).astype(f32) == turned
    is_log = (at >= HD + 8) & (at < HD + 8 + 3 * HEADS)
    key_aux[...] = jnp.where((is_class & same) | is_log, 1.0, 0.0).T.astype(bf16)
    own = turned[:, :length]
    kept = jnp.where(turn(pads[...])[:, :length] == 0, 1.0, 0.0)
    extra = jnp.where(is_class & ~same, masked_score, 0.0)[:, :length]
    query_aux[...] = jnp.where(at[:, :length] == KEEP_LANE, kept, extra).T.astype(bf16)
    starts = (core * length, (1 - core) * length)
    for n in range(length // BLOCK):
        mine = own[:, n * BLOCK : (n + 1) * BLOCK]
        first = jnp.min(mine)
        last = jnp.max(mine)
        low_key = jnp.sum(jnp.where(classes < first, 1.0, 0.0)).astype(jnp.int32)
        high_key = jnp.sum(jnp.where(classes <= last, 1.0, 0.0)).astype(jnp.int32)
        bounds = []
        for start in starts:
            low_part = jnp.clip(low_key - start, 0, length)
            high_part = jnp.clip(high_key - start, 0, length)
            low_block = low_part // BLOCK
            bounds.append((low_block, jnp.maximum((high_part + BLOCK - 1) // BLOCK - low_block, 0)))
        ranges[0, n] = bounds[0][0]
        ranges[1, n] = bounds[0][1]
        ranges[2, n] = bounds[1][0] + length // BLOCK - bounds[0][1]
        ranges[3, n] = bounds[0][1] + bounds[1][1]


def tables(where, ids, pads, offsets, waits):
    whole = ids.shape[1]
    length = whole // 2
    spec = pl.BlockSpec(memory_space=pltpu.VMEM)
    smem = pl.BlockSpec(memory_space=pltpu.SMEM)
    return pl.pallas_call(
        partial(tables_kernel, length),
        out_shape=[
            in_vmem((whole, LANES), f32),
            in_vmem((whole, LANES), f32),
            in_vmem((whole, LANES), bf16),
            in_vmem((length, LANES), bf16),
            jax.ShapeDtypeStruct((4, length // BLOCK), jnp.int32),
        ],
        in_specs=[smem, spec, spec, spec] + [pl.BlockSpec(memory_space=pl.ANY)] * len(waits),
        out_specs=[spec] * 4 + [smem],
        compiler_params=limit(LIMITS[0]),
        cost_estimate=cost(3 * 10**9, 4 * 2**20),
        name="tables",
    )(where, ids, pads, offsets, *waits)


def project_kernel(fused, own, there, cosine, sine, key_aux, query_aux, *refs):
    if fused:
        pieces = 1 << bit_groups(fused[0])[0][1]
        where, scratch = refs[0], refs[-2 * pieces - 3 : -1]
        qa, ka, va, kt, vt, w, gains, stage = refs[-2 * pieces - 11 : -2 * pieces - 3]
        copies = fetch((*refs[1 : 1 + 2 * pieces], own, there), scratch, refs[-1])
        mine, other, (own, there) = (
            scratch[:pieces], scratch[pieces : 2 * pieces], scratch[2 * pieces :]
        )
        arrive(copies)
        unpack(*fused, where, mine, other, stage, None)
        for i in range(9):
            w[:, i * LANES : (i + 1) * LANES] = stage[i].astype(bf16)
        gains[...] = stage[9].T[:8]
    else:
        w_in, gains_in, (qa, ka, va, kt, vt, w, gains) = *refs[:2], refs[-7:]
        w[...] = w_in[...]
        gains[...] = gains_in[...]
    low = lax.broadcasted_iota(jnp.int32, (BLOCK, LANES), 1) < HD
    lane = lax.broadcasted_iota(jnp.int32, (BLOCK, LANES), 1)
    value_extra = jnp.where((lane >= HD) & (lane < HD + 3), 1.0, 0.0)
    ones = jnp.ones((8, BLOCK), bf16)
    blocks = own.shape[0] // BLOCK

    def body(step, carry, source, base):
        rows, keys = block(step), block(base + step)
        x = source[rows, :].astype(f32)
        normed = (x * row_scale(x) * gains[0:1, :]).astype(bf16)
        cos, sin = cosine[keys, :], sine[keys, :]
        first = 0 if base == 0 else D
        products = dot(normed, w[:, first:], NN)
        products = [
            products[:, i * LANES - first : (i + 1) * LANES - first]
            for i in range(first // LANES, 9)
        ]
        if base == 0:
            query_extra = query_aux[rows, :].astype(f32)
            for pair in range(HEADS // 2):
                z = products[pair]
                z = (z * cos + swap_halves(z) * sin).astype(bf16).astype(f32) * HD**-0.5
                qa[2 * pair, rows, :] = jnp.where(low, z, query_extra).astype(bf16)
                qa[2 * pair + 1, rows, :] = jnp.where(
                    low, pltpu.roll(z, HD, 1), query_extra
                ).astype(bf16)
        key_extra = key_aux[keys, :].astype(f32)
        for pair in range(HEADS // 2):
            z = products[pair - 6]
            z = z * cos + swap_halves(z) * sin
            ka[2 * pair, keys, :] = jnp.where(low, z, key_extra).astype(bf16)
            ka[2 * pair + 1, keys, :] = jnp.where(
                low, pltpu.roll(z, HD, 1), key_extra
            ).astype(bf16)
            turned = z.T.astype(bf16)
            kt[2 * pair, :, keys] = turned[:HD]
            kt[2 * pair + 1, :, keys] = turned[HD:]
        for pair in range(HEADS // 2):
            z = products[pair - 3]
            va[2 * pair, keys, :] = jnp.where(low, z, value_extra).astype(bf16)
            va[2 * pair + 1, keys, :] = jnp.where(
                low, pltpu.roll(z, HD, 1), value_extra
            ).astype(bf16)
            turned = z.T.astype(bf16)
            for i in range(2):
                vt[2 * pair + i, :HD, keys] = turned[i * HD : (i + 1) * HD]
                vt[2 * pair + i, HD:, keys] = ones
        return carry

    lax.fori_loop(0, blocks, partial(body, source=own, base=0), 0)
    lax.fori_loop(0, blocks, partial(body, source=there, base=blocks), 0)


def project(own, there, cosine, sine, key_aux, query_aux, weights, fused, waits):
    length = own.shape[0]
    whole = 2 * length
    scratch, specs = [], [VMEM] * 6
    weight_specs = [VMEM] * 2
    if fused:
        specs = [HBM, ANY] + [VMEM] * 4
        weight_specs = [SMEM] + [ANY] * (len(weights) - 1)
        scratch = [pltpu.VMEM((10, D, LANES), f32)] + landing([*weights[1:], own, there])
    if fused:
        (own,) = in_hbm([own])
    return pl.pallas_call(
        partial(project_kernel, fused),
        out_shape=[
            in_vmem((HEADS, length, LANES), bf16),
            in_vmem((HEADS, whole, LANES), bf16),
            in_vmem((HEADS, whole, LANES), bf16),
            in_vmem((HEADS, HD, whole), bf16),
            in_vmem((HEADS, HD + 8, whole), bf16),
            in_vmem((D, 3 * D), bf16),
            in_vmem((8, D), f32),
        ],
        in_specs=specs + weight_specs + [ANY] * len(waits),
        out_specs=[VMEM] * 7,
        scratch_shapes=scratch,
        compiler_params=limit(LIMITS[1]),
        cost_estimate=cost(9 * 10**9, 16 * 2**20),
        name="project",
    )(own, there, cosine, sine, key_aux, query_aux, *weights, *waits)


def key_block(ranges, step, n):
    return jnp.where(n < ranges[1, step], ranges[0, step] + n, ranges[2, step] + n)


def attend_kernel(ranges, qa, ka, vt, *refs):
    mixed, exact, qb, total, peak = refs[-5:]
    lane = lax.broadcasted_iota(jnp.int32, (BLOCK, LANES), 1)

    def one(step, carry):
        queries = block(step)
        peak[...] = jnp.full((HEADS, 8, BLOCK), -3e38, f32)
        total[...] = jnp.zeros_like(total)

        def body(n, carry):
            rows = block(key_block(ranges, step, n))
            scores = [dot(ka[h, rows, :], qa[h, queries, :], NT) for h in range(HEADS)]
            weights = []
            for h in range(HEADS):
                old = peak[h][:1]
                new = jnp.maximum(old, jnp.max(scores[h], axis=0, keepdims=True))
                weights.append((jnp.exp(scores[h] - new).astype(bf16), jnp.exp(old - new)))
                peak[h] = jnp.broadcast_to(new, (8, BLOCK))
            for h in range(HEADS):
                weight, shrink = weights[h]
                total[h] = total[h] * shrink + dot(vt[h, :, rows], weight, NN)
            return carry

        lax.fori_loop(0, ranges[3, step], body, 0)
        means, pieces = [], []
        for h in range(HEADS):
            bottom = total[h][HD : HD + 1]
            means.append(total[h][:HD] / bottom)
            logs = -(peak[h][:1] + jnp.log(bottom))
            pieces.extend(piece.astype(f32) for piece in split_three(logs))
        for pair in range(HEADS // 2):
            both = jnp.concatenate(means[2 * pair : 2 * pair + 2], axis=0).T
            mixed[queries, pair * LANES : (pair + 1) * LANES] = both.astype(bf16)
            exact[queries, pair * LANES : (pair + 1) * LANES] = both
        table = jnp.concatenate(
            [jnp.zeros((HD + 8, BLOCK), f32)]
            + pieces
            + [jnp.zeros((LANES - HD - 8 - 3 * HEADS, BLOCK), f32)],
            axis=0,
        ).T
        for h in range(HEADS):
            start = HD + 8 + 3 * h
            qb[h, queries, :] = jnp.where(
                (lane >= start) & (lane < start + 3), table, qa[h, queries, :].astype(f32)
            ).astype(bf16)
        return carry

    lax.fori_loop(0, qa.shape[1] // BLOCK, one, 0)


def attend(ranges, qa, ka, vt, waits):
    heads, length, _ = qa.shape
    return pl.pallas_call(
        attend_kernel,
        out_shape=[
            in_vmem((length, D), bf16),
            in_vmem((length, D), f32),
            in_vmem(qa.shape, bf16),
        ],
        in_specs=[SMEM] + [VMEM] * 3 + [ANY] * len(waits),
        out_specs=[VMEM] * 3,
        scratch_shapes=[
            pltpu.VMEM((heads, HD + 8, BLOCK), f32),
            pltpu.VMEM((heads, 8, BLOCK), f32),
        ],
        compiler_params=limit(LIMITS[2]),
        cost_estimate=cost(18 * 10**9, 12 * 2**20),
        name="attend",
    )(ranges, qa, ka, vt, *waits)


def attend_back_kernel(ranges, qb, ka, da, va, kt, *refs):
    dq, sums, there, acc = refs[-4:]
    sums[...] = jnp.zeros_like(sums)
    zero = jnp.zeros((BLOCK, HD), bf16)

    def one(step, carry):
        queries = block(step)
        acc[...] = jnp.zeros_like(acc)

        def body(n, carry):
            rows = block(key_block(ranges, step, n))
            first = [
                (
                    dot(ka[h, rows, :], qb[h, queries, :], NT),
                    dot(va[h, rows, :], da[h, queries, :], NT),
                )
                for h in range(HEADS)
            ]
            second = []
            for scores, grads in first:
                probs = jnp.exp(scores)
                second.append((probs.astype(bf16), (probs * grads).astype(bf16)))
            for h in range(HEADS):
                probs_low, grads_low = second[h]
                grad_side = jnp.concatenate([da[h, queries, :HD], zero], axis=1)
                query_side = jnp.concatenate([zero, qb[h, queries, :HD]], axis=1)
                sums[h, rows, :] += dot(probs_low, grad_side, NN) + dot(grads_low, query_side, NN)
                acc[h] += dot(kt[h, :, rows], grads_low, NN)
            return carry

        lax.fori_loop(0, ranges[3, step], body, 0)
        for h in range(HEADS):
            dq[h, :, queries] = acc[h]
        return carry

    length = qb.shape[1]
    lax.fori_loop(0, length // BLOCK, one, 0)
    there[...] = sums[:, length:, :].astype(bf16)


def attend_back(ranges, qb, ka, da, va, kt, waits):
    heads, length, _ = qb.shape
    whole = ka.shape[1]
    return pl.pallas_call(
        attend_back_kernel,
        out_shape=[
            in_vmem((heads, HD, length), f32),
            in_vmem((heads, whole, LANES), f32),
            jax.ShapeDtypeStruct((heads, whole - length, LANES), bf16),
        ],
        in_specs=[SMEM] + [VMEM] * 5 + [ANY] * len(waits),
        out_specs=[VMEM] * 3,
        scratch_shapes=[pltpu.VMEM((heads, HD, BLOCK), f32)],
        compiler_params=limit(LIMITS[4]),
        cost_estimate=cost(34 * 10**9, 8 * 2**20),
        name="attend_back",
    )(ranges, qb, ka, da, va, kt, *waits)


FEED = 512


def feed_kernel(fused, own, mixed, exact, cotangent, query_aux, gains, *refs):
    if fused:
        pieces = fan = 1 << bit_groups(fused[0])[0][1]
        where, mine, other = refs[0], refs[1 : 1 + pieces], refs[1 + pieces : 1 + 2 * pieces]
        refs = refs[1 + 2 * pieces :]
        result, grad_middle, da, gives = *refs[:3], refs[3 : 3 + fan]
        normed_all, low_all, hidden_all, up_all, middle_all, wo, wgu, wd, stage, g_gain, sums = (
            refs[3 + fan : 14 + fan]
        )
        scratch = refs[14 + fan : -1]
        copies = fetch((*mine, *other, own, cotangent), scratch, refs[-1])
        mine, other, (own, cotangent) = (
            scratch[:pieces], scratch[pieces : 2 * pieces], scratch[2 * pieces :]
        )
        arrive(copies)
    else:
        wo, wgu, wd = refs[:3]
        result, grad_middle, da, g_out, g_gate_up, g_down, g_gain = refs[3:10]
        normed_all, low_all, hidden_all, up_all, middle_all = refs[10:]
    gain = gains[1:2, :]
    g_gain[...] = jnp.zeros_like(g_gain)
    if fused:
        unpack(*fused, where, mine, other, stage, wd)
        for i in range(3):
            wo[:, i * LANES : (i + 1) * LANES] = stage[i].astype(bf16)
        for i in range(16):
            wgu[:, i * LANES : (i + 1) * LANES] = stage[3 + i].astype(bf16)

    chunks = FF // BLOCK
    lane = lax.broadcasted_iota(jnp.int32, (FEED, LANES), 1)

    def body(step, carry):
        rows = block(step, FEED)
        x = own[rows, :].astype(f32)
        middle = x + dot(mixed[rows, :], wo[...], NN)
        scale = row_scale(middle)
        normed = (middle * scale * gain).astype(bf16)
        normed_all[rows, :] = normed
        kept = query_aux[rows, :].astype(f32)[:, KEEP_LANE : KEEP_LANE + 1]
        upstream = cotangent[rows, :].astype(f32) * kept
        up_low = upstream.astype(bf16)
        up_all[rows, :] = up_low
        gates = [dot(normed, wgu[:, c * BLOCK : (c + 1) * BLOCK], NN) for c in range(chunks)]
        ups = [dot(normed, wgu[:, FF + c * BLOCK : FF + (c + 1) * BLOCK], NN) for c in range(chunks)]
        hiddens = [dot(up_low, wd[c * BLOCK : (c + 1) * BLOCK, :], NT) for c in range(chunks)]
        for c in range(chunks):
            gate, up, grad_hidden = gates[c], ups[c], hiddens[c]
            sig = 1.0 / (1.0 + jnp.exp(-gate))
            silu = gate * sig
            hidden_all[rows, c * BLOCK : (c + 1) * BLOCK] = (silu * up).astype(bf16)
            low_all[rows, FF + c * BLOCK : FF + (c + 1) * BLOCK] = (grad_hidden * silu).astype(bf16)
            low_all[rows, c * BLOCK : (c + 1) * BLOCK] = (
                grad_hidden * up * (sig + silu * (1.0 - sig))
            ).astype(bf16)
        ffn = dot(hidden_all[rows, :], wd[...], NN)
        grad_normed = dot(low_all[rows, :], wgu[...], NT)
        result[rows, :] = (kept * (middle + ffn)).astype(bf16)
        g_gain[0:1, :] += jnp.sum(grad_normed * middle * scale, axis=0, keepdims=True)
        grad = upstream + norm_back(grad_normed * gain, middle, scale)
        grad_middle[rows, :] = grad
        low = grad.astype(bf16)
        middle_all[rows, :] = low
        grad_mixed = dot(low, wo[...], NT).astype(bf16).astype(f32)
        products = grad_mixed * exact[rows, :]
        for h in range(HEADS):
            pair = h // 2
            head = grad_mixed[:, pair * LANES : (pair + 1) * LANES]
            product = products[:, pair * LANES : (pair + 1) * LANES]
            mine_lanes = (lane < HD) if h % 2 == 0 else (lane >= HD)
            delta = -jnp.sum(jnp.where(mine_lanes, product, 0.0), axis=1, keepdims=True)
            if h % 2:
                head = pltpu.roll(head, HD, 1)
            high, mid, last = split_three(delta)
            extra = jnp.where(
                lane == HD,
                high.astype(f32),
                jnp.where(
                    lane == HD + 1,
                    mid.astype(f32),
                    jnp.where(lane == HD + 2, last.astype(f32), 0.0),
                ),
            )
            da[h, rows, :] = jnp.where(lane < HD, head, extra).astype(bf16)
        return carry

    lax.fori_loop(0, own.shape[0] // FEED, body, 0)
    if not fused:
        g_out[...] = dot(mixed[...], middle_all[...], TN)
        for c in range(2 * FF // 512):
            g_gate_up[:, c * 512 : (c + 1) * 512] = dot(
                normed_all[...], low_all[:, c * 512 : (c + 1) * 512], TN
            )
        for c in range(chunks):
            g_down[c * BLOCK : (c + 1) * BLOCK, :] = dot(
                hidden_all[:, c * BLOCK : (c + 1) * BLOCK], up_all[...], TN
            )
        return
    count, number, shard, down = fused

    def put(at, value):
        for i in range(value.shape[1] // LANES):
            put_slab(sums, 0, number, shard, at + i, value[:, i * LANES : (i + 1) * LANES])

    put(0, dot(mixed[...], middle_all[...], TN))
    for c in range(2 * FF // 512):
        put(3 + 4 * c, dot(normed_all[...], low_all[:, c * 512 : (c + 1) * 512], TN))
    put(19, gain_column(g_gain[...]))
    for c in range(chunks):
        value = dot(hidden_all[:, c * BLOCK : (c + 1) * BLOCK], up_all[...], TN)
        for i in range(3):
            put_down(
                sums, 0, number, shard, down, i,
                value[:, i * LANES : (i + 1) * LANES], c * BLOCK // (2 * down),
            )
    me = where[1] & (fan - 1)
    for high in range(count // fan):
        for flip in range(fan):
            for half in range(2):
                gives[flip][half * (count // fan) + high] = sums[
                    half, high * fan + (me ^ flip)
                ].astype(gives[flip].dtype)


def feed(own, mixed, exact, cotangent, query_aux, gains, weights, fused):
    length = own.shape[0]
    scratch = [
        pltpu.VMEM((length, D), bf16),
        pltpu.VMEM((length, 2 * FF), bf16),
        pltpu.VMEM((length, FF), bf16),
        pltpu.VMEM((length, D), bf16),
        pltpu.VMEM((length, D), bf16),
    ]
    out_shape = [
        jax.ShapeDtypeStruct((length, D), bf16),
        in_vmem((length, D), f32),
        in_vmem((HEADS, length, LANES), bf16),
    ]
    if fused:
        count, number, shard, down = fused
        rows = number * shard + 3 * down
        fan = 1 << bit_groups(count)[0][1]
        weight_specs = [SMEM] + [ANY] * (len(weights) - 1)
        specs = [HBM, VMEM, VMEM, HBM, VMEM, VMEM]
        out_shape += [
            jax.ShapeDtypeStruct((2 * count // fan, rows, LANES), bf16 if flip else f32)
            for flip in range(fan)
        ]
        scratch += [
            pltpu.VMEM((D, D), bf16),
            pltpu.VMEM((D, 2 * FF), bf16),
            pltpu.VMEM((FF, D), bf16),
            pltpu.VMEM((2 * number, D, LANES), f32),
            pltpu.VMEM((8, D), f32),
            pltpu.VMEM((2, count, rows, LANES), f32),
        ]
        scratch += landing([*weights[1:], own, cotangent])
    else:
        weight_specs = [VMEM] * 3
        specs = [VMEM] * 6
        out_shape += [
            jax.ShapeDtypeStruct((D, D), f32),
            jax.ShapeDtypeStruct((D, 2 * FF), f32),
            jax.ShapeDtypeStruct((FF, D), f32),
            jax.ShapeDtypeStruct((8, D), f32),
        ]
    if fused:
        own, cotangent = in_hbm([own, cotangent])
    return pl.pallas_call(
        partial(feed_kernel, fused),
        out_shape=out_shape,
        in_specs=specs + weight_specs,
        out_specs=[VMEM] * len(out_shape),
        scratch_shapes=scratch,
        compiler_params=limit(LIMITS[3]),
        cost_estimate=cost(14 * 10**9, 16 * 2**20),
        name="feed",
    )(own, mixed, exact, cotangent, query_aux, gains, *weights)


PARTS = ((0, 1, 2), (3, 4, 5, 6, 7, 8))


def project_back_kernel(number, fused, own, cosine, sine, w, gains, *refs):
    part = PARTS[number]
    low = lax.broadcasted_iota(jnp.int32, (BLOCK, LANES), 1) < HD
    gain = gains[0:1, :]
    if number == 0:
        dq = refs[0]
        partial_sum, grads, normed_all, low_all = refs[-6:-2]
        copies = fetch((own,), refs[-2:-1], refs[-1])
        own = refs[-2]
    else:
        kept, got, grad_middle, before, grads_before = refs[:5]
        if fused:
            where = refs[5]
            grad_tokens, keep, give, sums, g_gain, normed_all, low_all = refs[-10:-3]
        else:
            grad_tokens, grads, g_gain, normed_all, low_all = refs[-8:-3]
        g_gain[...] = jnp.zeros_like(g_gain)
        copies = fetch((own, got), refs[-3:-1], refs[-1])
        own, got = refs[-3:-1]
    arrive(copies)

    def body(step, carry):
        rows = block(step)
        cos, sin = cosine[rows, :], -sine[rows, :]
        x = own[rows, :].astype(f32)
        scale = row_scale(x)
        normed_all[rows, :] = (x * scale * gain).astype(bf16)
        for at, slab in enumerate(part):
            kind, pair = divmod(slab, 3)
            heads = (2 * pair, 2 * pair + 1)
            if kind == 0:
                z = jnp.concatenate([dq[h, :, rows] for h in heads], axis=0).T * HD**-0.5
            else:
                one, two = [kept[h, rows, :] + got[h, rows, :].astype(f32) for h in heads]
                if kind == 1:
                    z = jnp.where(low, pltpu.roll(one, HD, 1), two)
                else:
                    z = jnp.where(low, one, pltpu.roll(two, HD, 1))
            if kind < 2:
                z = z * cos + swap_halves(z) * sin
            low_all[rows, at * LANES : (at + 1) * LANES] = z.astype(bf16)
        first = part[0] * LANES
        grad_normed = dot(
            low_all[rows, :], w[:, first : first + len(part) * LANES], NT
        )
        if number == 0:
            partial_sum[rows, :] = grad_normed
        else:
            grad_normed = grad_normed + before[rows, :]
            g_gain[0:1, :] += jnp.sum(grad_normed * x * scale, axis=0, keepdims=True)
            grad_tokens[rows, :] = (
                grad_middle[rows, :] + norm_back(grad_normed * gain, x, scale)
            ).astype(bf16)
        return carry

    lax.fori_loop(0, own.shape[0] // BLOCK, body, 0)
    value = dot(normed_all[...], low_all[...], TN)
    if number == 0 or not fused:
        grads[...] = value
        return
    core = where[0]
    for done, source in ((PARTS[0], grads_before), (PARTS[1], value)):
        for at, slab in enumerate(done):
            put_slab(sums, core, *fused, slab, source[:, at * LANES : (at + 1) * LANES])
    put_slab(sums, core, *fused, 9, gain_column(g_gain[...]))
    keep[...] = sums[0]
    give[...] = sums[1].astype(bf16)


def project_back(number, fused, where, shared, arrays, waits):
    own, cosine, sine, w, gains = shared
    length = own.shape[0]
    columns = len(PARTS[number]) * LANES
    scratch = [pltpu.VMEM((length, D), bf16), pltpu.VMEM((length, columns), bf16)]
    specs = [VMEM] * len(arrays)
    if number:
        specs[1] = ANY
    scratch += landing([own] + list(arrays[1:2]))
    if number == 0:
        out_shape = [in_vmem((length, D), f32), in_vmem((D, columns), f32)]
    elif fused:
        size, shard = fused
        chunk = (D // shard, size * shard, LANES)
        specs.append(SMEM)
        arrays = [*arrays, where]
        out_shape = [
            jax.ShapeDtypeStruct((length, D), bf16),
            jax.ShapeDtypeStruct(chunk, f32),
            jax.ShapeDtypeStruct(chunk, bf16),
        ]
        scratch = [pltpu.VMEM((2,) + chunk, f32), pltpu.VMEM((8, D), f32)] + scratch
    else:
        out_shape = [
            jax.ShapeDtypeStruct((length, D), bf16),
            jax.ShapeDtypeStruct((D, columns), f32),
            jax.ShapeDtypeStruct((8, D), f32),
        ]
    (own,) = in_hbm([own])
    return pl.pallas_call(
        partial(project_back_kernel, number, fused),
        out_shape=out_shape,
        in_specs=[HBM] + [VMEM] * 4 + specs + [ANY] * len(waits),
        out_specs=[VMEM] * len(out_shape),
        scratch_shapes=scratch,
        compiler_params=limit(LIMITS[5]),
        cost_estimate=cost(4 * 10**9, 8 * 2**20),
        name="project_back",
    )(own, cosine, sine, w, gains, *arrays, *waits)


def squares_kernel(*refs):
    total = sum(jnp.sum(ref[...] * ref[...]) for ref in refs[0:4:2]) + 0.0
    other = sum(jnp.sum(ref[...] * ref[...]) for ref in refs[1:4:2]) + 0.0
    refs[4][...] = jnp.full((1, LANES), total + other, f32)


def squares(sums):
    spec = pl.BlockSpec(memory_space=pltpu.VMEM)
    return pl.pallas_call(
        squares_kernel,
        out_shape=jax.ShapeDtypeStruct((1, LANES), f32),
        in_specs=[spec] * 4,
        out_specs=spec,
        compiler_params=limit(16),
        name="squares",
    )(*sums)


def bring_kernel(*refs):
    number = (len(refs) - 1) // 2
    arrive(fetch(refs[:number], refs[-number - 1 : -1], refs[-1]))


def bring(arrays):
    return pl.pallas_call(
        bring_kernel,
        out_shape=[in_vmem(item.shape, item.dtype) for item in arrays],
        in_specs=[HBM] * len(arrays),
        out_specs=[VMEM] * len(arrays),
        scratch_shapes=[pltpu.SemaphoreType.DMA((len(arrays),))],
        compiler_params=limit(1),
        name="bring",
    )(*in_hbm(arrays))


def update_kernel(shard, down, where, total, *refs):
    core = where[0]
    chunks = refs[:4]
    norm = refs[19]
    outs = [refs[20 + 5 * i : 25 + 5 * i] for i in range(4)]
    low, high, square = refs[40:]
    masters, firsts, seconds = refs[4:9], refs[9:14], refs[14:19]
    split = 5 * shard

    @pl.when(core == 0)
    def _():
        for i, target in ((0, low), (1, high)):
            target[:split] = chunks[i][...]
            target[split:] = chunks[2 + i][...]

    @pl.when(core == 1)
    def _():
        for i, target in ((0, high), (1, low)):
            target[:split] = chunks[i][...]
            target[split:] = chunks[2 + i][...]

    length = jnp.sqrt(total[0:1, 0:1])
    norm[...] = length
    factor = clip_limit / jnp.maximum(length, clip_limit)
    halves = (low, high)

    def step(which, grad, rows, columns, rate, decay):
        at = (rows, columns)
        new = adam_update(
            masters[which][at], factor * grad, firsts[which][at], seconds[which][at], rate, decay
        )
        outs[0][which][at] = new[0]
        outs[1][which][at] = new[1]
        outs[2][which][at] = new[2]
        outs[3][which][at] = new[2].astype(bf16)

    every = slice(None)
    places = [(0, i, i // 5, (i % 5) * shard) for i in range(9)]
    for i in range(19):
        which, column = (1, i) if i < 3 else (2, i - 3)
        places.append((which, column, i // 10, (5 + i % 10) * shard))
    for which, column, half, row in places:
        rate = 4.0 * D**-0.5 if which == 1 else D**-0.5
        grad = halves[half][row : row + shard, :]
        step(which, grad, every, slice(column * LANES, (column + 1) * LANES), rate, decay_rate)
    for half in range(2):
        for i in range(3):
            row = 15 * shard + i * down
            step(
                3, halves[half][row : row + down, :], slice(half * down, (half + 1) * down),
                slice(i * LANES, (i + 1) * LANES), FF**-0.5, decay_rate,
            )
    gain_rows = []
    for row in (4 * shard, 14 * shard):
        square[...] = jnp.zeros_like(square)
        square[0:shard, :] = high[row : row + shard, :]
        gain_rows.append(square[...].T[0:1, :shard])
    for i in range(2):
        step(4, gain_rows[i], slice(i, i + 1), every, 0.5, 0.0)


def update(where, total, sums, masters, firsts, seconds):
    shard, down = masters[0].shape[0], masters[3].shape[0] // 2
    spec = pl.BlockSpec(memory_space=pltpu.VMEM)
    shapes = [item.shape for item in masters]
    outs = pl.pallas_call(
        partial(update_kernel, shard, down),
        out_shape=[jax.ShapeDtypeStruct((1, 1), f32)]
        + [jax.ShapeDtypeStruct(shape, f32) for _ in range(3) for shape in shapes]
        + [jax.ShapeDtypeStruct(shape, bf16) for shape in shapes],
        in_specs=[pl.BlockSpec(memory_space=pltpu.SMEM)] + [VMEM] * 20,
        out_specs=[spec] * 21,
        scratch_shapes=[
            pltpu.VMEM((15 * shard + 3 * down, LANES), f32),
            pltpu.VMEM((15 * shard + 3 * down, LANES), f32),
            pltpu.VMEM((LANES, LANES), f32),
        ],
        compiler_params=limit(LIMITS[6]),
        name="update",
    )(where, total, *sums, *masters, *firsts, *seconds)
    return outs[0][0, 0], outs[1:6], outs[6:11], outs[11:16], outs[16:21]


def update_plain(core, total, sums, masters, firsts, seconds):
    shard, down = masters[0].shape[0], masters[3].shape[0] // 2
    mine = jnp.concatenate([sums[0], sums[2]])
    there = jnp.concatenate([sums[1], sums[3]])
    low = jnp.where(core == 0, mine, there)
    high = jnp.where(core == 0, there, mine)
    five, fifteen = 5 * shard, 15 * shard
    first_shard = jnp.concatenate([low[:five], high[:five]]).reshape(10, shard, LANES)
    second_shard = jnp.concatenate([low[five:fifteen], high[five:fifteen]])
    second_shard = second_shard.reshape(20, shard, LANES)
    down_shard = jnp.stack(
        [item[fifteen:].reshape(3, down, LANES) for item in (low, high)], axis=1
    ).reshape(3, 2 * down, LANES)
    shard_grads = (
        unslab(first_shard[:9]),
        unslab(second_shard[:3]),
        unslab(second_shard[3:19]),
        unslab(down_shard),
        jnp.stack([first_shard[9, :, 0], second_shard[19, :, 0]]),
    )
    grad_norm = jnp.sqrt(total[0, 0])
    factor = clip_limit / jnp.maximum(grad_norm, clip_limit)
    rates = (D ** (-0.5), 4.0 * D ** (-0.5), D ** (-0.5), FF ** (-0.5), 0.5)
    decays = (decay_rate, decay_rate, decay_rate, decay_rate, 0.0)
    updates = [
        adam_update(
            masters[i], factor * shard_grads[i], firsts[i], seconds[i], rates[i], decays[i]
        )
        for i in range(5)
    ]
    new_first, new_second, new_master = zip(*updates)
    return grad_norm, new_first, new_second, new_master, [item.astype(bf16) for item in new_master]


def per_device(
    count,
    tokens,
    cotangent,
    sample_ids,
    pad_flags,
    offsets,
    w_qkv,
    w_out,
    w_gate_up,
    w_down,
    gains,
    m_qkv,
    m_out,
    m_gate_up,
    m_down,
    m_gains,
    v_qkv,
    v_out,
    v_gate_up,
    v_down,
    v_gains,
):
    owner = lax.axis_index("batch")
    core = lax.axis_index("tm")
    where = jnp.stack([core, owner]).astype(jnp.int32)
    shard = w_qkv.shape[0]
    down = w_down.shape[0] // 2
    own = tokens[0]
    fuse_in = can_unpack(shard, down)
    masters = (w_qkv, w_out, w_gate_up, w_down, gains)

    first = send_chunk(where, FIRST_PLAN, 0, [w_qkv, gains], [])
    there = swap_tm(own)
    cosine, sine, key_aux, query_aux, ranges = tables(
        where, sample_ids, pad_flags, offsets, [there]
    )
    first_held, first_pieces = gather(first, count, [query_aux])
    second = send_chunk(where, SECOND_PLAN, down, [w_out, w_gate_up, w_down], [first_held])

    def gathered(pieces, number, down):
        others = [swap_tm(piece) for piece in pieces]
        if fuse_in:
            return (where, *pieces, *others), (count, number, shard, down)
        return unpack_plain(count, number, shard, down, where, pieces, others), None

    weights, fused = gathered(first_pieces, 5, 0)
    qa, ka, va, kt, vt, attn_in, gain_pair = project(
        own, there, cosine, sine, key_aux, query_aux, weights, fused, []
    )
    second_held, second_pieces = gather(second, count, [gain_pair])
    mixed, exact, qb = attend(ranges, qa, ka, vt, [second_held])
    second_pieces[1:] = hold(second_pieces[1:], [mixed])
    weights, fused = gathered(second_pieces, 10, down)
    result, grad_middle, da, *grads = feed(
        own, mixed, exact, cotangent[0], query_aux, gain_pair, weights, fused
    )
    groups = bit_groups(count)
    fan = 1 << groups[0][1]

    def flips(halves):
        halves = halves.reshape((-1, fan) + halves.shape[-2:])
        mine = owner & (fan - 1)
        parts = [lax.dynamic_index_in_dim(halves, mine ^ k, 1, keepdims=False) for k in range(fan)]
        return [parts[0]] + [item.astype(bf16) for item in parts[1:]]

    if not fused:
        grads = flips(pack_plain(count, core, grads, 10, shard, down))
    got = [permute_batch(grads[k], k, count) for k in range(1, fan)]
    dq, kept, part = attend_back(ranges, qb, ka, da, va, kt, [])
    fused = (5, shard) if fuse_in else None
    shared = (own, cosine, sine, attn_in, gain_pair)
    before, grads_before = project_back(0, fused, where, shared, [dq], [])
    got = hold(got, [grads_before])
    part_there = swap_tm(hold([part], got)[0])
    left = count // fan
    keep, give = combine(where, [grads[0], *got], (1, 2, left, 0, 0))
    split = None
    if len(groups) > 1:
        split = (left >> groups[1][1], 1 << groups[1][1], 1, 1, groups[1][0])
    parts = combine(where, [keep, swap_tm(give)], split)
    grad_tokens, *grads = project_back(
        1, fused, where, shared, [kept, part_there, grad_middle, before, grads_before], [parts[0]]
    )
    if split:
        parts = [scatter_parts(where, parts, count, groups[1:], [grad_tokens])]
    second_sum = parts[0].reshape(-1, LANES)
    if fused:
        kept, given = grads
    else:
        grads = [jnp.concatenate([grads_before, grads[0]], axis=1), grads[1]]
        halves = pack_plain(count, core, grads, 5, shard, 0)
        kept = jnp.where(core == 0, halves[0], halves[1])
        given = jnp.where(core == 0, halves[1], halves[0]).astype(bf16)
    (given,) = hold([given], [second_sum])
    firsts = (m_qkv, m_out, m_gate_up, m_down, m_gains)
    seconds = (v_qkv, v_out, v_gate_up, v_down, v_gains)
    waits = []
    if fuse_in:
        brought = bring([*masters, *firsts, *seconds])
        masters, firsts, seconds = brought[:5], brought[5:10], brought[10:]
        waits = brought[:1]
    parts = combine(where, [kept, swap_tm(given)], (left, fan, 1, 1, 0), waits)
    first_sum = scatter_parts(where, parts, count, groups).reshape(-1, LANES)
    sums = (first_sum, swap_tm(first_sum), second_sum, swap_tm(second_sum))
    total = sum_batch(squares(sums), count)
    if fuse_in:
        updates = update(where, total, sums, masters, firsts, seconds)
    else:
        updates = update_plain(core, total, sums, masters, firsts, seconds)
    grad_norm, new_first, new_second, new_master, copies = updates
    return (
        result[None],
        grad_tokens[None],
        grad_norm,
        *new_first,
        *new_second,
        *new_master,
        *copies,
    )


def solution(mesh):
    in_specs = (
        P("batch", "tm", None),
        P("batch", "tm", None),
        P("batch", None),
        P("batch", None),
        P("batch", None),
        P("batch", None),
        P("batch", None),
        P("batch", None),
        P("batch", None),
        P(None, "batch"),
        P("batch", None),
        P("batch", None),
        P("batch", None),
        P("batch", None),
        P(None, "batch"),
        P("batch", None),
        P("batch", None),
        P("batch", None),
        P("batch", None),
        P(None, "batch"),
    )
    out_specs = (
        P("batch", "tm", None),
        P("batch", "tm", None),
        P(),
        P("batch", None),
        P("batch", None),
        P("batch", None),
        P("batch", None),
        P(None, "batch"),
        P("batch", None),
        P("batch", None),
        P("batch", None),
        P("batch", None),
        P(None, "batch"),
        P("batch", None),
        P("batch", None),
        P("batch", None),
        P("batch", None),
        P(None, "batch"),
        P("batch", None),
        P("batch", None),
        P("batch", None),
        P("batch", None),
        P(None, "batch"),
    )
    return jax.shard_map(
        partial(per_device, mesh.shape["batch"]), mesh=mesh, in_specs=in_specs, out_specs=out_specs, check_vma=False
    )
```

```python
import math
from functools import partial

import jax
import jax.numpy as jnp
from jax import lax
from jax.experimental import pallas as pl
from jax.experimental.pallas import tpu as pltpu
from jax.sharding import PartitionSpec as P

D = 384
FF = 1024
HEADS = 6
HD = 64
STEP = 3


norm_eps = 1e-06
beta_one = 0.5
beta_two = 0.5
adam_eps = 1e-08
decay_rate = 0.1
clip_limit = 1.0
masked_score = -1e30


def adam_update(master, grad, first, second, rate, decay):
    first_new = beta_one * first + (1.0 - beta_one) * grad
    second_new = beta_two * second + (1.0 - beta_two) * grad * grad
    direction = (
        first_new
        / (1.0 - beta_one**STEP)
        / (jnp.sqrt(second_new / (1.0 - beta_two**STEP)) + adam_eps)
    )
    return (first_new, second_new, master - rate * (direction + decay * master))


def bit_groups(count):
    groups = []
    low, bits = 0, count.bit_length() - 1
    while low < bits:
        width = min(2, bits - low)
        groups.append((low, width))
        low += width
    return groups


def permute_batch(value, flip, count):
    return lax.ppermute(value, "batch", [(i, i ^ flip) for i in range(count)])


def swap_tm(value):
    return lax.ppermute(value, "tm", [(0, 1), (1, 0)])


def slabs(matrix):
    rows, columns = matrix.shape
    return matrix.reshape(rows, columns // 128, 128).transpose(1, 0, 2)


def unslab(stack):
    count, rows, _ = stack.shape
    return stack.transpose(1, 0, 2).reshape(rows, count * 128)


bf16 = jnp.bfloat16
f32 = jnp.float32
BLOCK = 256
LANES = 128
KEEP_LANE = 96
LIMITS = (12, 20, 12, 38, 12, 20, 12)
WIDE = 512
NN = (((1,), (0,)), ((), ()))
NT = (((1,), (1,)), ((), ()))
TN = (((0,), (0,)), ((), ()))


def dot(left, right, dims):
    return lax.dot_general(left, right, dims, preferred_element_type=f32)


def cost(flops, moved):
    return pl.CostEstimate(flops=flops, bytes_accessed=moved, transcendentals=0)


def in_vmem(shape, dtype):
    return pltpu.VMEM(tuple(shape), dtype)


VMEM = pl.BlockSpec(memory_space=pltpu.VMEM)
SMEM = pl.BlockSpec(memory_space=pltpu.SMEM)
ANY = pl.BlockSpec(memory_space=pl.ANY)
HBM = pl.BlockSpec(memory_space=pltpu.HBM)


def fetch(sources, targets, semaphores):
    copies = [
        pltpu.make_async_copy(source, target, semaphores.at[i])
        for i, (source, target) in enumerate(zip(sources, targets))
    ]
    for copy in copies:
        copy.start()
    return copies


def landing(arrays):
    return [pltpu.VMEM(item.shape, item.dtype) for item in arrays] + [
        pltpu.SemaphoreType.DMA((len(arrays),))
    ]


def arrive(copies):
    for copy in copies:
        copy.wait()


def limit(mebibytes):
    return pltpu.CompilerParams(vmem_limit_bytes=mebibytes * 2**20)


def block(start, size=BLOCK):
    return pl.ds(pl.multiple_of(start * size, size), size)


def sum_batch(value, count):
    value = jnp.broadcast_to(value[:, None], (count, 1, LANES))
    value = lax.all_to_all(value, "batch", 0, 0, tiled=True)
    return jnp.sum(value, axis=0)


def row_scale(values):
    return lax.rsqrt(jnp.mean(values * values, axis=-1, keepdims=True) + norm_eps)


def norm_back(grad_normed, values, scale):
    return scale * grad_normed - values * scale * scale * scale * jnp.mean(
        grad_normed * values, axis=-1, keepdims=True
    )


def split_three(values):
    high = values.astype(bf16)
    rest = values - high.astype(f32)
    middle = rest.astype(bf16)
    return high, middle, (rest - middle.astype(f32)).astype(bf16)


def swap_halves(pair):
    lane = lax.broadcasted_iota(jnp.int32, pair.shape, 1)
    return jnp.where(lane % HD < HD // 2, pltpu.roll(pair, 96, 1), pltpu.roll(pair, 32, 1))


def relative_place(device, owner, count):
    flips = device ^ owner
    place, scale = 0, 1
    for low, width in reversed(bit_groups(count)):
        place = place + ((flips >> low) & ((1 << width) - 1)) * scale
        scale <<= width
    return place


def exchange_all(held, low, width, count):
    return [held] + [permute_batch(held, k << low, count) for k in range(1, 1 << width)]


def in_hbm(arrays):
    return [pltpu.with_memory_space_constraint(item, pltpu.HBM) for item in arrays]


def join_kernel(number, *refs):
    out = refs[-1]
    size = refs[0].shape[0]
    for i in range(number):
        out[i * size : (i + 1) * size] = refs[i][...]


def join(pieces, waits=()):
    first = pieces[0]
    shape = (len(pieces) * first.shape[0],) + first.shape[1:]
    return pl.pallas_call(
        partial(join_kernel, len(pieces)),
        out_shape=jax.ShapeDtypeStruct(shape, first.dtype),
        in_specs=[VMEM] * len(pieces) + [ANY] * len(waits),
        out_specs=VMEM,
        compiler_params=limit(4),
        name="join",
    )(*pieces, *waits)


def combine_kernel(number, split, where, *refs):
    items, outs = refs[:number], refs[-len(refs) + number :]
    outs = outs[-(split[1] if split else 1) :]

    def total(index):
        return sum(item[index].astype(f32) for item in items[1:]) + items[0][index].astype(f32)

    if not split:
        outs[0][...] = total(slice(None))
        return
    upper, fan, lower, which, low = split
    mine = (where[which] >> low) & (fan - 1)
    for a in range(upper):
        for b in range(lower):
            for flip in range(fan):
                index = (a * fan + (mine ^ flip)) * lower + b
                outs[flip][a * lower + b] = total(index).astype(outs[flip].dtype)


def combine(where, items, split, waits=()):
    count, rows, _ = items[0].shape
    if split:
        fan = split[1]
        shapes = [
            jax.ShapeDtypeStruct((count // fan, rows, LANES), bf16 if flip else f32)
            for flip in range(fan)
        ]
    else:
        shapes = [jax.ShapeDtypeStruct((count, rows, LANES), f32)]
    return pl.pallas_call(
        partial(combine_kernel, len(items), split),
        out_shape=shapes,
        in_specs=[SMEM] + [VMEM] * len(items) + [ANY] * len(waits),
        out_specs=[VMEM] * len(shapes),
        compiler_params=limit(12),
        name="combine",
    )(where, *items, *waits)


def scatter_parts(where, parts, count, groups, waits=None):
    for n, (low, width) in enumerate(groups):
        got = [permute_batch(item, k << low, count) for k, item in enumerate(parts) if k]
        if waits and n == 0:
            got = hold(got, waits)
        split = None
        if n + 1 < len(groups):
            fan = 1 << groups[n + 1][1]
            split = (parts[0].shape[0] // fan, fan, 1, 1, groups[n + 1][0])
        parts = combine(where, [parts[0], *got], split)
    return parts[0]


def hold(values, waits):
    spec = pl.BlockSpec(memory_space=pl.ANY)
    number = len(values)
    return pl.pallas_call(
        lambda *refs: None,
        out_shape=[jax.ShapeDtypeStruct(item.shape, item.dtype) for item in values],
        in_specs=[spec] * (number + len(waits)),
        out_specs=[spec] * number,
        input_output_aliases={i: i for i in range(number)},
        compiler_params=limit(1),
        name="hold",
    )(*values, *waits)


def send_kernel(shard, plan, down, where, *refs):
    number = (len(refs) - 4) // 2
    target, stage, square = refs[number : number + 3]
    sources = refs[number + 3 : -1]
    arrive(fetch(refs[:number], sources, refs[-1]))
    number = len(plan) // 2
    core = where[0]
    stage[...] = jnp.zeros_like(stage)
    gain_at = [i for i, item in enumerate(plan) if item == "gain"]
    if gain_at:
        square[...] = jnp.zeros_like(square)
        square[0:2, 0:shard] = sources[-1][...]
        column = square[...].T

    def fill(half):
        for i in range(number):
            item = plan[half * number + i]
            rows = slice(i * shard, (i + 1) * shard)
            if item == "gain":
                stage[rows, :] = column[:shard]
            elif item is not None:
                which, at = item
                stage[rows, :] = sources[which][:, at * LANES : (at + 1) * LANES]
        for i in range(3 if down else 0):
            start = number * shard + i * down
            stage[start : start + down, :] = sources[2][
                half * down : (half + 1) * down, i * LANES : (i + 1) * LANES
            ]

    @pl.when(core == 0)
    def _():
        fill(0)

    @pl.when(core == 1)
    def _():
        fill(1)

    target[...] = stage[...].astype(bf16)


def send_chunk(where, plan, down, sources, waits):
    shard = sources[0].shape[0]
    rows = len(plan) // 2 * shard + 3 * down
    rows = -(-rows // 16) * 16
    core = where[0]
    if shard % 8 == 0 and down % 8 == 0:
        spec = VMEM

        def kernel(where, *refs):
            kept = refs[: len(sources)] + refs[len(sources) + len(waits) :]
            send_kernel(shard, plan, down, where, *kept)

        return pl.pallas_call(
            kernel,
            out_shape=jax.ShapeDtypeStruct((rows, LANES), bf16),
            in_specs=[SMEM] + [HBM] * len(sources) + [ANY] * len(waits),
            out_specs=spec,
            scratch_shapes=[pltpu.VMEM((rows, LANES), f32), pltpu.VMEM((LANES, LANES), f32)]
            + landing(sources),
            compiler_params=limit(6),
            name="send_chunk",
        )(where, *in_hbm(sources), *waits)
    stacks = {i: slabs(item) for i, item in enumerate(sources) if item.shape[1] % LANES == 0}
    pieces = []
    for item in plan:
        if item == "gain":
            pieces.append(jnp.pad(sources[-1].T, ((0, 0), (0, LANES - 2))))
        elif item is None:
            pieces.append(jnp.zeros((shard, LANES), f32))
        else:
            pieces.append(stacks[item[0]][item[1]])
    half = len(plan) // 2
    halves = [jnp.concatenate(pieces[:half]), jnp.concatenate(pieces[half:])]
    if down:
        for i in range(2):
            part = stacks[2][:, i * down : (i + 1) * down].reshape(3 * down, LANES)
            halves[i] = jnp.concatenate([halves[i], part])
    chunk = jnp.where(core == 0, halves[0], halves[1]).astype(bf16)
    return jnp.pad(chunk, ((0, rows - chunk.shape[0]), (0, 0)))


FIRST_PLAN = tuple((0, i) for i in range(9)) + ("gain",)
SECOND_PLAN = tuple((0, i) for i in range(3)) + tuple((1, i) for i in range(16)) + (None,)


def gather(chunk, count, waits):
    held = chunk[None]
    groups = bit_groups(count)[::-1]
    for n, (low, width) in enumerate(groups):
        pieces = exchange_all(held, low, width, count)
        if n + 1 < len(groups):
            held = join(pieces, () if n else waits)
    return held, pieces


def unpack(count, number, shard, down, where, pieces, others, stage, w_down):
    core, owner = where[0], where[1]
    last = bit_groups(count)[0][1]
    for sources, half in ((pieces, core), (others, 1 - core)):
        for flip, source in enumerate(sources):

            def one(n, carry, source=source, half=half, flip=flip):
                device = owner ^ flip ^ (relative_flips(n, count) << last)
                chunk = source[n].astype(f32)
                for i in range(number):
                    start = (half * number + i) * D + device * shard
                    stage[pl.ds(pl.multiple_of(start, 8), shard), :] = chunk[
                        i * shard : (i + 1) * shard
                    ]
                for i in range(3 if down else 0):
                    start = number * shard + i * down
                    rows = pl.ds(pl.multiple_of((device * 2 + half) * down, 16), down)
                    w_down[rows, i * LANES : (i + 1) * LANES] = chunk[start : start + down].astype(
                        bf16
                    )
                return carry

            lax.fori_loop(0, source.shape[0], one, 0, unroll=True)


def relative_flips(place, count):
    last = bit_groups(count)[0][1]
    flips, scale = 0, 1
    for low, width in reversed(bit_groups(count)[1:]):
        flips = flips + (((place // scale) & ((1 << width) - 1)) << (low - last))
        scale <<= width
    return flips


def can_unpack(shard, down):
    return shard % 8 == 0 and down % 16 == 0


def unpack_plain(count, number, shard, down, where, mine, other):
    core, owner = where[0], where[1]
    places = relative_place(jnp.arange(count, dtype=jnp.int32), owner, count)
    mine, other = jnp.concatenate(mine), jnp.concatenate(other)
    low = jnp.take(jnp.where(core == 0, mine, other), places, axis=0)
    high = jnp.take(jnp.where(core == 0, other, mine), places, axis=0)

    def part(source):
        return (
            source[:, : number * shard]
            .reshape(count, number, shard, LANES)
            .transpose(1, 0, 2, 3)
            .reshape(number, D, LANES)
        )

    stack = jnp.concatenate([part(low), part(high)], axis=0)
    if number == 5:
        return unslab(stack[:9]), stack[9].T[:8].astype(f32)
    downs = [
        item[:, number * shard : number * shard + 3 * down].reshape(count, 3, down, LANES)
        for item in (low, high)
    ]
    w_down = jnp.stack(downs, axis=1).transpose(0, 1, 3, 2, 4).reshape(FF, D)
    return unslab(stack[:3]), unslab(stack[3:19]), w_down


def put_slab(stage, core, number, shard, at, slab):
    half, row = at // number, (at % number) * shard
    slot = core if half == 0 else 1 - core
    stage[slot, :, row : row + shard, :] = slab.reshape(-1, shard, LANES)


def gain_column(row):
    return jnp.concatenate([row, jnp.zeros((LANES - 8, D), f32)], axis=0).T


def pack_plain(count, core, grads, number, shard, down):
    column = jnp.pad(grads[-1][:1].T, ((0, 0), (0, LANES - 1)))[None]
    stack = jnp.concatenate([slabs(item) for item in (grads[:2] if down else grads[:1])] + [column])

    def by_device(part):
        return (
            part.reshape(number, count, shard, LANES)
            .transpose(1, 0, 2, 3)
            .reshape(count, number * shard, LANES)
        )

    halves = [by_device(stack[:number]), by_device(stack[number:])]
    if down:
        downs = (
            slabs(grads[2])
            .reshape(3, count, 2, down, LANES)
            .transpose(2, 1, 0, 3, 4)
            .reshape(2, count, 3 * down, LANES)
        )
        halves = [jnp.concatenate([halves[i], downs[i]], axis=1) for i in range(2)]
    return jnp.stack(halves)


def tables_kernel(length, where, ids, pads, offsets, *refs):
    cosine, sine, key_aux, query_aux, ranges = refs[-5:]
    core = where[0]
    whole = 2 * length

    def turn(row):
        low, high = row[:, :length], row[:, length:]
        return jnp.concatenate(
            [jnp.where(core == 0, low, high), jnp.where(core == 0, high, low)], axis=1
        )

    classes = (2 * ids[...] + pads[...]).astype(f32)
    spot = lax.broadcasted_iota(jnp.int32, (1, whole), 1)
    position = (turn(spot) + turn(offsets[...])).astype(f32)
    turned = turn(classes)
    index = lax.broadcasted_iota(jnp.int32, (HD // 2, whole), 0).astype(f32)
    angle = position * jnp.exp(index * (-2.0 * math.log(10000.0) / HD))
    cos, sin = jnp.cos(angle), jnp.sin(angle)
    cosine[...] = jnp.concatenate([cos, cos, cos, cos], axis=0).T
    sine[...] = jnp.concatenate([-sin, sin, -sin, sin], axis=0).T
    at = lax.broadcasted_iota(jnp.int32, (LANES, whole), 0)
    is_class = (at >= HD) & (at < HD + 8)
    same = (at - HD).astype(f32) == turned
    is_log = (at >= HD + 8) & (at < HD + 8 + 3 * HEADS)
    key_aux[...] = jnp.where((is_class & same) | is_log, 1.0, 0.0).T.astype(bf16)
    own = turned[:, :length]
    kept = jnp.where(turn(pads[...])[:, :length] == 0, 1.0, 0.0)
    extra = jnp.where(is_class & ~same, masked_score, 0.0)[:, :length]
    query_aux[...] = jnp.where(at[:, :length] == KEEP_LANE, kept, extra).T.astype(bf16)
    starts = (core * length, (1 - core) * length)
    for n in range(length // BLOCK):
        mine = own[:, n * BLOCK : (n + 1) * BLOCK]
        first = jnp.min(mine)
        last = jnp.max(mine)
        low_key = jnp.sum(jnp.where(classes < first, 1.0, 0.0)).astype(jnp.int32)
        high_key = jnp.sum(jnp.where(classes <= last, 1.0, 0.0)).astype(jnp.int32)
        bounds = []
        for start in starts:
            low_part = jnp.clip(low_key - start, 0, length)
            high_part = jnp.clip(high_key - start, 0, length)
            low_block = low_part // BLOCK
            bounds.append((low_block, jnp.maximum((high_part + BLOCK - 1) // BLOCK - low_block, 0)))
        ranges[0, n] = bounds[0][0]
        ranges[1, n] = bounds[0][1]
        ranges[2, n] = bounds[1][0] + length // BLOCK - bounds[0][1]
        ranges[3, n] = bounds[0][1] + bounds[1][1]


def tables(where, ids, pads, offsets, waits):
    whole = ids.shape[1]
    length = whole // 2
    spec = pl.BlockSpec(memory_space=pltpu.VMEM)
    smem = pl.BlockSpec(memory_space=pltpu.SMEM)
    return pl.pallas_call(
        partial(tables_kernel, length),
        out_shape=[
            in_vmem((whole, LANES), f32),
            in_vmem((whole, LANES), f32),
            in_vmem((whole, LANES), bf16),
            in_vmem((length, LANES), bf16),
            jax.ShapeDtypeStruct((4, length // BLOCK), jnp.int32),
        ],
        in_specs=[smem, spec, spec, spec] + [pl.BlockSpec(memory_space=pl.ANY)] * len(waits),
        out_specs=[spec] * 4 + [smem],
        compiler_params=limit(LIMITS[0]),
        cost_estimate=cost(3 * 10**9, 4 * 2**20),
        name="tables",
    )(where, ids, pads, offsets, *waits)


def project_kernel(fused, own, there, cosine, sine, key_aux, query_aux, *refs):
    if fused:
        pieces = 1 << bit_groups(fused[0])[0][1]
        where, mine, other = refs[0], refs[1 : 1 + pieces], refs[1 + pieces : 1 + 2 * pieces]
        qa, ka, va, kt, vt, w, gains, stage = refs[-11:-3]
        copies = fetch((own, there), refs[-3:-1], refs[-1])
        own, there = refs[-3:-1]
        unpack(*fused, where, mine, other, stage, None)
        for i in range(9):
            w[:, i * LANES : (i + 1) * LANES] = stage[i * D : (i + 1) * D].astype(bf16)
        gains[...] = stage[9 * D : 10 * D].T[:8]
        arrive(copies)
    else:
        w_in, gains_in, (qa, ka, va, kt, vt, w, gains) = *refs[:2], refs[-7:]
        w[...] = w_in[...]
        gains[...] = gains_in[...]
    low = lax.broadcasted_iota(jnp.int32, (WIDE, LANES), 1) < HD
    lane = lax.broadcasted_iota(jnp.int32, (WIDE, LANES), 1)
    value_extra = jnp.where((lane >= HD) & (lane < HD + 3), 1.0, 0.0)
    ones = jnp.ones((8, WIDE), bf16)
    blocks = own.shape[0] // WIDE

    def body(step, carry, source, base):
        rows, keys = block(step, WIDE), block(base + step, WIDE)
        x = source[rows, :].astype(f32)
        normed = (x * row_scale(x) * gains[0:1, :]).astype(bf16)
        cos, sin = cosine[keys, :], sine[keys, :]
        first = 0 if base == 0 else D
        products = dot(normed, w[:, first:], NN)
        products = [
            products[:, i * LANES - first : (i + 1) * LANES - first]
            for i in range(first // LANES, 9)
        ]
        if base == 0:
            query_extra = query_aux[rows, :].astype(f32)
            for pair in range(HEADS // 2):
                z = products[pair]
                z = (z * cos + swap_halves(z) * sin).astype(bf16).astype(f32) * HD**-0.5
                qa[2 * pair, rows, :] = jnp.where(low, z, query_extra).astype(bf16)
                qa[2 * pair + 1, rows, :] = jnp.where(
                    low, pltpu.roll(z, HD, 1), query_extra
                ).astype(bf16)
        key_extra = key_aux[keys, :].astype(f32)
        for pair in range(HEADS // 2):
            z = products[pair - 6]
            z = z * cos + swap_halves(z) * sin
            ka[2 * pair, keys, :] = jnp.where(low, z, key_extra).astype(bf16)
            ka[2 * pair + 1, keys, :] = jnp.where(
                low, pltpu.roll(z, HD, 1), key_extra
            ).astype(bf16)
            turned = z.T.astype(bf16)
            kt[2 * pair, :, keys] = turned[:HD]
            kt[2 * pair + 1, :, keys] = turned[HD:]
        for pair in range(HEADS // 2):
            z = products[pair - 3]
            va[2 * pair, keys, :] = jnp.where(low, z, value_extra).astype(bf16)
            va[2 * pair + 1, keys, :] = jnp.where(
                low, pltpu.roll(z, HD, 1), value_extra
            ).astype(bf16)
            turned = z.T.astype(bf16)
            for i in range(2):
                vt[2 * pair + i, :HD, keys] = turned[i * HD : (i + 1) * HD]
                vt[2 * pair + i, HD:, keys] = ones
        return carry

    lax.fori_loop(0, blocks, partial(body, source=own, base=0), 0)
    lax.fori_loop(0, blocks, partial(body, source=there, base=blocks), 0)


def project(own, there, cosine, sine, key_aux, query_aux, weights, fused, waits):
    length = own.shape[0]
    whole = 2 * length
    scratch, specs = [], [VMEM] * 6
    weight_specs = [VMEM] * 2
    if fused:
        specs = [HBM, ANY] + [VMEM] * 4
        weight_specs = [SMEM] + [VMEM] * (len(weights) - 1)
        scratch = [pltpu.VMEM((10 * D, LANES), f32)] + landing([own, there])
    if fused:
        (own,) = in_hbm([own])
    return pl.pallas_call(
        partial(project_kernel, fused),
        out_shape=[
            in_vmem((HEADS, length, LANES), bf16),
            in_vmem((HEADS, whole, LANES), bf16),
            in_vmem((HEADS, whole, LANES), bf16),
            in_vmem((HEADS, HD, whole), bf16),
            in_vmem((HEADS, HD + 8, whole), bf16),
            in_vmem((D, 3 * D), bf16),
            in_vmem((8, D), f32),
        ],
        in_specs=specs + weight_specs + [ANY] * len(waits),
        out_specs=[VMEM] * 7,
        scratch_shapes=scratch,
        compiler_params=limit(LIMITS[1]),
        cost_estimate=cost(9 * 10**9, 16 * 2**20),
        name="project",
    )(own, there, cosine, sine, key_aux, query_aux, *weights, *waits)


def key_block(ranges, step, n):
    return jnp.where(n < ranges[1, step], ranges[0, step] + n, ranges[2, step] + n)


def attend_kernel(ranges, qa, ka, vt, *refs):
    mixed, exact, qb, total, peak = refs[-5:]
    lane = lax.broadcasted_iota(jnp.int32, (BLOCK, LANES), 1)

    def one(step, carry):
        queries = block(step)
        peak[...] = jnp.full((HEADS, 8, BLOCK), -3e38, f32)
        total[...] = jnp.zeros_like(total)

        def body(n, carry):
            rows = block(key_block(ranges, step, n))
            scores = [dot(ka[h, rows, :], qa[h, queries, :], NT) for h in range(HEADS)]
            weights = []
            for h in range(HEADS):
                old = peak[h][:1]
                new = jnp.maximum(old, jnp.max(scores[h], axis=0, keepdims=True))
                weights.append((jnp.exp(scores[h] - new).astype(bf16), jnp.exp(old - new)))
                peak[h] = jnp.broadcast_to(new, (8, BLOCK))
            for h in range(HEADS):
                weight, shrink = weights[h]
                total[h] = total[h] * shrink + dot(vt[h, :, rows], weight, NN)
            return carry

        lax.fori_loop(0, ranges[3, step], body, 0)
        means, pieces = [], []
        for h in range(HEADS):
            bottom = total[h][HD : HD + 1]
            means.append(total[h][:HD] / bottom)
            logs = -(peak[h][:1] + jnp.log(bottom))
            pieces.extend(piece.astype(f32) for piece in split_three(logs))
        for pair in range(HEADS // 2):
            both = jnp.concatenate(means[2 * pair : 2 * pair + 2], axis=0).T
            mixed[queries, pair * LANES : (pair + 1) * LANES] = both.astype(bf16)
            exact[queries, pair * LANES : (pair + 1) * LANES] = both
        table = jnp.concatenate(
            [jnp.zeros((HD + 8, BLOCK), f32)]
            + pieces
            + [jnp.zeros((LANES - HD - 8 - 3 * HEADS, BLOCK), f32)],
            axis=0,
        ).T
        for h in range(HEADS):
            start = HD + 8 + 3 * h
            qb[h, queries, :] = jnp.where(
                (lane >= start) & (lane < start + 3), table, qa[h, queries, :].astype(f32)
            ).astype(bf16)
        return carry

    lax.fori_loop(0, qa.shape[1] // BLOCK, one, 0)


def attend(ranges, qa, ka, vt, waits):
    heads, length, _ = qa.shape
    return pl.pallas_call(
        attend_kernel,
        out_shape=[
            in_vmem((length, D), bf16),
            in_vmem((length, D), f32),
            in_vmem(qa.shape, bf16),
        ],
        in_specs=[SMEM] + [VMEM] * 3 + [ANY] * len(waits),
        out_specs=[VMEM] * 3,
        scratch_shapes=[
            pltpu.VMEM((heads, HD + 8, BLOCK), f32),
            pltpu.VMEM((heads, 8, BLOCK), f32),
        ],
        compiler_params=limit(LIMITS[2]),
        cost_estimate=cost(18 * 10**9, 12 * 2**20),
        name="attend",
    )(ranges, qa, ka, vt, *waits)


def attend_back_kernel(ranges, qb, ka, da, va, kt, *refs):
    dq, sums, there, acc = refs[-4:]
    sums[...] = jnp.zeros_like(sums)
    zero = jnp.zeros((BLOCK, HD), bf16)

    def one(step, carry):
        queries = block(step)
        acc[...] = jnp.zeros_like(acc)

        def body(n, carry):
            rows = block(key_block(ranges, step, n))
            first = [
                (
                    dot(ka[h, rows, :], qb[h, queries, :], NT),
                    dot(va[h, rows, :], da[h, queries, :], NT),
                )
                for h in range(HEADS)
            ]
            second = []
            for scores, grads in first:
                probs = jnp.exp(scores)
                second.append((probs.astype(bf16), (probs * grads).astype(bf16)))
            for h in range(HEADS):
                probs_low, grads_low = second[h]
                grad_side = jnp.concatenate([da[h, queries, :HD], zero], axis=1)
                query_side = jnp.concatenate([zero, qb[h, queries, :HD]], axis=1)
                sums[h, rows, :] += dot(probs_low, grad_side, NN) + dot(grads_low, query_side, NN)
                acc[h] += dot(kt[h, :, rows], grads_low, NN)
            return carry

        lax.fori_loop(0, ranges[3, step], body, 0)
        for h in range(HEADS):
            dq[h, :, queries] = acc[h]
        return carry

    length = qb.shape[1]
    lax.fori_loop(0, length // BLOCK, one, 0)
    there[...] = sums[:, length:, :].astype(bf16)


def attend_back(ranges, qb, ka, da, va, kt, waits):
    heads, length, _ = qb.shape
    whole = ka.shape[1]
    return pl.pallas_call(
        attend_back_kernel,
        out_shape=[
            in_vmem((heads, HD, length), f32),
            in_vmem((heads, whole, LANES), f32),
            jax.ShapeDtypeStruct((heads, whole - length, LANES), bf16),
        ],
        in_specs=[SMEM] + [VMEM] * 5 + [ANY] * len(waits),
        out_specs=[VMEM] * 3,
        scratch_shapes=[pltpu.VMEM((heads, HD, BLOCK), f32)],
        compiler_params=limit(LIMITS[4]),
        cost_estimate=cost(34 * 10**9, 8 * 2**20),
        name="attend_back",
    )(ranges, qb, ka, da, va, kt, *waits)


FEED = 1024


def feed_kernel(fused, own, mixed, exact, cotangent, query_aux, gains, *refs):
    if fused:
        pieces = fan = 1 << bit_groups(fused[0])[0][1]
        where, mine, other = refs[0], refs[1 : 1 + pieces], refs[1 + pieces : 1 + 2 * pieces]
        refs = refs[1 + 2 * pieces :]
        result, grad_middle, da, gives = *refs[:3], refs[3 : 3 + fan]
        normed_all, low_all, hidden_all, up_all, middle_all, wo, wgu, wd, g_gain, sums = refs[
            3 + fan : 13 + fan
        ]
        copies = fetch((own, cotangent), refs[13 + fan : 15 + fan], refs[-1])
        own, cotangent = refs[13 + fan : 15 + fan]
    else:
        wo, wgu, wd = refs[:3]
        result, grad_middle, da, g_out, g_gate_up, g_down, g_gain = refs[3:10]
        normed_all, low_all, hidden_all, up_all, middle_all = refs[10:]
    gain = gains[1:2, :]
    g_gain[...] = jnp.zeros_like(g_gain)
    if fused:
        unpack(*fused, where, mine, other, sums, wd)
        for i in range(3):
            wo[:, i * LANES : (i + 1) * LANES] = sums[i * D : (i + 1) * D].astype(bf16)
        for i in range(16):
            wgu[:, i * LANES : (i + 1) * LANES] = sums[(3 + i) * D : (4 + i) * D].astype(bf16)
        arrive(copies)

    chunks = FF // BLOCK
    lane = lax.broadcasted_iota(jnp.int32, (FEED, LANES), 1)

    def body(step, carry):
        rows = block(step, FEED)
        x = own[rows, :].astype(f32)
        middle = x + dot(mixed[rows, :], wo[...], NN)
        scale = row_scale(middle)
        normed = (middle * scale * gain).astype(bf16)
        normed_all[rows, :] = normed
        kept = query_aux[rows, :].astype(f32)[:, KEEP_LANE : KEEP_LANE + 1]
        upstream = cotangent[rows, :].astype(f32) * kept
        up_low = upstream.astype(bf16)
        up_all[rows, :] = up_low
        gates = [dot(normed, wgu[:, c * BLOCK : (c + 1) * BLOCK], NN) for c in range(chunks)]
        ups = [dot(normed, wgu[:, FF + c * BLOCK : FF + (c + 1) * BLOCK], NN) for c in range(chunks)]
        hiddens = [dot(up_low, wd[c * BLOCK : (c + 1) * BLOCK, :], NT) for c in range(chunks)]
        for c in range(chunks):
            gate, up, grad_hidden = gates[c], ups[c], hiddens[c]
            sig = 1.0 / (1.0 + jnp.exp(-gate))
            silu = gate * sig
            hidden_all[rows, c * BLOCK : (c + 1) * BLOCK] = (silu * up).astype(bf16)
            low_all[rows, FF + c * BLOCK : FF + (c + 1) * BLOCK] = (grad_hidden * silu).astype(bf16)
            low_all[rows, c * BLOCK : (c + 1) * BLOCK] = (
                grad_hidden * up * (sig + silu * (1.0 - sig))
            ).astype(bf16)
        ffn = dot(hidden_all[rows, :], wd[...], NN)
        grad_normed = dot(low_all[rows, :], wgu[...], NT)
        result[rows, :] = (kept * (middle + ffn)).astype(bf16)
        g_gain[0:1, :] += jnp.sum(grad_normed * middle * scale, axis=0, keepdims=True)
        grad = upstream + norm_back(grad_normed * gain, middle, scale)
        grad_middle[rows, :] = grad
        low = grad.astype(bf16)
        middle_all[rows, :] = low
        grad_mixed = dot(low, wo[...], NT).astype(bf16).astype(f32)
        products = grad_mixed * exact[rows, :]
        for h in range(HEADS):
            pair = h // 2
            head = grad_mixed[:, pair * LANES : (pair + 1) * LANES]
            product = products[:, pair * LANES : (pair + 1) * LANES]
            mine_lanes = (lane < HD) if h % 2 == 0 else (lane >= HD)
            delta = -jnp.sum(jnp.where(mine_lanes, product, 0.0), axis=1, keepdims=True)
            if h % 2:
                head = pltpu.roll(head, HD, 1)
            high, mid, last = split_three(delta)
            extra = jnp.where(
                lane == HD,
                high.astype(f32),
                jnp.where(
                    lane == HD + 1,
                    mid.astype(f32),
                    jnp.where(lane == HD + 2, last.astype(f32), 0.0),
                ),
            )
            da[h, rows, :] = jnp.where(lane < HD, head, extra).astype(bf16)
        return carry

    lax.fori_loop(0, own.shape[0] // FEED, body, 0)
    if not fused:
        g_out[...] = dot(mixed[...], middle_all[...], TN)
        for c in range(2 * FF // 512):
            g_gate_up[:, c * 512 : (c + 1) * 512] = dot(
                normed_all[...], low_all[:, c * 512 : (c + 1) * 512], TN
            )
        for c in range(chunks):
            g_down[c * BLOCK : (c + 1) * BLOCK, :] = dot(
                hidden_all[:, c * BLOCK : (c + 1) * BLOCK], up_all[...], TN
            )
        return
    count, number, shard, down = fused

    size = number * shard + 3 * down

    def put(at, value):
        for i in range(value.shape[1] // LANES):
            half, row = divmod(at + i, number)
            for device in range(count):
                start = (half * count + device) * size + row * shard
                sums[start : start + shard, :] = value[
                    device * shard : (device + 1) * shard, i * LANES : (i + 1) * LANES
                ]

    put(0, dot(mixed[...], middle_all[...], TN))
    for c in range(2 * FF // 512):
        put(3 + 4 * c, dot(normed_all[...], low_all[:, c * 512 : (c + 1) * 512], TN))
    put(19, gain_column(g_gain[...]))
    for c in range(chunks):
        value = dot(hidden_all[:, c * BLOCK : (c + 1) * BLOCK], up_all[...], TN)
        for n in range(BLOCK // down):
            device, half = divmod(c * BLOCK // down + n, 2)
            for i in range(3):
                start = (half * count + device) * size + number * shard + i * down
                sums[start : start + down, :] = value[
                    n * down : (n + 1) * down, i * LANES : (i + 1) * LANES
                ]
    me = where[1] & (fan - 1)
    for high in range(count // fan):
        for flip in range(fan):
            for half in range(2):
                start = (half * count + high * fan + (me ^ flip)) * size
                gives[flip][half * (count // fan) + high] = sums[
                    pl.ds(pl.multiple_of(start, 8), size), :
                ].astype(gives[flip].dtype)


def feed(own, mixed, exact, cotangent, query_aux, gains, weights, fused):
    length = own.shape[0]
    scratch = [
        pltpu.VMEM((length, D), bf16),
        pltpu.VMEM((length, 2 * FF), bf16),
        pltpu.VMEM((length, FF), bf16),
        pltpu.VMEM((length, D), bf16),
        pltpu.VMEM((length, D), bf16),
    ]
    out_shape = [
        jax.ShapeDtypeStruct((length, D), bf16),
        in_vmem((length, D), f32),
        in_vmem((HEADS, length, LANES), bf16),
    ]
    if fused:
        count, number, shard, down = fused
        rows = number * shard + 3 * down
        fan = 1 << bit_groups(count)[0][1]
        weight_specs = [SMEM] + [VMEM] * (len(weights) - 1)
        specs = [HBM, VMEM, VMEM, HBM, VMEM, VMEM]
        out_shape += [
            jax.ShapeDtypeStruct((2 * count // fan, rows, LANES), bf16 if flip else f32)
            for flip in range(fan)
        ]
        scratch += [
            pltpu.VMEM((D, D), bf16),
            pltpu.VMEM((D, 2 * FF), bf16),
            pltpu.VMEM((FF, D), bf16),
            pltpu.VMEM((8, D), f32),
            pltpu.VMEM((2 * count * rows, LANES), f32),
        ]
        scratch += landing([own, cotangent])
    else:
        weight_specs = [VMEM] * 3
        specs = [VMEM] * 6
        out_shape += [
            jax.ShapeDtypeStruct((D, D), f32),
            jax.ShapeDtypeStruct((D, 2 * FF), f32),
            jax.ShapeDtypeStruct((FF, D), f32),
            jax.ShapeDtypeStruct((8, D), f32),
        ]
    if fused:
        own, cotangent = in_hbm([own, cotangent])
    return pl.pallas_call(
        partial(feed_kernel, fused),
        out_shape=out_shape,
        in_specs=specs + weight_specs,
        out_specs=[VMEM] * len(out_shape),
        scratch_shapes=scratch,
        compiler_params=limit(LIMITS[3]),
        cost_estimate=cost(14 * 10**9, 16 * 2**20),
        name="feed",
    )(own, mixed, exact, cotangent, query_aux, gains, *weights)


PARTS = ((0, 1, 2), (3, 4, 5, 6, 7, 8))


def project_back_kernel(number, fused, own, cosine, sine, w, gains, *refs):
    part = PARTS[number]
    low = lax.broadcasted_iota(jnp.int32, (WIDE, LANES), 1) < HD
    gain = gains[0:1, :]
    if number == 0:
        dq = refs[0]
        partial_sum, grads, normed_all, low_all = refs[-6:-2]
        copies = fetch((own,), refs[-2:-1], refs[-1])
        own = refs[-2]
    else:
        kept, got, grad_middle, before, grads_before = refs[:5]
        if fused:
            where = refs[5]
            grad_tokens, keep, give, sums, g_gain, normed_all, low_all = refs[-10:-3]
        else:
            grad_tokens, grads, g_gain, normed_all, low_all = refs[-8:-3]
        g_gain[...] = jnp.zeros_like(g_gain)
        copies = fetch((own, got), refs[-3:-1], refs[-1])
        own, got = refs[-3:-1]
    arrive(copies)

    def body(step, carry):
        rows = block(step, WIDE)
        cos, sin = cosine[rows, :], -sine[rows, :]
        x = own[rows, :].astype(f32)
        scale = row_scale(x)
        normed_all[rows, :] = (x * scale * gain).astype(bf16)
        for at, slab in enumerate(part):
            kind, pair = divmod(slab, 3)
            heads = (2 * pair, 2 * pair + 1)
            if kind == 0:
                z = jnp.concatenate([dq[h, :, rows] for h in heads], axis=0).T * HD**-0.5
            else:
                one, two = [kept[h, rows, :] + got[h, rows, :].astype(f32) for h in heads]
                if kind == 1:
                    z = jnp.where(low, pltpu.roll(one, HD, 1), two)
                else:
                    z = jnp.where(low, one, pltpu.roll(two, HD, 1))
            if kind < 2:
                z = z * cos + swap_halves(z) * sin
            low_all[rows, at * LANES : (at + 1) * LANES] = z.astype(bf16)
        first = part[0] * LANES
        grad_normed = dot(
            low_all[rows, :], w[:, first : first + len(part) * LANES], NT
        )
        if number == 0:
            partial_sum[rows, :] = grad_normed
        else:
            grad_normed = grad_normed + before[rows, :]
            g_gain[0:1, :] += jnp.sum(grad_normed * x * scale, axis=0, keepdims=True)
            grad_tokens[rows, :] = (
                grad_middle[rows, :] + norm_back(grad_normed * gain, x, scale)
            ).astype(bf16)
        return carry

    lax.fori_loop(0, own.shape[0] // WIDE, body, 0)
    value = dot(normed_all[...], low_all[...], TN)
    if number == 0 or not fused:
        grads[...] = value
        return
    core = where[0]
    for done, source in ((PARTS[0], grads_before), (PARTS[1], value)):
        for at, slab in enumerate(done):
            put_slab(sums, core, *fused, slab, source[:, at * LANES : (at + 1) * LANES])
    put_slab(sums, core, *fused, 9, gain_column(g_gain[...]))
    keep[...] = sums[0]
    give[...] = sums[1].astype(bf16)


def project_back(number, fused, where, shared, arrays, waits):
    own, cosine, sine, w, gains = shared
    length = own.shape[0]
    columns = len(PARTS[number]) * LANES
    scratch = [pltpu.VMEM((length, D), bf16), pltpu.VMEM((length, columns), bf16)]
    specs = [VMEM] * len(arrays)
    if number:
        specs[1] = ANY
    scratch += landing([own] + list(arrays[1:2]))
    if number == 0:
        out_shape = [in_vmem((length, D), f32), in_vmem((D, columns), f32)]
    elif fused:
        size, shard = fused
        chunk = (D // shard, size * shard, LANES)
        specs.append(SMEM)
        arrays = [*arrays, where]
        out_shape = [
            jax.ShapeDtypeStruct((length, D), bf16),
            jax.ShapeDtypeStruct(chunk, f32),
            jax.ShapeDtypeStruct(chunk, bf16),
        ]
        scratch = [pltpu.VMEM((2,) + chunk, f32), pltpu.VMEM((8, D), f32)] + scratch
    else:
        out_shape = [
            jax.ShapeDtypeStruct((length, D), bf16),
            jax.ShapeDtypeStruct((D, columns), f32),
            jax.ShapeDtypeStruct((8, D), f32),
        ]
    (own,) = in_hbm([own])
    return pl.pallas_call(
        partial(project_back_kernel, number, fused),
        out_shape=out_shape,
        in_specs=[HBM] + [VMEM] * 4 + specs + [ANY] * len(waits),
        out_specs=[VMEM] * len(out_shape),
        scratch_shapes=scratch,
        compiler_params=limit(LIMITS[5]),
        cost_estimate=cost(4 * 10**9, 8 * 2**20),
        name="project_back",
    )(own, cosine, sine, w, gains, *arrays, *waits)


def squares_kernel(*refs):
    total = sum(jnp.sum(ref[...] * ref[...]) for ref in refs[0:4:2]) + 0.0
    other = sum(jnp.sum(ref[...] * ref[...]) for ref in refs[1:4:2]) + 0.0
    refs[4][...] = jnp.full((1, LANES), total + other, f32)


def squares(sums):
    spec = pl.BlockSpec(memory_space=pltpu.VMEM)
    return pl.pallas_call(
        squares_kernel,
        out_shape=jax.ShapeDtypeStruct((1, LANES), f32),
        in_specs=[spec] * 4,
        out_specs=spec,
        compiler_params=limit(16),
        name="squares",
    )(*sums)


def bring_kernel(*refs):
    number = (len(refs) - 1) // 2
    arrive(fetch(refs[:number], refs[-number - 1 : -1], refs[-1]))


def bring(arrays):
    return pl.pallas_call(
        bring_kernel,
        out_shape=[in_vmem(item.shape, item.dtype) for item in arrays],
        in_specs=[HBM] * len(arrays),
        out_specs=[VMEM] * len(arrays),
        scratch_shapes=[pltpu.SemaphoreType.DMA((len(arrays),))],
        compiler_params=limit(1),
        name="bring",
    )(*in_hbm(arrays))


def update_kernel(shard, down, where, total, *refs):
    core = where[0]
    chunks = refs[:4]
    norm = refs[19]
    outs = [refs[20 + 5 * i : 25 + 5 * i] for i in range(4)]
    low, high, square = refs[40:]
    masters, firsts, seconds = refs[4:9], refs[9:14], refs[14:19]
    split = 5 * shard

    @pl.when(core == 0)
    def _():
        for i, target in ((0, low), (1, high)):
            target[:split] = chunks[i][...]
            target[split:] = chunks[2 + i][...]

    @pl.when(core == 1)
    def _():
        for i, target in ((0, high), (1, low)):
            target[:split] = chunks[i][...]
            target[split:] = chunks[2 + i][...]

    length = jnp.sqrt(total[0:1, 0:1])
    norm[...] = length
    factor = clip_limit / jnp.maximum(length, clip_limit)
    halves = (low, high)

    def step(which, grad, rows, columns, rate, decay):
        at = (rows, columns)
        new = adam_update(
            masters[which][at], factor * grad, firsts[which][at], seconds[which][at], rate, decay
        )
        outs[0][which][at] = new[0]
        outs[1][which][at] = new[1]
        outs[2][which][at] = new[2]
        outs[3][which][at] = new[2].astype(bf16)

    every = slice(None)
    places = [(0, i, i // 5, (i % 5) * shard) for i in range(9)]
    for i in range(19):
        which, column = (1, i) if i < 3 else (2, i - 3)
        places.append((which, column, i // 10, (5 + i % 10) * shard))
    for which, column, half, row in places:
        rate = 4.0 * D**-0.5 if which == 1 else D**-0.5
        grad = halves[half][row : row + shard, :]
        step(which, grad, every, slice(column * LANES, (column + 1) * LANES), rate, decay_rate)
    for half in range(2):
        for i in range(3):
            row = 15 * shard + i * down
            step(
                3, halves[half][row : row + down, :], slice(half * down, (half + 1) * down),
                slice(i * LANES, (i + 1) * LANES), FF**-0.5, decay_rate,
            )
    gain_rows = []
    for row in (4 * shard, 14 * shard):
        square[...] = jnp.zeros_like(square)
        square[0:shard, :] = high[row : row + shard, :]
        gain_rows.append(square[...].T[0:1, :shard])
    for i in range(2):
        step(4, gain_rows[i], slice(i, i + 1), every, 0.5, 0.0)


def update(where, total, sums, masters, firsts, seconds):
    shard, down = masters[0].shape[0], masters[3].shape[0] // 2
    spec = pl.BlockSpec(memory_space=pltpu.VMEM)
    shapes = [item.shape for item in masters]
    outs = pl.pallas_call(
        partial(update_kernel, shard, down),
        out_shape=[jax.ShapeDtypeStruct((1, 1), f32)]
        + [jax.ShapeDtypeStruct(shape, f32) for _ in range(3) for shape in shapes]
        + [jax.ShapeDtypeStruct(shape, bf16) for shape in shapes],
        in_specs=[pl.BlockSpec(memory_space=pltpu.SMEM)] + [VMEM] * 20,
        out_specs=[spec] * 21,
        scratch_shapes=[
            pltpu.VMEM((15 * shard + 3 * down, LANES), f32),
            pltpu.VMEM((15 * shard + 3 * down, LANES), f32),
            pltpu.VMEM((LANES, LANES), f32),
        ],
        compiler_params=limit(LIMITS[6]),
        name="update",
    )(where, total, *sums, *masters, *firsts, *seconds)
    return outs[0][0, 0], outs[1:6], outs[6:11], outs[11:16], outs[16:21]


def update_plain(core, total, sums, masters, firsts, seconds):
    shard, down = masters[0].shape[0], masters[3].shape[0] // 2
    mine = jnp.concatenate([sums[0], sums[2]])
    there = jnp.concatenate([sums[1], sums[3]])
    low = jnp.where(core == 0, mine, there)
    high = jnp.where(core == 0, there, mine)
    five, fifteen = 5 * shard, 15 * shard
    first_shard = jnp.concatenate([low[:five], high[:five]]).reshape(10, shard, LANES)
    second_shard = jnp.concatenate([low[five:fifteen], high[five:fifteen]])
    second_shard = second_shard.reshape(20, shard, LANES)
    down_shard = jnp.stack(
        [item[fifteen:].reshape(3, down, LANES) for item in (low, high)], axis=1
    ).reshape(3, 2 * down, LANES)
    shard_grads = (
        unslab(first_shard[:9]),
        unslab(second_shard[:3]),
        unslab(second_shard[3:19]),
        unslab(down_shard),
        jnp.stack([first_shard[9, :, 0], second_shard[19, :, 0]]),
    )
    grad_norm = jnp.sqrt(total[0, 0])
    factor = clip_limit / jnp.maximum(grad_norm, clip_limit)
    rates = (D ** (-0.5), 4.0 * D ** (-0.5), D ** (-0.5), FF ** (-0.5), 0.5)
    decays = (decay_rate, decay_rate, decay_rate, decay_rate, 0.0)
    updates = [
        adam_update(
            masters[i], factor * shard_grads[i], firsts[i], seconds[i], rates[i], decays[i]
        )
        for i in range(5)
    ]
    new_first, new_second, new_master = zip(*updates)
    return grad_norm, new_first, new_second, new_master, [item.astype(bf16) for item in new_master]


def per_device(
    count,
    tokens,
    cotangent,
    sample_ids,
    pad_flags,
    offsets,
    w_qkv,
    w_out,
    w_gate_up,
    w_down,
    gains,
    m_qkv,
    m_out,
    m_gate_up,
    m_down,
    m_gains,
    v_qkv,
    v_out,
    v_gate_up,
    v_down,
    v_gains,
):
    owner = lax.axis_index("batch")
    core = lax.axis_index("tm")
    where = jnp.stack([core, owner]).astype(jnp.int32)
    shard = w_qkv.shape[0]
    down = w_down.shape[0] // 2
    own = tokens[0]
    fuse_in = can_unpack(shard, down)
    masters = (w_qkv, w_out, w_gate_up, w_down, gains)

    first = send_chunk(where, FIRST_PLAN, 0, [w_qkv, gains], [])
    there = swap_tm(own)
    cosine, sine, key_aux, query_aux, ranges = tables(
        where, sample_ids, pad_flags, offsets, [there]
    )
    first_held, first_pieces = gather(first, count, [query_aux])
    second = send_chunk(where, SECOND_PLAN, down, [w_out, w_gate_up, w_down], [first_held])

    def gathered(pieces, number, down):
        others = [swap_tm(piece) for piece in pieces]
        if fuse_in:
            return (where, *pieces, *others), (count, number, shard, down)
        return unpack_plain(count, number, shard, down, where, pieces, others), None

    weights, fused = gathered(first_pieces, 5, 0)
    qa, ka, va, kt, vt, attn_in, gain_pair = project(
        own, there, cosine, sine, key_aux, query_aux, weights, fused, []
    )
    second_held, second_pieces = gather(second, count, [gain_pair])
    mixed, exact, qb = attend(ranges, qa, ka, vt, [second_held])
    second_pieces[1:] = hold(second_pieces[1:], [mixed])
    weights, fused = gathered(second_pieces, 10, down)
    result, grad_middle, da, *grads = feed(
        own, mixed, exact, cotangent[0], query_aux, gain_pair, weights, fused
    )
    groups = bit_groups(count)
    fan = 1 << groups[0][1]

    def flips(halves):
        halves = halves.reshape((-1, fan) + halves.shape[-2:])
        mine = owner & (fan - 1)
        parts = [lax.dynamic_index_in_dim(halves, mine ^ k, 1, keepdims=False) for k in range(fan)]
        return [parts[0]] + [item.astype(bf16) for item in parts[1:]]

    if not fused:
        grads = flips(pack_plain(count, core, grads, 10, shard, down))
    got = [permute_batch(grads[k], k, count) for k in range(1, fan)]
    dq, kept, part = attend_back(ranges, qb, ka, da, va, kt, [])
    fused = (5, shard) if fuse_in else None
    shared = (own, cosine, sine, attn_in, gain_pair)
    before, grads_before = project_back(0, fused, where, shared, [dq], [])
    got = hold(got, [grads_before])
    part_there = swap_tm(hold([part], got)[0])
    left = count // fan
    keep, give = combine(where, [grads[0], *got], (1, 2, left, 0, 0))
    split = None
    if len(groups) > 1:
        split = (left >> groups[1][1], 1 << groups[1][1], 1, 1, groups[1][0])
    parts = combine(where, [keep, swap_tm(give)], split)
    grad_tokens, *grads = project_back(
        1, fused, where, shared, [kept, part_there, grad_middle, before, grads_before], [parts[0]]
    )
    if split:
        parts = [scatter_parts(where, parts, count, groups[1:], [grads[1]])]
    second_sum = parts[0].reshape(-1, LANES)
    if fused:
        kept, given = grads
    else:
        grads = [jnp.concatenate([grads_before, grads[0]], axis=1), grads[1]]
        halves = pack_plain(count, core, grads, 5, shard, 0)
        kept = jnp.where(core == 0, halves[0], halves[1])
        given = jnp.where(core == 0, halves[1], halves[0]).astype(bf16)
    (given,) = hold([given], [second_sum])
    firsts = (m_qkv, m_out, m_gate_up, m_down, m_gains)
    seconds = (v_qkv, v_out, v_gate_up, v_down, v_gains)
    waits = []
    if fuse_in:
        brought = bring([*masters, *firsts, *seconds])
        masters, firsts, seconds = brought[:5], brought[5:10], brought[10:]
        waits = brought[:1]
    parts = combine(where, [kept, swap_tm(given)], (left, fan, 1, 1, 0), waits)
    first_sum = scatter_parts(where, parts, count, groups).reshape(-1, LANES)
    sums = (first_sum, swap_tm(first_sum), second_sum, swap_tm(second_sum))
    total = sum_batch(squares(sums), count)
    if fuse_in:
        updates = update(where, total, sums, masters, firsts, seconds)
    else:
        updates = update_plain(core, total, sums, masters, firsts, seconds)
    grad_norm, new_first, new_second, new_master, copies = updates
    return (
        result[None],
        grad_tokens[None],
        grad_norm,
        *new_first,
        *new_second,
        *new_master,
        *copies,
    )


def solution(mesh):
    in_specs = (
        P("batch", "tm", None),
        P("batch", "tm", None),
        P("batch", None),
        P("batch", None),
        P("batch", None),
        P("batch", None),
        P("batch", None),
        P("batch", None),
        P("batch", None),
        P(None, "batch"),
        P("batch", None),
        P("batch", None),
        P("batch", None),
        P("batch", None),
        P(None, "batch"),
        P("batch", None),
        P("batch", None),
        P("batch", None),
        P("batch", None),
        P(None, "batch"),
    )
    out_specs = (
        P("batch", "tm", None),
        P("batch", "tm", None),
        P(),
        P("batch", None),
        P("batch", None),
        P("batch", None),
        P("batch", None),
        P(None, "batch"),
        P("batch", None),
        P("batch", None),
        P("batch", None),
        P("batch", None),
        P(None, "batch"),
        P("batch", None),
        P("batch", None),
        P("batch", None),
        P("batch", None),
        P(None, "batch"),
        P("batch", None),
        P("batch", None),
        P("batch", None),
        P("batch", None),
        P(None, "batch"),
    )
    return jax.shard_map(
        partial(per_device, mesh.shape["batch"]), mesh=mesh, in_specs=in_specs, out_specs=out_specs, check_vma=False
    )
```

```python
import math
from functools import partial

import jax
import jax.numpy as jnp
from jax import lax
from jax.experimental import pallas as pl
from jax.experimental.pallas import tpu as pltpu
from jax.sharding import PartitionSpec as P

D = 384
FF = 1024
HEADS = 6
HD = 64
STEP = 3


norm_eps = 1e-06
beta_one = 0.5
beta_two = 0.5
adam_eps = 1e-08
decay_rate = 0.1
clip_limit = 1.0
masked_score = -1e30


def adam_update(master, grad, first, second, rate, decay):
    first_new = beta_one * first + (1.0 - beta_one) * grad
    second_new = beta_two * second + (1.0 - beta_two) * grad * grad
    direction = (
        first_new
        / (1.0 - beta_one**STEP)
        / (jnp.sqrt(second_new / (1.0 - beta_two**STEP)) + adam_eps)
    )
    return (first_new, second_new, master - rate * (direction + decay * master))


def bit_groups(count):
    groups = []
    low, bits = 0, count.bit_length() - 1
    while low < bits:
        width = min(2, bits - low)
        groups.append((low, width))
        low += width
    return groups


def permute_batch(value, flip, count):
    return lax.ppermute(value, "batch", [(i, i ^ flip) for i in range(count)])


def swap_tm(value):
    return lax.ppermute(value, "tm", [(0, 1), (1, 0)])


def slabs(matrix):
    rows, columns = matrix.shape
    return matrix.reshape(rows, columns // 128, 128).transpose(1, 0, 2)


def unslab(stack):
    count, rows, _ = stack.shape
    return stack.transpose(1, 0, 2).reshape(rows, count * 128)


bf16 = jnp.bfloat16
f32 = jnp.float32
BLOCK = 256
LANES = 128
KEEP_LANE = 96
LIMITS = (12, 20, 12, 36, 12, 20, 12)
WIDE = 512
NN = (((1,), (0,)), ((), ()))
NT = (((1,), (1,)), ((), ()))
TN = (((0,), (0,)), ((), ()))


def dot(left, right, dims):
    return lax.dot_general(left, right, dims, preferred_element_type=f32)


def cost(flops, moved):
    return pl.CostEstimate(flops=flops, bytes_accessed=moved, transcendentals=0)


def in_vmem(shape, dtype):
    return pltpu.VMEM(tuple(shape), dtype)


VMEM = pl.BlockSpec(memory_space=pltpu.VMEM)
SMEM = pl.BlockSpec(memory_space=pltpu.SMEM)
ANY = pl.BlockSpec(memory_space=pl.ANY)
HBM = pl.BlockSpec(memory_space=pltpu.HBM)


def fetch(sources, targets, semaphores):
    copies = [
        pltpu.make_async_copy(source, target, semaphores.at[i])
        for i, (source, target) in enumerate(zip(sources, targets))
    ]
    for copy in copies:
        copy.start()
    return copies


def landing(arrays):
    return [pltpu.VMEM(item.shape, item.dtype) for item in arrays] + [
        pltpu.SemaphoreType.DMA((len(arrays),))
    ]


def arrive(copies):
    for copy in copies:
        copy.wait()


def limit(mebibytes):
    return pltpu.CompilerParams(vmem_limit_bytes=mebibytes * 2**20)


def block(start, size=BLOCK):
    return pl.ds(pl.multiple_of(start * size, size), size)


def sum_batch(value, count):
    value = jnp.broadcast_to(value[:, None], (count, 1, LANES))
    value = lax.all_to_all(value, "batch", 0, 0, tiled=True)
    return jnp.sum(value, axis=0)


def row_scale(values):
    return lax.rsqrt(jnp.mean(values * values, axis=-1, keepdims=True) + norm_eps)


def norm_back(grad_normed, values, scale):
    return scale * grad_normed - values * scale * scale * scale * jnp.mean(
        grad_normed * values, axis=-1, keepdims=True
    )


def split_three(values):
    high = values.astype(bf16)
    rest = values - high.astype(f32)
    middle = rest.astype(bf16)
    return high, middle, (rest - middle.astype(f32)).astype(bf16)


def swap_halves(pair):
    lane = lax.broadcasted_iota(jnp.int32, pair.shape, 1)
    return jnp.where(lane % HD < HD // 2, pltpu.roll(pair, 96, 1), pltpu.roll(pair, 32, 1))


def relative_place(device, owner, count):
    flips = device ^ owner
    place, scale = 0, 1
    for low, width in reversed(bit_groups(count)):
        place = place + ((flips >> low) & ((1 << width) - 1)) * scale
        scale <<= width
    return place


def exchange_all(held, low, width, count):
    return [held] + [permute_batch(held, k << low, count) for k in range(1, 1 << width)]


def in_hbm(arrays):
    return [pltpu.with_memory_space_constraint(item, pltpu.HBM) for item in arrays]


def join_kernel(number, *refs):
    out = refs[-1]
    size = refs[0].shape[0]
    for i in range(number):
        out[i * size : (i + 1) * size] = refs[i][...]


def join(pieces, waits=()):
    first = pieces[0]
    shape = (len(pieces) * first.shape[0],) + first.shape[1:]
    return pl.pallas_call(
        partial(join_kernel, len(pieces)),
        out_shape=jax.ShapeDtypeStruct(shape, first.dtype),
        in_specs=[VMEM] * len(pieces) + [ANY] * len(waits),
        out_specs=VMEM,
        compiler_params=limit(4),
        name="join",
    )(*pieces, *waits)


def combine_kernel(number, split, where, *refs):
    items, outs = refs[:number], refs[-len(refs) + number :]
    outs = outs[-(split[1] if split else 1) :]

    def total(index):
        return sum(item[index].astype(f32) for item in items[1:]) + items[0][index].astype(f32)

    if not split:
        outs[0][...] = total(slice(None))
        return
    upper, fan, lower, which, low = split
    mine = (where[which] >> low) & (fan - 1)
    for a in range(upper):
        for b in range(lower):
            for flip in range(fan):
                index = (a * fan + (mine ^ flip)) * lower + b
                outs[flip][a * lower + b] = total(index).astype(outs[flip].dtype)


def combine(where, items, split, waits=()):
    count, rows, _ = items[0].shape
    if split:
        fan = split[1]
        shapes = [
            jax.ShapeDtypeStruct((count // fan, rows, LANES), bf16 if flip else f32)
            for flip in range(fan)
        ]
    else:
        shapes = [jax.ShapeDtypeStruct((count, rows, LANES), f32)]
    return pl.pallas_call(
        partial(combine_kernel, len(items), split),
        out_shape=shapes,
        in_specs=[SMEM] + [VMEM] * len(items) + [ANY] * len(waits),
        out_specs=[VMEM] * len(shapes),
        compiler_params=limit(12),
        name="combine",
    )(where, *items, *waits)


def scatter_parts(where, parts, count, groups, waits=None):
    for n, (low, width) in enumerate(groups):
        got = [permute_batch(item, k << low, count) for k, item in enumerate(parts) if k]
        if waits and n == 0:
            got = hold(got, waits)
        split = None
        if n + 1 < len(groups):
            fan = 1 << groups[n + 1][1]
            split = (parts[0].shape[0] // fan, fan, 1, 1, groups[n + 1][0])
        parts = combine(where, [parts[0], *got], split)
    return parts[0]


def hold(values, waits):
    spec = pl.BlockSpec(memory_space=pl.ANY)
    number = len(values)
    return pl.pallas_call(
        lambda *refs: None,
        out_shape=[jax.ShapeDtypeStruct(item.shape, item.dtype) for item in values],
        in_specs=[spec] * (number + len(waits)),
        out_specs=[spec] * number,
        input_output_aliases={i: i for i in range(number)},
        compiler_params=limit(1),
        name="hold",
    )(*values, *waits)


def send_kernel(shard, plan, down, where, *refs):
    number = (len(refs) - 4) // 2
    target, stage, square = refs[number : number + 3]
    sources = refs[number + 3 : -1]
    arrive(fetch(refs[:number], sources, refs[-1]))
    number = len(plan) // 2
    core = where[0]
    stage[...] = jnp.zeros_like(stage)
    gain_at = [i for i, item in enumerate(plan) if item == "gain"]
    if gain_at:
        square[...] = jnp.zeros_like(square)
        square[0:2, 0:shard] = sources[-1][...]
        column = square[...].T

    def fill(half):
        for i in range(number):
            item = plan[half * number + i]
            rows = slice(i * shard, (i + 1) * shard)
            if item == "gain":
                stage[rows, :] = column[:shard]
            elif item is not None:
                which, at = item
                stage[rows, :] = sources[which][:, at * LANES : (at + 1) * LANES]
        for i in range(3 if down else 0):
            start = number * shard + i * down
            stage[start : start + down, :] = sources[2][
                half * down : (half + 1) * down, i * LANES : (i + 1) * LANES
            ]

    @pl.when(core == 0)
    def _():
        fill(0)

    @pl.when(core == 1)
    def _():
        fill(1)

    target[...] = stage[...].astype(bf16)


def send_chunk(where, plan, down, sources, waits):
    shard = sources[0].shape[0]
    rows = len(plan) // 2 * shard + 3 * down
    rows = -(-rows // 16) * 16
    core = where[0]
    if shard % 8 == 0 and down % 8 == 0:
        spec = VMEM

        def kernel(where, *refs):
            kept = refs[: len(sources)] + refs[len(sources) + len(waits) :]
            send_kernel(shard, plan, down, where, *kept)

        return pl.pallas_call(
            kernel,
            out_shape=jax.ShapeDtypeStruct((rows, LANES), bf16),
            in_specs=[SMEM] + [HBM] * len(sources) + [ANY] * len(waits),
            out_specs=spec,
            scratch_shapes=[pltpu.VMEM((rows, LANES), f32), pltpu.VMEM((LANES, LANES), f32)]
            + landing(sources),
            compiler_params=limit(6),
            name="send_chunk",
        )(where, *in_hbm(sources), *waits)
    stacks = {i: slabs(item) for i, item in enumerate(sources) if item.shape[1] % LANES == 0}
    pieces = []
    for item in plan:
        if item == "gain":
            pieces.append(jnp.pad(sources[-1].T, ((0, 0), (0, LANES - 2))))
        elif item is None:
            pieces.append(jnp.zeros((shard, LANES), f32))
        else:
            pieces.append(stacks[item[0]][item[1]])
    half = len(plan) // 2
    halves = [jnp.concatenate(pieces[:half]), jnp.concatenate(pieces[half:])]
    if down:
        for i in range(2):
            part = stacks[2][:, i * down : (i + 1) * down].reshape(3 * down, LANES)
            halves[i] = jnp.concatenate([halves[i], part])
    chunk = jnp.where(core == 0, halves[0], halves[1]).astype(bf16)
    return jnp.pad(chunk, ((0, rows - chunk.shape[0]), (0, 0)))


FIRST_PLAN = tuple((0, i) for i in range(9)) + ("gain",)
SECOND_PLAN = tuple((0, i) for i in range(3)) + tuple((1, i) for i in range(16)) + (None,)


def gather(chunk, count, waits):
    held = chunk[None]
    groups = bit_groups(count)[::-1]
    for n, (low, width) in enumerate(groups):
        pieces = exchange_all(held, low, width, count)
        if n + 1 < len(groups):
            held = join(pieces, () if n else waits)
    return held, pieces


def unpack(count, number, shard, down, where, pieces, others, stage, w_down):
    core, owner = where[0], where[1]
    last = bit_groups(count)[0][1]
    for sources, half in ((pieces, core), (others, 1 - core)):
        for flip, source in enumerate(sources):

            def one(n, carry, source=source, half=half, flip=flip):
                device = owner ^ flip ^ (relative_flips(n, count) << last)
                chunk = source[n].astype(f32)
                for i in range(number):
                    start = (half * number + i) * D + device * shard
                    stage[pl.ds(pl.multiple_of(start, 8), shard), :] = chunk[
                        i * shard : (i + 1) * shard
                    ]
                for i in range(3 if down else 0):
                    start = number * shard + i * down
                    rows = pl.ds(pl.multiple_of((device * 2 + half) * down, 16), down)
                    w_down[rows, i * LANES : (i + 1) * LANES] = chunk[start : start + down].astype(
                        bf16
                    )
                return carry

            lax.fori_loop(0, source.shape[0], one, 0, unroll=True)


def relative_flips(place, count):
    last = bit_groups(count)[0][1]
    flips, scale = 0, 1
    for low, width in reversed(bit_groups(count)[1:]):
        flips = flips + (((place // scale) & ((1 << width) - 1)) << (low - last))
        scale <<= width
    return flips


def can_unpack(shard, down):
    return shard % 8 == 0 and down % 16 == 0


def unpack_plain(count, number, shard, down, where, mine, other):
    core, owner = where[0], where[1]
    places = relative_place(jnp.arange(count, dtype=jnp.int32), owner, count)
    mine, other = jnp.concatenate(mine), jnp.concatenate(other)
    low = jnp.take(jnp.where(core == 0, mine, other), places, axis=0)
    high = jnp.take(jnp.where(core == 0, other, mine), places, axis=0)

    def part(source):
        return (
            source[:, : number * shard]
            .reshape(count, number, shard, LANES)
            .transpose(1, 0, 2, 3)
            .reshape(number, D, LANES)
        )

    stack = jnp.concatenate([part(low), part(high)], axis=0)
    if number == 5:
        return unslab(stack[:9]), stack[9].T[:8].astype(f32)
    downs = [
        item[:, number * shard : number * shard + 3 * down].reshape(count, 3, down, LANES)
        for item in (low, high)
    ]
    w_down = jnp.stack(downs, axis=1).transpose(0, 1, 3, 2, 4).reshape(FF, D)
    return unslab(stack[:3]), unslab(stack[3:19]), w_down


def put_slab(stage, core, number, shard, at, slab):
    half, row = at // number, (at % number) * shard
    slot = core if half == 0 else 1 - core
    stage[slot, :, row : row + shard, :] = slab.reshape(-1, shard, LANES)


def gain_column(row):
    return jnp.concatenate([row, jnp.zeros((LANES - 8, D), f32)], axis=0).T


def pack_plain(count, core, grads, number, shard, down):
    column = jnp.pad(grads[-1][:1].T, ((0, 0), (0, LANES - 1)))[None]
    stack = jnp.concatenate([slabs(item) for item in (grads[:2] if down else grads[:1])] + [column])

    def by_device(part):
        return (
            part.reshape(number, count, shard, LANES)
            .transpose(1, 0, 2, 3)
            .reshape(count, number * shard, LANES)
        )

    halves = [by_device(stack[:number]), by_device(stack[number:])]
    if down:
        downs = (
            slabs(grads[2])
            .reshape(3, count, 2, down, LANES)
            .transpose(2, 1, 0, 3, 4)
            .reshape(2, count, 3 * down, LANES)
        )
        halves = [jnp.concatenate([halves[i], downs[i]], axis=1) for i in range(2)]
    return jnp.stack(halves)


def tables_kernel(length, where, ids, pads, offsets, *refs):
    cosine, sine, key_aux, query_aux, ranges = refs[-9:-4]
    copies = fetch((ids, pads, offsets), refs[-4:-1], refs[-1])
    ids, pads, offsets = refs[-4:-1]
    arrive(copies)
    core = where[0]
    whole = 2 * length

    def turn(row):
        low, high = row[:, :length], row[:, length:]
        return jnp.concatenate(
            [jnp.where(core == 0, low, high), jnp.where(core == 0, high, low)], axis=1
        )

    classes = (2 * ids[...] + pads[...]).astype(f32)
    spot = lax.broadcasted_iota(jnp.int32, (1, whole), 1)
    position = (turn(spot) + turn(offsets[...])).astype(f32)
    turned = turn(classes)
    index = lax.broadcasted_iota(jnp.int32, (HD // 2, whole), 0).astype(f32)
    angle = position * jnp.exp(index * (-2.0 * math.log(10000.0) / HD))
    cos, sin = jnp.cos(angle), jnp.sin(angle)
    cosine[...] = jnp.concatenate([cos, cos, cos, cos], axis=0).T
    sine[...] = jnp.concatenate([-sin, sin, -sin, sin], axis=0).T
    at = lax.broadcasted_iota(jnp.int32, (LANES, whole), 0)
    is_class = (at >= HD) & (at < HD + 8)
    same = (at - HD).astype(f32) == turned
    is_log = (at >= HD + 8) & (at < HD + 8 + 3 * HEADS)
    key_aux[...] = jnp.where((is_class & same) | is_log, 1.0, 0.0).T.astype(bf16)
    own = turned[:, :length]
    kept = jnp.where(turn(pads[...])[:, :length] == 0, 1.0, 0.0)
    extra = jnp.where(is_class & ~same, masked_score, 0.0)[:, :length]
    query_aux[...] = jnp.where(at[:, :length] == KEEP_LANE, kept, extra).T.astype(bf16)
    starts = (core * length, (1 - core) * length)
    for n in range(length // BLOCK):
        mine = own[:, n * BLOCK : (n + 1) * BLOCK]
        first = jnp.min(mine)
        last = jnp.max(mine)
        low_key = jnp.sum(jnp.where(classes < first, 1.0, 0.0)).astype(jnp.int32)
        high_key = jnp.sum(jnp.where(classes <= last, 1.0, 0.0)).astype(jnp.int32)
        bounds = []
        for start in starts:
            low_part = jnp.clip(low_key - start, 0, length)
            high_part = jnp.clip(high_key - start, 0, length)
            low_block = low_part // BLOCK
            bounds.append((low_block, jnp.maximum((high_part + BLOCK - 1) // BLOCK - low_block, 0)))
        ranges[0, n] = bounds[0][0]
        ranges[1, n] = bounds[0][1]
        ranges[2, n] = bounds[1][0] + length // BLOCK - bounds[0][1]
        ranges[3, n] = bounds[0][1] + bounds[1][1]


def tables(where, ids, pads, offsets, waits):
    whole = ids.shape[1]
    length = whole // 2
    spec = pl.BlockSpec(memory_space=pltpu.VMEM)
    smem = pl.BlockSpec(memory_space=pltpu.SMEM)
    return pl.pallas_call(
        partial(tables_kernel, length),
        out_shape=[
            in_vmem((whole, LANES), f32),
            in_vmem((whole, LANES), f32),
            in_vmem((whole, LANES), bf16),
            in_vmem((length, LANES), bf16),
            jax.ShapeDtypeStruct((4, length // BLOCK), jnp.int32),
        ],
        in_specs=[smem, HBM, HBM, HBM] + [pl.BlockSpec(memory_space=pl.ANY)] * len(waits),
        out_specs=[spec] * 4 + [smem],
        scratch_shapes=landing([ids, pads, offsets]),
        compiler_params=limit(LIMITS[0]),
        cost_estimate=cost(3 * 10**9, 4 * 2**20),
        name="tables",
    )(where, *in_hbm([ids, pads, offsets]), *waits)


def project_kernel(fused, own, there, cosine, sine, key_aux, query_aux, *refs):
    if fused:
        pieces = 1 << bit_groups(fused[0])[0][1]
        where, mine, other = refs[0], refs[1 : 1 + pieces], refs[1 + pieces : 1 + 2 * pieces]
        qa, ka, va, kt, vt, w, gains, stage = refs[-11:-3]
        copies = fetch((own, there), refs[-3:-1], refs[-1])
        own, there = refs[-3:-1]
        unpack(*fused, where, mine, other, stage, None)
        for i in range(9):
            w[:, i * LANES : (i + 1) * LANES] = stage[i * D : (i + 1) * D].astype(bf16)
        gains[...] = stage[9 * D : 10 * D].T[:8]
        arrive(copies)
    else:
        w_in, gains_in, (qa, ka, va, kt, vt, w, gains) = *refs[:2], refs[-7:]
        w[...] = w_in[...]
        gains[...] = gains_in[...]
    low = lax.broadcasted_iota(jnp.int32, (WIDE, LANES), 1) < HD
    lane = lax.broadcasted_iota(jnp.int32, (WIDE, LANES), 1)
    value_extra = jnp.where((lane >= HD) & (lane < HD + 3), 1.0, 0.0)
    ones = jnp.ones((8, WIDE), bf16)
    blocks = own.shape[0] // WIDE

    def body(step, carry, source, base):
        rows, keys = block(step, WIDE), block(base + step, WIDE)
        x = source[rows, :].astype(f32)
        normed = (x * row_scale(x) * gains[0:1, :]).astype(bf16)
        cos, sin = cosine[keys, :], sine[keys, :]
        first = 0 if base == 0 else D
        products = dot(normed, w[:, first:], NN)
        products = [
            products[:, i * LANES - first : (i + 1) * LANES - first]
            for i in range(first // LANES, 9)
        ]
        if base == 0:
            query_extra = query_aux[rows, :].astype(f32)
            for pair in range(HEADS // 2):
                z = products[pair]
                z = (z * cos + swap_halves(z) * sin).astype(bf16).astype(f32) * HD**-0.5
                qa[2 * pair, rows, :] = jnp.where(low, z, query_extra).astype(bf16)
                qa[2 * pair + 1, rows, :] = jnp.where(
                    low, pltpu.roll(z, HD, 1), query_extra
                ).astype(bf16)
        key_extra = key_aux[keys, :].astype(f32)
        for pair in range(HEADS // 2):
            z = products[pair - 6]
            z = z * cos + swap_halves(z) * sin
            ka[2 * pair, keys, :] = jnp.where(low, z, key_extra).astype(bf16)
            ka[2 * pair + 1, keys, :] = jnp.where(
                low, pltpu.roll(z, HD, 1), key_extra
            ).astype(bf16)
            turned = z.T.astype(bf16)
            kt[2 * pair, :, keys] = turned[:HD]
            kt[2 * pair + 1, :, keys] = turned[HD:]
        for pair in range(HEADS // 2):
            z = products[pair - 3]
            va[2 * pair, keys, :] = jnp.where(low, z, value_extra).astype(bf16)
            va[2 * pair + 1, keys, :] = jnp.where(
                low, pltpu.roll(z, HD, 1), value_extra
            ).astype(bf16)
            turned = z.T.astype(bf16)
            for i in range(2):
                vt[2 * pair + i, :HD, keys] = turned[i * HD : (i + 1) * HD]
                vt[2 * pair + i, HD:, keys] = ones
        return carry

    lax.fori_loop(0, blocks, partial(body, source=own, base=0), 0)
    lax.fori_loop(0, blocks, partial(body, source=there, base=blocks), 0)


def project(own, there, cosine, sine, key_aux, query_aux, weights, fused, waits):
    length = own.shape[0]
    whole = 2 * length
    scratch, specs = [], [VMEM] * 6
    weight_specs = [VMEM] * 2
    if fused:
        specs = [HBM, ANY] + [VMEM] * 4
        weight_specs = [SMEM] + [VMEM] * (len(weights) - 1)
        scratch = [pltpu.VMEM((10 * D, LANES), f32)] + landing([own, there])
    if fused:
        (own,) = in_hbm([own])
    return pl.pallas_call(
        partial(project_kernel, fused),
        out_shape=[
            in_vmem((HEADS, length, LANES), bf16),
            in_vmem((HEADS, whole, LANES), bf16),
            in_vmem((HEADS, whole, LANES), bf16),
            in_vmem((HEADS, HD, whole), bf16),
            in_vmem((HEADS, HD + 8, whole), bf16),
            in_vmem((D, 3 * D), bf16),
            in_vmem((8, D), f32),
        ],
        in_specs=specs + weight_specs + [ANY] * len(waits),
        out_specs=[VMEM] * 7,
        scratch_shapes=scratch,
        compiler_params=limit(LIMITS[1]),
        cost_estimate=cost(9 * 10**9, 16 * 2**20),
        name="project",
    )(own, there, cosine, sine, key_aux, query_aux, *weights, *waits)


def key_block(ranges, step, n):
    return jnp.where(n < ranges[1, step], ranges[0, step] + n, ranges[2, step] + n)


def attend_kernel(ranges, qa, ka, vt, *refs):
    mixed, exact, qb, total, peak = refs[-5:]
    lane = lax.broadcasted_iota(jnp.int32, (BLOCK, LANES), 1)

    def one(step, carry):
        queries = block(step)
        peak[...] = jnp.full((HEADS, 8, BLOCK), -3e38, f32)
        total[...] = jnp.zeros_like(total)

        def body(n, carry):
            rows = block(key_block(ranges, step, n))
            scores = [dot(ka[h, rows, :], qa[h, queries, :], NT) for h in range(HEADS)]
            weights = []
            for h in range(HEADS):
                old = peak[h][:1]
                new = jnp.maximum(old, jnp.max(scores[h], axis=0, keepdims=True))
                weights.append((jnp.exp(scores[h] - new).astype(bf16), jnp.exp(old - new)))
                peak[h] = jnp.broadcast_to(new, (8, BLOCK))
            for h in range(HEADS):
                weight, shrink = weights[h]
                total[h] = total[h] * shrink + dot(vt[h, :, rows], weight, NN)
            return carry

        lax.fori_loop(0, ranges[3, step], body, 0)
        means, pieces = [], []
        for h in range(HEADS):
            bottom = total[h][HD : HD + 1]
            means.append(total[h][:HD] / bottom)
            logs = -(peak[h][:1] + jnp.log(bottom))
            pieces.extend(piece.astype(f32) for piece in split_three(logs))
        for pair in range(HEADS // 2):
            both = jnp.concatenate(means[2 * pair : 2 * pair + 2], axis=0).T
            mixed[queries, pair * LANES : (pair + 1) * LANES] = both.astype(bf16)
            exact[queries, pair * LANES : (pair + 1) * LANES] = both
        table = jnp.concatenate(
            [jnp.zeros((HD + 8, BLOCK), f32)]
            + pieces
            + [jnp.zeros((LANES - HD - 8 - 3 * HEADS, BLOCK), f32)],
            axis=0,
        ).T
        for h in range(HEADS):
            start = HD + 8 + 3 * h
            qb[h, queries, :] = jnp.where(
                (lane >= start) & (lane < start + 3), table, qa[h, queries, :].astype(f32)
            ).astype(bf16)
        return carry

    lax.fori_loop(0, qa.shape[1] // BLOCK, one, 0)


def attend(ranges, qa, ka, vt, waits):
    heads, length, _ = qa.shape
    return pl.pallas_call(
        attend_kernel,
        out_shape=[
            in_vmem((length, D), bf16),
            in_vmem((length, D), f32),
            in_vmem(qa.shape, bf16),
        ],
        in_specs=[SMEM] + [VMEM] * 3 + [ANY] * len(waits),
        out_specs=[VMEM] * 3,
        scratch_shapes=[
            pltpu.VMEM((heads, HD + 8, BLOCK), f32),
            pltpu.VMEM((heads, 8, BLOCK), f32),
        ],
        compiler_params=limit(LIMITS[2]),
        cost_estimate=cost(18 * 10**9, 12 * 2**20),
        name="attend",
    )(ranges, qa, ka, vt, *waits)


def attend_back_kernel(ranges, qb, ka, da, va, kt, *refs):
    dq, sums, there, acc = refs[-4:]
    sums[...] = jnp.zeros_like(sums)
    zero = jnp.zeros((BLOCK, HD), bf16)

    def one(step, carry):
        queries = block(step)
        acc[...] = jnp.zeros_like(acc)

        def body(n, carry):
            rows = block(key_block(ranges, step, n))
            first = [
                (
                    dot(ka[h, rows, :], qb[h, queries, :], NT),
                    dot(va[h, rows, :], da[h, queries, :], NT),
                )
                for h in range(HEADS)
            ]
            second = []
            for scores, grads in first:
                probs = jnp.exp(scores)
                second.append((probs.astype(bf16), (probs * grads).astype(bf16)))
            for h in range(HEADS):
                probs_low, grads_low = second[h]
                grad_side = jnp.concatenate([da[h, queries, :HD], zero], axis=1)
                query_side = jnp.concatenate([zero, qb[h, queries, :HD]], axis=1)
                sums[h, rows, :] += dot(probs_low, grad_side, NN) + dot(grads_low, query_side, NN)
                acc[h] += dot(kt[h, :, rows], grads_low, NN)
            return carry

        lax.fori_loop(0, ranges[3, step], body, 0)
        for h in range(HEADS):
            dq[h, :, queries] = acc[h]
        return carry

    length = qb.shape[1]
    lax.fori_loop(0, length // BLOCK, one, 0)
    there[...] = sums[:, length:, :].astype(bf16)


def attend_back(ranges, qb, ka, da, va, kt, waits):
    heads, length, _ = qb.shape
    whole = ka.shape[1]
    return pl.pallas_call(
        attend_back_kernel,
        out_shape=[
            in_vmem((heads, HD, length), f32),
            in_vmem((heads, whole, LANES), f32),
            jax.ShapeDtypeStruct((heads, whole - length, LANES), bf16),
        ],
        in_specs=[SMEM] + [VMEM] * 5 + [ANY] * len(waits),
        out_specs=[VMEM] * 3,
        scratch_shapes=[pltpu.VMEM((heads, HD, BLOCK), f32)],
        compiler_params=limit(LIMITS[4]),
        cost_estimate=cost(34 * 10**9, 8 * 2**20),
        name="attend_back",
    )(ranges, qb, ka, da, va, kt, *waits)


FEED = 1024


def feed_kernel(fused, own, mixed, exact, cotangent, query_aux, gains, *refs):
    if fused:
        pieces = fan = 1 << bit_groups(fused[0])[0][1]
        where, mine, other = refs[0], refs[1 : 1 + pieces], refs[1 + pieces : 1 + 2 * pieces]
        refs = refs[1 + 2 * pieces :]
        result, grad_middle, da, gives = *refs[:3], refs[3 : 3 + fan]
        normed_all, low_all, hidden_all, up_all, middle_all, wo, wgu, wd, g_gain, sums = refs[
            3 + fan : 13 + fan
        ]
        copies = fetch((own, cotangent), refs[13 + fan : 15 + fan], refs[-1])
        own, cotangent = refs[13 + fan : 15 + fan]
    else:
        wo, wgu, wd = refs[:3]
        result, grad_middle, da, g_out, g_gate_up, g_down, g_gain = refs[3:10]
        normed_all, low_all, hidden_all, up_all, middle_all = refs[10:]
    gain = gains[1:2, :]
    g_gain[...] = jnp.zeros_like(g_gain)
    if fused:
        unpack(*fused, where, mine, other, sums, wd)
        for i in range(3):
            wo[:, i * LANES : (i + 1) * LANES] = sums[i * D : (i + 1) * D].astype(bf16)
        for i in range(16):
            wgu[:, i * LANES : (i + 1) * LANES] = sums[(3 + i) * D : (4 + i) * D].astype(bf16)
        arrive(copies)

    chunks = FF // BLOCK
    lane = lax.broadcasted_iota(jnp.int32, (FEED, LANES), 1)

    def body(step, carry):
        rows = block(step, FEED)
        x = own[rows, :].astype(f32)
        middle = x + dot(mixed[rows, :], wo[...], NN)
        scale = row_scale(middle)
        normed = (middle * scale * gain).astype(bf16)
        normed_all[rows, :] = normed
        kept = query_aux[rows, :].astype(f32)[:, KEEP_LANE : KEEP_LANE + 1]
        upstream = cotangent[rows, :].astype(f32) * kept
        up_low = upstream.astype(bf16)
        up_all[rows, :] = up_low
        gates = [dot(normed, wgu[:, c * BLOCK : (c + 1) * BLOCK], NN) for c in range(chunks)]
        ups = [dot(normed, wgu[:, FF + c * BLOCK : FF + (c + 1) * BLOCK], NN) for c in range(chunks)]
        hiddens = [dot(up_low, wd[c * BLOCK : (c + 1) * BLOCK, :], NT) for c in range(chunks)]
        for c in range(chunks):
            gate, up, grad_hidden = gates[c], ups[c], hiddens[c]
            sig = 1.0 / (1.0 + jnp.exp(-gate))
            silu = gate * sig
            hidden_all[rows, c * BLOCK : (c + 1) * BLOCK] = (silu * up).astype(bf16)
            low_all[rows, FF + c * BLOCK : FF + (c + 1) * BLOCK] = (grad_hidden * silu).astype(bf16)
            low_all[rows, c * BLOCK : (c + 1) * BLOCK] = (
                grad_hidden * up * (sig + silu * (1.0 - sig))
            ).astype(bf16)
        ffn = dot(hidden_all[rows, :], wd[...], NN)
        grad_normed = dot(low_all[rows, :], wgu[...], NT)
        result[rows, :] = (kept * (middle + ffn)).astype(bf16)
        g_gain[0:1, :] += jnp.sum(grad_normed * middle * scale, axis=0, keepdims=True)
        grad = upstream + norm_back(grad_normed * gain, middle, scale)
        grad_middle[rows, :] = grad
        low = grad.astype(bf16)
        middle_all[rows, :] = low
        grad_mixed = dot(low, wo[...], NT).astype(bf16).astype(f32)
        products = grad_mixed * exact[rows, :]
        for h in range(HEADS):
            pair = h // 2
            head = grad_mixed[:, pair * LANES : (pair + 1) * LANES]
            product = products[:, pair * LANES : (pair + 1) * LANES]
            mine_lanes = (lane < HD) if h % 2 == 0 else (lane >= HD)
            delta = -jnp.sum(jnp.where(mine_lanes, product, 0.0), axis=1, keepdims=True)
            if h % 2:
                head = pltpu.roll(head, HD, 1)
            high, mid, last = split_three(delta)
            extra = jnp.where(
                lane == HD,
                high.astype(f32),
                jnp.where(
                    lane == HD + 1,
                    mid.astype(f32),
                    jnp.where(lane == HD + 2, last.astype(f32), 0.0),
                ),
            )
            da[h, rows, :] = jnp.where(lane < HD, head, extra).astype(bf16)
        return carry

    lax.fori_loop(0, own.shape[0] // FEED, body, 0)
    if not fused:
        g_out[...] = dot(mixed[...], middle_all[...], TN)
        for c in range(2 * FF // 512):
            g_gate_up[:, c * 512 : (c + 1) * 512] = dot(
                normed_all[...], low_all[:, c * 512 : (c + 1) * 512], TN
            )
        for c in range(chunks):
            g_down[c * BLOCK : (c + 1) * BLOCK, :] = dot(
                hidden_all[:, c * BLOCK : (c + 1) * BLOCK], up_all[...], TN
            )
        return
    count, number, shard, down = fused

    size = number * shard + 3 * down

    def put(at, value):
        for i in range(value.shape[1] // LANES):
            half, row = divmod(at + i, number)
            for device in range(count):
                start = (half * count + device) * size + row * shard
                sums[start : start + shard, :] = value[
                    device * shard : (device + 1) * shard, i * LANES : (i + 1) * LANES
                ]

    put(0, dot(mixed[...], middle_all[...], TN))
    for c in range(2 * FF // 512):
        put(3 + 4 * c, dot(normed_all[...], low_all[:, c * 512 : (c + 1) * 512], TN))
    put(19, gain_column(g_gain[...]))
    for c in range(chunks):
        value = dot(hidden_all[:, c * BLOCK : (c + 1) * BLOCK], up_all[...], TN)
        for n in range(BLOCK // down):
            device, half = divmod(c * BLOCK // down + n, 2)
            for i in range(3):
                start = (half * count + device) * size + number * shard + i * down
                sums[start : start + down, :] = value[
                    n * down : (n + 1) * down, i * LANES : (i + 1) * LANES
                ]
    me = where[1] & (fan - 1)
    for high in range(count // fan):
        for flip in range(fan):
            for half in range(2):
                start = (half * count + high * fan + (me ^ flip)) * size
                gives[flip][half * (count // fan) + high] = sums[
                    pl.ds(pl.multiple_of(start, 8), size), :
                ].astype(gives[flip].dtype)


def feed(own, mixed, exact, cotangent, query_aux, gains, weights, fused):
    length = own.shape[0]
    scratch = [
        pltpu.VMEM((length, D), bf16),
        pltpu.VMEM((length, 2 * FF), bf16),
        pltpu.VMEM((length, FF), bf16),
        pltpu.VMEM((length, D), bf16),
        pltpu.VMEM((length, D), bf16),
    ]
    out_shape = [
        jax.ShapeDtypeStruct((length, D), bf16),
        in_vmem((length, D), f32),
        in_vmem((HEADS, length, LANES), bf16),
    ]
    if fused:
        count, number, shard, down = fused
        rows = number * shard + 3 * down
        fan = 1 << bit_groups(count)[0][1]
        weight_specs = [SMEM] + [VMEM] * (len(weights) - 1)
        specs = [HBM, VMEM, VMEM, HBM, VMEM, VMEM]
        out_shape += [
            jax.ShapeDtypeStruct((2 * count // fan, rows, LANES), bf16 if flip else f32)
            for flip in range(fan)
        ]
        scratch += [
            pltpu.VMEM((D, D), bf16),
            pltpu.VMEM((D, 2 * FF), bf16),
            pltpu.VMEM((FF, D), bf16),
            pltpu.VMEM((8, D), f32),
            pltpu.VMEM((2 * count * rows, LANES), f32),
        ]
        scratch += landing([own, cotangent])
    else:
        weight_specs = [VMEM] * 3
        specs = [VMEM] * 6
        out_shape += [
            jax.ShapeDtypeStruct((D, D), f32),
            jax.ShapeDtypeStruct((D, 2 * FF), f32),
            jax.ShapeDtypeStruct((FF, D), f32),
            jax.ShapeDtypeStruct((8, D), f32),
        ]
    if fused:
        own, cotangent = in_hbm([own, cotangent])
    return pl.pallas_call(
        partial(feed_kernel, fused),
        out_shape=out_shape,
        in_specs=specs + weight_specs,
        out_specs=[VMEM] * len(out_shape),
        scratch_shapes=scratch,
        compiler_params=limit(LIMITS[3]),
        cost_estimate=cost(14 * 10**9, 16 * 2**20),
        name="feed",
    )(own, mixed, exact, cotangent, query_aux, gains, *weights)


PARTS = ((0, 1, 2), (3, 4, 5, 6, 7, 8))


def project_back_kernel(number, fused, own, cosine, sine, w, gains, *refs):
    part = PARTS[number]
    low = lax.broadcasted_iota(jnp.int32, (WIDE, LANES), 1) < HD
    gain = gains[0:1, :]
    if number == 0:
        dq = refs[0]
        partial_sum, grads, normed_all, low_all = refs[-6:-2]
        copies = fetch((own,), refs[-2:-1], refs[-1])
        own = refs[-2]
    else:
        kept, got, grad_middle, before, grads_before = refs[:5]
        if fused:
            where = refs[5]
            grad_tokens, keep, give, sums, g_gain, normed_all, low_all = refs[-10:-3]
        else:
            grad_tokens, grads, g_gain, normed_all, low_all = refs[-8:-3]
        g_gain[...] = jnp.zeros_like(g_gain)
        copies = fetch((own, got), refs[-3:-1], refs[-1])
        own, got = refs[-3:-1]
    arrive(copies)

    def body(step, carry):
        rows = block(step, WIDE)
        cos, sin = cosine[rows, :], -sine[rows, :]
        x = own[rows, :].astype(f32)
        scale = row_scale(x)
        normed_all[rows, :] = (x * scale * gain).astype(bf16)
        for at, slab in enumerate(part):
            kind, pair = divmod(slab, 3)
            heads = (2 * pair, 2 * pair + 1)
            if kind == 0:
                z = jnp.concatenate([dq[h, :, rows] for h in heads], axis=0).T * HD**-0.5
            else:
                one, two = [kept[h, rows, :] + got[h, rows, :].astype(f32) for h in heads]
                if kind == 1:
                    z = jnp.where(low, pltpu.roll(one, HD, 1), two)
                else:
                    z = jnp.where(low, one, pltpu.roll(two, HD, 1))
            if kind < 2:
                z = z * cos + swap_halves(z) * sin
            low_all[rows, at * LANES : (at + 1) * LANES] = z.astype(bf16)
        first = part[0] * LANES
        grad_normed = dot(
            low_all[rows, :], w[:, first : first + len(part) * LANES], NT
        )
        if number == 0:
            partial_sum[rows, :] = grad_normed
        else:
            grad_normed = grad_normed + before[rows, :]
            g_gain[0:1, :] += jnp.sum(grad_normed * x * scale, axis=0, keepdims=True)
            grad_tokens[rows, :] = (
                grad_middle[rows, :] + norm_back(grad_normed * gain, x, scale)
            ).astype(bf16)
        return carry

    lax.fori_loop(0, own.shape[0] // WIDE, body, 0)
    value = dot(normed_all[...], low_all[...], TN)
    if number == 0 or not fused:
        grads[...] = value
        return
    core = where[0]
    for done, source in ((PARTS[0], grads_before), (PARTS[1], value)):
        for at, slab in enumerate(done):
            put_slab(sums, core, *fused, slab, source[:, at * LANES : (at + 1) * LANES])
    put_slab(sums, core, *fused, 9, gain_column(g_gain[...]))
    keep[...] = sums[0]
    give[...] = sums[1].astype(bf16)


def project_back(number, fused, where, shared, arrays, waits):
    own, cosine, sine, w, gains = shared
    length = own.shape[0]
    columns = len(PARTS[number]) * LANES
    scratch = [pltpu.VMEM((length, D), bf16), pltpu.VMEM((length, columns), bf16)]
    specs = [VMEM] * len(arrays)
    if number:
        specs[1] = ANY
    scratch += landing([own] + list(arrays[1:2]))
    if number == 0:
        out_shape = [in_vmem((length, D), f32), in_vmem((D, columns), f32)]
    elif fused:
        size, shard = fused
        chunk = (D // shard, size * shard, LANES)
        specs.append(SMEM)
        arrays = [*arrays, where]
        out_shape = [
            jax.ShapeDtypeStruct((length, D), bf16),
            jax.ShapeDtypeStruct(chunk, f32),
            jax.ShapeDtypeStruct(chunk, bf16),
        ]
        scratch = [pltpu.VMEM((2,) + chunk, f32), pltpu.VMEM((8, D), f32)] + scratch
    else:
        out_shape = [
            jax.ShapeDtypeStruct((length, D), bf16),
            jax.ShapeDtypeStruct((D, columns), f32),
            jax.ShapeDtypeStruct((8, D), f32),
        ]
    (own,) = in_hbm([own])
    return pl.pallas_call(
        partial(project_back_kernel, number, fused),
        out_shape=out_shape,
        in_specs=[HBM] + [VMEM] * 4 + specs + [ANY] * len(waits),
        out_specs=[VMEM] * len(out_shape),
        scratch_shapes=scratch,
        compiler_params=limit(LIMITS[5]),
        cost_estimate=cost(4 * 10**9, 8 * 2**20),
        name="project_back",
    )(own, cosine, sine, w, gains, *arrays, *waits)


def squares_kernel(*refs):
    total = sum(jnp.sum(ref[...] * ref[...]) for ref in refs[0:4:2]) + 0.0
    other = sum(jnp.sum(ref[...] * ref[...]) for ref in refs[1:4:2]) + 0.0
    refs[4][...] = jnp.full((1, LANES), total + other, f32)


def squares(sums):
    spec = pl.BlockSpec(memory_space=pltpu.VMEM)
    return pl.pallas_call(
        squares_kernel,
        out_shape=jax.ShapeDtypeStruct((1, LANES), f32),
        in_specs=[spec] * 4,
        out_specs=spec,
        compiler_params=limit(16),
        name="squares",
    )(*sums)


def bring_kernel(*refs):
    number = (len(refs) - 1) // 2
    arrive(fetch(refs[:number], refs[-number - 1 : -1], refs[-1]))


def bring(arrays):
    return pl.pallas_call(
        bring_kernel,
        out_shape=[in_vmem(item.shape, item.dtype) for item in arrays],
        in_specs=[HBM] * len(arrays),
        out_specs=[VMEM] * len(arrays),
        scratch_shapes=[pltpu.SemaphoreType.DMA((len(arrays),))],
        compiler_params=limit(1),
        name="bring",
    )(*in_hbm(arrays))


def update_kernel(shard, down, where, total, *refs):
    core = where[0]
    chunks = refs[:4]
    norm = refs[19]
    outs = [refs[20 + 5 * i : 25 + 5 * i] for i in range(4)]
    low, high, square = refs[40:]
    masters, firsts, seconds = refs[4:9], refs[9:14], refs[14:19]
    split = 5 * shard

    @pl.when(core == 0)
    def _():
        for i, target in ((0, low), (1, high)):
            target[:split] = chunks[i][...]
            target[split:] = chunks[2 + i][...]

    @pl.when(core == 1)
    def _():
        for i, target in ((0, high), (1, low)):
            target[:split] = chunks[i][...]
            target[split:] = chunks[2 + i][...]

    length = jnp.sqrt(total[0:1, 0:1])
    norm[...] = length
    factor = clip_limit / jnp.maximum(length, clip_limit)
    halves = (low, high)

    def step(which, grad, rows, columns, rate, decay):
        at = (rows, columns)
        new = adam_update(
            masters[which][at], factor * grad, firsts[which][at], seconds[which][at], rate, decay
        )
        outs[0][which][at] = new[0]
        outs[1][which][at] = new[1]
        outs[2][which][at] = new[2]
        outs[3][which][at] = new[2].astype(bf16)

    every = slice(None)
    places = [(0, i, i // 5, (i % 5) * shard) for i in range(9)]
    for i in range(19):
        which, column = (1, i) if i < 3 else (2, i - 3)
        places.append((which, column, i // 10, (5 + i % 10) * shard))
    for which, column, half, row in places:
        rate = 4.0 * D**-0.5 if which == 1 else D**-0.5
        grad = halves[half][row : row + shard, :]
        step(which, grad, every, slice(column * LANES, (column + 1) * LANES), rate, decay_rate)
    for half in range(2):
        for i in range(3):
            row = 15 * shard + i * down
            step(
                3, halves[half][row : row + down, :], slice(half * down, (half + 1) * down),
                slice(i * LANES, (i + 1) * LANES), FF**-0.5, decay_rate,
            )
    gain_rows = []
    for row in (4 * shard, 14 * shard):
        square[...] = jnp.zeros_like(square)
        square[0:shard, :] = high[row : row + shard, :]
        gain_rows.append(square[...].T[0:1, :shard])
    for i in range(2):
        step(4, gain_rows[i], slice(i, i + 1), every, 0.5, 0.0)


def update(where, total, sums, masters, firsts, seconds):
    shard, down = masters[0].shape[0], masters[3].shape[0] // 2
    spec = pl.BlockSpec(memory_space=pltpu.VMEM)
    shapes = [item.shape for item in masters]
    outs = pl.pallas_call(
        partial(update_kernel, shard, down),
        out_shape=[jax.ShapeDtypeStruct((1, 1), f32)]
        + [jax.ShapeDtypeStruct(shape, f32) for _ in range(3) for shape in shapes]
        + [jax.ShapeDtypeStruct(shape, bf16) for shape in shapes],
        in_specs=[pl.BlockSpec(memory_space=pltpu.SMEM)] + [VMEM] * 20,
        out_specs=[spec] * 21,
        scratch_shapes=[
            pltpu.VMEM((15 * shard + 3 * down, LANES), f32),
            pltpu.VMEM((15 * shard + 3 * down, LANES), f32),
            pltpu.VMEM((LANES, LANES), f32),
        ],
        compiler_params=limit(LIMITS[6]),
        name="update",
    )(where, total, *sums, *masters, *firsts, *seconds)
    return outs[0][0, 0], outs[1:6], outs[6:11], outs[11:16], outs[16:21]


def update_plain(core, total, sums, masters, firsts, seconds):
    shard, down = masters[0].shape[0], masters[3].shape[0] // 2
    mine = jnp.concatenate([sums[0], sums[2]])
    there = jnp.concatenate([sums[1], sums[3]])
    low = jnp.where(core == 0, mine, there)
    high = jnp.where(core == 0, there, mine)
    five, fifteen = 5 * shard, 15 * shard
    first_shard = jnp.concatenate([low[:five], high[:five]]).reshape(10, shard, LANES)
    second_shard = jnp.concatenate([low[five:fifteen], high[five:fifteen]])
    second_shard = second_shard.reshape(20, shard, LANES)
    down_shard = jnp.stack(
        [item[fifteen:].reshape(3, down, LANES) for item in (low, high)], axis=1
    ).reshape(3, 2 * down, LANES)
    shard_grads = (
        unslab(first_shard[:9]),
        unslab(second_shard[:3]),
        unslab(second_shard[3:19]),
        unslab(down_shard),
        jnp.stack([first_shard[9, :, 0], second_shard[19, :, 0]]),
    )
    grad_norm = jnp.sqrt(total[0, 0])
    factor = clip_limit / jnp.maximum(grad_norm, clip_limit)
    rates = (D ** (-0.5), 4.0 * D ** (-0.5), D ** (-0.5), FF ** (-0.5), 0.5)
    decays = (decay_rate, decay_rate, decay_rate, decay_rate, 0.0)
    updates = [
        adam_update(
            masters[i], factor * shard_grads[i], firsts[i], seconds[i], rates[i], decays[i]
        )
        for i in range(5)
    ]
    new_first, new_second, new_master = zip(*updates)
    return grad_norm, new_first, new_second, new_master, [item.astype(bf16) for item in new_master]


def per_device(
    count,
    tokens,
    cotangent,
    sample_ids,
    pad_flags,
    offsets,
    w_qkv,
    w_out,
    w_gate_up,
    w_down,
    gains,
    m_qkv,
    m_out,
    m_gate_up,
    m_down,
    m_gains,
    v_qkv,
    v_out,
    v_gate_up,
    v_down,
    v_gains,
):
    owner = lax.axis_index("batch")
    core = lax.axis_index("tm")
    where = jnp.stack([core, owner]).astype(jnp.int32)
    shard = w_qkv.shape[0]
    down = w_down.shape[0] // 2
    own = tokens[0]
    fuse_in = can_unpack(shard, down)
    masters = (w_qkv, w_out, w_gate_up, w_down, gains)

    first = send_chunk(where, FIRST_PLAN, 0, [w_qkv, gains], [])
    there = swap_tm(own)
    cosine, sine, key_aux, query_aux, ranges = tables(
        where, sample_ids, pad_flags, offsets, [there]
    )
    first_held, first_pieces = gather(first, count, [query_aux])
    second = send_chunk(where, SECOND_PLAN, down, [w_out, w_gate_up, w_down], [first_held])

    def gathered(pieces, number, down):
        others = [swap_tm(piece) for piece in pieces]
        if fuse_in:
            return (where, *pieces, *others), (count, number, shard, down)
        return unpack_plain(count, number, shard, down, where, pieces, others), None

    weights, fused = gathered(first_pieces, 5, 0)
    qa, ka, va, kt, vt, attn_in, gain_pair = project(
        own, there, cosine, sine, key_aux, query_aux, weights, fused, []
    )
    second_held, second_pieces = gather(second, count, [gain_pair])
    mixed, exact, qb = attend(ranges, qa, ka, vt, [second_held])
    second_pieces[1:] = hold(second_pieces[1:], [mixed])
    weights, fused = gathered(second_pieces, 10, down)
    result, grad_middle, da, *grads = feed(
        own, mixed, exact, cotangent[0], query_aux, gain_pair, weights, fused
    )
    groups = bit_groups(count)
    fan = 1 << groups[0][1]

    def flips(halves):
        halves = halves.reshape((-1, fan) + halves.shape[-2:])
        mine = owner & (fan - 1)
        parts = [lax.dynamic_index_in_dim(halves, mine ^ k, 1, keepdims=False) for k in range(fan)]
        return [parts[0]] + [item.astype(bf16) for item in parts[1:]]

    if not fused:
        grads = flips(pack_plain(count, core, grads, 10, shard, down))
    got = [permute_batch(grads[k], k, count) for k in range(1, fan)]
    dq, kept, part = attend_back(ranges, qb, ka, da, va, kt, [])
    fused = (5, shard) if fuse_in else None
    shared = (own, cosine, sine, attn_in, gain_pair)
    before, grads_before = project_back(0, fused, where, shared, [dq], [])
    got = hold(got, [grads_before])
    part_there = swap_tm(hold([part], got)[0])
    left = count // fan
    keep, give = combine(where, [grads[0], *got], (1, 2, left, 0, 0))
    split = None
    if len(groups) > 1:
        split = (left >> groups[1][1], 1 << groups[1][1], 1, 1, groups[1][0])
    parts = combine(where, [keep, swap_tm(give)], split)
    grad_tokens, *grads = project_back(
        1, fused, where, shared, [kept, part_there, grad_middle, before, grads_before], [parts[0]]
    )
    if split:
        parts = [scatter_parts(where, parts, count, groups[1:], [grads[1]])]
    second_sum = parts[0].reshape(-1, LANES)
    if fused:
        kept, given = grads
    else:
        grads = [jnp.concatenate([grads_before, grads[0]], axis=1), grads[1]]
        halves = pack_plain(count, core, grads, 5, shard, 0)
        kept = jnp.where(core == 0, halves[0], halves[1])
        given = jnp.where(core == 0, halves[1], halves[0]).astype(bf16)
    (given,) = hold([given], [second_sum])
    firsts = (m_qkv, m_out, m_gate_up, m_down, m_gains)
    seconds = (v_qkv, v_out, v_gate_up, v_down, v_gains)
    waits = []
    if fuse_in:
        brought = bring([*masters, *firsts, *seconds])
        masters, firsts, seconds = brought[:5], brought[5:10], brought[10:]
        waits = brought[:1]
    parts = combine(where, [kept, swap_tm(given)], (left, fan, 1, 1, 0), waits)
    first_sum = scatter_parts(where, parts, count, groups).reshape(-1, LANES)
    sums = (first_sum, swap_tm(first_sum), second_sum, swap_tm(second_sum))
    total = sum_batch(squares(sums), count)
    if fuse_in:
        updates = update(where, total, sums, masters, firsts, seconds)
    else:
        updates = update_plain(core, total, sums, masters, firsts, seconds)
    grad_norm, new_first, new_second, new_master, copies = updates
    return (
        result[None],
        grad_tokens[None],
        grad_norm,
        *new_first,
        *new_second,
        *new_master,
        *copies,
    )


def solution(mesh):
    in_specs = (
        P("batch", "tm", None),
        P("batch", "tm", None),
        P("batch", None),
        P("batch", None),
        P("batch", None),
        P("batch", None),
        P("batch", None),
        P("batch", None),
        P("batch", None),
        P(None, "batch"),
        P("batch", None),
        P("batch", None),
        P("batch", None),
        P("batch", None),
        P(None, "batch"),
        P("batch", None),
        P("batch", None),
        P("batch", None),
        P("batch", None),
        P(None, "batch"),
    )
    out_specs = (
        P("batch", "tm", None),
        P("batch", "tm", None),
        P(),
        P("batch", None),
        P("batch", None),
        P("batch", None),
        P("batch", None),
        P(None, "batch"),
        P("batch", None),
        P("batch", None),
        P("batch", None),
        P("batch", None),
        P(None, "batch"),
        P("batch", None),
        P("batch", None),
        P("batch", None),
        P("batch", None),
        P(None, "batch"),
        P("batch", None),
        P("batch", None),
        P("batch", None),
        P("batch", None),
        P(None, "batch"),
    )
    return jax.shard_map(
        partial(per_device, mesh.shape["batch"]), mesh=mesh, in_specs=in_specs, out_specs=out_specs, check_vma=False
    )
```

```python
import math
from functools import partial

import jax
import jax.numpy as jnp
from jax import lax
from jax.experimental import pallas as pl
from jax.experimental.pallas import tpu as pltpu
from jax.sharding import PartitionSpec as P

D = 384
FF = 1024
HEADS = 6
HD = 64
STEP = 3


norm_eps = 1e-06
beta_one = 0.5
beta_two = 0.5
adam_eps = 1e-08
decay_rate = 0.1
clip_limit = 1.0
masked_score = -1e30


def adam_update(master, grad, first, second, rate, decay):
    first_new = beta_one * first + (1.0 - beta_one) * grad
    second_new = beta_two * second + (1.0 - beta_two) * grad * grad
    direction = (
        first_new
        / (1.0 - beta_one**STEP)
        / (jnp.sqrt(second_new / (1.0 - beta_two**STEP)) + adam_eps)
    )
    return (first_new, second_new, master - rate * (direction + decay * master))


def bit_groups(count):
    groups = []
    low, bits = 0, count.bit_length() - 1
    while low < bits:
        width = min(2, bits - low)
        groups.append((low, width))
        low += width
    return groups


def permute_batch(value, flip, count):
    return lax.ppermute(value, "batch", [(i, i ^ flip) for i in range(count)])


def swap_tm(value):
    return lax.ppermute(value, "tm", [(0, 1), (1, 0)])


def slabs(matrix):
    rows, columns = matrix.shape
    return matrix.reshape(rows, columns // 128, 128).transpose(1, 0, 2)


def unslab(stack):
    count, rows, _ = stack.shape
    return stack.transpose(1, 0, 2).reshape(rows, count * 128)


bf16 = jnp.bfloat16
f32 = jnp.float32
BLOCK = 256
LANES = 128
KEEP_LANE = 96
LIMITS = (12, 20, 12, 36, 12, 20, 12)
WIDE = 512
NN = (((1,), (0,)), ((), ()))
NT = (((1,), (1,)), ((), ()))
TN = (((0,), (0,)), ((), ()))


def dot(left, right, dims):
    return lax.dot_general(left, right, dims, preferred_element_type=f32)


def cost(flops, moved):
    return pl.CostEstimate(flops=flops, bytes_accessed=moved, transcendentals=0)


def in_vmem(shape, dtype):
    return pltpu.VMEM(tuple(shape), dtype)


VMEM = pl.BlockSpec(memory_space=pltpu.VMEM)
SMEM = pl.BlockSpec(memory_space=pltpu.SMEM)
ANY = pl.BlockSpec(memory_space=pl.ANY)
HBM = pl.BlockSpec(memory_space=pltpu.HBM)


def fetch(sources, targets, semaphores):
    copies = [
        pltpu.make_async_copy(source, target, semaphores.at[i])
        for i, (source, target) in enumerate(zip(sources, targets))
    ]
    for copy in copies:
        copy.start()
    return copies


def landing(arrays):
    return [pltpu.VMEM(item.shape, item.dtype) for item in arrays] + [
        pltpu.SemaphoreType.DMA((len(arrays),))
    ]


def arrive(copies):
    for copy in copies:
        copy.wait()


def limit(mebibytes):
    return pltpu.CompilerParams(vmem_limit_bytes=mebibytes * 2**20)


def block(start, size=BLOCK):
    return pl.ds(pl.multiple_of(start * size, size), size)


def sum_batch(value, count):
    value = jnp.broadcast_to(value[:, None], (count, 1, LANES))
    value = lax.all_to_all(value, "batch", 0, 0, tiled=True)
    return jnp.sum(value, axis=0)


def row_scale(values):
    return lax.rsqrt(jnp.mean(values * values, axis=-1, keepdims=True) + norm_eps)


def norm_back(grad_normed, values, scale):
    return scale * grad_normed - values * scale * scale * scale * jnp.mean(
        grad_normed * values, axis=-1, keepdims=True
    )


def split_three(values):
    high = values.astype(bf16)
    rest = values - high.astype(f32)
    middle = rest.astype(bf16)
    return high, middle, (rest - middle.astype(f32)).astype(bf16)


def swap_halves(pair):
    lane = lax.broadcasted_iota(jnp.int32, pair.shape, 1)
    return jnp.where(lane % HD < HD // 2, pltpu.roll(pair, 96, 1), pltpu.roll(pair, 32, 1))


def relative_place(device, owner, count):
    flips = device ^ owner
    place, scale = 0, 1
    for low, width in reversed(bit_groups(count)):
        place = place + ((flips >> low) & ((1 << width) - 1)) * scale
        scale <<= width
    return place


def exchange_all(held, low, width, count):
    return [held] + [permute_batch(held, k << low, count) for k in range(1, 1 << width)]


def in_hbm(arrays):
    return [pltpu.with_memory_space_constraint(item, pltpu.HBM) for item in arrays]


def join_kernel(number, *refs):
    out = refs[-1]
    size = refs[0].shape[0]
    for i in range(number):
        out[i * size : (i + 1) * size] = refs[i][...]


def join(pieces, waits=()):
    first = pieces[0]
    shape = (len(pieces) * first.shape[0],) + first.shape[1:]
    return pl.pallas_call(
        partial(join_kernel, len(pieces)),
        out_shape=jax.ShapeDtypeStruct(shape, first.dtype),
        in_specs=[VMEM] * len(pieces) + [ANY] * len(waits),
        out_specs=VMEM,
        compiler_params=limit(4),
        name="join",
    )(*pieces, *waits)


def combine_kernel(number, split, where, *refs):
    items, outs = refs[:number], refs[-len(refs) + number :]
    outs = outs[-(split[1] if split else 1) :]

    def total(index):
        return sum(item[index].astype(f32) for item in items[1:]) + items[0][index].astype(f32)

    if not split:
        outs[0][...] = total(slice(None))
        return
    upper, fan, lower, which, low = split
    mine = (where[which] >> low) & (fan - 1)
    for a in range(upper):
        for b in range(lower):
            for flip in range(fan):
                index = (a * fan + (mine ^ flip)) * lower + b
                outs[flip][a * lower + b] = total(index).astype(outs[flip].dtype)


def combine(where, items, split, waits=()):
    count, rows, _ = items[0].shape
    if split:
        fan = split[1]
        shapes = [
            jax.ShapeDtypeStruct((count // fan, rows, LANES), bf16 if flip else f32)
            for flip in range(fan)
        ]
    else:
        shapes = [jax.ShapeDtypeStruct((count, rows, LANES), f32)]
    return pl.pallas_call(
        partial(combine_kernel, len(items), split),
        out_shape=shapes,
        in_specs=[SMEM] + [VMEM] * len(items) + [ANY] * len(waits),
        out_specs=[VMEM] * len(shapes),
        compiler_params=limit(12),
        name="combine",
    )(where, *items, *waits)


def scatter_parts(where, parts, count, groups, waits=None, before_sum=()):
    for n, (low, width) in enumerate(groups):
        got = [permute_batch(item, k << low, count) for k, item in enumerate(parts) if k]
        if waits and n == 0:
            got = hold(got, waits)
        split = None
        if n + 1 < len(groups):
            fan = 1 << groups[n + 1][1]
            split = (parts[0].shape[0] // fan, fan, 1, 1, groups[n + 1][0])
        parts = combine(where, [parts[0], *got], split, () if n else before_sum)
    return parts[0]


def hold(values, waits):
    spec = pl.BlockSpec(memory_space=pl.ANY)
    number = len(values)
    return pl.pallas_call(
        lambda *refs: None,
        out_shape=[jax.ShapeDtypeStruct(item.shape, item.dtype) for item in values],
        in_specs=[spec] * (number + len(waits)),
        out_specs=[spec] * number,
        input_output_aliases={i: i for i in range(number)},
        compiler_params=limit(1),
        name="hold",
    )(*values, *waits)


def send_kernel(shard, plan, down, where, *refs):
    number = (len(refs) - 4) // 2
    target, stage, square = refs[number : number + 3]
    sources = refs[number + 3 : -1]
    arrive(fetch(refs[:number], sources, refs[-1]))
    number = len(plan) // 2
    core = where[0]
    stage[...] = jnp.zeros_like(stage)
    gain_at = [i for i, item in enumerate(plan) if item == "gain"]
    if gain_at:
        square[...] = jnp.zeros_like(square)
        square[0:2, 0:shard] = sources[-1][...]
        column = square[...].T

    def fill(half):
        for i in range(number):
            item = plan[half * number + i]
            rows = slice(i * shard, (i + 1) * shard)
            if item == "gain":
                stage[rows, :] = column[:shard]
            elif item is not None:
                which, at = item
                stage[rows, :] = sources[which][:, at * LANES : (at + 1) * LANES]
        for i in range(3 if down else 0):
            start = number * shard + i * down
            stage[start : start + down, :] = sources[2][
                half * down : (half + 1) * down, i * LANES : (i + 1) * LANES
            ]

    @pl.when(core == 0)
    def _():
        fill(0)

    @pl.when(core == 1)
    def _():
        fill(1)

    target[...] = stage[...].astype(bf16)


def send_chunk(where, plan, down, sources, waits):
    shard = sources[0].shape[0]
    rows = len(plan) // 2 * shard + 3 * down
    rows = -(-rows // 16) * 16
    core = where[0]
    if shard % 8 == 0 and down % 8 == 0:
        spec = VMEM

        def kernel(where, *refs):
            kept = refs[: len(sources)] + refs[len(sources) + len(waits) :]
            send_kernel(shard, plan, down, where, *kept)

        return pl.pallas_call(
            kernel,
            out_shape=jax.ShapeDtypeStruct((rows, LANES), bf16),
            in_specs=[SMEM] + [HBM] * len(sources) + [ANY] * len(waits),
            out_specs=spec,
            scratch_shapes=[pltpu.VMEM((rows, LANES), f32), pltpu.VMEM((LANES, LANES), f32)]
            + landing(sources),
            compiler_params=limit(6),
            name="send_chunk",
        )(where, *in_hbm(sources), *waits)
    stacks = {i: slabs(item) for i, item in enumerate(sources) if item.shape[1] % LANES == 0}
    pieces = []
    for item in plan:
        if item == "gain":
            pieces.append(jnp.pad(sources[-1].T, ((0, 0), (0, LANES - 2))))
        elif item is None:
            pieces.append(jnp.zeros((shard, LANES), f32))
        else:
            pieces.append(stacks[item[0]][item[1]])
    half = len(plan) // 2
    halves = [jnp.concatenate(pieces[:half]), jnp.concatenate(pieces[half:])]
    if down:
        for i in range(2):
            part = stacks[2][:, i * down : (i + 1) * down].reshape(3 * down, LANES)
            halves[i] = jnp.concatenate([halves[i], part])
    chunk = jnp.where(core == 0, halves[0], halves[1]).astype(bf16)
    return jnp.pad(chunk, ((0, rows - chunk.shape[0]), (0, 0)))


FIRST_PLAN = tuple((0, i) for i in range(9)) + ("gain",)
SECOND_PLAN = tuple((0, i) for i in range(3)) + tuple((1, i) for i in range(16)) + (None,)


def gather(chunk, count, waits):
    held = chunk[None]
    groups = bit_groups(count)[::-1]
    for n, (low, width) in enumerate(groups):
        pieces = exchange_all(held, low, width, count)
        if n + 1 < len(groups):
            held = join(pieces, () if n else waits)
    return held, pieces


def unpack(count, number, shard, down, where, pieces, others, stage, w_down):
    core, owner = where[0], where[1]
    last = bit_groups(count)[0][1]
    for sources, half in ((pieces, core), (others, 1 - core)):
        for flip, source in enumerate(sources):

            def one(n, carry, source=source, half=half, flip=flip):
                device = owner ^ flip ^ (relative_flips(n, count) << last)
                chunk = source[n].astype(f32)
                for i in range(number):
                    start = (half * number + i) * D + device * shard
                    stage[pl.ds(pl.multiple_of(start, 8), shard), :] = chunk[
                        i * shard : (i + 1) * shard
                    ]
                for i in range(3 if down else 0):
                    start = number * shard + i * down
                    rows = pl.ds(pl.multiple_of((device * 2 + half) * down, 16), down)
                    w_down[rows, i * LANES : (i + 1) * LANES] = chunk[start : start + down].astype(
                        bf16
                    )
                return carry

            lax.fori_loop(0, source.shape[0], one, 0, unroll=True)


def relative_flips(place, count):
    last = bit_groups(count)[0][1]
    flips, scale = 0, 1
    for low, width in reversed(bit_groups(count)[1:]):
        flips = flips + (((place // scale) & ((1 << width) - 1)) << (low - last))
        scale <<= width
    return flips


def can_unpack(shard, down):
    return shard % 8 == 0 and down % 16 == 0


def unpack_plain(count, number, shard, down, where, mine, other):
    core, owner = where[0], where[1]
    places = relative_place(jnp.arange(count, dtype=jnp.int32), owner, count)
    mine, other = jnp.concatenate(mine), jnp.concatenate(other)
    low = jnp.take(jnp.where(core == 0, mine, other), places, axis=0)
    high = jnp.take(jnp.where(core == 0, other, mine), places, axis=0)

    def part(source):
        return (
            source[:, : number * shard]
            .reshape(count, number, shard, LANES)
            .transpose(1, 0, 2, 3)
            .reshape(number, D, LANES)
        )

    stack = jnp.concatenate([part(low), part(high)], axis=0)
    if number == 5:
        return unslab(stack[:9]), stack[9].T[:8].astype(f32)
    downs = [
        item[:, number * shard : number * shard + 3 * down].reshape(count, 3, down, LANES)
        for item in (low, high)
    ]
    w_down = jnp.stack(downs, axis=1).transpose(0, 1, 3, 2, 4).reshape(FF, D)
    return unslab(stack[:3]), unslab(stack[3:19]), w_down


def put_slab(stage, core, number, shard, at, slab):
    half, row = at // number, (at % number) * shard
    slot = core if half == 0 else 1 - core
    stage[slot, :, row : row + shard, :] = slab.reshape(-1, shard, LANES)


def gain_column(row):
    return jnp.concatenate([row, jnp.zeros((LANES - 8, D), f32)], axis=0).T


def pack_plain(count, core, grads, number, shard, down):
    column = jnp.pad(grads[-1][:1].T, ((0, 0), (0, LANES - 1)))[None]
    stack = jnp.concatenate([slabs(item) for item in (grads[:2] if down else grads[:1])] + [column])

    def by_device(part):
        return (
            part.reshape(number, count, shard, LANES)
            .transpose(1, 0, 2, 3)
            .reshape(count, number * shard, LANES)
        )

    halves = [by_device(stack[:number]), by_device(stack[number:])]
    if down:
        downs = (
            slabs(grads[2])
            .reshape(3, count, 2, down, LANES)
            .transpose(2, 1, 0, 3, 4)
            .reshape(2, count, 3 * down, LANES)
        )
        halves = [jnp.concatenate([halves[i], downs[i]], axis=1) for i in range(2)]
    return jnp.stack(halves)


def tables_kernel(length, where, ids, pads, offsets, *refs):
    cosine, sine, key_aux, query_aux, ranges = refs[-9:-4]
    copies = fetch((ids, pads, offsets), refs[-4:-1], refs[-1])
    ids, pads, offsets = refs[-4:-1]
    arrive(copies)
    core = where[0]
    whole = 2 * length

    def turn(row):
        low, high = row[:, :length], row[:, length:]
        return jnp.concatenate(
            [jnp.where(core == 0, low, high), jnp.where(core == 0, high, low)], axis=1
        )

    classes = (2 * ids[...] + pads[...]).astype(f32)
    spot = lax.broadcasted_iota(jnp.int32, (1, whole), 1)
    position = (turn(spot) + turn(offsets[...])).astype(f32)
    turned = turn(classes)
    index = lax.broadcasted_iota(jnp.int32, (HD // 2, whole), 0).astype(f32)
    angle = position * jnp.exp(index * (-2.0 * math.log(10000.0) / HD))
    cos, sin = jnp.cos(angle), jnp.sin(angle)
    cosine[...] = jnp.concatenate([cos, cos, cos, cos], axis=0).T
    sine[...] = jnp.concatenate([-sin, sin, -sin, sin], axis=0).T
    at = lax.broadcasted_iota(jnp.int32, (LANES, whole), 0)
    is_class = (at >= HD) & (at < HD + 8)
    same = (at - HD).astype(f32) == turned
    is_log = (at >= HD + 8) & (at < HD + 8 + 3 * HEADS)
    key_aux[...] = jnp.where((is_class & same) | is_log, 1.0, 0.0).T.astype(bf16)
    own = turned[:, :length]
    kept = jnp.where(turn(pads[...])[:, :length] == 0, 1.0, 0.0)
    extra = jnp.where(is_class & ~same, masked_score, 0.0)[:, :length]
    query_aux[...] = jnp.where(at[:, :length] == KEEP_LANE, kept, extra).T.astype(bf16)
    starts = (core * length, (1 - core) * length)
    for n in range(length // BLOCK):
        mine = own[:, n * BLOCK : (n + 1) * BLOCK]
        first = jnp.min(mine)
        last = jnp.max(mine)
        low_key = jnp.sum(jnp.where(classes < first, 1.0, 0.0)).astype(jnp.int32)
        high_key = jnp.sum(jnp.where(classes <= last, 1.0, 0.0)).astype(jnp.int32)
        bounds = []
        for start in starts:
            low_part = jnp.clip(low_key - start, 0, length)
            high_part = jnp.clip(high_key - start, 0, length)
            low_block = low_part // BLOCK
            bounds.append((low_block, jnp.maximum((high_part + BLOCK - 1) // BLOCK - low_block, 0)))
        ranges[0, n] = bounds[0][0]
        ranges[1, n] = bounds[0][1]
        ranges[2, n] = bounds[1][0] + length // BLOCK - bounds[0][1]
        ranges[3, n] = bounds[0][1] + bounds[1][1]


def tables(where, ids, pads, offsets, waits):
    whole = ids.shape[1]
    length = whole // 2
    spec = pl.BlockSpec(memory_space=pltpu.VMEM)
    smem = pl.BlockSpec(memory_space=pltpu.SMEM)
    return pl.pallas_call(
        partial(tables_kernel, length),
        out_shape=[
            in_vmem((whole, LANES), f32),
            in_vmem((whole, LANES), f32),
            in_vmem((whole, LANES), bf16),
            in_vmem((length, LANES), bf16),
            jax.ShapeDtypeStruct((4, length // BLOCK), jnp.int32),
        ],
        in_specs=[smem, HBM, HBM, HBM] + [pl.BlockSpec(memory_space=pl.ANY)] * len(waits),
        out_specs=[spec] * 4 + [smem],
        scratch_shapes=landing([ids, pads, offsets]),
        compiler_params=limit(LIMITS[0]),
        cost_estimate=cost(3 * 10**9, 4 * 2**20),
        name="tables",
    )(where, *in_hbm([ids, pads, offsets]), *waits)


def project_kernel(fused, own, there, cosine, sine, key_aux, query_aux, *refs):
    if fused:
        pieces = 1 << bit_groups(fused[0])[0][1]
        where, mine, other = refs[0], refs[1 : 1 + pieces], refs[1 + pieces : 1 + 2 * pieces]
        qa, ka, va, kt, vt, w, gains, stage = refs[-11:-3]
        copies = fetch((own, there), refs[-3:-1], refs[-1])
        own, there = refs[-3:-1]
        unpack(*fused, where, mine, other, stage, None)
        for i in range(9):
            w[:, i * LANES : (i + 1) * LANES] = stage[i * D : (i + 1) * D].astype(bf16)
        gains[...] = stage[9 * D : 10 * D].T[:8]
        arrive(copies)
    else:
        w_in, gains_in, (qa, ka, va, kt, vt, w, gains) = *refs[:2], refs[-7:]
        w[...] = w_in[...]
        gains[...] = gains_in[...]
    low = lax.broadcasted_iota(jnp.int32, (WIDE, LANES), 1) < HD
    lane = lax.broadcasted_iota(jnp.int32, (WIDE, LANES), 1)
    value_extra = jnp.where((lane >= HD) & (lane < HD + 3), 1.0, 0.0)
    ones = jnp.ones((8, WIDE), bf16)
    blocks = own.shape[0] // WIDE

    def body(step, carry, source, base):
        rows, keys = block(step, WIDE), block(base + step, WIDE)
        x = source[rows, :].astype(f32)
        normed = (x * row_scale(x) * gains[0:1, :]).astype(bf16)
        cos, sin = cosine[keys, :], sine[keys, :]
        first = 0 if base == 0 else D
        products = dot(normed, w[:, first:], NN)
        products = [
            products[:, i * LANES - first : (i + 1) * LANES - first]
            for i in range(first // LANES, 9)
        ]
        if base == 0:
            query_extra = query_aux[rows, :].astype(f32)
            for pair in range(HEADS // 2):
                z = products[pair]
                z = (z * cos + swap_halves(z) * sin).astype(bf16).astype(f32) * HD**-0.5
                qa[2 * pair, rows, :] = jnp.where(low, z, query_extra).astype(bf16)
                qa[2 * pair + 1, rows, :] = jnp.where(
                    low, pltpu.roll(z, HD, 1), query_extra
                ).astype(bf16)
        key_extra = key_aux[keys, :].astype(f32)
        for pair in range(HEADS // 2):
            z = products[pair - 6]
            z = z * cos + swap_halves(z) * sin
            ka[2 * pair, keys, :] = jnp.where(low, z, key_extra).astype(bf16)
            ka[2 * pair + 1, keys, :] = jnp.where(
                low, pltpu.roll(z, HD, 1), key_extra
            ).astype(bf16)
            turned = z.T.astype(bf16)
            kt[2 * pair, :, keys] = turned[:HD]
            kt[2 * pair + 1, :, keys] = turned[HD:]
        for pair in range(HEADS // 2):
            z = products[pair - 3]
            va[2 * pair, keys, :] = jnp.where(low, z, value_extra).astype(bf16)
            va[2 * pair + 1, keys, :] = jnp.where(
                low, pltpu.roll(z, HD, 1), value_extra
            ).astype(bf16)
            turned = z.T.astype(bf16)
            for i in range(2):
                vt[2 * pair + i, :HD, keys] = turned[i * HD : (i + 1) * HD]
                vt[2 * pair + i, HD:, keys] = ones
        return carry

    lax.fori_loop(0, blocks, partial(body, source=own, base=0), 0)
    lax.fori_loop(0, blocks, partial(body, source=there, base=blocks), 0)


def project(own, there, cosine, sine, key_aux, query_aux, weights, fused, waits):
    length = own.shape[0]
    whole = 2 * length
    scratch, specs = [], [VMEM] * 6
    weight_specs = [VMEM] * 2
    if fused:
        specs = [HBM, ANY] + [VMEM] * 4
        weight_specs = [SMEM] + [VMEM] * (len(weights) - 1)
        scratch = [pltpu.VMEM((10 * D, LANES), f32)] + landing([own, there])
    if fused:
        (own,) = in_hbm([own])
    return pl.pallas_call(
        partial(project_kernel, fused),
        out_shape=[
            in_vmem((HEADS, length, LANES), bf16),
            in_vmem((HEADS, whole, LANES), bf16),
            in_vmem((HEADS, whole, LANES), bf16),
            in_vmem((HEADS, HD, whole), bf16),
            in_vmem((HEADS, HD + 8, whole), bf16),
            in_vmem((D, 3 * D), bf16),
            in_vmem((8, D), f32),
        ],
        in_specs=specs + weight_specs + [ANY] * len(waits),
        out_specs=[VMEM] * 7,
        scratch_shapes=scratch,
        compiler_params=limit(LIMITS[1]),
        cost_estimate=cost(9 * 10**9, 16 * 2**20),
        name="project",
    )(own, there, cosine, sine, key_aux, query_aux, *weights, *waits)


def key_block(ranges, step, n):
    return jnp.where(n < ranges[1, step], ranges[0, step] + n, ranges[2, step] + n)


def attend_kernel(ranges, qa, ka, vt, *refs):
    mixed, exact, qb, total, peak = refs[-5:]
    lane = lax.broadcasted_iota(jnp.int32, (BLOCK, LANES), 1)

    def one(step, carry):
        queries = block(step)
        peak[...] = jnp.full((HEADS, 8, BLOCK), -3e38, f32)
        total[...] = jnp.zeros_like(total)

        def body(n, carry):
            rows = block(key_block(ranges, step, n))
            scores = [dot(ka[h, rows, :], qa[h, queries, :], NT) for h in range(HEADS)]
            weights = []
            for h in range(HEADS):
                old = peak[h][:1]
                new = jnp.maximum(old, jnp.max(scores[h], axis=0, keepdims=True))
                weights.append((jnp.exp(scores[h] - new).astype(bf16), jnp.exp(old - new)))
                peak[h] = jnp.broadcast_to(new, (8, BLOCK))
            for h in range(HEADS):
                weight, shrink = weights[h]
                total[h] = total[h] * shrink + dot(vt[h, :, rows], weight, NN)
            return carry

        lax.fori_loop(0, ranges[3, step], body, 0)
        means, pieces = [], []
        for h in range(HEADS):
            bottom = total[h][HD : HD + 1]
            means.append(total[h][:HD] / bottom)
            logs = -(peak[h][:1] + jnp.log(bottom))
            pieces.extend(piece.astype(f32) for piece in split_three(logs))
        for pair in range(HEADS // 2):
            both = jnp.concatenate(means[2 * pair : 2 * pair + 2], axis=0).T
            mixed[queries, pair * LANES : (pair + 1) * LANES] = both.astype(bf16)
            exact[queries, pair * LANES : (pair + 1) * LANES] = both
        table = jnp.concatenate(
            [jnp.zeros((HD + 8, BLOCK), f32)]
            + pieces
            + [jnp.zeros((LANES - HD - 8 - 3 * HEADS, BLOCK), f32)],
            axis=0,
        ).T
        for h in range(HEADS):
            start = HD + 8 + 3 * h
            qb[h, queries, :] = jnp.where(
                (lane >= start) & (lane < start + 3), table, qa[h, queries, :].astype(f32)
            ).astype(bf16)
        return carry

    lax.fori_loop(0, qa.shape[1] // BLOCK, one, 0)


def attend(ranges, qa, ka, vt, waits):
    heads, length, _ = qa.shape
    return pl.pallas_call(
        attend_kernel,
        out_shape=[
            in_vmem((length, D), bf16),
            in_vmem((length, D), f32),
            in_vmem(qa.shape, bf16),
        ],
        in_specs=[SMEM] + [VMEM] * 3 + [ANY] * len(waits),
        out_specs=[VMEM] * 3,
        scratch_shapes=[
            pltpu.VMEM((heads, HD + 8, BLOCK), f32),
            pltpu.VMEM((heads, 8, BLOCK), f32),
        ],
        compiler_params=limit(LIMITS[2]),
        cost_estimate=cost(18 * 10**9, 12 * 2**20),
        name="attend",
    )(ranges, qa, ka, vt, *waits)


def attend_back_kernel(ranges, qb, ka, da, va, kt, *refs):
    dq, sums, there, acc = refs[-4:]
    sums[...] = jnp.zeros_like(sums)
    zero = jnp.zeros((BLOCK, HD), bf16)

    def one(step, carry):
        queries = block(step)
        acc[...] = jnp.zeros_like(acc)

        def body(n, carry):
            rows = block(key_block(ranges, step, n))
            first = [
                (
                    dot(ka[h, rows, :], qb[h, queries, :], NT),
                    dot(va[h, rows, :], da[h, queries, :], NT),
                )
                for h in range(HEADS)
            ]
            second = []
            for scores, grads in first:
                probs = jnp.exp(scores)
                second.append((probs.astype(bf16), (probs * grads).astype(bf16)))
            for h in range(HEADS):
                probs_low, grads_low = second[h]
                grad_side = jnp.concatenate([da[h, queries, :HD], zero], axis=1)
                query_side = jnp.concatenate([zero, qb[h, queries, :HD]], axis=1)
                sums[h, rows, :] += dot(probs_low, grad_side, NN) + dot(grads_low, query_side, NN)
                acc[h] += dot(kt[h, :, rows], grads_low, NN)
            return carry

        lax.fori_loop(0, ranges[3, step], body, 0)
        for h in range(HEADS):
            dq[h, :, queries] = acc[h]
        return carry

    length = qb.shape[1]
    lax.fori_loop(0, length // BLOCK, one, 0)
    there[...] = sums[:, length:, :].astype(bf16)


def attend_back(ranges, qb, ka, da, va, kt, waits):
    heads, length, _ = qb.shape
    whole = ka.shape[1]
    return pl.pallas_call(
        attend_back_kernel,
        out_shape=[
            in_vmem((heads, HD, length), f32),
            in_vmem((heads, whole, LANES), f32),
            jax.ShapeDtypeStruct((heads, whole - length, LANES), bf16),
        ],
        in_specs=[SMEM] + [VMEM] * 5 + [ANY] * len(waits),
        out_specs=[VMEM] * 3,
        scratch_shapes=[pltpu.VMEM((heads, HD, BLOCK), f32)],
        compiler_params=limit(LIMITS[4]),
        cost_estimate=cost(34 * 10**9, 8 * 2**20),
        name="attend_back",
    )(ranges, qb, ka, da, va, kt, *waits)


FEED = 1024


def feed_kernel(fused, own, mixed, exact, cotangent, query_aux, gains, *refs):
    if fused:
        pieces = fan = 1 << bit_groups(fused[0])[0][1]
        where, mine, other = refs[0], refs[1 : 1 + pieces], refs[1 + pieces : 1 + 2 * pieces]
        refs = refs[1 + 2 * pieces :]
        result, grad_middle, da, gives = *refs[:3], refs[3 : 3 + fan]
        normed_all, low_all, hidden_all, up_all, middle_all, wo, wgu, wd, g_gain, sums = refs[
            3 + fan : 13 + fan
        ]
        copies = fetch((own, cotangent), refs[13 + fan : 15 + fan], refs[-1])
        own, cotangent = refs[13 + fan : 15 + fan]
    else:
        wo, wgu, wd = refs[:3]
        result, grad_middle, da, g_out, g_gate_up, g_down, g_gain = refs[3:10]
        normed_all, low_all, hidden_all, up_all, middle_all = refs[10:]
    gain = gains[1:2, :]
    g_gain[...] = jnp.zeros_like(g_gain)
    if fused:
        unpack(*fused, where, mine, other, sums, wd)
        for i in range(3):
            wo[:, i * LANES : (i + 1) * LANES] = sums[i * D : (i + 1) * D].astype(bf16)
        for i in range(16):
            wgu[:, i * LANES : (i + 1) * LANES] = sums[(3 + i) * D : (4 + i) * D].astype(bf16)
        arrive(copies)

    chunks = FF // BLOCK
    lane = lax.broadcasted_iota(jnp.int32, (FEED, LANES), 1)

    def body(step, carry):
        rows = block(step, FEED)
        x = own[rows, :].astype(f32)
        middle = x + dot(mixed[rows, :], wo[...], NN)
        scale = row_scale(middle)
        normed = (middle * scale * gain).astype(bf16)
        normed_all[rows, :] = normed
        kept = query_aux[rows, :].astype(f32)[:, KEEP_LANE : KEEP_LANE + 1]
        upstream = cotangent[rows, :].astype(f32) * kept
        up_low = upstream.astype(bf16)
        up_all[rows, :] = up_low
        gates = [dot(normed, wgu[:, c * BLOCK : (c + 1) * BLOCK], NN) for c in range(chunks)]
        ups = [dot(normed, wgu[:, FF + c * BLOCK : FF + (c + 1) * BLOCK], NN) for c in range(chunks)]
        hiddens = [dot(up_low, wd[c * BLOCK : (c + 1) * BLOCK, :], NT) for c in range(chunks)]
        for c in range(chunks):
            gate, up, grad_hidden = gates[c], ups[c], hiddens[c]
            sig = 1.0 / (1.0 + jnp.exp(-gate))
            silu = gate * sig
            hidden_all[rows, c * BLOCK : (c + 1) * BLOCK] = (silu * up).astype(bf16)
            low_all[rows, FF + c * BLOCK : FF + (c + 1) * BLOCK] = (grad_hidden * silu).astype(bf16)
            low_all[rows, c * BLOCK : (c + 1) * BLOCK] = (
                grad_hidden * up * (sig + silu * (1.0 - sig))
            ).astype(bf16)
        ffn = dot(hidden_all[rows, :], wd[...], NN)
        grad_normed = dot(low_all[rows, :], wgu[...], NT)
        result[rows, :] = (kept * (middle + ffn)).astype(bf16)
        g_gain[0:1, :] += jnp.sum(grad_normed * middle * scale, axis=0, keepdims=True)
        grad = upstream + norm_back(grad_normed * gain, middle, scale)
        grad_middle[rows, :] = grad
        low = grad.astype(bf16)
        middle_all[rows, :] = low
        grad_mixed = dot(low, wo[...], NT).astype(bf16).astype(f32)
        products = grad_mixed * exact[rows, :]
        for h in range(HEADS):
            pair = h // 2
            head = grad_mixed[:, pair * LANES : (pair + 1) * LANES]
            product = products[:, pair * LANES : (pair + 1) * LANES]
            mine_lanes = (lane < HD) if h % 2 == 0 else (lane >= HD)
            delta = -jnp.sum(jnp.where(mine_lanes, product, 0.0), axis=1, keepdims=True)
            if h % 2:
                head = pltpu.roll(head, HD, 1)
            high, mid, last = split_three(delta)
            extra = jnp.where(
                lane == HD,
                high.astype(f32),
                jnp.where(
                    lane == HD + 1,
                    mid.astype(f32),
                    jnp.where(lane == HD + 2, last.astype(f32), 0.0),
                ),
            )
            da[h, rows, :] = jnp.where(lane < HD, head, extra).astype(bf16)
        return carry

    lax.fori_loop(0, own.shape[0] // FEED, body, 0)
    if not fused:
        g_out[...] = dot(mixed[...], middle_all[...], TN)
        for c in range(2 * FF // 512):
            g_gate_up[:, c * 512 : (c + 1) * 512] = dot(
                normed_all[...], low_all[:, c * 512 : (c + 1) * 512], TN
            )
        for c in range(chunks):
            g_down[c * BLOCK : (c + 1) * BLOCK, :] = dot(
                hidden_all[:, c * BLOCK : (c + 1) * BLOCK], up_all[...], TN
            )
        return
    count, number, shard, down = fused

    size = number * shard + 3 * down

    def put(at, value):
        for i in range(value.shape[1] // LANES):
            half, row = divmod(at + i, number)
            for device in range(count):
                start = (half * count + device) * size + row * shard
                sums[start : start + shard, :] = value[
                    device * shard : (device + 1) * shard, i * LANES : (i + 1) * LANES
                ]

    put(0, dot(mixed[...], middle_all[...], TN))
    for c in range(2 * FF // 512):
        put(3 + 4 * c, dot(normed_all[...], low_all[:, c * 512 : (c + 1) * 512], TN))
    put(19, gain_column(g_gain[...]))
    for c in range(chunks):
        value = dot(hidden_all[:, c * BLOCK : (c + 1) * BLOCK], up_all[...], TN)
        for n in range(BLOCK // down):
            device, half = divmod(c * BLOCK // down + n, 2)
            for i in range(3):
                start = (half * count + device) * size + number * shard + i * down
                sums[start : start + down, :] = value[
                    n * down : (n + 1) * down, i * LANES : (i + 1) * LANES
                ]
    me = where[1] & (fan - 1)
    for high in range(count // fan):
        for flip in range(fan):
            for half in range(2):
                start = (half * count + high * fan + (me ^ flip)) * size
                gives[flip][half * (count // fan) + high] = sums[
                    pl.ds(pl.multiple_of(start, 8), size), :
                ].astype(gives[flip].dtype)


def feed(own, mixed, exact, cotangent, query_aux, gains, weights, fused):
    length = own.shape[0]
    scratch = [
        pltpu.VMEM((length, D), bf16),
        pltpu.VMEM((length, 2 * FF), bf16),
        pltpu.VMEM((length, FF), bf16),
        pltpu.VMEM((length, D), bf16),
        pltpu.VMEM((length, D), bf16),
    ]
    out_shape = [
        jax.ShapeDtypeStruct((length, D), bf16),
        in_vmem((length, D), f32),
        in_vmem((HEADS, length, LANES), bf16),
    ]
    if fused:
        count, number, shard, down = fused
        rows = number * shard + 3 * down
        fan = 1 << bit_groups(count)[0][1]
        weight_specs = [SMEM] + [VMEM] * (len(weights) - 1)
        specs = [HBM, VMEM, VMEM, HBM, VMEM, VMEM]
        out_shape += [
            jax.ShapeDtypeStruct((2 * count // fan, rows, LANES), bf16 if flip else f32)
            for flip in range(fan)
        ]
        scratch += [
            pltpu.VMEM((D, D), bf16),
            pltpu.VMEM((D, 2 * FF), bf16),
            pltpu.VMEM((FF, D), bf16),
            pltpu.VMEM((8, D), f32),
            pltpu.VMEM((2 * count * rows, LANES), f32),
        ]
        scratch += landing([own, cotangent])
    else:
        weight_specs = [VMEM] * 3
        specs = [VMEM] * 6
        out_shape += [
            jax.ShapeDtypeStruct((D, D), f32),
            jax.ShapeDtypeStruct((D, 2 * FF), f32),
            jax.ShapeDtypeStruct((FF, D), f32),
            jax.ShapeDtypeStruct((8, D), f32),
        ]
    if fused:
        own, cotangent = in_hbm([own, cotangent])
    return pl.pallas_call(
        partial(feed_kernel, fused),
        out_shape=out_shape,
        in_specs=specs + weight_specs,
        out_specs=[VMEM] * len(out_shape),
        scratch_shapes=scratch,
        compiler_params=limit(LIMITS[3]),
        cost_estimate=cost(14 * 10**9, 16 * 2**20),
        name="feed",
    )(own, mixed, exact, cotangent, query_aux, gains, *weights)


PARTS = ((0, 1, 2), (3, 4, 5, 6, 7, 8))


def project_back_kernel(number, fused, own, cosine, sine, w, gains, *refs):
    part = PARTS[number]
    low = lax.broadcasted_iota(jnp.int32, (WIDE, LANES), 1) < HD
    gain = gains[0:1, :]
    if number == 0:
        dq = refs[0]
        partial_sum, grads, normed_all, low_all = refs[-6:-2]
        copies = fetch((own,), refs[-2:-1], refs[-1])
        own = refs[-2]
    else:
        kept, got, grad_middle, before, grads_before = refs[:5]
        if fused:
            where = refs[5]
            grad_tokens, keep, give, sums, g_gain, normed_all, low_all = refs[-10:-3]
        else:
            grad_tokens, grads, g_gain, normed_all, low_all = refs[-8:-3]
        g_gain[...] = jnp.zeros_like(g_gain)
        copies = fetch((own, got), refs[-3:-1], refs[-1])
        own, got = refs[-3:-1]
    arrive(copies)

    def body(step, carry):
        rows = block(step, WIDE)
        cos, sin = cosine[rows, :], -sine[rows, :]
        x = own[rows, :].astype(f32)
        scale = row_scale(x)
        normed_all[rows, :] = (x * scale * gain).astype(bf16)
        for at, slab in enumerate(part):
            kind, pair = divmod(slab, 3)
            heads = (2 * pair, 2 * pair + 1)
            if kind == 0:
                z = jnp.concatenate([dq[h, :, rows] for h in heads], axis=0).T * HD**-0.5
            else:
                one, two = [kept[h, rows, :] + got[h, rows, :].astype(f32) for h in heads]
                if kind == 1:
                    z = jnp.where(low, pltpu.roll(one, HD, 1), two)
                else:
                    z = jnp.where(low, one, pltpu.roll(two, HD, 1))
            if kind < 2:
                z = z * cos + swap_halves(z) * sin
            low_all[rows, at * LANES : (at + 1) * LANES] = z.astype(bf16)
        first = part[0] * LANES
        grad_normed = dot(
            low_all[rows, :], w[:, first : first + len(part) * LANES], NT
        )
        if number == 0:
            partial_sum[rows, :] = grad_normed
        else:
            grad_normed = grad_normed + before[rows, :]
            g_gain[0:1, :] += jnp.sum(grad_normed * x * scale, axis=0, keepdims=True)
            grad_tokens[rows, :] = (
                grad_middle[rows, :] + norm_back(grad_normed * gain, x, scale)
            ).astype(bf16)
        return carry

    lax.fori_loop(0, own.shape[0] // WIDE, body, 0)
    value = dot(normed_all[...], low_all[...], TN)
    if number == 0 or not fused:
        grads[...] = value
        return
    core = where[0]
    for done, source in ((PARTS[0], grads_before), (PARTS[1], value)):
        for at, slab in enumerate(done):
            put_slab(sums, core, *fused, slab, source[:, at * LANES : (at + 1) * LANES])
    put_slab(sums, core, *fused, 9, gain_column(g_gain[...]))
    keep[...] = sums[0]
    give[...] = sums[1].astype(bf16)


def project_back(number, fused, where, shared, arrays, waits):
    own, cosine, sine, w, gains = shared
    length = own.shape[0]
    columns = len(PARTS[number]) * LANES
    scratch = [pltpu.VMEM((length, D), bf16), pltpu.VMEM((length, columns), bf16)]
    specs = [VMEM] * len(arrays)
    if number:
        specs[1] = ANY
    scratch += landing([own] + list(arrays[1:2]))
    if number == 0:
        out_shape = [in_vmem((length, D), f32), in_vmem((D, columns), f32)]
    elif fused:
        size, shard = fused
        chunk = (D // shard, size * shard, LANES)
        specs.append(SMEM)
        arrays = [*arrays, where]
        out_shape = [
            jax.ShapeDtypeStruct((length, D), bf16),
            jax.ShapeDtypeStruct(chunk, f32),
            jax.ShapeDtypeStruct(chunk, bf16),
        ]
        scratch = [pltpu.VMEM((2,) + chunk, f32), pltpu.VMEM((8, D), f32)] + scratch
    else:
        out_shape = [
            jax.ShapeDtypeStruct((length, D), bf16),
            jax.ShapeDtypeStruct((D, columns), f32),
            jax.ShapeDtypeStruct((8, D), f32),
        ]
    (own,) = in_hbm([own])
    return pl.pallas_call(
        partial(project_back_kernel, number, fused),
        out_shape=out_shape,
        in_specs=[HBM] + [VMEM] * 4 + specs + [ANY] * len(waits),
        out_specs=[VMEM] * len(out_shape),
        scratch_shapes=scratch,
        compiler_params=limit(LIMITS[5]),
        cost_estimate=cost(4 * 10**9, 8 * 2**20),
        name="project_back",
    )(own, cosine, sine, w, gains, *arrays, *waits)


def squares_kernel(*refs):
    total = sum(jnp.sum(ref[...] * ref[...]) for ref in refs[0:4:2]) + 0.0
    other = sum(jnp.sum(ref[...] * ref[...]) for ref in refs[1:4:2]) + 0.0
    refs[4][...] = jnp.full((1, LANES), total + other, f32)


def squares(sums):
    spec = pl.BlockSpec(memory_space=pltpu.VMEM)
    return pl.pallas_call(
        squares_kernel,
        out_shape=jax.ShapeDtypeStruct((1, LANES), f32),
        in_specs=[spec] * 4,
        out_specs=spec,
        compiler_params=limit(16),
        name="squares",
    )(*sums)


def bring_kernel(*refs):
    number = (len(refs) - 1) // 2
    arrive(fetch(refs[:number], refs[-number - 1 : -1], refs[-1]))


def bring(arrays):
    return pl.pallas_call(
        bring_kernel,
        out_shape=[in_vmem(item.shape, item.dtype) for item in arrays],
        in_specs=[HBM] * len(arrays),
        out_specs=[VMEM] * len(arrays),
        scratch_shapes=[pltpu.SemaphoreType.DMA((len(arrays),))],
        compiler_params=limit(1),
        name="bring",
    )(*in_hbm(arrays))


def update_kernel(shard, down, where, total, *refs):
    core = where[0]
    chunks = refs[:4]
    norm = refs[19]
    outs = [refs[20 + 5 * i : 25 + 5 * i] for i in range(4)]
    low, high, square = refs[40:]
    masters, firsts, seconds = refs[4:9], refs[9:14], refs[14:19]
    split = 5 * shard

    @pl.when(core == 0)
    def _():
        for i, target in ((0, low), (1, high)):
            target[:split] = chunks[i][...]
            target[split:] = chunks[2 + i][...]

    @pl.when(core == 1)
    def _():
        for i, target in ((0, high), (1, low)):
            target[:split] = chunks[i][...]
            target[split:] = chunks[2 + i][...]

    length = jnp.sqrt(total[0:1, 0:1])
    norm[...] = length
    factor = clip_limit / jnp.maximum(length, clip_limit)
    halves = (low, high)

    def step(which, grad, rows, columns, rate, decay):
        at = (rows, columns)
        new = adam_update(
            masters[which][at], factor * grad, firsts[which][at], seconds[which][at], rate, decay
        )
        outs[0][which][at] = new[0]
        outs[1][which][at] = new[1]
        outs[2][which][at] = new[2]
        outs[3][which][at] = new[2].astype(bf16)

    every = slice(None)
    places = [(0, i, i // 5, (i % 5) * shard) for i in range(9)]
    for i in range(19):
        which, column = (1, i) if i < 3 else (2, i - 3)
        places.append((which, column, i // 10, (5 + i % 10) * shard))
    for which, column, half, row in places:
        rate = 4.0 * D**-0.5 if which == 1 else D**-0.5
        grad = halves[half][row : row + shard, :]
        step(which, grad, every, slice(column * LANES, (column + 1) * LANES), rate, decay_rate)
    for half in range(2):
        for i in range(3):
            row = 15 * shard + i * down
            step(
                3, halves[half][row : row + down, :], slice(half * down, (half + 1) * down),
                slice(i * LANES, (i + 1) * LANES), FF**-0.5, decay_rate,
            )
    gain_rows = []
    for row in (4 * shard, 14 * shard):
        square[...] = jnp.zeros_like(square)
        square[0:shard, :] = high[row : row + shard, :]
        gain_rows.append(square[...].T[0:1, :shard])
    for i in range(2):
        step(4, gain_rows[i], slice(i, i + 1), every, 0.5, 0.0)


def update(where, total, sums, masters, firsts, seconds):
    shard, down = masters[0].shape[0], masters[3].shape[0] // 2
    spec = pl.BlockSpec(memory_space=pltpu.VMEM)
    shapes = [item.shape for item in masters]
    outs = pl.pallas_call(
        partial(update_kernel, shard, down),
        out_shape=[jax.ShapeDtypeStruct((1, 1), f32)]
        + [jax.ShapeDtypeStruct(shape, f32) for _ in range(3) for shape in shapes]
        + [jax.ShapeDtypeStruct(shape, bf16) for shape in shapes],
        in_specs=[pl.BlockSpec(memory_space=pltpu.SMEM)] + [VMEM] * 20,
        out_specs=[spec] * 21,
        scratch_shapes=[
            pltpu.VMEM((15 * shard + 3 * down, LANES), f32),
            pltpu.VMEM((15 * shard + 3 * down, LANES), f32),
            pltpu.VMEM((LANES, LANES), f32),
        ],
        compiler_params=limit(LIMITS[6]),
        name="update",
    )(where, total, *sums, *masters, *firsts, *seconds)
    return outs[0][0, 0], outs[1:6], outs[6:11], outs[11:16], outs[16:21]


def update_plain(core, total, sums, masters, firsts, seconds):
    shard, down = masters[0].shape[0], masters[3].shape[0] // 2
    mine = jnp.concatenate([sums[0], sums[2]])
    there = jnp.concatenate([sums[1], sums[3]])
    low = jnp.where(core == 0, mine, there)
    high = jnp.where(core == 0, there, mine)
    five, fifteen = 5 * shard, 15 * shard
    first_shard = jnp.concatenate([low[:five], high[:five]]).reshape(10, shard, LANES)
    second_shard = jnp.concatenate([low[five:fifteen], high[five:fifteen]])
    second_shard = second_shard.reshape(20, shard, LANES)
    down_shard = jnp.stack(
        [item[fifteen:].reshape(3, down, LANES) for item in (low, high)], axis=1
    ).reshape(3, 2 * down, LANES)
    shard_grads = (
        unslab(first_shard[:9]),
        unslab(second_shard[:3]),
        unslab(second_shard[3:19]),
        unslab(down_shard),
        jnp.stack([first_shard[9, :, 0], second_shard[19, :, 0]]),
    )
    grad_norm = jnp.sqrt(total[0, 0])
    factor = clip_limit / jnp.maximum(grad_norm, clip_limit)
    rates = (D ** (-0.5), 4.0 * D ** (-0.5), D ** (-0.5), FF ** (-0.5), 0.5)
    decays = (decay_rate, decay_rate, decay_rate, decay_rate, 0.0)
    updates = [
        adam_update(
            masters[i], factor * shard_grads[i], firsts[i], seconds[i], rates[i], decays[i]
        )
        for i in range(5)
    ]
    new_first, new_second, new_master = zip(*updates)
    return grad_norm, new_first, new_second, new_master, [item.astype(bf16) for item in new_master]


def per_device(
    count,
    tokens,
    cotangent,
    sample_ids,
    pad_flags,
    offsets,
    w_qkv,
    w_out,
    w_gate_up,
    w_down,
    gains,
    m_qkv,
    m_out,
    m_gate_up,
    m_down,
    m_gains,
    v_qkv,
    v_out,
    v_gate_up,
    v_down,
    v_gains,
):
    owner = lax.axis_index("batch")
    core = lax.axis_index("tm")
    where = jnp.stack([core, owner]).astype(jnp.int32)
    shard = w_qkv.shape[0]
    down = w_down.shape[0] // 2
    own = tokens[0]
    fuse_in = can_unpack(shard, down)
    masters = (w_qkv, w_out, w_gate_up, w_down, gains)

    first = send_chunk(where, FIRST_PLAN, 0, [w_qkv, gains], [])
    there = swap_tm(own)
    cosine, sine, key_aux, query_aux, ranges = tables(
        where, sample_ids, pad_flags, offsets, [there]
    )
    first_held, first_pieces = gather(first, count, [query_aux])
    second = send_chunk(where, SECOND_PLAN, down, [w_out, w_gate_up, w_down], [first_held])

    def gathered(pieces, number, down):
        others = [swap_tm(piece) for piece in pieces]
        if fuse_in:
            return (where, *pieces, *others), (count, number, shard, down)
        return unpack_plain(count, number, shard, down, where, pieces, others), None

    weights, fused = gathered(first_pieces, 5, 0)
    qa, ka, va, kt, vt, attn_in, gain_pair = project(
        own, there, cosine, sine, key_aux, query_aux, weights, fused, []
    )
    second_held, second_pieces = gather(second, count, [gain_pair])
    mixed, exact, qb = attend(ranges, qa, ka, vt, [second_held])
    second_pieces[1:] = hold(second_pieces[1:], [mixed])
    weights, fused = gathered(second_pieces, 10, down)
    result, grad_middle, da, *grads = feed(
        own, mixed, exact, cotangent[0], query_aux, gain_pair, weights, fused
    )
    groups = bit_groups(count)
    fan = 1 << groups[0][1]

    def flips(halves):
        halves = halves.reshape((-1, fan) + halves.shape[-2:])
        mine = owner & (fan - 1)
        parts = [lax.dynamic_index_in_dim(halves, mine ^ k, 1, keepdims=False) for k in range(fan)]
        return [parts[0]] + [item.astype(bf16) for item in parts[1:]]

    if not fused:
        grads = flips(pack_plain(count, core, grads, 10, shard, down))
    got = [permute_batch(grads[k], k, count) for k in range(1, fan)]
    dq, kept, part = attend_back(ranges, qb, ka, da, va, kt, [])
    fused = (5, shard) if fuse_in else None
    shared = (own, cosine, sine, attn_in, gain_pair)
    before, grads_before = project_back(0, fused, where, shared, [dq], [])
    got = hold(got, [grads_before])
    part_there = swap_tm(hold([part], got)[0])
    left = count // fan
    keep, give = combine(where, [grads[0], *got], (1, 2, left, 0, 0))
    split = None
    if len(groups) > 1:
        split = (left >> groups[1][1], 1 << groups[1][1], 1, 1, groups[1][0])
    parts = combine(where, [keep, swap_tm(give)], split)
    grad_tokens, *grads = project_back(
        1, fused, where, shared, [kept, part_there, grad_middle, before, grads_before], [parts[0]]
    )
    if split:
        parts = [scatter_parts(where, parts, count, groups[1:], [grads[1]])]
    second_sum = parts[0].reshape(-1, LANES)
    if fused:
        kept, given = grads
    else:
        grads = [jnp.concatenate([grads_before, grads[0]], axis=1), grads[1]]
        halves = pack_plain(count, core, grads, 5, shard, 0)
        kept = jnp.where(core == 0, halves[0], halves[1])
        given = jnp.where(core == 0, halves[1], halves[0]).astype(bf16)
    (given,) = hold([given], [second_sum])
    firsts = (m_qkv, m_out, m_gate_up, m_down, m_gains)
    seconds = (v_qkv, v_out, v_gate_up, v_down, v_gains)
    waits = []
    if fuse_in:
        brought = bring([*masters, *firsts, *seconds])
        masters, firsts, seconds = brought[:5], brought[5:10], brought[10:]
        waits = brought[:1]
    parts = combine(where, [kept, swap_tm(given)], (left, fan, 1, 1, 0))
    first_sum = scatter_parts(where, parts, count, groups, None, waits).reshape(-1, LANES)
    sums = (first_sum, swap_tm(first_sum), second_sum, swap_tm(second_sum))
    total = sum_batch(squares(sums), count)
    if fuse_in:
        updates = update(where, total, sums, masters, firsts, seconds)
    else:
        updates = update_plain(core, total, sums, masters, firsts, seconds)
    grad_norm, new_first, new_second, new_master, copies = updates
    return (
        result[None],
        grad_tokens[None],
        grad_norm,
        *new_first,
        *new_second,
        *new_master,
        *copies,
    )


def solution(mesh):
    in_specs = (
        P("batch", "tm", None),
        P("batch", "tm", None),
        P("batch", None),
        P("batch", None),
        P("batch", None),
        P("batch", None),
        P("batch", None),
        P("batch", None),
        P("batch", None),
        P(None, "batch"),
        P("batch", None),
        P("batch", None),
        P("batch", None),
        P("batch", None),
        P(None, "batch"),
        P("batch", None),
        P("batch", None),
        P("batch", None),
        P("batch", None),
        P(None, "batch"),
    )
    out_specs = (
        P("batch", "tm", None),
        P("batch", "tm", None),
        P(),
        P("batch", None),
        P("batch", None),
        P("batch", None),
        P("batch", None),
        P(None, "batch"),
        P("batch", None),
        P("batch", None),
        P("batch", None),
        P("batch", None),
        P(None, "batch"),
        P("batch", None),
        P("batch", None),
        P("batch", None),
        P("batch", None),
        P(None, "batch"),
        P("batch", None),
        P("batch", None),
        P("batch", None),
        P("batch", None),
        P(None, "batch"),
    )
    return jax.shard_map(
        partial(per_device, mesh.shape["batch"]), mesh=mesh, in_specs=in_specs, out_specs=out_specs, check_vma=False
    )
```
